32 devices in a mesh: groups: 2 (over y), wide: 4 (over z), narrow: 4 (over x, core).
Axes of the slice: x: 2, y: 2, z: 4, core: 2. Of those that a mesh axis runs over, the one named last changes fastest.
Arguments:
- embeddings: bfloat16 [32768, 1024], P(('groups', 'wide'), 'narrow'), parts along dimension 0, may hold values from -6 to 6
- pair_list: int32 [32, 2], P(('groups', 'wide')), parts along dimension 0, may hold values from 0 to 31, as said below
Outputs:
- weights: float32 [32768], P(('groups', 'wide')), parts along dimension 0
- neighbour_mean: bfloat16 [32768, 1024], P(('groups', 'wide'), 'narrow'), parts along dimension 0
The draws below stay inside these ranges and needn't reach their ends.
There are 2 independent parts, one for each index of `groups`. The reference program is written for one: setup_inputs(seed, part) draws one part's arguments, and reference() takes and returns one part's arrays. A program takes and returns all parts, laid end to end along the dimension named above; each array names one. Nothing has to cross between parts.
Inputs may be any that keep to these rules, and one draw needn't show every extreme that they name: `pair_list`: the pairs on the shard of wide index w all have a row block owned by w, that is a // 8 == w. Among those pairs, at most 2 have a column block owned by any one index of wide, and for every w some index of wide owns exactly 2 of them.
All inputs are finite; a program needn't handle non-finite values.
Results may differ from the reference program's by a relative error of at most 0.002.
Values may be sent and summed in bfloat16 or wider, within the bound.
No kernel may reach another device: no remote copies, remote signals or barrier semaphores. Data moves between devices by JAX's collectives and lax.ppermute only.
A program may use at most 64 MiB of HBM per device.

```python
import jax
import jax.numpy as jnp
from jax import lax

F = 1024
BR = 512
BLK_DEV = 8
NBLK = 32
ROWS = 16384
PW = 4
NPAIR = 16
CAP = 2


def draw_pair_list(key, part):
    key = jax.random.fold_in(key, 11)
    owners = NPAIR // PW

    def one_owner(index):
        keys = jax.random.split(jax.random.fold_in(key, index), 5)
        heavy = jax.random.randint(keys[0], (), 0, owners)
        slots = jnp.arange(owners * CAP, dtype=jnp.int32)
        scores = jax.random.permutation(keys[1], owners * CAP).astype(jnp.int32)
        scores = jnp.where(slots // CAP == heavy, -1 - slots, scores)
        order = jnp.argsort(scores, stable=True)[:PW].astype(jnp.int32)
        col_owner = (order // CAP)[jax.random.permutation(keys[2], PW)]
        col_block = col_owner * BLK_DEV + jax.random.randint(keys[3], (PW,), 0, BLK_DEV)
        row_block = index * BLK_DEV + jax.random.randint(keys[4], (PW,), 0, BLK_DEV)
        return jnp.stack([row_block, col_block], axis=-1).astype(jnp.int32)
    return jax.vmap(one_owner)(jnp.arange(owners, dtype=jnp.int32)).reshape(NPAIR, 2)


def shard_levels(rng, extent, pieces, smallest, high):
    level, own = 1.0, jax.random.fold_in(rng, 6)
    for dim, shards_of in pieces:
        draws = jnp.exp(jax.random.uniform(jax.random.fold_in(own, dim), (shards_of,), jnp.float32, smallest / len(pieces), high / len(pieces)))
        level = level * jnp.repeat(draws, extent[dim] // shards_of).reshape([-1 if axis == dim else 1 for axis in range(len(extent))])
    return level


def noise(own_key, extent, spread, most, cuts=(), kind=jnp.bfloat16):
    loudness = shard_levels(own_key, extent, cuts, -0.22, 0.18) if cuts else 1.0
    entries = jax.random.normal(own_key, extent, jnp.float32) * spread * loudness
    return jnp.minimum(jnp.maximum(entries, -most), most).astype(kind)


def setup_inputs(seed: int = 0, part: int = 0) -> dict:
    key_of = jax.random.split(jax.random.key(seed), 3)
    part_splits = jax.random.split(jax.random.fold_in(key_of[2], part), 3)
    embeddings = noise(part_splits[0], (ROWS, F), 1.0, 6.0, ((0, 4), (1, 4)))
    pair_list = draw_pair_list(jax.random.fold_in(jax.random.fold_in(key_of[2], part), 71), part)
    return dict(embeddings=embeddings, pair_list=pair_list)


def reference(embeddings, pair_list):
    blocks = embeddings.reshape(NBLK, BR, F)
    squares = jnp.sum(jnp.square(blocks.astype(jnp.float32)), axis=-1)

    def step(carry, pair):
        row_mass, col_mass, sums = carry
        row_block = pair[0]
        col_block = pair[1]
        left = blocks[row_block]
        right = blocks[col_block]
        gram = jnp.dot(left, right.T, preferred_element_type=jnp.float32)
        dist = squares[row_block][:, None] + squares[col_block][None, :] - 2.0 * gram
        kernel = jnp.exp(-dist / F)
        part = jnp.dot(kernel.astype(jnp.bfloat16), right, preferred_element_type=jnp.float32).astype(jnp.bfloat16)
        part = lax.optimization_barrier(part)
        row_mass = row_mass.at[row_block].add(jnp.sum(kernel, axis=1))
        col_mass = col_mass.at[col_block].add(jnp.sum(kernel, axis=0))
        sums = sums.at[row_block].add(part.astype(jnp.float32))
        return (row_mass, col_mass, sums), None

    start = (jnp.zeros((NBLK, BR), jnp.float32), jnp.zeros((NBLK, BR), jnp.float32), jnp.zeros((NBLK, BR, F), jnp.float32))
    (row_mass, col_mass, sums), unused = lax.scan(step, start, pair_list)
    weights = 1.0 / (1.0 + (row_mass + col_mass) / BR)
    neighbour_mean = (blocks.astype(jnp.float32) + sums) / (1.0 + row_mass)[:, :, None]
    return weights.reshape(ROWS), neighbour_mean.astype(jnp.bfloat16).reshape(ROWS, F)
```

```python
import functools

import jax
import jax.numpy as jnp
from jax import lax
from jax.experimental import pallas as pl
from jax.experimental.pallas import tpu as pltpu
from jax.sharding import PartitionSpec as P

F = 1024
BR = 512
BLK_DEV = 8
CHUNKS = ((0, 256), (256, 128), (384, 128))
VMEM_LIMIT = 48 * 1024 * 1024


def vmem():
    return pl.BlockSpec(memory_space=pltpu.VMEM)


def smem():
    return pl.BlockSpec(memory_space=pltpu.SMEM)


def anywhere():
    return pl.BlockSpec(memory_space=pl.ANY)


def params():
    return pltpu.CompilerParams(vmem_limit_bytes=VMEM_LIMIT)


def pack_kernel(wide_count, pair_count, capacity, me_ref, pairs_ref, blocks_ref, *rest):
    outs, sems = rest[:-1], rest[-1]
    me = me_ref[0]
    copies = []
    for shift in range(1, wide_count):
        target = lax.rem(me + shift, wide_count)
        picks = [jnp.int32(0)] * capacity
        count = jnp.int32(0)
        for pair in range(pair_count):
            col = pairs_ref[target, 2 * pair + 1]
            mine = col // BLK_DEV == me
            local = lax.rem(col, BLK_DEV)
            for slot in range(capacity):
                picks[slot] = jnp.where(mine & (count == slot), local, picks[slot])
            count = count + mine.astype(jnp.int32)
        for chunk, (start, size) in enumerate(CHUNKS):
            out = outs[(shift - 1) * len(CHUNKS) + chunk]
            for slot in range(capacity):
                copies.append(
                    pltpu.make_async_copy(
                        blocks_ref.at[picks[slot], pl.ds(start, size)],
                        out.at[slot],
                        sems.at[len(copies)],
                    )
                )
                copies[-1].start()
    for copy in copies:
        copy.wait()


def pack(me, pairs, blocks, wide_count, pair_count, capacity):
    feat = blocks.shape[-1]
    shapes = [
        jax.ShapeDtypeStruct((capacity, size, feat), blocks.dtype)
        for _ in range(1, wide_count)
        for _, size in CHUNKS
    ]
    return pl.pallas_call(
        functools.partial(pack_kernel, wide_count, pair_count, capacity),
        out_shape=shapes,
        in_specs=[smem(), smem(), anywhere()],
        out_specs=[anywhere()] * len(shapes),
        scratch_shapes=[pltpu.SemaphoreType.DMA((len(shapes) * capacity,))],
        compiler_params=params(),
        name="pack",
    )(me, pairs, blocks)


def select_kernel(wide_count, pair_count, start, size, me_ref, pairs_ref, blocks_ref, *rest):
    received, out_ref, sems = rest[:-2], rest[-2], rest[-1]
    me = me_ref[0]
    owners = [pairs_ref[me, 2 * pair + 1] // BLK_DEV for pair in range(pair_count)]
    for pair in range(pair_count):
        local = lax.rem(pairs_ref[me, 2 * pair + 1], BLK_DEV)
        shift = lax.rem(me - owners[pair] + wide_count, wide_count)
        rank = jnp.int32(0)
        for before in range(pair):
            rank = rank + (owners[before] == owners[pair]).astype(jnp.int32)
        out = out_ref.at[pair]

        @pl.when(shift == 0)
        def _():
            pltpu.make_async_copy(
                blocks_ref.at[local, pl.ds(start, size)], out, sems.at[pair]
            ).start()

        for other in range(1, wide_count):

            @pl.when(shift == other)
            def _():
                pltpu.make_async_copy(received[other - 1].at[rank], out, sems.at[pair]).start()

    for pair in range(pair_count):
        pltpu.make_async_copy(
            blocks_ref.at[0, pl.ds(start, size)], out_ref.at[pair], sems.at[pair]
        ).wait()


def select(me, pairs, blocks, received, wide_count, pair_count, start, size):
    feat = blocks.shape[-1]
    return pl.pallas_call(
        functools.partial(select_kernel, wide_count, pair_count, start, size),
        out_shape=jax.ShapeDtypeStruct((pair_count, size, feat), blocks.dtype),
        in_specs=[smem(), smem()] + [anywhere()] * (1 + len(received)),
        out_specs=anywhere(),
        scratch_shapes=[pltpu.SemaphoreType.DMA((pair_count,))],
        compiler_params=params(),
        name="select",
    )(me, pairs, blocks, *received)


def tree(parts):
    while len(parts) > 1:
        half = len(parts) // 2
        parts = [parts[i] + parts[i + half] for i in range(half)]
    return parts[0]


def across(left, right):
    return lax.dot_general(
        left, right, (((1,), (1,)), ((), ())), preferred_element_type=jnp.float32
    )


def col_square(block):
    square = jnp.square(block.astype(jnp.float32))
    high = square.astype(jnp.bfloat16)
    low = (square - high.astype(jnp.float32)).astype(jnp.bfloat16)
    ones = jnp.ones((8, block.shape[1]), jnp.bfloat16)
    return (across(ones, high) + across(ones, low))[:1]


def kernel_kernel(narrow_count, first, *refs):
    rows = refs[:narrow_count]
    cols = refs[narrow_count : 2 * narrow_count]
    rest = refs[2 * narrow_count :]
    if first:
        kernel_ref, col_ref, mass_ref, square_ref = rest
    else:
        square_ref, before_ref, kernel_ref, col_ref, mass_ref = rest
    for pair in range(rows[0].shape[0]):
        if first:
            square = tree(
                [
                    jnp.sum(jnp.square(row[pair].astype(jnp.float32)), axis=1, keepdims=True)
                    for row in rows
                ]
            )
            square_ref[pair] = square
        else:
            square = square_ref[pair]
        gram = tree([across(row[pair], col[pair]) for row, col in zip(rows, cols)])
        other = tree([col_square(col[pair]) for col in cols])
        kernel = jnp.exp((square + other - 2.0 * gram) * (-1.0 / F))
        kernel_ref[pair] = kernel.astype(jnp.bfloat16)
        col_ref[pair : pair + 1] = jnp.sum(kernel, axis=0, keepdims=True)
        mass = jnp.sum(kernel, axis=1, keepdims=True)
        mass_ref[pair] = mass if first else before_ref[pair] + mass


def kernels(rows, cols, square, before, size):
    pair_count = rows[0].shape[0]
    first = square is None
    column = jax.ShapeDtypeStruct((pair_count, BR, 1), jnp.float32)
    shapes = [
        jax.ShapeDtypeStruct((pair_count, BR, size), jnp.bfloat16),
        jax.ShapeDtypeStruct((pair_count, size), jnp.float32),
        column,
    ] + ([column] if first else [])
    args = [*rows, *cols] + ([] if first else [square, before])
    return pl.pallas_call(
        functools.partial(kernel_kernel, len(rows), first),
        out_shape=shapes,
        in_specs=[vmem()] * len(args),
        out_specs=[vmem()] * len(shapes),
        compiler_params=params(),
        name="kernels",
    )(*args)


def mean_kernel(pair_count, local_ref, *refs):
    chunks = len(CHUNKS)
    kernel_refs, col_refs = refs[:chunks], refs[chunks : 2 * chunks]
    block_ref, mass_ref, out_ref, total, weight = refs[2 * chunks :]
    here = pl.program_id(0)
    total[...] = jnp.zeros_like(total)
    weight[...] = jnp.zeros_like(weight)
    for pair in range(pair_count):

        @pl.when(local_ref[pair] == here)
        def _():
            part = jnp.zeros(total.shape, jnp.float32)
            for kernel_ref, col_ref in zip(kernel_refs, col_refs):
                part = part + jnp.dot(
                    kernel_ref[pair], col_ref[pair], preferred_element_type=jnp.float32
                )
            total[...] += part.astype(jnp.bfloat16).astype(jnp.float32)
            weight[...] += mass_ref[pair]

    mean = (block_ref[0].astype(jnp.float32) + total[...]) / (1.0 + weight[...])
    out_ref[0] = mean.astype(jnp.bfloat16)


def means(row_local, kernel_parts, col_parts, blocks, mass):
    pair_count = mass.shape[0]
    feat = blocks.shape[-1]
    whole = [
        pl.BlockSpec(part.shape, lambda k, local: (0, 0, 0)) for part in [*kernel_parts, *col_parts]
    ]
    block = pl.BlockSpec((1, BR, feat), lambda k, local: (k, 0, 0))
    return pl.pallas_call(
        functools.partial(mean_kernel, pair_count),
        out_shape=jax.ShapeDtypeStruct(blocks.shape, jnp.bfloat16),
        grid_spec=pltpu.PrefetchScalarGridSpec(
            num_scalar_prefetch=1,
            grid=(BLK_DEV,),
            in_specs=[*whole, block, pl.BlockSpec(mass.shape, lambda k, local: (0, 0, 0))],
            out_specs=block,
            scratch_shapes=[
                pltpu.VMEM((BR, feat), jnp.float32),
                pltpu.VMEM((BR, 1), jnp.float32),
            ],
        ),
        compiler_params=params(),
        name="means",
    )(row_local, *kernel_parts, *col_parts, blocks, mass)


def gather_narrow(part):
    count = lax.axis_size("narrow")
    parts = [part]
    step = count // 2
    while step:
        perm = [(i, i ^ step) for i in range(count)]
        parts = parts + [lax.ppermute(x, "narrow", perm) for x in parts]
        step //= 2
    return parts


def on_device(embeddings, pair_list):
    wide_count = lax.axis_size("wide")
    me = lax.axis_index("wide").astype(jnp.int32).reshape(1)
    pair_count = pair_list.shape[0]
    capacity = max(2, 2 * pair_count // wide_count)
    feat = embeddings.shape[1]
    blocks = embeddings.reshape(BLK_DEV, BR, feat)
    row_local = pair_list[:, 0] % BLK_DEV
    rows = gather_narrow(blocks[row_local])
    every_pair = lax.all_gather(pair_list.reshape(1, 2 * pair_count), "wide", axis=0, tiled=True)
    outgoing = pack(me, every_pair, blocks, wide_count, pair_count, capacity)
    kernel_parts, col_parts, col_sums = [], [], []
    square = mass = None
    for chunk, (start, size) in enumerate(CHUNKS):
        received = [
            lax.ppermute(
                outgoing[(shift - 1) * len(CHUNKS) + chunk],
                "wide",
                [(i, (i + shift) % wide_count) for i in range(wide_count)],
            )
            for shift in range(1, wide_count)
        ]
        col_part = select(me, every_pair, blocks, received, wide_count, pair_count, start, size)
        cols = gather_narrow(col_part)
        if chunk == 0:
            kernel, col_sum, mass, square = kernels(rows, cols, None, None, size)
        else:
            kernel, col_sum, mass = kernels(rows, cols, square, mass, size)
        kernel_parts.append(kernel)
        col_parts.append(col_part)
        col_sums.append(col_sum)
    mean = means(row_local, kernel_parts, col_parts, blocks, mass)
    col_sum = jnp.concatenate(col_sums, axis=1)
    every_sum = lax.all_gather(col_sum, "wide", axis=0, tiled=True)
    mine = every_pair.reshape(-1, 2)[:, 1][None, :] == (
        me[0] * BLK_DEV + jnp.arange(BLK_DEV, dtype=jnp.int32)[:, None]
    )
    col_mass = jnp.sum(jnp.where(mine[:, :, None], every_sum[None], 0.0), axis=1)
    here = row_local[None, :] == jnp.arange(BLK_DEV, dtype=jnp.int32)[:, None]
    row_mass = jnp.sum(jnp.where(here[:, :, None], mass.reshape(pair_count, BR)[None], 0.0), axis=1)
    weights = 1.0 / (1.0 + (row_mass + col_mass) / BR)
    return weights.reshape(BLK_DEV * BR), mean.reshape(BLK_DEV * BR, feat)


def solution(mesh):
    in_specs = (P(("groups", "wide"), "narrow"), P(("groups", "wide"), None))
    out_specs = (P(("groups", "wide")), P(("groups", "wide"), "narrow"))
    return jax.shard_map(
        on_device, mesh=mesh, in_specs=in_specs, out_specs=out_specs, check_vma=False
    )
```

```python
import functools

import jax
import jax.numpy as jnp
from jax import lax
from jax.experimental import pallas as pl
from jax.experimental.pallas import tpu as pltpu
from jax.sharding import PartitionSpec as P

F = 1024
BR = 512
BLK_DEV = 8
LANES = 128
CHUNKS = ((0, 384), (384, 128))
VMEM_LIMIT = 48 * 1024 * 1024


def smem():
    return pl.BlockSpec(memory_space=pltpu.SMEM)


def anywhere():
    return pl.BlockSpec(memory_space=pl.ANY)


def params():
    return pltpu.CompilerParams(vmem_limit_bytes=VMEM_LIMIT)


def pack_kernel(wide_count, pair_count, capacity, me_ref, pairs_ref, blocks_ref, *rest):
    outs, rows_ref, sems = rest[: len(CHUNKS)], rest[-2], rest[-1]
    me = me_ref[0]
    copies = []

    def send(source, target):
        copies.append(pltpu.make_async_copy(source, target, sems.at[len(copies)]))
        copies[-1].start()

    for target in range(wide_count):
        picks = [jnp.int32(0)] * capacity
        count = jnp.int32(0)
        for pair in range(pair_count):
            col = pairs_ref[target, 2 * pair + 1]
            mine = (col >> 3) == me
            for slot in range(capacity):
                picks[slot] = jnp.where(mine & (count == slot), col & 7, picks[slot])
            count = count + mine.astype(jnp.int32)
        for slot in range(capacity):
            for out, (start, size) in zip(outs, CHUNKS):
                send(blocks_ref.at[picks[slot], pl.ds(start, size)], out.at[target, slot])
    for pair in range(pair_count):
        send(blocks_ref.at[pairs_ref[me, 2 * pair] & 7], rows_ref.at[pair])
    for copy in copies:
        copy.wait()


def pack(me, pairs, blocks, wide_count, pair_count, capacity):
    feat = blocks.shape[-1]
    shapes = [
        jax.ShapeDtypeStruct((wide_count, capacity, size, feat), blocks.dtype)
        for _, size in CHUNKS
    ] + [jax.ShapeDtypeStruct((pair_count, BR, feat), blocks.dtype)]
    copies = wide_count * capacity * len(CHUNKS) + pair_count
    return pl.pallas_call(
        functools.partial(pack_kernel, wide_count, pair_count, capacity),
        out_shape=shapes,
        in_specs=[smem(), smem(), anywhere()],
        out_specs=[anywhere()] * len(shapes),
        scratch_shapes=[pltpu.SemaphoreType.DMA((copies,))],
        compiler_params=params(),
        name="pack",
    )(me, pairs, blocks)


def select_kernel(pair_count, me_ref, pairs_ref, received_ref, out_ref, sems):
    me = me_ref[0]
    owners = [pairs_ref[me, 2 * pair + 1] >> 3 for pair in range(pair_count)]
    copies = []
    for pair in range(pair_count):
        rank = jnp.int32(0)
        for before in range(pair):
            rank = rank + (owners[before] == owners[pair]).astype(jnp.int32)
        copies.append(
            pltpu.make_async_copy(
                received_ref.at[owners[pair], rank], out_ref.at[pair], sems.at[pair]
            )
        )
        copies[-1].start()
    for copy in copies:
        copy.wait()


def select(me, pairs, received, pair_count):
    _, _, size, feat = received.shape
    return pl.pallas_call(
        functools.partial(select_kernel, pair_count),
        out_shape=jax.ShapeDtypeStruct((pair_count, size, feat), received.dtype),
        in_specs=[smem(), smem(), anywhere()],
        out_specs=anywhere(),
        scratch_shapes=[pltpu.SemaphoreType.DMA((pair_count,))],
        compiler_params=params(),
        name="select",
    )(me, pairs, received)


def tree(parts):
    while len(parts) > 1:
        half = len(parts) // 2
        parts = [parts[i] + parts[i + half] for i in range(half)]
    return parts[0]


def across(left, right):
    return lax.dot_general(
        left, right, (((1,), (1,)), ((), ())), preferred_element_type=jnp.float32
    )


def col_square(block):
    square = jnp.square(block.astype(jnp.float32))
    high = square.astype(jnp.bfloat16)
    low = (square - high.astype(jnp.float32)).astype(jnp.bfloat16)
    ones = jnp.ones((8, block.shape[1]), jnp.bfloat16)
    return (across(ones, high) + across(ones, low))[:1]


def chunk_kernel(narrow_count, first, last, *refs):
    rows, cols = refs[:narrow_count], refs[narrow_count : 2 * narrow_count]
    rest = list(refs[2 * narrow_count :])
    if first:
        square = tree(
            [
                jnp.sum(jnp.square(row[0].astype(jnp.float32)), axis=1, keepdims=True)
                for row in rows
            ]
        )
        square = jnp.broadcast_to(square, (BR, LANES))
    else:
        square_ref, mass_in, total_in, sums_in = rest[:4]
        rest = rest[4:]
        square = square_ref[0]
    gram = tree([across(row[0], col[0]) for row, col in zip(rows, cols)])
    other = tree([col_square(col[0]) for col in cols])
    size = gram.shape[1]
    pieces, mass = [], None
    for at in range(0, size, LANES):
        here = slice(at, at + LANES)
        piece = jnp.exp((square + other[:, here] - 2.0 * gram[:, here]) * (-1.0 / F))
        mass = piece if mass is None else mass + piece
        pieces.append(piece)
    kernel = jnp.concatenate(pieces, axis=1) if len(pieces) > 1 else pieces[0]
    sums = jnp.sum(kernel, axis=0, keepdims=True)
    total = jnp.dot(kernel.astype(jnp.bfloat16), cols[0][0], preferred_element_type=jnp.float32)
    if not first:
        mass = mass_in[0] + mass
        total = total_in[0] + total
        sums = jnp.concatenate([sums_in[0], sums], axis=1)
    if last:
        part_ref, mass_ref, row_ref, sums_ref = rest
        part_ref[0] = total.astype(jnp.bfloat16)
        mass_ref[0] = jnp.broadcast_to(jnp.sum(mass, axis=1, keepdims=True), (BR, LANES))
        row_ref[0] = jnp.sum(mass.T, axis=0, keepdims=True)
        for wide in range(sums_ref.shape[0]):
            sums_ref[wide, 0] = sums
    else:
        square_ref, mass_ref, total_ref, sums_ref = rest
        if first:
            square_ref[0] = square
        mass_ref[0] = mass
        total_ref[0] = total
        sums_ref[0] = sums


def by_pair(shape):
    return pl.BlockSpec((1, *shape[1:]), lambda p: (p,) + (0,) * (len(shape) - 1))


def chunk_step(rows, cols, carry, done, last, wide_count):
    pair_count, size, feat = cols[0].shape
    first = carry is None
    lanes = jax.ShapeDtypeStruct((pair_count, BR, LANES), jnp.float32)
    if last:
        shapes = [
            jax.ShapeDtypeStruct((pair_count, BR, feat), jnp.bfloat16),
            lanes,
            jax.ShapeDtypeStruct((pair_count, 1, BR), jnp.float32),
            jax.ShapeDtypeStruct((wide_count, pair_count, 1, BR), jnp.float32),
        ]
        out_specs = [by_pair(s.shape) for s in shapes[:3]] + [
            pl.BlockSpec((wide_count, 1, 1, BR), lambda p: (0, p, 0, 0))
        ]
    else:
        shapes = [
            lanes,
            lanes,
            jax.ShapeDtypeStruct((pair_count, BR, feat), jnp.float32),
            jax.ShapeDtypeStruct((pair_count, 1, done + size), jnp.float32),
        ]
        out_specs = [by_pair(s.shape) for s in shapes]
    args = [*rows, *cols, *([] if first else carry)]
    return pl.pallas_call(
        functools.partial(chunk_kernel, len(rows), first, last),
        grid=(pair_count,),
        out_shape=shapes,
        in_specs=[by_pair(a.shape) for a in args],
        out_specs=out_specs,
        compiler_params=params(),
        cost_estimate=pl.CostEstimate(
            flops=2 * pair_count * BR * size * (F + feat),
            transcendentals=pair_count * BR * size,
            bytes_accessed=8 * 1024 * 1024,
        ),
        name="chunk",
    )(*args)


def mean_kernel(pair_count, local_ref, part_ref, mass_ref, block_ref, _, out_ref, total, weight):
    here = local_ref[pl.program_id(0)]
    total[...] = block_ref[0].astype(jnp.float32)
    weight[...] = jnp.ones_like(weight)
    for pair in range(pair_count):

        @pl.when(local_ref[pair] == here)
        def _():
            total[...] += part_ref[pair].astype(jnp.float32)
            weight[...] += mass_ref[pair]

    scale = 1.0 / weight[...]
    for at in range(0, total.shape[1], LANES):
        lanes = slice(at, at + LANES)
        out_ref[0, :, lanes] = (total[:, lanes] * scale).astype(jnp.bfloat16)


def means(row_local, part, mass, blocks):
    pair_count = mass.shape[0]
    feat = blocks.shape[-1]
    block = pl.BlockSpec((1, BR, feat), lambda p, local: (local[p], 0, 0))
    return pl.pallas_call(
        functools.partial(mean_kernel, pair_count),
        out_shape=jax.ShapeDtypeStruct(blocks.shape, jnp.bfloat16),
        grid_spec=pltpu.PrefetchScalarGridSpec(
            num_scalar_prefetch=1,
            grid=(pair_count,),
            in_specs=[
                pl.BlockSpec(part.shape, lambda p, local: (0, 0, 0)),
                pl.BlockSpec(mass.shape, lambda p, local: (0, 0, 0)),
                block,
                anywhere(),
            ],
            out_specs=block,
            scratch_shapes=[
                pltpu.VMEM((BR, feat), jnp.float32),
                pltpu.VMEM((BR, LANES), jnp.float32),
            ],
        ),
        input_output_aliases={4: 0},
        compiler_params=params(),
        cost_estimate=pl.CostEstimate(
            flops=pair_count * BR * feat * 4, transcendentals=0, bytes_accessed=4 * 1024 * 1024
        ),
        name="means",
    )(row_local, part, mass, blocks, blocks + jnp.zeros((), blocks.dtype))


def gather_narrow(part):
    count = lax.axis_size("narrow")
    parts = [part]
    step = count // 2
    while step:
        perm = [(i, i ^ step) for i in range(count)]
        parts = parts + [lax.ppermute(x, "narrow", perm) for x in parts]
        step //= 2
    return parts


def to_all(parts):
    return lax.all_to_all(parts, "wide", split_axis=0, concat_axis=0, tiled=True)


def on_device(embeddings, pair_list):
    wide_count = lax.axis_size("wide")
    me = lax.axis_index("wide").astype(jnp.int32).reshape(1)
    pair_count = pair_list.shape[0]
    capacity = max(2, 2 * pair_count // wide_count)
    feat = embeddings.shape[1]
    blocks = embeddings.reshape(BLK_DEV, BR, feat)
    row_local = pair_list[:, 0] % BLK_DEV
    every_pair = to_all(
        jnp.broadcast_to(pair_list.reshape(1, 2 * pair_count), (wide_count, 2 * pair_count))
    )
    *outgoing, row_slices = pack(me, every_pair, blocks, wide_count, pair_count, capacity)
    rows = gather_narrow(row_slices)
    carry, done = None, 0
    for chunk, (start, size) in enumerate(CHUNKS):
        received = to_all(outgoing[chunk])
        cols = gather_narrow(select(me, every_pair, received, pair_count))
        carry = chunk_step(rows, cols, carry, done, chunk == len(CHUNKS) - 1, wide_count)
        done += size
    part, mass, row_sums, col_sums = carry
    every_sum = to_all(col_sums).reshape(wide_count * pair_count, BR)
    mean = means(row_local, part, mass, blocks)
    block_ids = jnp.arange(BLK_DEV, dtype=jnp.int32)[:, None]
    mine = every_pair.reshape(-1, 2)[:, 1][None, :] == me[0] * BLK_DEV + block_ids
    col_mass = jnp.sum(jnp.where(mine[:, :, None], every_sum[None], 0.0), axis=1)
    here = row_local[None, :] == block_ids
    row_mass = jnp.sum(jnp.where(here[:, :, None], row_sums.reshape(1, pair_count, BR), 0.0), axis=1)
    weights = 1.0 / (1.0 + (row_mass + col_mass) / BR)
    return weights.reshape(BLK_DEV * BR), mean.reshape(BLK_DEV * BR, feat)


def solution(mesh):
    in_specs = (P(("groups", "wide"), "narrow"), P(("groups", "wide"), None))
    out_specs = (P(("groups", "wide")), P(("groups", "wide"), "narrow"))
    return jax.shard_map(
        on_device, mesh=mesh, in_specs=in_specs, out_specs=out_specs, check_vma=False
    )
```

```python
import functools

import jax
import jax.numpy as jnp
from jax import lax
from jax.experimental import pallas as pl
from jax.experimental.pallas import tpu as pltpu
from jax.sharding import PartitionSpec as P

F = 1024
BR = 512
BLK_DEV = 8
LANES = 128
CHUNKS = ((0, 384), (384, 128))


def smem():
    return pl.BlockSpec(memory_space=pltpu.SMEM)


def vmem():
    return pl.BlockSpec(memory_space=pltpu.VMEM)


def anywhere():
    return pl.BlockSpec(memory_space=pl.ANY)


def in_vmem(x):
    return pltpu.with_memory_space_constraint(x, pltpu.VMEM)


def in_hbm(x):
    return pltpu.with_memory_space_constraint(x, pltpu.HBM)


def params(mebibytes):
    return pltpu.CompilerParams(vmem_limit_bytes=mebibytes * 1024 * 1024)


def pack_kernel(wide_count, pair_count, capacity, me_ref, *refs):
    lists, blocks_ref, outs = refs[:wide_count], refs[wide_count], refs[wide_count + 1 : -2]
    rows_ref, sems = refs[-2:]
    me = me_ref[0]
    copies = []

    def send(source, target):
        copies.append(pltpu.make_async_copy(source, target, sems.at[len(copies)]))
        copies[-1].start()

    for chunk, (start, size) in enumerate(CHUNKS):
        for shift in range(1, wide_count):
            asked = lists[wide_count - shift]
            picks = [jnp.int32(0)] * capacity
            count = jnp.int32(0)
            for pair in range(pair_count):
                col = asked[pair, 1]
                mine = (col >> 3) == me
                for slot in range(capacity):
                    picks[slot] = jnp.where(mine & (count == slot), col & 7, picks[slot])
                count = count + mine.astype(jnp.int32)
            out = outs[chunk * (wide_count - 1) + shift - 1]
            for slot in range(capacity):
                send(blocks_ref.at[picks[slot], pl.ds(start, size)], out.at[slot])
    for pair in range(pair_count):
        send(blocks_ref.at[lists[0][pair, 0] & 7], rows_ref.at[pair])
    for copy in copies:
        copy.wait()


def pack(me, lists, blocks, capacity):
    wide_count, pair_count = len(lists), lists[0].shape[0]
    feat = blocks.shape[-1]
    shapes = [
        pltpu.VMEM((capacity, size, feat), blocks.dtype)
        for _, size in CHUNKS
        for _ in range(1, wide_count)
    ] + [pltpu.HBM((pair_count, BR, feat), blocks.dtype)]
    copies = (len(shapes) - 1) * capacity + pair_count
    outs = pl.pallas_call(
        functools.partial(pack_kernel, wide_count, pair_count, capacity),
        out_shape=shapes,
        in_specs=[smem()] * (1 + wide_count) + [anywhere()],
        out_specs=[anywhere()] * len(shapes),
        scratch_shapes=[pltpu.SemaphoreType.DMA((copies,))],
        compiler_params=params(4),
        name="pack",
    )(me, *lists, in_hbm(blocks))
    each = wide_count - 1
    return [outs[c * each : (c + 1) * each] for c in range(len(CHUNKS))], outs[-1]


def select_kernel(wide_count, pair_count, start, size, me_ref, list_ref, blocks_ref, *refs):
    received, out_ref, sems = refs[:-2], refs[-2], refs[-1]
    me = me_ref[0]
    owners = [list_ref[pair, 1] >> 3 for pair in range(pair_count)]
    for pair in range(pair_count):
        shift = me - owners[pair]
        shift = jnp.where(shift < 0, shift + wide_count, shift)
        rank = jnp.int32(0)
        for before in range(pair):
            rank = rank + (owners[before] == owners[pair]).astype(jnp.int32)

        @pl.when(shift == 0)
        def _():
            source = blocks_ref.at[list_ref[pair, 1] & 7, pl.ds(start, size)]
            pltpu.make_async_copy(source, out_ref.at[pair], sems.at[pair]).start()

        for other in range(1, wide_count):

            @pl.when(shift == other)
            def _():
                source = received[other - 1].at[rank]
                pltpu.make_async_copy(source, out_ref.at[pair], sems.at[pair]).start()

    for pair in range(pair_count):
        source = blocks_ref.at[0, pl.ds(start, size)]
        pltpu.make_async_copy(source, out_ref.at[pair], sems.at[pair]).wait()


def select(me, pairs, blocks, received, start, size):
    pair_count, feat = pairs.shape[0], blocks.shape[-1]
    return pl.pallas_call(
        functools.partial(select_kernel, len(received) + 1, pair_count, start, size),
        out_shape=pltpu.HBM((pair_count, size, feat), blocks.dtype),
        in_specs=[smem(), smem(), anywhere()] + [anywhere()] * len(received),
        out_specs=anywhere(),
        scratch_shapes=[pltpu.SemaphoreType.DMA((pair_count,))],
        compiler_params=params(4),
        name="select",
    )(me, pairs, in_hbm(blocks), *[in_vmem(x) for x in received])


def tree(parts):
    while len(parts) > 1:
        half = len(parts) // 2
        parts = [parts[i] + parts[i + half] for i in range(half)]
    return parts[0]


def across(left, right):
    return lax.dot_general(
        left, right, (((1,), (1,)), ((), ())), preferred_element_type=jnp.float32
    )


def lane_sum(block):
    square = jnp.square(block.astype(jnp.float32))
    return sum(square[:, at : at + LANES] for at in range(0, square.shape[1], LANES))


def chunk_kernel(narrow_count, first, last, *refs):
    rows, cols = refs[:narrow_count], refs[narrow_count : 2 * narrow_count]
    rest = list(refs[2 * narrow_count :])
    if not first:
        square_in, mass_in, total_in, sums_in = rest[:4]
        rest = rest[4:]
    if last:
        part_ref, mass_ref, row_ref, sums_ref = rest
    else:
        square_ref, mass_ref, total_ref, sums_ref = rest
    for pair in range(rows[0].shape[0]):
        if first:
            square = jnp.sum(tree([lane_sum(row[pair]) for row in rows]), axis=1, keepdims=True)
            square = jnp.broadcast_to(square, (BR, LANES))
        else:
            square = square_in[pair]
        gram = tree([across(row[pair], col[pair]) for row, col in zip(rows, cols)])
        other = jnp.sum(tree([lane_sum(col[pair]) for col in cols]).T, axis=0, keepdims=True)
        size = gram.shape[1]
        pieces, mass = [], None
        for at in range(0, size, LANES):
            here = slice(at, at + LANES)
            piece = jnp.exp((square + other[:, here] - 2.0 * gram[:, here]) * (-1.0 / F))
            mass = piece if mass is None else mass + piece
            pieces.append(piece)
        kernel = jnp.concatenate(pieces, axis=1) if len(pieces) > 1 else pieces[0]
        sums = jnp.sum(kernel, axis=0, keepdims=True)
        total = jnp.dot(
            kernel.astype(jnp.bfloat16), cols[0][pair], preferred_element_type=jnp.float32
        )
        if not first:
            mass = mass_in[pair] + mass
            total = total_in[pair] + total
            sums = jnp.concatenate([sums_in[pair : pair + 1], sums], axis=1)
        sums_ref[pair : pair + 1] = sums
        if last:
            part_ref[pair] = total.astype(jnp.bfloat16)
            mass_ref[pair] = jnp.broadcast_to(jnp.sum(mass, axis=1, keepdims=True), (BR, LANES))
            row_ref[pair : pair + 1] = jnp.sum(mass.T, axis=0, keepdims=True)
        else:
            if first:
                square_ref[pair] = square
            mass_ref[pair] = mass
            total_ref[pair] = total


def chunk_step(rows, cols, carry, done, last):
    pair_count, size, feat = cols[0].shape
    first = carry is None
    lanes = pltpu.VMEM((pair_count, BR, LANES), jnp.float32)
    sums = pltpu.VMEM((pair_count, done + size), jnp.float32)
    if last:
        shapes = [
            pltpu.VMEM((pair_count, BR, feat), jnp.bfloat16),
            lanes,
            pltpu.VMEM((pair_count, BR), jnp.float32),
            sums,
        ]
    else:
        shapes = [lanes, lanes, pltpu.VMEM((pair_count, BR, feat), jnp.float32), sums]
    args = [*rows, *cols, *([] if first else carry)]
    return pl.pallas_call(
        functools.partial(chunk_kernel, len(rows), first, last),
        out_shape=shapes,
        in_specs=[vmem()] * len(args),
        out_specs=[vmem()] * len(shapes),
        compiler_params=params(16),
        cost_estimate=pl.CostEstimate(
            flops=2 * pair_count * BR * size * (F + feat),
            transcendentals=pair_count * BR * size,
            bytes_accessed=8 * 1024 * 1024,
        ),
        name="chunk",
    )(*[in_vmem(x) for x in args])


def mean_kernel(pair_count, local_ref, part_ref, mass_ref, block_ref, _, out_ref, total, weight):
    here = local_ref[pl.program_id(0)]
    total[...] = block_ref[0].astype(jnp.float32)
    weight[...] = jnp.ones_like(weight)
    for pair in range(pair_count):

        @pl.when(local_ref[pair] == here)
        def _():
            total[...] += part_ref[pair].astype(jnp.float32)
            weight[...] += mass_ref[pair]

    scale = 1.0 / weight[...]
    for at in range(0, total.shape[1], LANES):
        lanes = slice(at, at + LANES)
        out_ref[0, :, lanes] = (total[:, lanes] * scale).astype(jnp.bfloat16)


def means(row_local, part, mass, blocks):
    pair_count = mass.shape[0]
    feat = blocks.shape[-1]
    block = pl.BlockSpec((1, BR, feat), lambda p, local: (local[p], 0, 0))
    return pl.pallas_call(
        functools.partial(mean_kernel, pair_count),
        out_shape=jax.ShapeDtypeStruct(blocks.shape, jnp.bfloat16),
        grid_spec=pltpu.PrefetchScalarGridSpec(
            num_scalar_prefetch=1,
            grid=(pair_count,),
            in_specs=[
                pl.BlockSpec(part.shape, lambda p, local: (0, 0, 0)),
                pl.BlockSpec(mass.shape, lambda p, local: (0, 0, 0)),
                block,
                anywhere(),
            ],
            out_specs=block,
            scratch_shapes=[
                pltpu.VMEM((BR, feat), jnp.float32),
                pltpu.VMEM((BR, LANES), jnp.float32),
            ],
        ),
        input_output_aliases={4: 0},
        compiler_params=params(16),
        cost_estimate=pl.CostEstimate(
            flops=pair_count * BR * feat * 4, transcendentals=0, bytes_accessed=4 * 1024 * 1024
        ),
        name="means",
    )(row_local, part, mass, in_hbm(blocks), in_hbm(blocks))


def gather_narrow(part, before=None):
    count = lax.axis_size("narrow")
    parts = [part]
    step = count // 2
    while step:
        perm = [(i, i ^ step) for i in range(count)]
        if step == 1 and before is not None:
            came, before = lax.optimization_barrier((parts[1:], before))
            parts = [part, *came]
        parts = parts + [lax.ppermute(x, "narrow", perm) for x in parts]
        step //= 2
    return parts, before


def from_others(part):
    count = lax.axis_size("wide")
    return [part] + [
        lax.ppermute(part, "wide", [(i, (i + shift) % count) for i in range(count)])
        for shift in range(1, count)
    ]


def on_device(embeddings, pair_list):
    wide_count = lax.axis_size("wide")
    me = lax.axis_index("wide").astype(jnp.int32).reshape(1)
    pair_count = pair_list.shape[0]
    capacity = max(2, 2 * pair_count // wide_count)
    feat = embeddings.shape[1]
    blocks = embeddings.reshape(BLK_DEV, BR, feat)
    row_local = pair_list[:, 0] % BLK_DEV
    lists = from_others(pair_list)
    outgoing, row_slices = pack(me, lists, blocks, capacity)
    rows, _ = gather_narrow(row_slices)
    carry, done = None, 0
    for chunk, (start, size) in enumerate(CHUNKS):
        received = [
            lax.ppermute(
                outgoing[chunk][shift - 1],
                "wide",
                [(i, (i + shift) % wide_count) for i in range(wide_count)],
            )
            for shift in range(1, wide_count)
        ]
        if chunk == 0:
            rows, received = lax.optimization_barrier((rows, received))
        col_part = select(me, pair_list, blocks, received, start, size)
        cols, carry = gather_narrow(col_part, carry)
        carry = chunk_step(rows, cols, carry, done, chunk == len(CHUNKS) - 1)
        done += size
    part, mass, row_sums, col_sums = carry
    every_sum = jnp.concatenate(from_others(col_sums), axis=0)
    mean = means(row_local, part, mass, blocks)
    block_ids = jnp.arange(BLK_DEV, dtype=jnp.int32)[:, None]
    every_col = jnp.concatenate([x[:, 1] for x in lists])
    mine = every_col[None, :] == me[0] * BLK_DEV + block_ids
    col_mass = jnp.sum(jnp.where(mine[:, :, None], every_sum[None], 0.0), axis=1)
    here = row_local[None, :] == block_ids
    row_mass = jnp.sum(jnp.where(here[:, :, None], row_sums[None], 0.0), axis=1)
    weights = 1.0 / (1.0 + (row_mass + col_mass) / BR)
    return weights.reshape(BLK_DEV * BR), mean.reshape(BLK_DEV * BR, feat)


def solution(mesh):
    in_specs = (P(("groups", "wide"), "narrow"), P(("groups", "wide"), None))
    out_specs = (P(("groups", "wide")), P(("groups", "wide"), "narrow"))
    return jax.shard_map(
        on_device, mesh=mesh, in_specs=in_specs, out_specs=out_specs, check_vma=False
    )
```

```python
import functools

import jax
import jax.numpy as jnp
from jax import lax
from jax.experimental import pallas as pl
from jax.experimental.pallas import tpu as pltpu
from jax.sharding import PartitionSpec as P

F = 1024
BR = 512
BLK_DEV = 8
LANES = 128
CHUNKS = ((0, 256), (256, 128), (384, 128))


def smem():
    return pl.BlockSpec(memory_space=pltpu.SMEM)


def vmem():
    return pl.BlockSpec(memory_space=pltpu.VMEM)


def anywhere():
    return pl.BlockSpec(memory_space=pl.ANY)


def in_vmem(x):
    return pltpu.with_memory_space_constraint(x, pltpu.VMEM)


def in_hbm(x):
    return pltpu.with_memory_space_constraint(x, pltpu.HBM)


def params(mebibytes):
    return pltpu.CompilerParams(vmem_limit_bytes=mebibytes * 1024 * 1024)


def pack_kernel(wide_count, pair_count, capacity, me_ref, *refs):
    lists, blocks_ref, outs = refs[:wide_count], refs[wide_count], refs[wide_count + 1 : -2]
    rows_ref, sems = refs[-2:]
    me = me_ref[0]
    copies = []

    def send(source, target):
        copies.append(pltpu.make_async_copy(source, target, sems.at[len(copies)]))
        copies[-1].start()

    for chunk, (start, size) in enumerate(CHUNKS):
        for shift in range(1, wide_count):
            asked = lists[wide_count - shift]
            picks = [jnp.int32(0)] * capacity
            count = jnp.int32(0)
            for pair in range(pair_count):
                col = asked[pair, 1]
                mine = (col >> 3) == me
                for slot in range(capacity):
                    picks[slot] = jnp.where(mine & (count == slot), col & 7, picks[slot])
                count = count + mine.astype(jnp.int32)
            out = outs[chunk * (wide_count - 1) + shift - 1]
            for slot in range(capacity):
                send(blocks_ref.at[picks[slot], pl.ds(start, size)], out.at[slot])
    for pair in range(pair_count):
        send(blocks_ref.at[lists[0][pair, 0] & 7], rows_ref.at[pair])
    for copy in copies:
        copy.wait()


def pack(me, lists, blocks, capacity):
    wide_count, pair_count = len(lists), lists[0].shape[0]
    feat = blocks.shape[-1]
    shapes = [
        pltpu.VMEM((capacity, size, feat), blocks.dtype)
        for _, size in CHUNKS
        for _ in range(1, wide_count)
    ] + [pltpu.VMEM((pair_count, BR, feat), blocks.dtype)]
    copies = (len(shapes) - 1) * capacity + pair_count
    outs = pl.pallas_call(
        functools.partial(pack_kernel, wide_count, pair_count, capacity),
        out_shape=shapes,
        in_specs=[smem()] * (1 + wide_count) + [anywhere()],
        out_specs=[anywhere()] * len(shapes),
        scratch_shapes=[pltpu.SemaphoreType.DMA((copies,))],
        compiler_params=params(4),
        name="pack",
    )(me, *lists, in_hbm(blocks))
    each = wide_count - 1
    return [outs[c * each : (c + 1) * each] for c in range(len(CHUNKS))], outs[-1]


def select_kernel(wide_count, pair_count, start, size, me_ref, list_ref, blocks_ref, *refs):
    received, out_ref, sems = refs[:-2], refs[-2], refs[-1]
    me = me_ref[0]
    owners = [list_ref[pair, 1] >> 3 for pair in range(pair_count)]
    for pair in range(pair_count):
        shift = me - owners[pair]
        shift = jnp.where(shift < 0, shift + wide_count, shift)
        rank = jnp.int32(0)
        for before in range(pair):
            rank = rank + (owners[before] == owners[pair]).astype(jnp.int32)

        @pl.when(shift == 0)
        def _():
            source = blocks_ref.at[list_ref[pair, 1] & 7, pl.ds(start, size)]
            pltpu.make_async_copy(source, out_ref.at[pair], sems.at[pair]).start()

        for other in range(1, wide_count):

            @pl.when(shift == other)
            def _():
                source = received[other - 1].at[rank]
                pltpu.make_async_copy(source, out_ref.at[pair], sems.at[pair]).start()

    for pair in range(pair_count):
        source = blocks_ref.at[0, pl.ds(start, size)]
        pltpu.make_async_copy(source, out_ref.at[pair], sems.at[pair]).wait()


def select(me, pairs, blocks, received, start, size):
    pair_count, feat = pairs.shape[0], blocks.shape[-1]
    return pl.pallas_call(
        functools.partial(select_kernel, len(received) + 1, pair_count, start, size),
        out_shape=pltpu.VMEM((pair_count, size, feat), blocks.dtype),
        in_specs=[smem(), smem(), anywhere()] + [anywhere()] * len(received),
        out_specs=anywhere(),
        scratch_shapes=[pltpu.SemaphoreType.DMA((pair_count,))],
        compiler_params=params(4),
        name="select",
    )(me, pairs, in_hbm(blocks), *[in_vmem(x) for x in received])


def tree(parts):
    while len(parts) > 1:
        half = len(parts) // 2
        parts = [parts[i] + parts[i + half] for i in range(half)]
    return parts[0]


def across(left, right):
    return lax.dot_general(
        left, right, (((1,), (1,)), ((), ())), preferred_element_type=jnp.float32
    )


def lane_sum(block):
    square = jnp.square(block.astype(jnp.float32))
    return sum(square[:, at : at + LANES] for at in range(0, square.shape[1], LANES))


def chunk_kernel(first, last, *refs):
    all_rows, all_cols, rest = refs[:2], refs[2:4], refs[4:]
    half_count, pair_count = refs[0].shape[:2]
    if not first:
        square_in, mass_in, total_in, sums_in = rest[:4]
        rest = rest[4:]
    if last:
        part_ref, mass_ref, row_ref, sums_ref = rest
    elif first:
        square_ref, mass_ref, total_ref, sums_ref = rest
    else:
        mass_ref, total_ref, sums_ref = rest
    for pair in range(pair_count):
        rows = [ref.at[i, pair] for ref in all_rows for i in range(half_count)]
        cols = [ref.at[i, pair] for ref in all_cols for i in range(half_count)]
        if first:
            square = jnp.sum(tree([lane_sum(row[...]) for row in rows]), axis=1, keepdims=True)
            square = jnp.broadcast_to(square, (BR, LANES))
        else:
            square = square_in[pair]
        gram = tree([across(row[...], col[...]) for row, col in zip(rows, cols)])
        other = jnp.sum(tree([lane_sum(col[...]) for col in cols]).T, axis=0, keepdims=True)
        size = gram.shape[1]
        pieces, mass = [], None
        for at in range(0, size, LANES):
            here = slice(at, at + LANES)
            piece = jnp.exp((square + other[:, here] - 2.0 * gram[:, here]) * (-1.0 / F))
            mass = piece if mass is None else mass + piece
            pieces.append(piece)
        kernel = jnp.concatenate(pieces, axis=1) if len(pieces) > 1 else pieces[0]
        sums = jnp.sum(kernel, axis=0, keepdims=True)
        total = jnp.dot(
            kernel.astype(jnp.bfloat16), cols[0][...], preferred_element_type=jnp.float32
        )
        if not first:
            mass = mass_in[pair] + mass
            total = total_in[pair] + total
            sums = jnp.concatenate([sums_in[pair : pair + 1], sums], axis=1)
        sums_ref[pair : pair + 1] = sums
        if last:
            part_ref[pair] = total.astype(jnp.bfloat16)
            mass_ref[pair] = jnp.broadcast_to(jnp.sum(mass, axis=1, keepdims=True), (BR, LANES))
            row_ref[pair : pair + 1] = jnp.sum(mass.T, axis=0, keepdims=True)
        else:
            if first:
                square_ref[pair] = square
            mass_ref[pair] = mass
            total_ref[pair] = total


def chunk_step(rows, cols, carry, done, last):
    _, pair_count, size, feat = cols[0].shape
    first = carry is None
    lanes = pltpu.VMEM((pair_count, BR, LANES), jnp.float32)
    sums = pltpu.VMEM((pair_count, done + size), jnp.float32)
    if last:
        shapes = [
            pltpu.VMEM((pair_count, BR, feat), jnp.bfloat16),
            lanes,
            pltpu.VMEM((pair_count, BR), jnp.float32),
            sums,
        ]
    else:
        shapes = [lanes] * (1 + first) + [pltpu.VMEM((pair_count, BR, feat), jnp.float32), sums]
    args = [*rows, *cols, *([] if first else carry)]
    outs = pl.pallas_call(
        functools.partial(chunk_kernel, first, last),
        out_shape=shapes,
        in_specs=[vmem()] * len(args),
        out_specs=[vmem()] * len(shapes),
        compiler_params=params(16),
        cost_estimate=pl.CostEstimate(
            flops=2 * pair_count * BR * size * (F + feat),
            transcendentals=pair_count * BR * size,
            bytes_accessed=8 * 1024 * 1024,
        ),
        name="chunk",
    )(*[in_vmem(x) for x in args])
    return outs if first or last else [carry[0], *outs]


def mean_kernel(pair_count, local_ref, part_ref, mass_ref, block_ref, _, out_ref, total, weight):
    here = local_ref[pl.program_id(0)]
    total[...] = block_ref[0].astype(jnp.float32)
    weight[...] = jnp.ones_like(weight)
    for pair in range(pair_count):

        @pl.when(local_ref[pair] == here)
        def _():
            total[...] += part_ref[pair].astype(jnp.float32)
            weight[...] += mass_ref[pair]

    scale = 1.0 / weight[...]
    for at in range(0, total.shape[1], LANES):
        lanes = slice(at, at + LANES)
        out_ref[0, :, lanes] = (total[:, lanes] * scale).astype(jnp.bfloat16)


def means(row_local, part, mass, blocks):
    pair_count = mass.shape[0]
    feat = blocks.shape[-1]
    block = pl.BlockSpec((1, BR, feat), lambda p, local: (local[p], 0, 0))
    return pl.pallas_call(
        functools.partial(mean_kernel, pair_count),
        out_shape=jax.ShapeDtypeStruct(blocks.shape, jnp.bfloat16),
        grid_spec=pltpu.PrefetchScalarGridSpec(
            num_scalar_prefetch=1,
            grid=(pair_count,),
            in_specs=[
                pl.BlockSpec(part.shape, lambda p, local: (0, 0, 0)),
                pl.BlockSpec(mass.shape, lambda p, local: (0, 0, 0)),
                block,
                anywhere(),
            ],
            out_specs=block,
            scratch_shapes=[
                pltpu.VMEM((BR, feat), jnp.float32),
                pltpu.VMEM((BR, LANES), jnp.float32),
            ],
        ),
        input_output_aliases={4: 0},
        compiler_params=params(16),
        cost_estimate=pl.CostEstimate(
            flops=pair_count * BR * feat * 4, transcendentals=0, bytes_accessed=4 * 1024 * 1024
        ),
        name="means",
    )(row_local, part, mass, in_hbm(blocks), in_hbm(blocks))


def hop(parts, step):
    count = lax.axis_size("narrow")
    return parts, lax.ppermute(parts, "narrow", [(i, i ^ step) for i in range(count)])


def first_hops(part):
    parts = part[None]
    step = lax.axis_size("narrow") // 2
    while step > 1:
        parts = jnp.concatenate(hop(parts, step), axis=0)
        step //= 2
    return parts


def to_wide(pieces):
    count = lax.axis_size("wide")
    return [
        lax.ppermute(piece, "wide", [(i, (i + shift) % count) for i in range(count)])
        for shift, piece in enumerate(pieces, 1)
    ]


def from_others(part):
    count = lax.axis_size("wide")
    return [part] + [
        lax.ppermute(part, "wide", [(i, (i + shift) % count) for i in range(count)])
        for shift in range(1, count)
    ]


def on_device(embeddings, pair_list):
    wide_count = lax.axis_size("wide")
    me = lax.axis_index("wide").astype(jnp.int32).reshape(1)
    pair_count = pair_list.shape[0]
    capacity = max(2, 2 * pair_count // wide_count)
    feat = embeddings.shape[1]
    blocks = embeddings.reshape(BLK_DEV, BR, feat)
    row_local = pair_list[:, 0] % BLK_DEV
    lists = from_others(pair_list)
    outgoing, row_slices = pack(me, lists, blocks, capacity)
    chunks = len(CHUNKS)
    fixed = lax.optimization_barrier
    rows_half, received = fixed((first_hops(row_slices), to_wide(outgoing[0])))
    rows = carry = half = None
    done = 0
    for phase in range(1, chunks + 2):
        last_half = half
        if phase <= chunks:
            start, size = CHUNKS[phase - 1]
            picked = select(me, pair_list, blocks, received, start, size)
            half = first_hops(picked)
        else:
            half = None
        if phase < chunks:
            received = to_wide(outgoing[phase])
        if phase == 1:
            rows = hop(rows_half, 1)
            half, received, rows = fixed((half, received, rows))
            continue
        whole = hop(last_half, 1)
        carry = chunk_step(rows, whole, carry, done, phase == chunks + 1)
        done += CHUNKS[phase - 2][1]
        if phase < chunks:
            half, received, carry = fixed((half, received, carry))
        elif phase == chunks:
            half, carry = fixed((half, carry))
    part, mass, row_sums, col_sums = carry
    every_sum = jnp.concatenate(from_others(col_sums), axis=0)
    mean = means(row_local, part, mass, blocks)
    block_ids = jnp.arange(BLK_DEV, dtype=jnp.int32)[:, None]
    every_col = jnp.concatenate([x[:, 1] for x in lists])
    mine = every_col[None, :] == me[0] * BLK_DEV + block_ids
    col_mass = jnp.sum(jnp.where(mine[:, :, None], every_sum[None], 0.0), axis=1)
    here = row_local[None, :] == block_ids
    row_mass = jnp.sum(jnp.where(here[:, :, None], row_sums[None], 0.0), axis=1)
    weights = 1.0 / (1.0 + (row_mass + col_mass) / BR)
    return weights.reshape(BLK_DEV * BR), mean.reshape(BLK_DEV * BR, feat)


def solution(mesh):
    in_specs = (P(("groups", "wide"), "narrow"), P(("groups", "wide"), None))
    out_specs = (P(("groups", "wide")), P(("groups", "wide"), "narrow"))
    return jax.shard_map(
        on_device, mesh=mesh, in_specs=in_specs, out_specs=out_specs, check_vma=False
    )
```

```python
import functools

import jax
import jax.numpy as jnp
from jax import lax
from jax.experimental import pallas as pl
from jax.experimental.pallas import tpu as pltpu
from jax.sharding import PartitionSpec as P

F = 1024
BR = 512
BLK_DEV = 8
LANES = 128
CHUNKS = ((0, 320), (320, 192))
WINDOWS = ((0, 256), (256, 512))


def smem():
    return pl.BlockSpec(memory_space=pltpu.SMEM)


def vmem():
    return pl.BlockSpec(memory_space=pltpu.VMEM)


def anywhere():
    return pl.BlockSpec(memory_space=pl.ANY)


def in_vmem(x):
    return pltpu.with_memory_space_constraint(x, pltpu.VMEM)


def in_hbm(x):
    return pltpu.with_memory_space_constraint(x, pltpu.HBM)


def params(mebibytes):
    return pltpu.CompilerParams(vmem_limit_bytes=mebibytes * 1024 * 1024)


def pack_kernel(wide_count, pair_count, capacity, me_ref, *refs):
    lists, blocks_ref, outs = refs[:wide_count], refs[wide_count], refs[wide_count + 1 : -2]
    rows_ref, sems = refs[-2:]
    me = me_ref[0]
    copies = []

    def send(source, target):
        copies.append(pltpu.make_async_copy(source, target, sems.at[len(copies)]))
        copies[-1].start()

    for chunk, (start, size) in enumerate(CHUNKS):
        for shift in range(1, wide_count):
            asked = lists[wide_count - shift]
            picks = [jnp.int32(0)] * capacity
            count = jnp.int32(0)
            for pair in range(pair_count):
                col = asked[pair, 1]
                mine = (col >> 3) == me
                for slot in range(capacity):
                    picks[slot] = jnp.where(mine & (count == slot), col & 7, picks[slot])
                count = count + mine.astype(jnp.int32)
            out = outs[chunk * (wide_count - 1) + shift - 1]
            for slot in range(capacity):
                send(blocks_ref.at[picks[slot], pl.ds(start, size)], out.at[slot])
    for pair in range(pair_count):
        send(blocks_ref.at[lists[0][pair, 0] & 7], rows_ref.at[pair])
    for copy in copies:
        copy.wait()


def pack(me, lists, blocks, capacity):
    wide_count, pair_count = len(lists), lists[0].shape[0]
    feat = blocks.shape[-1]
    shapes = [
        pltpu.VMEM((capacity, size, feat), blocks.dtype)
        for _, size in CHUNKS
        for _ in range(1, wide_count)
    ] + [pltpu.VMEM((pair_count, BR, feat), blocks.dtype)]
    copies = (len(shapes) - 1) * capacity + pair_count
    outs = pl.pallas_call(
        functools.partial(pack_kernel, wide_count, pair_count, capacity),
        out_shape=shapes,
        in_specs=[smem()] * (1 + wide_count) + [anywhere()],
        out_specs=[anywhere()] * len(shapes),
        scratch_shapes=[pltpu.SemaphoreType.DMA((copies,))],
        compiler_params=params(4),
        name="pack",
    )(me, *lists, in_hbm(blocks))
    each = wide_count - 1
    return [outs[c * each : (c + 1) * each] for c in range(len(CHUNKS))], outs[-1]


def select_kernel(wide_count, pair_count, start, size, me_ref, list_ref, blocks_ref, *refs):
    received, out_ref, sems = refs[:-2], refs[-2], refs[-1]
    me = me_ref[0]
    owners = [list_ref[pair, 1] >> 3 for pair in range(pair_count)]
    for pair in range(pair_count):
        shift = me - owners[pair]
        shift = jnp.where(shift < 0, shift + wide_count, shift)
        rank = jnp.int32(0)
        for before in range(pair):
            rank = rank + (owners[before] == owners[pair]).astype(jnp.int32)

        @pl.when(shift == 0)
        def _():
            source = blocks_ref.at[list_ref[pair, 1] & 7, pl.ds(start, size)]
            pltpu.make_async_copy(source, out_ref.at[pair], sems.at[pair]).start()

        for other in range(1, wide_count):

            @pl.when(shift == other)
            def _():
                source = received[other - 1].at[rank]
                pltpu.make_async_copy(source, out_ref.at[pair], sems.at[pair]).start()

    for pair in range(pair_count):
        source = blocks_ref.at[0, pl.ds(start, size)]
        pltpu.make_async_copy(source, out_ref.at[pair], sems.at[pair]).wait()


def select(me, pairs, blocks, received, start, size):
    pair_count, feat = pairs.shape[0], blocks.shape[-1]
    return pl.pallas_call(
        functools.partial(select_kernel, len(received) + 1, pair_count, start, size),
        out_shape=pltpu.VMEM((pair_count, size, feat), blocks.dtype),
        in_specs=[smem(), smem(), anywhere()] + [anywhere()] * len(received),
        out_specs=anywhere(),
        scratch_shapes=[pltpu.SemaphoreType.DMA((pair_count,))],
        compiler_params=params(4),
        name="select",
    )(me, pairs, in_hbm(blocks), *[in_vmem(x) for x in received])


def tree(parts):
    while len(parts) > 1:
        half = len(parts) // 2
        parts = [parts[i] + parts[i + half] for i in range(half)]
    return parts[0]


def across(left, right):
    return lax.dot_general(
        left, right, (((1,), (1,)), ((), ())), preferred_element_type=jnp.float32
    )


def lane_sum(block):
    square = jnp.square(block.astype(jnp.float32))
    return sum(square[:, at : at + LANES] for at in range(0, square.shape[1], LANES))


def segments(window):
    low, high = window
    held = []
    for chunk, (start, size) in enumerate(CHUNKS):
        first, end = max(low, start), min(high, start + size)
        if first < end:
            held.append((chunk, first - start, end - first))
    return held


def window_kernel(narrow_count, window, first, last, *refs):
    held = segments(window)
    all_rows, rest = refs[:narrow_count], refs[narrow_count:]
    all_cols = [rest[i * narrow_count : (i + 1) * narrow_count] for i in range(len(held))]
    rest = rest[len(held) * narrow_count :]
    if not first:
        square_in, mass_in, total_in, sums_in = rest[:4]
        rest = rest[4:]
    if last:
        part_ref, mass_ref, row_ref, sums_ref = rest
    elif first:
        square_ref, mass_ref, total_ref, sums_ref = rest
    else:
        mass_ref, total_ref, sums_ref = rest
    for pair in range(all_rows[0].shape[0]):
        rows = [ref[pair] for ref in all_rows]
        cols = []
        for narrow in range(narrow_count):
            pieces = [
                refs[narrow][pair, at : at + size] for refs, (_, at, size) in zip(all_cols, held)
            ]
            cols.append(jnp.concatenate(pieces, axis=0) if len(pieces) > 1 else pieces[0])
        if first:
            square = jnp.sum(tree([lane_sum(row) for row in rows]), axis=1, keepdims=True)
            square = jnp.broadcast_to(square, (BR, LANES))
        else:
            square = square_in[pair]
        gram = tree([across(row, col) for row, col in zip(rows, cols)])
        other = jnp.sum(tree([lane_sum(col) for col in cols]).T, axis=0, keepdims=True)
        pieces, mass = [], None
        for at in range(0, gram.shape[1], LANES):
            here = slice(at, at + LANES)
            piece = jnp.exp((square + other[:, here] - 2.0 * gram[:, here]) * (-1.0 / F))
            mass = piece if mass is None else mass + piece
            pieces.append(piece)
        kernel = jnp.concatenate(pieces, axis=1) if len(pieces) > 1 else pieces[0]
        sums = jnp.sum(kernel, axis=0, keepdims=True)
        total = jnp.dot(kernel.astype(jnp.bfloat16), cols[0], preferred_element_type=jnp.float32)
        if not first:
            mass = mass_in[pair] + mass
            total = total_in[pair] + total
            sums = jnp.concatenate([sums_in[pair : pair + 1], sums], axis=1)
        sums_ref[pair : pair + 1] = sums
        if last:
            part_ref[pair] = total.astype(jnp.bfloat16)
            mass_ref[pair] = jnp.broadcast_to(jnp.sum(mass, axis=1, keepdims=True), (BR, LANES))
            row_ref[pair : pair + 1] = jnp.sum(mass.T, axis=0, keepdims=True)
        else:
            if first:
                square_ref[pair] = square
            mass_ref[pair] = mass
            total_ref[pair] = total


def window_step(rows, cols, index, carry):
    pair_count, _, feat = rows[0].shape
    window = WINDOWS[index]
    size = window[1] - window[0]
    first, last = index == 0, index == len(WINDOWS) - 1
    lanes = pltpu.VMEM((pair_count, BR, LANES), jnp.float32)
    sums = pltpu.VMEM((pair_count, window[1]), jnp.float32)
    if last:
        shapes = [
            pltpu.VMEM((pair_count, BR, feat), jnp.bfloat16),
            lanes,
            pltpu.VMEM((pair_count, BR), jnp.float32),
            sums,
        ]
    else:
        shapes = [lanes] * (1 + first) + [pltpu.VMEM((pair_count, BR, feat), jnp.float32), sums]
    args = list(rows)
    for chunk, _, _ in segments(window):
        args += cols[chunk]
    args += [] if first else carry
    outs = pl.pallas_call(
        functools.partial(window_kernel, len(rows), window, first, last),
        out_shape=shapes,
        in_specs=[vmem()] * len(args),
        out_specs=[vmem()] * len(shapes),
        compiler_params=params(16),
        cost_estimate=pl.CostEstimate(
            flops=2 * pair_count * BR * size * (F + feat),
            transcendentals=pair_count * BR * size,
            bytes_accessed=8 * 1024 * 1024,
        ),
        name="window",
    )(*[in_vmem(x) for x in args])
    return outs if first or last else [carry[0], *outs]


def keep_kernel(block_ref, out_ref):
    out_ref[...] = block_ref[...]


def keep(blocks):
    block = pl.BlockSpec((1, *blocks.shape[1:]), lambda k: (k, 0, 0))
    return pl.pallas_call(
        keep_kernel,
        out_shape=pltpu.HBM(blocks.shape, blocks.dtype),
        grid=(blocks.shape[0],),
        in_specs=[block],
        out_specs=block,
        compiler_params=params(4),
        name="keep",
    )(in_hbm(blocks))


def mean_kernel(local_ref, rows_ref, part_ref, mass_ref, _, out_ref, made, sems):
    pair_count, _, feat = rows_ref.shape
    local = [local_ref[pair, 0] & 7 for pair in range(pair_count)]

    def copy(pair):
        return pltpu.make_async_copy(made.at[pair], out_ref.at[local[pair]], sems.at[pair])

    firsts = []
    for pair in range(pair_count):
        same = [local[other] == local[pair] for other in range(pair)]
        firsts.append(jnp.logical_not(functools.reduce(jnp.logical_or, same, jnp.bool_(False))))
    for pair in range(pair_count):

        @pl.when(firsts[pair])
        def _():
            mass = 1.0 + mass_ref[pair]
            total = rows_ref[pair].astype(jnp.float32) + part_ref[pair].astype(jnp.float32)
            for other in range(pair + 1, pair_count):
                both = (local[other] == local[pair]).astype(jnp.float32)
                mass = mass + both * mass_ref[other]
                total = total + both * part_ref[other].astype(jnp.float32)
            scale = 1.0 / mass
            for at in range(0, feat, LANES):
                lanes = slice(at, at + LANES)
                made[pair, :, lanes] = (total[:, lanes] * scale).astype(jnp.bfloat16)
            copy(pair).start()

    for pair in range(pair_count):

        @pl.when(firsts[pair])
        def _():
            copy(pair).wait()


def means(pairs, rows, part, mass, blocks):
    pair_count, _, feat = part.shape
    return pl.pallas_call(
        mean_kernel,
        out_shape=pltpu.HBM(blocks.shape, jnp.bfloat16),
        in_specs=[smem(), vmem(), vmem(), vmem(), anywhere()],
        out_specs=anywhere(),
        scratch_shapes=[
            pltpu.VMEM((pair_count, BR, feat), jnp.bfloat16),
            pltpu.SemaphoreType.DMA((pair_count,)),
        ],
        input_output_aliases={4: 0},
        compiler_params=params(16),
        name="means",
    )(pairs, *[in_vmem(x) for x in (rows, part, mass)], in_hbm(keep(blocks)))


def hop(parts, step):
    count = lax.axis_size("narrow")
    return [lax.ppermute(part, "narrow", [(i, i ^ step) for i in range(count)]) for part in parts]


def first_hops(part):
    parts = [part]
    step = lax.axis_size("narrow") // 2
    while step > 1:
        parts = parts + hop(parts, step)
        step //= 2
    return parts


def to_wide(pieces):
    count = lax.axis_size("wide")
    return [
        lax.ppermute(piece, "wide", [(i, (i + shift) % count) for i in range(count)])
        for shift, piece in enumerate(pieces, 1)
    ]


def from_others(part):
    count = lax.axis_size("wide")
    return [part] + [
        lax.ppermute(part, "wide", [(i, (i + shift) % count) for i in range(count)])
        for shift in range(1, count)
    ]


def on_device(embeddings, pair_list):
    wide_count = lax.axis_size("wide")
    me = lax.axis_index("wide").astype(jnp.int32).reshape(1)
    pair_count = pair_list.shape[0]
    capacity = max(2, 2 * pair_count // wide_count)
    feat = embeddings.shape[1]
    blocks = embeddings.reshape(BLK_DEV, BR, feat)
    lists = from_others(pair_list)
    outgoing, row_slices = pack(me, lists, blocks, capacity)
    fixed = lax.optimization_barrier

    def pick(received, chunk):
        return select(me, pair_list, blocks, received, *CHUNKS[chunk])

    rows = first_hops(row_slices)
    rows_last = hop(rows[:1], 1)
    rows, rows_last, received = fixed((rows, rows_last, to_wide(outgoing[0])))
    cols_a = first_hops(pick(received, 0))
    rows = rows + rows_last + hop(rows[1:], 1)
    cols_a, rows, received = fixed((cols_a, rows, to_wide(outgoing[1])))
    cols_b = first_hops(pick(received, 1))
    last_b = hop(cols_b[:1], 1)
    cols_a = cols_a + hop(cols_a, 1)
    carry = window_step(rows, [cols_a], 0, None)
    cols_b, last_b, carry = fixed((cols_b, last_b, carry))
    cols_b = cols_b + last_b + hop(cols_b[1:], 1)
    carry = window_step(rows, [cols_a, cols_b], 1, carry)
    part, mass, row_sums, col_sums = carry
    every_sum = jnp.concatenate(from_others(col_sums), axis=0)
    mean = means(pair_list, row_slices, part, mass, blocks)
    block_ids = jnp.arange(BLK_DEV, dtype=jnp.int32)[:, None]
    every_col = jnp.concatenate([x[:, 1] for x in lists])
    mine = every_col[None, :] == me[0] * BLK_DEV + block_ids
    col_mass = jnp.sum(jnp.where(mine[:, :, None], every_sum[None], 0.0), axis=1)
    here = pair_list[:, 0][None, :] % BLK_DEV == block_ids
    row_mass = jnp.sum(jnp.where(here[:, :, None], row_sums[None], 0.0), axis=1)
    weights = 1.0 / (1.0 + (row_mass + col_mass) / BR)
    return weights.reshape(BLK_DEV * BR), mean.reshape(BLK_DEV * BR, feat)


def solution(mesh):
    in_specs = (P(("groups", "wide"), "narrow"), P(("groups", "wide"), None))
    out_specs = (P(("groups", "wide")), P(("groups", "wide"), "narrow"))
    return jax.shard_map(
        on_device, mesh=mesh, in_specs=in_specs, out_specs=out_specs, check_vma=False
    )
```

```python
import functools

import jax
import jax.numpy as jnp
from jax import lax
from jax.experimental import pallas as pl
from jax.experimental.pallas import tpu as pltpu
from jax.sharding import PartitionSpec as P

F = 1024
BR = 512
BLK_DEV = 8
LANES = 128
CHUNKS = ((0, 320), (320, 192))
WINDOWS = ((0, 256), (256, 512))


def smem():
    return pl.BlockSpec(memory_space=pltpu.SMEM)


def vmem():
    return pl.BlockSpec(memory_space=pltpu.VMEM)


def anywhere():
    return pl.BlockSpec(memory_space=pl.ANY)


def in_vmem(x):
    return pltpu.with_memory_space_constraint(x, pltpu.VMEM)


def in_hbm(x):
    return pltpu.with_memory_space_constraint(x, pltpu.HBM)


def params(mebibytes):
    return pltpu.CompilerParams(vmem_limit_bytes=mebibytes * 1024 * 1024)


def pack_kernel(wide_count, pair_count, capacity, me_ref, *refs):
    lists, blocks_ref, outs = refs[:wide_count], refs[wide_count], refs[wide_count + 1 : -2]
    rows_ref, sems = refs[-2:]
    me = me_ref[0]
    copies = []

    def send(source, target):
        copies.append(pltpu.make_async_copy(source, target, sems.at[len(copies)]))
        copies[-1].start()

    for chunk, (start, size) in enumerate(CHUNKS):
        for shift in range(1, wide_count):
            asked = lists[wide_count - shift]
            picks = [jnp.int32(0)] * capacity
            count = jnp.int32(0)
            for pair in range(pair_count):
                col = asked[1, pair]
                mine = (col >> 3) == me
                for slot in range(capacity):
                    picks[slot] = jnp.where(mine & (count == slot), col & 7, picks[slot])
                count = count + mine.astype(jnp.int32)
            out = outs[chunk * (wide_count - 1) + shift - 1]
            for slot in range(capacity):
                send(blocks_ref.at[picks[slot], pl.ds(start, size)], out.at[slot])
    for pair in range(pair_count):
        send(blocks_ref.at[lists[0][0, pair] & 7], rows_ref.at[pair])
    for copy in copies:
        copy.wait()


def pack(me, lists, blocks, capacity):
    wide_count, pair_count = len(lists), lists[0].shape[1]
    feat = blocks.shape[-1]
    shapes = [
        pltpu.VMEM((capacity, size, feat), blocks.dtype)
        for _, size in CHUNKS
        for _ in range(1, wide_count)
    ] + [pltpu.VMEM((pair_count, BR, feat), blocks.dtype)]
    copies = (len(shapes) - 1) * capacity + pair_count
    outs = pl.pallas_call(
        functools.partial(pack_kernel, wide_count, pair_count, capacity),
        out_shape=shapes,
        in_specs=[smem()] * (1 + wide_count) + [anywhere()],
        out_specs=[anywhere()] * len(shapes),
        scratch_shapes=[pltpu.SemaphoreType.DMA((copies,))],
        compiler_params=params(4),
        name="pack",
    )(me, *lists, in_hbm(blocks))
    each = wide_count - 1
    return [outs[c * each : (c + 1) * each] for c in range(len(CHUNKS))], outs[-1]


def select_kernel(wide_count, pair_count, start, size, me_ref, list_ref, blocks_ref, *refs):
    received, out_ref, sems = refs[:-2], refs[-2], refs[-1]
    me = me_ref[0]
    owners = [list_ref[1, pair] >> 3 for pair in range(pair_count)]
    for pair in range(pair_count):
        shift = me - owners[pair]
        shift = jnp.where(shift < 0, shift + wide_count, shift)
        rank = jnp.int32(0)
        for before in range(pair):
            rank = rank + (owners[before] == owners[pair]).astype(jnp.int32)

        @pl.when(shift == 0)
        def _():
            source = blocks_ref.at[list_ref[1, pair] & 7, pl.ds(start, size)]
            pltpu.make_async_copy(source, out_ref.at[pair], sems.at[pair]).start()

        for other in range(1, wide_count):

            @pl.when(shift == other)
            def _():
                source = received[other - 1].at[rank]
                pltpu.make_async_copy(source, out_ref.at[pair], sems.at[pair]).start()

    for pair in range(pair_count):
        source = blocks_ref.at[0, pl.ds(start, size)]
        pltpu.make_async_copy(source, out_ref.at[pair], sems.at[pair]).wait()


def select(me, pairs, blocks, received, start, size):
    pair_count, feat = pairs.shape[1], blocks.shape[-1]
    return pl.pallas_call(
        functools.partial(select_kernel, len(received) + 1, pair_count, start, size),
        out_shape=pltpu.VMEM((pair_count, size, feat), blocks.dtype),
        in_specs=[smem(), smem(), anywhere()] + [anywhere()] * len(received),
        out_specs=anywhere(),
        scratch_shapes=[pltpu.SemaphoreType.DMA((pair_count,))],
        compiler_params=params(4),
        name="select",
    )(me, pairs, in_hbm(blocks), *[in_vmem(x) for x in received])


def tree(parts):
    while len(parts) > 1:
        half = len(parts) // 2
        parts = [parts[i] + parts[i + half] for i in range(half)]
    return parts[0]


def across(left, right):
    return lax.dot_general(
        left, right, (((1,), (1,)), ((), ())), preferred_element_type=jnp.float32
    )


def lane_sum(block):
    square = jnp.square(block.astype(jnp.float32))
    return sum(square[:, at : at + LANES] for at in range(0, square.shape[1], LANES))


def segments(window):
    low, high = window
    held = []
    for chunk, (start, size) in enumerate(CHUNKS):
        first, end = max(low, start), min(high, start + size)
        if first < end:
            held.append((chunk, first - start, end - first))
    return held


def window_kernel(window, first, last, *refs):
    held = segments(window)
    all_rows, rest = refs[:2], refs[2:]
    half_count, pair_count = refs[0].shape[:2]
    narrow_count = 2 * half_count
    all_cols = [rest[i * narrow_count : (i + 1) * narrow_count] for i in range(len(held))]
    rest = rest[len(held) * narrow_count :]
    if not first:
        square_in, mass_in, total_in, sums_in = rest[:4]
        rest = rest[4:]
    if last:
        part_ref, mass_ref, row_ref, sums_ref = rest
    elif first:
        square_ref, mass_ref, total_ref, sums_ref = rest
    else:
        mass_ref, total_ref, sums_ref = rest
    for pair in range(pair_count):
        rows = [ref[i, pair] for ref in all_rows for i in range(half_count)]
        cols = []
        for narrow in range(narrow_count):
            pieces = [
                refs[narrow][pair, at : at + size] for refs, (_, at, size) in zip(all_cols, held)
            ]
            cols.append(jnp.concatenate(pieces, axis=0) if len(pieces) > 1 else pieces[0])
        if first:
            square = jnp.sum(tree([lane_sum(row) for row in rows]), axis=1, keepdims=True)
            square = jnp.broadcast_to(square, (BR, LANES))
        else:
            square = square_in[pair]
        gram = tree([across(row, col) for row, col in zip(rows, cols)])
        other = jnp.sum(tree([lane_sum(col) for col in cols]).T, axis=0, keepdims=True)
        pieces, mass = [], None
        for at in range(0, gram.shape[1], LANES):
            here = slice(at, at + LANES)
            piece = jnp.exp((square + other[:, here] - 2.0 * gram[:, here]) * (-1.0 / F))
            mass = piece if mass is None else mass + piece
            pieces.append(piece)
        kernel = jnp.concatenate(pieces, axis=1) if len(pieces) > 1 else pieces[0]
        sums = jnp.sum(kernel, axis=0, keepdims=True)
        total = jnp.dot(kernel.astype(jnp.bfloat16), cols[0], preferred_element_type=jnp.float32)
        if not first:
            mass = mass_in[pair] + mass
            total = total_in[pair] + total
            sums = jnp.concatenate([sums_in[pair : pair + 1], sums], axis=1)
        sums_ref[pair : pair + 1] = sums
        if last:
            part_ref[pair] = total.astype(jnp.bfloat16)
            mass_ref[pair] = jnp.broadcast_to(jnp.sum(mass, axis=1, keepdims=True), (BR, LANES))
            row_ref[pair : pair + 1] = jnp.sum(mass.T, axis=0, keepdims=True)
        else:
            if first:
                square_ref[pair] = square
            mass_ref[pair] = mass
            total_ref[pair] = total


def window_step(rows, cols, index, carry):
    _, pair_count, _, feat = rows[0].shape
    window = WINDOWS[index]
    size = window[1] - window[0]
    first, last = index == 0, index == len(WINDOWS) - 1
    lanes = pltpu.VMEM((pair_count, BR, LANES), jnp.float32)
    sums = pltpu.VMEM((pair_count, window[1]), jnp.float32)
    if last:
        shapes = [
            pltpu.VMEM((pair_count, BR, feat), jnp.bfloat16),
            lanes,
            pltpu.VMEM((pair_count, BR), jnp.float32),
            sums,
        ]
    else:
        shapes = [lanes] * (1 + first) + [pltpu.VMEM((pair_count, BR, feat), jnp.float32), sums]
    args = list(rows)
    for chunk, _, _ in segments(window):
        args += cols[chunk]
    args += [] if first else carry
    outs = pl.pallas_call(
        functools.partial(window_kernel, window, first, last),
        out_shape=shapes,
        in_specs=[vmem()] * len(args),
        out_specs=[vmem()] * len(shapes),
        compiler_params=params(16),
        cost_estimate=pl.CostEstimate(
            flops=2 * pair_count * BR * size * (F + feat),
            transcendentals=pair_count * BR * size,
            bytes_accessed=8 * 1024 * 1024,
        ),
        name="window",
    )(*[in_vmem(x) for x in args])
    return outs if first or last else [carry[0], *outs]


def keep_kernel(block_ref, out_ref):
    out_ref[...] = block_ref[...]


def keep(blocks):
    block = pl.BlockSpec((1, *blocks.shape[1:]), lambda k: (k, 0, 0))
    return pl.pallas_call(
        keep_kernel,
        out_shape=pltpu.HBM(blocks.shape, blocks.dtype),
        grid=(blocks.shape[0],),
        in_specs=[block],
        out_specs=block,
        compiler_params=params(4),
        name="keep",
    )(in_hbm(blocks))


def mean_kernel(local_ref, rows_ref, part_ref, mass_ref, _, out_ref, made, sems):
    pair_count, _, feat = rows_ref.shape
    local = [local_ref[0, pair] & 7 for pair in range(pair_count)]

    def copy(pair):
        return pltpu.make_async_copy(made.at[pair], out_ref.at[local[pair]], sems.at[pair])

    firsts = []
    for pair in range(pair_count):
        same = [local[other] == local[pair] for other in range(pair)]
        firsts.append(jnp.logical_not(functools.reduce(jnp.logical_or, same, jnp.bool_(False))))
    for pair in range(pair_count):

        @pl.when(firsts[pair])
        def _():
            mass = 1.0 + mass_ref[pair]
            total = rows_ref[pair].astype(jnp.float32) + part_ref[pair].astype(jnp.float32)
            for other in range(pair + 1, pair_count):
                both = (local[other] == local[pair]).astype(jnp.float32)
                mass = mass + both * mass_ref[other]
                total = total + both * part_ref[other].astype(jnp.float32)
            scale = 1.0 / mass
            for at in range(0, feat, LANES):
                lanes = slice(at, at + LANES)
                made[pair, :, lanes] = (total[:, lanes] * scale).astype(jnp.bfloat16)
            copy(pair).start()

    for pair in range(pair_count):

        @pl.when(firsts[pair])
        def _():
            copy(pair).wait()


def means(pairs, rows, part, mass, kept):
    pair_count, _, feat = part.shape
    return pl.pallas_call(
        mean_kernel,
        out_shape=pltpu.HBM(kept.shape, jnp.bfloat16),
        in_specs=[smem(), vmem(), vmem(), vmem(), anywhere()],
        out_specs=anywhere(),
        scratch_shapes=[
            pltpu.VMEM((pair_count, BR, feat), jnp.bfloat16),
            pltpu.SemaphoreType.DMA((pair_count,)),
        ],
        input_output_aliases={4: 0},
        compiler_params=params(16),
        name="means",
    )(pairs, *[in_vmem(x) for x in (rows, part, mass)], in_hbm(kept))


def weight_kernel(wide_count, me_ref, *refs):
    lists, rows_ref, sums, out_ref = refs[:wide_count], refs[wide_count], refs[wide_count + 1 : -1], refs[-1]
    pair_count = rows_ref.shape[0]
    first = me_ref[0] * BLK_DEV
    for block in range(BLK_DEV):
        mass = jnp.zeros((1, BR), jnp.float32)
        for pair in range(pair_count):
            here = (lists[0][0, pair] == first + block).astype(jnp.float32)
            mass = mass + here * rows_ref[pair : pair + 1]
            for asked, sums_ref in zip(lists, sums):
                here = (asked[1, pair] == first + block).astype(jnp.float32)
                mass = mass + here * sums_ref[pair : pair + 1]
        weight = 1.0 / (1.0 + mass / BR)
        for part in range(BR // LANES):
            row = block * (BR // LANES) + part
            out_ref[row : row + 1] = weight[:, part * LANES : (part + 1) * LANES]


def block_weights(me, lists, row_sums, col_sums):
    out = pl.pallas_call(
        functools.partial(weight_kernel, len(lists)),
        out_shape=jax.ShapeDtypeStruct((BLK_DEV * BR // LANES, LANES), jnp.float32),
        in_specs=[smem()] * (1 + len(lists)) + [vmem()] * (1 + len(col_sums)),
        out_specs=vmem(),
        compiler_params=params(4),
        name="weights",
    )(me, *lists, row_sums, *col_sums)
    return out.reshape(BLK_DEV * BR)


def hop(parts, step):
    count = lax.axis_size("narrow")
    return [lax.ppermute(part, "narrow", [(i, i ^ step) for i in range(count)]) for part in parts]


def first_hops(part):
    parts = [part]
    step = lax.axis_size("narrow") // 2
    while step > 1:
        parts = parts + hop(parts, step)
        step //= 2
    return parts


def to_wide(pieces):
    count = lax.axis_size("wide")
    return [
        lax.ppermute(piece, "wide", [(i, (i + shift) % count) for i in range(count)])
        for shift, piece in enumerate(pieces, 1)
    ]


def from_others(part):
    count = lax.axis_size("wide")
    return [part] + [
        lax.ppermute(part, "wide", [(i, (i + shift) % count) for i in range(count)])
        for shift in range(1, count)
    ]


def on_device(embeddings, pair_list):
    wide_count = lax.axis_size("wide")
    me = lax.axis_index("wide").astype(jnp.int32).reshape(1)
    pairs = pair_list.T
    pair_count = pairs.shape[1]
    capacity = max(2, 2 * pair_count // wide_count)
    feat = embeddings.shape[1]
    blocks = embeddings.reshape(BLK_DEV, BR, feat)
    lists = from_others(pairs)
    outgoing, row_slices = pack(me, lists, blocks, capacity)
    fixed = lax.optimization_barrier

    def pick(received, chunk):
        return select(me, pairs, blocks, received, *CHUNKS[chunk])

    rows = jnp.stack(first_hops(row_slices))
    rows, received, kept = fixed((rows, to_wide(outgoing[0]), keep(blocks)))
    cols_a = first_hops(pick(received, 0))
    rows = [rows, *hop([rows], 1)]
    cols_a, rows, received = fixed((cols_a, rows, to_wide(outgoing[1])))
    cols_b = first_hops(pick(received, 1))
    last_b = hop(cols_b[:1], 1)
    cols_a = cols_a + hop(cols_a, 1)
    carry = window_step(rows, [cols_a], 0, None)
    cols_b, last_b, carry = fixed((cols_b, last_b, carry))
    cols_b = cols_b + last_b + hop(cols_b[1:], 1)
    part, mass, row_sums, col_sums = window_step(rows, [cols_a, cols_b], 1, carry)
    every_sum = from_others(col_sums)
    mean = means(pairs, row_slices, part, mass, kept)
    weights = block_weights(me, lists, row_sums, every_sum)
    return weights, mean.reshape(BLK_DEV * BR, feat)


def solution(mesh):
    in_specs = (P(("groups", "wide"), "narrow"), P(("groups", "wide"), None))
    out_specs = (P(("groups", "wide")), P(("groups", "wide"), "narrow"))
    return jax.shard_map(
        on_device, mesh=mesh, in_specs=in_specs, out_specs=out_specs, check_vma=False
    )
```

```python
import functools

import jax
import jax.numpy as jnp
from jax import lax
from jax.experimental import pallas as pl
from jax.experimental.pallas import tpu as pltpu
from jax.sharding import PartitionSpec as P

F = 1024
BR = 512
BLK_DEV = 8
LANES = 128
CHUNKS = ((0, 320), (320, 192))
WINDOWS = ((0, 256), (256, 512))


def smem():
    return pl.BlockSpec(memory_space=pltpu.SMEM)


def vmem():
    return pl.BlockSpec(memory_space=pltpu.VMEM)


def anywhere():
    return pl.BlockSpec(memory_space=pl.ANY)


def in_vmem(x):
    return pltpu.with_memory_space_constraint(x, pltpu.VMEM)


def in_hbm(x):
    return pltpu.with_memory_space_constraint(x, pltpu.HBM)


def params(mebibytes):
    return pltpu.CompilerParams(vmem_limit_bytes=mebibytes * 1024 * 1024)


def pack_kernel(wide_count, pair_count, capacity, me_ref, *refs):
    lists, blocks_ref = refs[: wide_count - 1], refs[wide_count - 1]
    outs, sems = refs[wide_count:-1], refs[-1]
    me = me_ref[0]
    copies = []

    def send(source, target):
        copies.append(pltpu.make_async_copy(source, target, sems.at[len(copies)]))
        copies[-1].start()

    for chunk, (start, size) in enumerate(CHUNKS):
        for shift in range(1, wide_count):
            asked = lists[wide_count - shift - 1]
            picks = [jnp.int32(0)] * capacity
            count = jnp.int32(0)
            for pair in range(pair_count):
                col = asked[1, pair]
                mine = (col >> 3) == me
                for slot in range(capacity):
                    picks[slot] = jnp.where(mine & (count == slot), col & 7, picks[slot])
                count = count + mine.astype(jnp.int32)
            out = outs[chunk * (wide_count - 1) + shift - 1]
            for slot in range(capacity):
                send(blocks_ref.at[picks[slot], pl.ds(start, size)], out.at[slot])
    for copy in copies:
        copy.wait()


def pack(me, lists, blocks, capacity):
    wide_count, pair_count = len(lists) + 1, lists[0].shape[1]
    feat = blocks.shape[-1]
    shapes = [
        pltpu.VMEM((capacity, size, feat), blocks.dtype)
        for _, size in CHUNKS
        for _ in range(1, wide_count)
    ]
    outs = pl.pallas_call(
        functools.partial(pack_kernel, wide_count, pair_count, capacity),
        out_shape=shapes,
        in_specs=[smem()] * wide_count + [anywhere()],
        out_specs=[anywhere()] * len(shapes),
        scratch_shapes=[pltpu.SemaphoreType.DMA((len(shapes) * capacity,))],
        compiler_params=params(4),
        name="pack",
    )(me, *lists, in_hbm(blocks))
    each = wide_count - 1
    return [outs[c * each : (c + 1) * each] for c in range(len(CHUNKS))]


def take_kernel(pairs_ref, blocks_ref, out_ref, sems):
    copies = []
    for pair in range(out_ref.shape[0]):
        source = blocks_ref.at[pairs_ref[0, pair] & 7]
        copies.append(pltpu.make_async_copy(source, out_ref.at[pair], sems.at[pair]))
        copies[-1].start()
    for copy in copies:
        copy.wait()


def take(pairs, blocks):
    pair_count = pairs.shape[1]
    return pl.pallas_call(
        take_kernel,
        out_shape=pltpu.VMEM((pair_count, *blocks.shape[1:]), blocks.dtype),
        in_specs=[smem(), anywhere()],
        out_specs=anywhere(),
        scratch_shapes=[pltpu.SemaphoreType.DMA((pair_count,))],
        compiler_params=params(4),
        name="take",
    )(pairs, in_hbm(blocks))


def select_kernel(wide_count, pair_count, start, size, me_ref, list_ref, blocks_ref, *refs):
    received, out_ref, sems = refs[:-2], refs[-2], refs[-1]
    me = me_ref[0]
    owners = [list_ref[1, pair] >> 3 for pair in range(pair_count)]
    for pair in range(pair_count):
        shift = me - owners[pair]
        shift = jnp.where(shift < 0, shift + wide_count, shift)
        rank = jnp.int32(0)
        for before in range(pair):
            rank = rank + (owners[before] == owners[pair]).astype(jnp.int32)

        @pl.when(shift == 0)
        def _():
            source = blocks_ref.at[list_ref[1, pair] & 7, pl.ds(start, size)]
            pltpu.make_async_copy(source, out_ref.at[pair], sems.at[pair]).start()

        for other in range(1, wide_count):

            @pl.when(shift == other)
            def _():
                source = received[other - 1].at[rank]
                pltpu.make_async_copy(source, out_ref.at[pair], sems.at[pair]).start()

    for pair in range(pair_count):
        source = blocks_ref.at[0, pl.ds(start, size)]
        pltpu.make_async_copy(source, out_ref.at[pair], sems.at[pair]).wait()


def select(me, pairs, blocks, received, start, size):
    pair_count, feat = pairs.shape[1], blocks.shape[-1]
    return pl.pallas_call(
        functools.partial(select_kernel, len(received) + 1, pair_count, start, size),
        out_shape=pltpu.VMEM((pair_count, size, feat), blocks.dtype),
        in_specs=[smem(), smem(), anywhere()] + [anywhere()] * len(received),
        out_specs=anywhere(),
        scratch_shapes=[pltpu.SemaphoreType.DMA((pair_count,))],
        compiler_params=params(4),
        name="select",
    )(me, pairs, in_hbm(blocks), *[in_vmem(x) for x in received])


def tree(parts):
    while len(parts) > 1:
        half = len(parts) // 2
        parts = [parts[i] + parts[i + half] for i in range(half)]
    return parts[0]


def across(left, right):
    return lax.dot_general(
        left, right, (((1,), (1,)), ((), ())), preferred_element_type=jnp.float32
    )


def lane_sum(block):
    square = jnp.square(block.astype(jnp.float32))
    return sum(square[:, at : at + LANES] for at in range(0, square.shape[1], LANES))


def segments(window):
    low, high = window
    held = []
    for chunk, (start, size) in enumerate(CHUNKS):
        first, end = max(low, start), min(high, start + size)
        if first < end:
            held.append((chunk, first - start, end - first))
    return held


def scores(rows, cols, square):
    gram = tree([across(row, col) for row, col in zip(rows, cols)])
    other = jnp.sum(tree([lane_sum(col) for col in cols]).T, axis=0, keepdims=True)
    pieces, mass = [], None
    for at in range(0, gram.shape[1], LANES):
        here = slice(at, at + LANES)
        piece = jnp.exp((square + other[:, here] - 2.0 * gram[:, here]) * (-1.0 / F))
        mass = piece if mass is None else mass + piece
        pieces.append(piece)
    kernel = jnp.concatenate(pieces, axis=1) if len(pieces) > 1 else pieces[0]
    return kernel.astype(jnp.bfloat16), jnp.sum(kernel, axis=0, keepdims=True), mass


def window_parts(window, refs, pair):
    held = segments(window)
    half_count = refs[0].shape[0]
    narrow_count = 2 * half_count
    rows = [ref[i, pair] for ref in refs[:2] for i in range(half_count)]
    chunks = [refs[2 + i * narrow_count :][:narrow_count] for i in range(len(held))]
    cols = [own_columns(window, [chunk[i] for chunk in chunks], pair) for i in range(narrow_count)]
    return rows, cols


def own_columns(window, chunks, pair):
    held = segments(window)
    pieces = [ref[pair, at : at + size] for ref, (_, at, size) in zip(chunks, held)]
    return jnp.concatenate(pieces, axis=0) if len(pieces) > 1 else pieces[0]


def first_kernel(window, *refs):
    square_ref, mass_ref, total_ref, sums_ref = refs[-4:]
    for pair in range(square_ref.shape[0]):
        rows, cols = window_parts(window, refs, pair)
        square = jnp.sum(tree([lane_sum(row) for row in rows]), axis=1, keepdims=True)
        square = jnp.broadcast_to(square, (BR, LANES))
        kernel, sums, mass = scores(rows, cols, square)
        square_ref[pair] = square
        mass_ref[pair] = mass
        sums_ref[pair : pair + 1] = sums
        total_ref[pair] = jnp.dot(kernel, cols[0], preferred_element_type=jnp.float32)


def last_kernel(window, wide_count, me_ref, pairs_ref, *refs):
    square_in, mass_in, sums_in = refs[-6 - wide_count : -3 - wide_count]
    kernel_ref, mass_ref, row_ref = refs[-3 - wide_count : -wide_count]
    shares = refs[-wide_count:]
    for ref in (row_ref, *shares):
        ref[...] = jnp.zeros_like(ref)
    for pair in range(square_in.shape[0]):
        rows, cols = window_parts(window, refs, pair)
        kernel, sums, mass = scores(rows, cols, square_in[pair])
        kernel_ref[pair] = kernel
        sums = jnp.concatenate([sums_in[pair : pair + 1], sums], axis=1)
        mass = mass_in[pair] + mass
        mass_ref[pair] = mass
        row_ref[pl.ds(pairs_ref[0, pair] & 7, 1)] += jnp.sum(mass.T, axis=0, keepdims=True)
        col = pairs_ref[1, pair]
        shift = (col >> 3) - me_ref[0]
        shift = jnp.where(shift < 0, shift + wide_count, shift)
        for other, ref in enumerate(shares):
            ref[pl.ds(col & 7, 1)] += jnp.where(shift == other, sums, 0.0)


def estimate(pair_count, size):
    return pl.CostEstimate(
        flops=2 * pair_count * BR * size * F,
        transcendentals=pair_count * BR * size,
        bytes_accessed=8 * 1024 * 1024,
    )


def first_window(rows, cols):
    _, pair_count, _, feat = rows[0].shape
    window = WINDOWS[0]
    lanes = pltpu.VMEM((pair_count, BR, LANES), jnp.float32)
    total = pltpu.VMEM((pair_count, BR, feat), jnp.float32)
    args = list(rows)
    for chunk, _, _ in segments(window):
        args += cols[chunk]
    return pl.pallas_call(
        functools.partial(first_kernel, window),
        out_shape=[lanes, lanes, total, pltpu.VMEM((pair_count, window[1]), jnp.float32)],
        in_specs=[vmem()] * len(args),
        out_specs=[vmem()] * 4,
        compiler_params=params(16),
        cost_estimate=estimate(pair_count, window[1]),
        name="first_window",
    )(*[in_vmem(x) for x in args])


def last_window(me, pairs, rows, cols, square, mass, sums, wide_count):
    pair_count = rows[0].shape[1]
    window = WINDOWS[1]
    size = window[1] - window[0]
    by_block = pltpu.VMEM((BLK_DEV, BR), jnp.float32)
    shapes = [
        pltpu.VMEM((pair_count, BR, size), jnp.bfloat16),
        pltpu.VMEM((pair_count, BR, LANES), jnp.float32),
    ] + [by_block] * (1 + wide_count)
    args = list(rows)
    for chunk, _, _ in segments(window):
        args += cols[chunk]
    args += [square, mass, sums]
    kernel, mass, row_sums, *shares = pl.pallas_call(
        functools.partial(last_kernel, window, wide_count),
        out_shape=shapes,
        in_specs=[smem(), smem()] + [vmem()] * len(args),
        out_specs=[vmem()] * len(shapes),
        compiler_params=params(16),
        cost_estimate=estimate(pair_count, size),
        name="last_window",
    )(me, pairs, *[in_vmem(x) for x in args])
    return kernel, mass, row_sums, shares


def keep_kernel(block_ref, out_ref):
    out_ref[...] = block_ref[...]


def keep(blocks):
    block = pl.BlockSpec((1, *blocks.shape[1:]), lambda k: (k, 0, 0))
    return pl.pallas_call(
        keep_kernel,
        out_shape=pltpu.HBM(blocks.shape, blocks.dtype),
        grid=(blocks.shape[0],),
        in_specs=[block],
        out_specs=block,
        compiler_params=params(4),
        name="keep",
    )(in_hbm(blocks))


def mean_kernel(window, local_ref, rows_ref, kernel_ref, mass_ref, total_ref, *refs):
    *chunks, _, out_ref, part, weight, total, mass, made, sems = refs
    pair_count, _, feat = rows_ref.shape
    local = [local_ref[0, pair] & 7 for pair in range(pair_count)]

    def copy(pair):
        return pltpu.make_async_copy(made.at[pair], out_ref.at[local[pair]], sems.at[pair])

    firsts = []
    for pair in range(pair_count):
        sums = total_ref[pair] + jnp.dot(
            kernel_ref[pair], own_columns(window, chunks, pair), preferred_element_type=jnp.float32
        )
        part[pair] = sums.astype(jnp.bfloat16)
        weight[pair] = jnp.broadcast_to(
            jnp.sum(mass_ref[pair], axis=1, keepdims=True), (BR, LANES)
        )
        same = [local[other] == local[pair] for other in range(pair)]
        firsts.append(jnp.logical_not(functools.reduce(jnp.logical_or, same, jnp.bool_(False))))
    for pair in range(pair_count):

        @pl.when(firsts[pair])
        def _():
            total[...] = rows_ref[pair].astype(jnp.float32) + part[pair].astype(jnp.float32)
            mass[...] = 1.0 + weight[pair]
            for other in range(pair + 1, pair_count):

                @pl.when(local[other] == local[pair])
                def _():
                    total[...] += part[other].astype(jnp.float32)
                    mass[...] += weight[other]

            scale = 1.0 / mass[...]
            for at in range(0, feat, LANES):
                lanes = slice(at, at + LANES)
                made[pair, :, lanes] = (total[:, lanes] * scale).astype(jnp.bfloat16)
            copy(pair).start()

    for pair in range(pair_count):

        @pl.when(firsts[pair])
        def _():
            copy(pair).wait()


def means(pairs, rows, kernel, mass, total, cols, kept):
    pair_count, _, feat = rows.shape
    window = WINDOWS[1]
    own = [cols[chunk][0] for chunk, _, _ in segments(window)]
    args = [in_vmem(x) for x in (rows, kernel, mass, total, *own)]
    return pl.pallas_call(
        functools.partial(mean_kernel, window),
        out_shape=pltpu.HBM(kept.shape, jnp.bfloat16),
        in_specs=[smem()] + [vmem()] * len(args) + [anywhere()],
        out_specs=anywhere(),
        scratch_shapes=[
            pltpu.VMEM((pair_count, BR, feat), jnp.bfloat16),
            pltpu.VMEM((pair_count, BR, LANES), jnp.float32),
            pltpu.VMEM((BR, feat), jnp.float32),
            pltpu.VMEM((BR, LANES), jnp.float32),
            pltpu.VMEM((pair_count, BR, feat), jnp.bfloat16),
            pltpu.SemaphoreType.DMA((pair_count,)),
        ],
        input_output_aliases={1 + len(args): 0},
        compiler_params=params(16),
        cost_estimate=estimate(pair_count, 128),
        name="means",
    )(pairs, *args, in_hbm(kept))


def weight_kernel(*refs):
    out_ref = refs[-1]
    mass = refs[0][...]
    for ref in refs[1:-1]:
        mass = mass + ref[...]
    weight = 1.0 / (1.0 + mass / BR)
    parts = BR // LANES
    for block in range(BLK_DEV):
        for part in range(parts):
            lanes = slice(part * LANES, (part + 1) * LANES)
            out_ref[block * parts + part : block * parts + part + 1] = weight[block : block + 1, lanes]


def block_weights(sums):
    out = pl.pallas_call(
        weight_kernel,
        out_shape=jax.ShapeDtypeStruct((BLK_DEV * BR // LANES, LANES), jnp.float32),
        in_specs=[vmem()] * len(sums),
        out_specs=vmem(),
        compiler_params=params(4),
        name="weights",
    )(*[in_vmem(x) for x in sums])
    return out.reshape(BLK_DEV * BR)


def hop(parts, step):
    count = lax.axis_size("narrow")
    return [lax.ppermute(part, "narrow", [(i, i ^ step) for i in range(count)]) for part in parts]


def first_hops(part):
    parts = [part]
    step = lax.axis_size("narrow") // 2
    while step > 1:
        parts = parts + hop(parts, step)
        step //= 2
    return parts


def to_wide(pieces):
    count = lax.axis_size("wide")
    return [
        lax.ppermute(piece, "wide", [(i, (i + shift) % count) for i in range(count)])
        for shift, piece in enumerate(pieces, 1)
    ]


def on_device(embeddings, pair_list):
    wide_count = lax.axis_size("wide")
    me = lax.axis_index("wide").astype(jnp.int32).reshape(1)
    pairs = pair_list.T
    pair_count = pairs.shape[1]
    capacity = max(2, 2 * pair_count // wide_count)
    feat = embeddings.shape[1]
    blocks = embeddings.reshape(BLK_DEV, BR, feat)
    lists = to_wide([pairs] * (wide_count - 1))
    fixed = lax.optimization_barrier
    lists, row_slices = fixed((lists, take(pairs, blocks)))
    outgoing = pack(me, lists, blocks, capacity)

    def pick(received, chunk):
        return select(me, pairs, blocks, received, *CHUNKS[chunk])

    rows = jnp.stack(first_hops(row_slices))
    rows, received, kept = fixed((rows, to_wide(outgoing[0]), keep(blocks)))
    cols_a = first_hops(pick(received, 0))
    rows = [rows, *hop([rows], 1)]
    cols_a, rows, received = fixed((cols_a, rows, to_wide(outgoing[1])))
    cols_b = first_hops(pick(received, 1))
    last_b = hop(cols_b[:1], 1)
    cols_a = cols_a + hop(cols_a, 1)
    carry = first_window(rows, [cols_a])
    cols_b, last_b, carry = fixed((cols_b, last_b, carry))
    cols_b = cols_b + last_b + hop(cols_b[1:], 1)
    square, mass, total, sums = carry
    kernel, mass, row_sums, shares = last_window(
        me, pairs, rows, [cols_a, cols_b], square, mass, sums, wide_count
    )
    came = to_wide(shares[1:])
    mean = means(pairs, row_slices, kernel, mass, total, [cols_a, cols_b], kept)
    weights = block_weights([row_sums, shares[0], *came])
    return weights, mean.reshape(BLK_DEV * BR, feat)


def solution(mesh):
    in_specs = (P(("groups", "wide"), "narrow"), P(("groups", "wide"), None))
    out_specs = (P(("groups", "wide")), P(("groups", "wide"), "narrow"))
    return jax.shard_map(
        on_device, mesh=mesh, in_specs=in_specs, out_specs=out_specs, check_vma=False
    )
```

```python
import functools

import jax
import jax.numpy as jnp
from jax import lax
from jax.experimental import pallas as pl
from jax.experimental.pallas import tpu as pltpu
from jax.sharding import PartitionSpec as P

F = 1024
BR = 512
BLK_DEV = 8
LANES = 128
CHUNKS = ((0, 368), (368, 144))
WINDOWS = ((0, 256), (256, 512))


def smem():
    return pl.BlockSpec(memory_space=pltpu.SMEM)


def vmem():
    return pl.BlockSpec(memory_space=pltpu.VMEM)


def anywhere():
    return pl.BlockSpec(memory_space=pl.ANY)


def in_vmem(x):
    return pltpu.with_memory_space_constraint(x, pltpu.VMEM)


def in_hbm(x):
    return pltpu.with_memory_space_constraint(x, pltpu.HBM)


def params(mebibytes):
    return pltpu.CompilerParams(vmem_limit_bytes=mebibytes * 1024 * 1024)


def pack_kernel(wide_count, pair_count, capacity, me_ref, *refs):
    lists, blocks_ref = refs[: wide_count - 1], refs[wide_count - 1]
    outs, sems = refs[wide_count:-1], refs[-1]
    me = me_ref[0]
    copies = []

    def send(source, target):
        copies.append(pltpu.make_async_copy(source, target, sems.at[len(copies)]))
        copies[-1].start()

    for chunk, (start, size) in enumerate(CHUNKS):
        for shift in range(1, wide_count):
            asked = lists[wide_count - shift - 1]
            picks = [jnp.int32(0)] * capacity
            count = jnp.int32(0)
            for pair in range(pair_count):
                col = asked[1, pair]
                mine = (col >> 3) == me
                for slot in range(capacity):
                    picks[slot] = jnp.where(mine & (count == slot), col & 7, picks[slot])
                count = count + mine.astype(jnp.int32)
            out = outs[chunk * (wide_count - 1) + shift - 1]
            for slot in range(capacity):
                send(blocks_ref.at[picks[slot], pl.ds(start, size)], out.at[slot])
    for copy in copies:
        copy.wait()


def pack(me, lists, blocks, capacity):
    wide_count, pair_count = len(lists) + 1, lists[0].shape[1]
    feat = blocks.shape[-1]
    shapes = [
        pltpu.VMEM((capacity, size, feat), blocks.dtype)
        for _, size in CHUNKS
        for _ in range(1, wide_count)
    ]
    outs = pl.pallas_call(
        functools.partial(pack_kernel, wide_count, pair_count, capacity),
        out_shape=shapes,
        in_specs=[smem()] * wide_count + [anywhere()],
        out_specs=[anywhere()] * len(shapes),
        scratch_shapes=[pltpu.SemaphoreType.DMA((len(shapes) * capacity,))],
        compiler_params=params(4),
        name="pack",
    )(me, *lists, in_hbm(blocks))
    each = wide_count - 1
    return [outs[c * each : (c + 1) * each] for c in range(len(CHUNKS))]


def take_kernel(pairs_ref, blocks_ref, rows_ref, cols_ref, sems):
    copies = []
    for pair in range(rows_ref.shape[0]):
        for side, out in enumerate((rows_ref, cols_ref)):
            source = blocks_ref.at[pairs_ref[side, pair] & 7]
            copies.append(pltpu.make_async_copy(source, out.at[pair], sems.at[len(copies)]))
            copies[-1].start()
    for copy in copies:
        copy.wait()


def take(pairs, blocks):
    pair_count = pairs.shape[1]
    taken = pltpu.VMEM((pair_count, *blocks.shape[1:]), blocks.dtype)
    return pl.pallas_call(
        take_kernel,
        out_shape=[taken, taken],
        in_specs=[smem(), anywhere()],
        out_specs=[anywhere(), anywhere()],
        scratch_shapes=[pltpu.SemaphoreType.DMA((2 * pair_count,))],
        compiler_params=params(4),
        name="take",
    )(pairs, in_hbm(blocks))


def select_kernel(start, me_ref, pairs_ref, own_ref, *refs):
    received, out_ref = refs[:-1], refs[-1]
    wide_count = len(received) + 1
    pair_count, size, _ = out_ref.shape
    owners = [pairs_ref[1, pair] >> 3 for pair in range(pair_count)]
    for pair in range(pair_count):
        shift = me_ref[0] - owners[pair]
        shift = jnp.where(shift < 0, shift + wide_count, shift)
        rank = jnp.int32(0)
        for before in range(pair):
            rank = rank + (owners[before] == owners[pair]).astype(jnp.int32)

        @pl.when(shift == 0)
        def _():
            out_ref[pair] = own_ref[pair, start : start + size]

        for other in range(1, wide_count):

            @pl.when(shift == other)
            def _():
                out_ref[pair] = received[other - 1][rank]


def select(me, pairs, own, received, start, size):
    pair_count, _, feat = own.shape
    return pl.pallas_call(
        functools.partial(select_kernel, start),
        out_shape=pltpu.VMEM((pair_count, size, feat), own.dtype),
        in_specs=[smem(), smem()] + [vmem()] * (1 + len(received)),
        out_specs=vmem(),
        compiler_params=params(4),
        name="select",
    )(me, pairs, *[in_vmem(x) for x in (own, *received)])


def tree(parts):
    while len(parts) > 1:
        half = len(parts) // 2
        parts = [parts[i] + parts[i + half] for i in range(half)]
    return parts[0]


def across(left, right):
    return lax.dot_general(
        left, right, (((1,), (1,)), ((), ())), preferred_element_type=jnp.float32
    )


def lane_sum(block):
    square = jnp.square(block.astype(jnp.float32))
    return sum(square[:, at : at + LANES] for at in range(0, square.shape[1], LANES))


def segments(window):
    low, high = window
    held = []
    for chunk, (start, size) in enumerate(CHUNKS):
        first, end = max(low, start), min(high, start + size)
        if first < end:
            held.append((chunk, first - start, end - first))
    return held


def scores(rows, cols, square):
    gram = tree([across(row, col) for row, col in zip(rows, cols)])
    other = jnp.sum(tree([lane_sum(col) for col in cols]).T, axis=0, keepdims=True)
    pieces, mass = [], None
    for at in range(0, gram.shape[1], LANES):
        here = slice(at, at + LANES)
        piece = jnp.exp((square + other[:, here] - 2.0 * gram[:, here]) * (-1.0 / F))
        mass = piece if mass is None else mass + piece
        pieces.append(piece)
    kernel = jnp.concatenate(pieces, axis=1) if len(pieces) > 1 else pieces[0]
    return kernel.astype(jnp.bfloat16), jnp.sum(kernel, axis=0, keepdims=True), mass


def window_parts(window, refs, pair):
    held = segments(window)
    half_count = refs[0].shape[0]
    narrow_count = 2 * half_count
    rows = [ref[i, pair] for ref in refs[:2] for i in range(half_count)]
    chunks = [refs[2 + i * narrow_count :][:narrow_count] for i in range(len(held))]
    cols = [own_columns(window, [chunk[i] for chunk in chunks], pair) for i in range(narrow_count)]
    return rows, cols


def own_columns(window, chunks, pair):
    held = segments(window)
    pieces = [ref[pair, at : at + size] for ref, (_, at, size) in zip(chunks, held)]
    return jnp.concatenate(pieces, axis=0) if len(pieces) > 1 else pieces[0]


def first_kernel(window, *refs):
    square_ref, mass_ref, total_ref, sums_ref = refs[-4:]
    for pair in range(square_ref.shape[0]):
        rows, cols = window_parts(window, refs, pair)
        square = jnp.sum(tree([lane_sum(row) for row in rows]), axis=1, keepdims=True)
        square = jnp.broadcast_to(square, (BR, LANES))
        kernel, sums, mass = scores(rows, cols, square)
        square_ref[pair] = square
        mass_ref[pair] = mass
        sums_ref[pair : pair + 1] = sums
        total_ref[pair] = jnp.dot(kernel, cols[0], preferred_element_type=jnp.float32)


def last_kernel(window, wide_count, me_ref, pairs_ref, *refs):
    square_in, mass_in, sums_in = refs[-6 - wide_count : -3 - wide_count]
    kernel_ref, mass_ref, row_ref = refs[-3 - wide_count : -wide_count]
    shares = refs[-wide_count:]
    for ref in (row_ref, *shares):
        ref[...] = jnp.zeros_like(ref)
    for pair in range(square_in.shape[0]):
        rows, cols = window_parts(window, refs, pair)
        kernel, sums, mass = scores(rows, cols, square_in[pair])
        kernel_ref[pair] = kernel
        sums = jnp.concatenate([sums_in[pair : pair + 1], sums], axis=1)
        mass = mass_in[pair] + mass
        mass_ref[pair] = mass
        row_ref[pl.ds(pairs_ref[0, pair] & 7, 1)] += jnp.sum(mass.T, axis=0, keepdims=True)
        col = pairs_ref[1, pair]
        shift = (col >> 3) - me_ref[0]
        shift = jnp.where(shift < 0, shift + wide_count, shift)
        for other, ref in enumerate(shares):
            ref[pl.ds(col & 7, 1)] += jnp.where(shift == other, sums, 0.0)


def estimate(pair_count, size):
    return pl.CostEstimate(
        flops=2 * pair_count * BR * size * F,
        transcendentals=pair_count * BR * size,
        bytes_accessed=8 * 1024 * 1024,
    )


def first_window(rows, cols):
    _, pair_count, _, feat = rows[0].shape
    window = WINDOWS[0]
    lanes = pltpu.VMEM((pair_count, BR, LANES), jnp.float32)
    total = pltpu.VMEM((pair_count, BR, feat), jnp.float32)
    args = list(rows)
    for chunk, _, _ in segments(window):
        args += cols[chunk]
    return pl.pallas_call(
        functools.partial(first_kernel, window),
        out_shape=[lanes, lanes, total, pltpu.VMEM((pair_count, window[1]), jnp.float32)],
        in_specs=[vmem()] * len(args),
        out_specs=[vmem()] * 4,
        compiler_params=params(16),
        cost_estimate=estimate(pair_count, window[1]),
        name="first_window",
    )(*[in_vmem(x) for x in args])


def last_window(me, pairs, rows, cols, square, mass, sums, wide_count):
    pair_count = rows[0].shape[1]
    window = WINDOWS[1]
    size = window[1] - window[0]
    by_block = pltpu.VMEM((BLK_DEV, BR), jnp.float32)
    shapes = [
        pltpu.VMEM((pair_count, BR, size), jnp.bfloat16),
        pltpu.VMEM((pair_count, BR, LANES), jnp.float32),
    ] + [by_block] * (1 + wide_count)
    args = list(rows)
    for chunk, _, _ in segments(window):
        args += cols[chunk]
    args += [square, mass, sums]
    kernel, mass, row_sums, *shares = pl.pallas_call(
        functools.partial(last_kernel, window, wide_count),
        out_shape=shapes,
        in_specs=[smem(), smem()] + [vmem()] * len(args),
        out_specs=[vmem()] * len(shapes),
        compiler_params=params(16),
        cost_estimate=estimate(pair_count, size),
        name="last_window",
    )(me, pairs, *[in_vmem(x) for x in args])
    return kernel, mass, row_sums, shares


def keep_kernel(block_ref, out_ref):
    out_ref[...] = block_ref[...]


def keep(blocks):
    block = pl.BlockSpec((1, *blocks.shape[1:]), lambda k: (k, 0, 0))
    return pl.pallas_call(
        keep_kernel,
        out_shape=pltpu.HBM(blocks.shape, blocks.dtype),
        grid=(blocks.shape[0],),
        in_specs=[block],
        out_specs=block,
        compiler_params=params(4),
        name="keep",
    )(in_hbm(blocks))


def mean_kernel(window, local_ref, rows_ref, kernel_ref, mass_ref, total_ref, *refs):
    *chunks, _, out_ref, part, weight, total, mass, made, sems = refs
    pair_count, _, feat = rows_ref.shape
    local = [local_ref[0, pair] & 7 for pair in range(pair_count)]

    def copy(pair):
        return pltpu.make_async_copy(made.at[pair], out_ref.at[local[pair]], sems.at[pair])

    firsts = []
    for pair in range(pair_count):
        sums = total_ref[pair] + jnp.dot(
            kernel_ref[pair], own_columns(window, chunks, pair), preferred_element_type=jnp.float32
        )
        part[pair] = sums.astype(jnp.bfloat16)
        weight[pair] = jnp.broadcast_to(
            jnp.sum(mass_ref[pair], axis=1, keepdims=True), (BR, LANES)
        )
        same = [local[other] == local[pair] for other in range(pair)]
        firsts.append(jnp.logical_not(functools.reduce(jnp.logical_or, same, jnp.bool_(False))))
    for pair in range(pair_count):

        @pl.when(firsts[pair])
        def _():
            total[...] = rows_ref[pair].astype(jnp.float32) + part[pair].astype(jnp.float32)
            mass[...] = 1.0 + weight[pair]
            for other in range(pair + 1, pair_count):

                @pl.when(local[other] == local[pair])
                def _():
                    total[...] += part[other].astype(jnp.float32)
                    mass[...] += weight[other]

            scale = 1.0 / mass[...]
            for at in range(0, feat, LANES):
                lanes = slice(at, at + LANES)
                made[pair, :, lanes] = (total[:, lanes] * scale).astype(jnp.bfloat16)
            copy(pair).start()

    for pair in range(pair_count):

        @pl.when(firsts[pair])
        def _():
            copy(pair).wait()


def means(pairs, rows, kernel, mass, total, cols, kept):
    pair_count, _, feat = rows.shape
    window = WINDOWS[1]
    own = [cols[chunk][0] for chunk, _, _ in segments(window)]
    args = [in_vmem(x) for x in (rows, kernel, mass, total, *own)]
    return pl.pallas_call(
        functools.partial(mean_kernel, window),
        out_shape=pltpu.HBM(kept.shape, jnp.bfloat16),
        in_specs=[smem()] + [vmem()] * len(args) + [anywhere()],
        out_specs=anywhere(),
        scratch_shapes=[
            pltpu.VMEM((pair_count, BR, feat), jnp.bfloat16),
            pltpu.VMEM((pair_count, BR, LANES), jnp.float32),
            pltpu.VMEM((BR, feat), jnp.float32),
            pltpu.VMEM((BR, LANES), jnp.float32),
            pltpu.VMEM((pair_count, BR, feat), jnp.bfloat16),
            pltpu.SemaphoreType.DMA((pair_count,)),
        ],
        input_output_aliases={1 + len(args): 0},
        compiler_params=params(16),
        cost_estimate=estimate(pair_count, 128),
        name="means",
    )(pairs, *args, in_hbm(kept))


def weight_kernel(*refs):
    out_ref = refs[-1]
    mass = refs[0][...]
    for ref in refs[1:-1]:
        mass = mass + ref[...]
    weight = 1.0 / (1.0 + mass / BR)
    parts = BR // LANES
    for block in range(BLK_DEV):
        for part in range(parts):
            lanes = slice(part * LANES, (part + 1) * LANES)
            out_ref[block * parts + part : block * parts + part + 1] = weight[block : block + 1, lanes]


def block_weights(sums):
    out = pl.pallas_call(
        weight_kernel,
        out_shape=jax.ShapeDtypeStruct((BLK_DEV * BR // LANES, LANES), jnp.float32),
        in_specs=[vmem()] * len(sums),
        out_specs=vmem(),
        compiler_params=params(4),
        name="weights",
    )(*[in_vmem(x) for x in sums])
    return out.reshape(BLK_DEV * BR)


def hop(parts, step):
    count = lax.axis_size("narrow")
    return [lax.ppermute(part, "narrow", [(i, i ^ step) for i in range(count)]) for part in parts]


def first_hops(part):
    parts = [part]
    step = lax.axis_size("narrow") // 2
    while step > 1:
        parts = parts + hop(parts, step)
        step //= 2
    return parts


def to_wide(pieces):
    count = lax.axis_size("wide")
    return [
        lax.ppermute(piece, "wide", [(i, (i + shift) % count) for i in range(count)])
        for shift, piece in enumerate(pieces, 1)
    ]


def on_device(embeddings, pair_list):
    wide_count = lax.axis_size("wide")
    me = lax.axis_index("wide").astype(jnp.int32).reshape(1)
    pairs = pair_list.T
    pair_count = pairs.shape[1]
    capacity = max(2, 2 * pair_count // wide_count)
    feat = embeddings.shape[1]
    blocks = embeddings.reshape(BLK_DEV, BR, feat)
    lists = to_wide([pairs] * (wide_count - 1))
    fixed = lax.optimization_barrier
    lists, (row_slices, own) = fixed((lists, take(pairs, blocks)))
    outgoing = pack(me, lists, blocks, capacity)

    def pick(received, chunk):
        return select(me, pairs, own, received, *CHUNKS[chunk])

    rows = jnp.stack(first_hops(row_slices))
    rows, received, kept = fixed((rows, to_wide(outgoing[0]), keep(blocks)))
    cols_a = first_hops(pick(received, 0))
    rows = [rows, *hop([rows], 1)]
    cols_a, rows, received = fixed((cols_a, rows, to_wide(outgoing[1])))
    cols_b = first_hops(pick(received, 1))
    last_b = hop(cols_b[:1], 1)
    cols_a = cols_a + hop(cols_a, 1)
    carry = first_window(rows, [cols_a])
    cols_b, last_b, carry = fixed((cols_b, last_b, carry))
    cols_b = cols_b + last_b + hop(cols_b[1:], 1)
    square, mass, total, sums = carry
    kernel, mass, row_sums, shares = last_window(
        me, pairs, rows, [cols_a, cols_b], square, mass, sums, wide_count
    )
    came = to_wide(shares[1:])
    mean = means(pairs, row_slices, kernel, mass, total, [cols_a, cols_b], kept)
    weights = block_weights([row_sums, shares[0], *came])
    return weights, mean.reshape(BLK_DEV * BR, feat)


def solution(mesh):
    in_specs = (P(("groups", "wide"), "narrow"), P(("groups", "wide"), None))
    out_specs = (P(("groups", "wide")), P(("groups", "wide"), "narrow"))
    return jax.shard_map(
        on_device, mesh=mesh, in_specs=in_specs, out_specs=out_specs, check_vma=False
    )
```

```python
import functools

import jax
import jax.numpy as jnp
from jax import lax
from jax.experimental import pallas as pl
from jax.experimental.pallas import tpu as pltpu
from jax.sharding import PartitionSpec as P

F = 1024
BR = 512
BLK_DEV = 8
LANES = 128
CHUNKS = ((0, 336), (336, 176))
PIECES = (2, 1)
WINDOWS = ((0, 256), (256, 512))


def smem():
    return pl.BlockSpec(memory_space=pltpu.SMEM)


def vmem():
    return pl.BlockSpec(memory_space=pltpu.VMEM)


def anywhere():
    return pl.BlockSpec(memory_space=pl.ANY)


def in_vmem(x):
    return pltpu.with_memory_space_constraint(x, pltpu.VMEM)


def in_hbm(x):
    return pltpu.with_memory_space_constraint(x, pltpu.HBM)


def params(mebibytes):
    return pltpu.CompilerParams(vmem_limit_bytes=mebibytes * 1024 * 1024)


def pack_kernel(wide_count, pair_count, capacity, me_ref, *refs):
    lists, blocks_ref = refs[: wide_count - 1], refs[wide_count - 1]
    outs, sems = refs[wide_count:-1], refs[-1]
    me = me_ref[0]
    copies = []

    def send(source, target):
        copies.append(pltpu.make_async_copy(source, target, sems.at[len(copies)]))
        copies[-1].start()

    for chunk, (start, size) in enumerate(CHUNKS):
        for shift in range(1, wide_count):
            asked = lists[wide_count - shift - 1]
            picks = [jnp.int32(0)] * capacity
            count = jnp.int32(0)
            for pair in range(pair_count):
                col = asked[1, pair]
                mine = (col >> 3) == me
                for slot in range(capacity):
                    picks[slot] = jnp.where(mine & (count == slot), col & 7, picks[slot])
                count = count + mine.astype(jnp.int32)
            out = outs[chunk * (wide_count - 1) + shift - 1]
            for slot in range(capacity):
                send(blocks_ref.at[picks[slot], pl.ds(start, size)], out.at[slot])
    for copy in copies:
        copy.wait()


def pack(me, lists, blocks, capacity):
    wide_count, pair_count = len(lists) + 1, lists[0].shape[1]
    feat = blocks.shape[-1]
    shapes = [
        pltpu.VMEM((capacity, size, feat), blocks.dtype)
        for _, size in CHUNKS
        for _ in range(1, wide_count)
    ]
    outs = pl.pallas_call(
        functools.partial(pack_kernel, wide_count, pair_count, capacity),
        out_shape=shapes,
        in_specs=[smem()] * wide_count + [anywhere()],
        out_specs=[anywhere()] * len(shapes),
        scratch_shapes=[pltpu.SemaphoreType.DMA((len(shapes) * capacity,))],
        compiler_params=params(4),
        name="pack",
    )(me, *lists, in_hbm(blocks))
    each = wide_count - 1
    return [outs[c * each : (c + 1) * each] for c in range(len(CHUNKS))]


def take_kernel(pairs_ref, blocks_ref, rows_ref, cols_ref, sems):
    copies = []
    for pair in range(rows_ref.shape[0]):
        for side, out in enumerate((rows_ref, cols_ref)):
            source = blocks_ref.at[pairs_ref[side, pair] & 7]
            copies.append(pltpu.make_async_copy(source, out.at[pair], sems.at[len(copies)]))
            copies[-1].start()
    for copy in copies:
        copy.wait()


def take(pairs, blocks):
    pair_count = pairs.shape[1]
    taken = pltpu.VMEM((pair_count, *blocks.shape[1:]), blocks.dtype)
    return pl.pallas_call(
        take_kernel,
        out_shape=[taken, taken],
        in_specs=[smem(), anywhere()],
        out_specs=[anywhere(), anywhere()],
        scratch_shapes=[pltpu.SemaphoreType.DMA((2 * pair_count,))],
        compiler_params=params(4),
        name="take",
    )(pairs, in_hbm(blocks))


def select_kernel(wide_count, start, me_ref, pairs_ref, own_ref, *refs):
    pair_count = own_ref.shape[0]
    outs = refs[wide_count - 1 :]
    received = refs[: wide_count - 1]
    each, size, _ = outs[0].shape
    owners = [pairs_ref[1, pair] >> 3 for pair in range(pair_count)]
    for pair in range(pair_count):
        shift = me_ref[0] - owners[pair]
        shift = jnp.where(shift < 0, shift + wide_count, shift)
        rank = jnp.int32(0)
        for before in range(pair):
            rank = rank + (owners[before] == owners[pair]).astype(jnp.int32)

        out = outs[pair // each].at[pair % each]

        @pl.when(shift == 0)
        def _():
            out[...] = own_ref[pair, start : start + size]

        for other in range(1, wide_count):

            @pl.when(shift == other)
            def _():
                out[...] = received[other - 1][rank]


def select(me, pairs, own, received, start, size, pieces):
    pair_count, _, feat = own.shape
    return pl.pallas_call(
        functools.partial(select_kernel, len(received) + 1, start),
        out_shape=[pltpu.VMEM((pair_count // pieces, size, feat), own.dtype)] * pieces,
        in_specs=[smem(), smem()] + [vmem()] * (1 + len(received)),
        out_specs=[vmem()] * pieces,
        compiler_params=params(4),
        name="select",
    )(me, pairs, *[in_vmem(x) for x in (own, *received)])


def tree(parts):
    while len(parts) > 1:
        half = len(parts) // 2
        parts = [parts[i] + parts[i + half] for i in range(half)]
    return parts[0]


def across(left, right):
    return lax.dot_general(
        left, right, (((1,), (1,)), ((), ())), preferred_element_type=jnp.float32
    )


def lane_sum(block):
    square = jnp.square(block.astype(jnp.float32))
    return sum(square[:, at : at + LANES] for at in range(0, square.shape[1], LANES))


def segments(window):
    low, high = window
    held = []
    for chunk, (start, size) in enumerate(CHUNKS):
        first, end = max(low, start), min(high, start + size)
        if first < end:
            held.append((chunk, first - start, end - first))
    return held


def scores(rows, cols, square):
    gram = tree([across(row, col) for row, col in zip(rows, cols)])
    other = jnp.sum(tree([lane_sum(col) for col in cols]).T, axis=0, keepdims=True)
    pieces, mass = [], None
    for at in range(0, gram.shape[1], LANES):
        here = slice(at, at + LANES)
        piece = jnp.exp((square + other[:, here] - 2.0 * gram[:, here]) * (-1.0 / F))
        mass = piece if mass is None else mass + piece
        pieces.append(piece)
    kernel = jnp.concatenate(pieces, axis=1) if len(pieces) > 1 else pieces[0]
    return kernel.astype(jnp.bfloat16), jnp.sum(kernel, axis=0, keepdims=True), mass


def take_parts(refs, narrow_count, pieces):
    parts = [refs[i * pieces : (i + 1) * pieces] for i in range(narrow_count)]
    return parts, refs[narrow_count * pieces :]


def of_pair(part, pair):
    each = part[0].shape[0]
    return part[pair // each].at[pair % each]


def window_parts(window, narrow_count, refs):
    rows, refs = take_parts(refs, narrow_count, 1)
    chunks = []
    for chunk, _, _ in segments(window):
        cols, refs = take_parts(refs, narrow_count, PIECES[chunk])
        chunks.append(cols)
    return rows, chunks


def own_columns(window, chunks, pair):
    held = segments(window)
    pieces = [of_pair(part, pair)[at : at + size] for part, (_, at, size) in zip(chunks, held)]
    return jnp.concatenate(pieces, axis=0) if len(pieces) > 1 else pieces[0]


def pair_parts(window, rows, chunks, pair):
    cols = [own_columns(window, [c[i] for c in chunks], pair) for i in range(len(rows))]
    return [of_pair(part, pair)[...] for part in rows], cols


def first_kernel(window, narrow_count, *refs):
    square_ref, mass_ref, total_ref, sums_ref = refs[-4:]
    all_rows, chunks = window_parts(window, narrow_count, refs)
    for pair in range(square_ref.shape[0]):
        rows, cols = pair_parts(window, all_rows, chunks, pair)
        square = jnp.sum(tree([lane_sum(row) for row in rows]), axis=1, keepdims=True)
        square = jnp.broadcast_to(square, (BR, LANES))
        kernel, sums, mass = scores(rows, cols, square)
        square_ref[pair] = square
        mass_ref[pair] = mass
        sums_ref[pair : pair + 1] = sums
        total_ref[pair] = jnp.dot(kernel, cols[0], preferred_element_type=jnp.float32)


def last_kernel(window, narrow_count, wide_count, me_ref, pairs_ref, *refs):
    square_in, mass_in, sums_in = refs[-6 - wide_count : -3 - wide_count]
    kernel_ref, mass_ref, row_ref = refs[-3 - wide_count : -wide_count]
    shares = refs[-wide_count:]
    for ref in (row_ref, *shares):
        ref[...] = jnp.zeros_like(ref)
    all_rows, chunks = window_parts(window, narrow_count, refs)
    for pair in range(square_in.shape[0]):
        rows, cols = pair_parts(window, all_rows, chunks, pair)
        kernel, sums, mass = scores(rows, cols, square_in[pair])
        kernel_ref[pair] = kernel
        sums = jnp.concatenate([sums_in[pair : pair + 1], sums], axis=1)
        mass = mass_in[pair] + mass
        mass_ref[pair] = mass
        row_ref[pl.ds(pairs_ref[0, pair] & 7, 1)] += jnp.sum(mass.T, axis=0, keepdims=True)
        col = pairs_ref[1, pair]
        shift = (col >> 3) - me_ref[0]
        shift = jnp.where(shift < 0, shift + wide_count, shift)
        for other, ref in enumerate(shares):
            ref[pl.ds(col & 7, 1)] += jnp.where(shift == other, sums, 0.0)


def estimate(pair_count, size):
    return pl.CostEstimate(
        flops=2 * pair_count * BR * size * F,
        transcendentals=pair_count * BR * size,
        bytes_accessed=8 * 1024 * 1024,
    )


def operands(parts):
    return [piece for part in parts for piece in part]


def first_window(rows, cols):
    pair_count, _, feat = rows[0][0].shape
    window = WINDOWS[0]
    lanes = pltpu.VMEM((pair_count, BR, LANES), jnp.float32)
    total = pltpu.VMEM((pair_count, BR, feat), jnp.float32)
    args = operands(rows)
    for chunk, _, _ in segments(window):
        args += operands(cols[chunk])
    return pl.pallas_call(
        functools.partial(first_kernel, window, len(rows)),
        out_shape=[lanes, lanes, total, pltpu.VMEM((pair_count, window[1]), jnp.float32)],
        in_specs=[vmem()] * len(args),
        out_specs=[vmem()] * 4,
        compiler_params=params(16),
        cost_estimate=pl.CostEstimate(flops=0, transcendentals=0, bytes_accessed=0),
        name="first_window",
    )(*[in_vmem(x) for x in args])


def last_window(me, pairs, rows, cols, square, mass, sums, wide_count):
    pair_count = rows[0][0].shape[0]
    window = WINDOWS[1]
    size = window[1] - window[0]
    by_block = pltpu.VMEM((BLK_DEV, BR), jnp.float32)
    shapes = [
        pltpu.VMEM((pair_count, BR, size), jnp.bfloat16),
        pltpu.VMEM((pair_count, BR, LANES), jnp.float32),
    ] + [by_block] * (1 + wide_count)
    args = operands(rows)
    for chunk, _, _ in segments(window):
        args += operands(cols[chunk])
    args += [square, mass, sums]
    kernel, mass, row_sums, *shares = pl.pallas_call(
        functools.partial(last_kernel, window, len(rows), wide_count),
        out_shape=shapes,
        in_specs=[smem(), smem()] + [vmem()] * len(args),
        out_specs=[vmem()] * len(shapes),
        compiler_params=params(16),
        cost_estimate=estimate(pair_count, size),
        name="last_window",
    )(me, pairs, *[in_vmem(x) for x in args])
    return kernel, mass, row_sums, shares


def keep_kernel(block_ref, out_ref):
    out_ref[...] = block_ref[...]


def keep(blocks):
    block = pl.BlockSpec((1, *blocks.shape[1:]), lambda k: (k, 0, 0))
    return pl.pallas_call(
        keep_kernel,
        out_shape=pltpu.HBM(blocks.shape, blocks.dtype),
        grid=(blocks.shape[0],),
        in_specs=[block],
        out_specs=block,
        compiler_params=params(4),
        name="keep",
    )(in_hbm(blocks))


def mean_kernel(window, local_ref, rows_ref, kernel_ref, mass_ref, total_ref, *refs):
    *refs, _, out_ref, part, weight, total, mass, made, sems = refs
    chunks = []
    for chunk, _, _ in segments(window):
        (own,), refs = take_parts(refs, 1, PIECES[chunk])
        chunks.append(own)
    pair_count, _, feat = rows_ref.shape
    local = [local_ref[0, pair] & 7 for pair in range(pair_count)]

    def copy(pair):
        return pltpu.make_async_copy(made.at[pair], out_ref.at[local[pair]], sems.at[pair])

    firsts = []
    for pair in range(pair_count):
        sums = total_ref[pair] + jnp.dot(
            kernel_ref[pair], own_columns(window, chunks, pair), preferred_element_type=jnp.float32
        )
        part[pair] = sums.astype(jnp.bfloat16)
        weight[pair] = jnp.broadcast_to(
            jnp.sum(mass_ref[pair], axis=1, keepdims=True), (BR, LANES)
        )
        same = [local[other] == local[pair] for other in range(pair)]
        firsts.append(jnp.logical_not(functools.reduce(jnp.logical_or, same, jnp.bool_(False))))
    for pair in range(pair_count):

        @pl.when(firsts[pair])
        def _():
            total[...] = rows_ref[pair].astype(jnp.float32) + part[pair].astype(jnp.float32)
            mass[...] = 1.0 + weight[pair]
            for other in range(pair + 1, pair_count):

                @pl.when(local[other] == local[pair])
                def _():
                    total[...] += part[other].astype(jnp.float32)
                    mass[...] += weight[other]

            scale = 1.0 / mass[...]
            for at in range(0, feat, LANES):
                lanes = slice(at, at + LANES)
                made[pair, :, lanes] = (total[:, lanes] * scale).astype(jnp.bfloat16)
            copy(pair).start()

    for pair in range(pair_count):

        @pl.when(firsts[pair])
        def _():
            copy(pair).wait()


def means(pairs, rows, kernel, mass, total, cols, kept):
    pair_count, _, feat = rows.shape
    window = WINDOWS[1]
    own = operands(cols[chunk][0] for chunk, _, _ in segments(window))
    args = [in_vmem(x) for x in (rows, kernel, mass, total, *own)]
    return pl.pallas_call(
        functools.partial(mean_kernel, window),
        out_shape=pltpu.HBM(kept.shape, jnp.bfloat16),
        in_specs=[smem()] + [vmem()] * len(args) + [anywhere()],
        out_specs=anywhere(),
        scratch_shapes=[
            pltpu.VMEM((pair_count, BR, feat), jnp.bfloat16),
            pltpu.VMEM((pair_count, BR, LANES), jnp.float32),
            pltpu.VMEM((BR, feat), jnp.float32),
            pltpu.VMEM((BR, LANES), jnp.float32),
            pltpu.VMEM((pair_count, BR, feat), jnp.bfloat16),
            pltpu.SemaphoreType.DMA((pair_count,)),
        ],
        input_output_aliases={1 + len(args): 0},
        compiler_params=params(16),
        cost_estimate=estimate(pair_count, 128),
        name="means",
    )(pairs, *args, in_hbm(kept))


def weight_kernel(*refs):
    out_ref = refs[-1]
    mass = refs[0][...]
    for ref in refs[1:-1]:
        mass = mass + ref[...]
    weight = 1.0 / (1.0 + mass / BR)
    parts = BR // LANES
    for block in range(BLK_DEV):
        for part in range(parts):
            lanes = slice(part * LANES, (part + 1) * LANES)
            out_ref[block * parts + part : block * parts + part + 1] = weight[block : block + 1, lanes]


def block_weights(sums):
    out = pl.pallas_call(
        weight_kernel,
        out_shape=jax.ShapeDtypeStruct((BLK_DEV * BR // LANES, LANES), jnp.float32),
        in_specs=[vmem()] * len(sums),
        out_specs=vmem(),
        compiler_params=params(4),
        name="weights",
    )(*[in_vmem(x) for x in sums])
    return out.reshape(BLK_DEV * BR)


def hop(parts, step):
    count = lax.axis_size("narrow")
    perm = [(i, i ^ step) for i in range(count)]
    return [[lax.ppermute(piece, "narrow", perm) for piece in part] for part in parts]


def first_hops(part):
    parts = [part]
    step = lax.axis_size("narrow") // 2
    while step > 1:
        parts = parts + hop(parts, step)
        step //= 2
    return parts


def to_wide(pieces):
    count = lax.axis_size("wide")
    return [
        lax.ppermute(piece, "wide", [(i, (i + shift) % count) for i in range(count)])
        for shift, piece in enumerate(pieces, 1)
    ]


def on_device(embeddings, pair_list):
    wide_count = lax.axis_size("wide")
    me = lax.axis_index("wide").astype(jnp.int32).reshape(1)
    pairs = pair_list.T
    pair_count = pairs.shape[1]
    capacity = max(2, 2 * pair_count // wide_count)
    feat = embeddings.shape[1]
    blocks = embeddings.reshape(BLK_DEV, BR, feat)
    lists = to_wide([pairs] * (wide_count - 1))
    fixed = lax.optimization_barrier
    lists, (row_slices, own) = fixed((lists, take(pairs, blocks)))
    outgoing = pack(me, lists, blocks, capacity)

    def pick(received, chunk):
        return select(me, pairs, own, received, *CHUNKS[chunk], PIECES[chunk])

    rows = first_hops([row_slices])
    rows_last = hop(rows[:1], 1)
    rows, rows_last, received, kept = fixed((rows, rows_last, to_wide(outgoing[0]), keep(blocks)))
    cols_a = first_hops(pick(received, 0))
    rows = rows + rows_last + hop(rows[1:], 1)
    cols_a, rows, received = fixed((cols_a, rows, to_wide(outgoing[1])))
    cols_b = first_hops(pick(received, 1))
    last_b = hop(cols_b[:1], 1)
    cols_a = cols_a + hop(cols_a, 1)
    carry = first_window(rows, [cols_a])
    cols_b, carry = fixed((cols_b, carry))
    cols_b = cols_b + last_b + hop(cols_b[1:], 1)
    square, mass, total, sums = carry
    kernel, mass, row_sums, shares = last_window(
        me, pairs, rows, [cols_a, cols_b], square, mass, sums, wide_count
    )
    came = to_wide(shares[1:])
    mean = means(pairs, row_slices, kernel, mass, total, [cols_a, cols_b], kept)
    weights = block_weights([row_sums, shares[0], *came])
    return weights, mean.reshape(BLK_DEV * BR, feat)


def solution(mesh):
    in_specs = (P(("groups", "wide"), "narrow"), P(("groups", "wide"), None))
    out_specs = (P(("groups", "wide")), P(("groups", "wide"), "narrow"))
    return jax.shard_map(
        on_device, mesh=mesh, in_specs=in_specs, out_specs=out_specs, check_vma=False
    )
```

```python
import functools

import jax
import jax.numpy as jnp
from jax import lax
from jax.experimental import pallas as pl
from jax.experimental.pallas import tpu as pltpu
from jax.sharding import PartitionSpec as P

F = 1024
BR = 512
BLK_DEV = 8
LANES = 128
CHUNKS = ((0, 320), (320, 192))
PIECES = (2, 1)
WINDOWS = ((0, 256), (256, 512))


def smem():
    return pl.BlockSpec(memory_space=pltpu.SMEM)


def vmem():
    return pl.BlockSpec(memory_space=pltpu.VMEM)


def anywhere():
    return pl.BlockSpec(memory_space=pl.ANY)


def in_vmem(x):
    return pltpu.with_memory_space_constraint(x, pltpu.VMEM)


def in_hbm(x):
    return pltpu.with_memory_space_constraint(x, pltpu.HBM)


def params(mebibytes):
    return pltpu.CompilerParams(vmem_limit_bytes=mebibytes * 1024 * 1024)


def pack_kernel(wide_count, pair_count, capacity, me_ref, pairs_ref, *refs):
    lists, blocks_ref = refs[: wide_count - 1], refs[wide_count - 1]
    *outs, rows_ref, sems = refs[wide_count:]
    me = me_ref[0]
    copies = []

    def send(source, target):
        copies.append(pltpu.make_async_copy(source, target, sems.at[len(copies)]))
        copies[-1].start()

    for chunk, (start, size) in enumerate(CHUNKS):
        for shift in range(1, wide_count):
            asked = lists[wide_count - shift - 1]
            picks = [jnp.int32(0)] * capacity
            count = jnp.int32(0)
            for pair in range(pair_count):
                col = asked[1, pair]
                mine = (col >> 3) == me
                for slot in range(capacity):
                    picks[slot] = jnp.where(mine & (count == slot), col & 7, picks[slot])
                count = count + mine.astype(jnp.int32)
            out = outs[chunk * (wide_count - 1) + shift - 1]
            for slot in range(capacity):
                send(blocks_ref.at[picks[slot], pl.ds(start, size)], out.at[slot])
    for pair in range(pair_count):
        send(blocks_ref.at[pairs_ref[0, pair] & 7], rows_ref.at[pair])
    for copy in copies:
        copy.wait()


def pack(me, pairs, lists, blocks, capacity):
    wide_count, pair_count = len(lists) + 1, pairs.shape[1]
    feat = blocks.shape[-1]
    shapes = [
        pltpu.VMEM((capacity, size, feat), blocks.dtype)
        for _, size in CHUNKS
        for _ in range(1, wide_count)
    ] + [pltpu.VMEM((pair_count, BR, feat), blocks.dtype)]
    copies = (len(shapes) - 1) * capacity + pair_count
    outs = pl.pallas_call(
        functools.partial(pack_kernel, wide_count, pair_count, capacity),
        out_shape=shapes,
        in_specs=[smem()] * (1 + wide_count) + [anywhere()],
        out_specs=[anywhere()] * len(shapes),
        scratch_shapes=[pltpu.SemaphoreType.DMA((copies,))],
        compiler_params=params(4),
        name="pack",
    )(me, in_hbm(pairs), *lists, in_hbm(blocks))
    each = wide_count - 1
    return [outs[c * each : (c + 1) * each] for c in range(len(CHUNKS))], outs[-1]


def select_kernel(wide_count, start, me_ref, pairs_ref, own_ref, *refs):
    pair_count = own_ref.shape[0]
    outs = refs[wide_count - 1 :]
    received = refs[: wide_count - 1]
    each, size, _ = outs[0].shape
    owners = [pairs_ref[1, pair] >> 3 for pair in range(pair_count)]
    for pair in range(pair_count):
        shift = me_ref[0] - owners[pair]
        shift = jnp.where(shift < 0, shift + wide_count, shift)
        rank = jnp.int32(0)
        for before in range(pair):
            rank = rank + (owners[before] == owners[pair]).astype(jnp.int32)

        out = outs[pair // each].at[pair % each]

        @pl.when(shift == 0)
        def _():
            out[...] = own_ref[pair, start : start + size]

        for other in range(1, wide_count):

            @pl.when(shift == other)
            def _():
                out[...] = received[other - 1][rank]


def select(me, pairs, own, received, start, size, pieces):
    pair_count, _, feat = own.shape
    return pl.pallas_call(
        functools.partial(select_kernel, len(received) + 1, start),
        out_shape=[pltpu.VMEM((pair_count // pieces, size, feat), own.dtype)] * pieces,
        in_specs=[smem(), smem()] + [vmem()] * (1 + len(received)),
        out_specs=[vmem()] * pieces,
        compiler_params=params(4),
        name="select",
    )(me, in_hbm(pairs), *[in_vmem(x) for x in (own, *received)])


def tree(parts):
    while len(parts) > 1:
        half = len(parts) // 2
        parts = [parts[i] + parts[i + half] for i in range(half)]
    return parts[0]


def across(left, right):
    return lax.dot_general(
        left, right, (((1,), (1,)), ((), ())), preferred_element_type=jnp.float32
    )


def lane_sum(block):
    square = jnp.square(block.astype(jnp.float32))
    return sum(square[:, at : at + LANES] for at in range(0, square.shape[1], LANES))


def segments(window):
    low, high = window
    held = []
    for chunk, (start, size) in enumerate(CHUNKS):
        first, end = max(low, start), min(high, start + size)
        if first < end:
            held.append((chunk, first - start, end - first))
    return held


def scores(rows, cols, square):
    gram = tree([across(row, col) for row, col in zip(rows, cols)])
    other = jnp.sum(tree([lane_sum(col) for col in cols]).T, axis=0, keepdims=True)
    pieces, mass = [], None
    for at in range(0, gram.shape[1], LANES):
        here = slice(at, at + LANES)
        piece = jnp.exp((square + other[:, here] - 2.0 * gram[:, here]) * (-1.0 / F))
        mass = piece if mass is None else mass + piece
        pieces.append(piece)
    kernel = jnp.concatenate(pieces, axis=1) if len(pieces) > 1 else pieces[0]
    return kernel.astype(jnp.bfloat16), jnp.sum(kernel, axis=0, keepdims=True), mass


def take_parts(refs, narrow_count, pieces):
    parts = [refs[i * pieces : (i + 1) * pieces] for i in range(narrow_count)]
    return parts, refs[narrow_count * pieces :]


def of_pair(part, pair):
    each = part[0].shape[0]
    return part[pair // each].at[pair % each]


def window_parts(window, narrow_count, refs):
    rows, refs = [ref.at[i] for ref in refs[:2] for i in range(narrow_count // 2)], refs[2:]
    chunks = []
    for chunk, _, _ in segments(window):
        cols, refs = take_parts(refs, narrow_count, PIECES[chunk])
        chunks.append(cols)
    return rows, chunks


def own_columns(window, chunks, pair):
    held = segments(window)
    pieces = [of_pair(part, pair)[at : at + size] for part, (_, at, size) in zip(chunks, held)]
    return jnp.concatenate(pieces, axis=0) if len(pieces) > 1 else pieces[0]


def pair_parts(window, rows, chunks, pair):
    cols = [own_columns(window, [c[i] for c in chunks], pair) for i in range(len(rows))]
    return [part[pair] for part in rows], cols


def first_kernel(window, narrow_count, *refs):
    square_ref, mass_ref, total_ref, sums_ref = refs[-4:]
    all_rows, chunks = window_parts(window, narrow_count, refs)
    for pair in range(square_ref.shape[0]):
        rows, cols = pair_parts(window, all_rows, chunks, pair)
        square = jnp.sum(tree([lane_sum(row) for row in rows]), axis=1, keepdims=True)
        square = jnp.broadcast_to(square, (BR, LANES))
        kernel, sums, mass = scores(rows, cols, square)
        square_ref[pair] = square
        mass_ref[pair] = mass
        sums_ref[pair : pair + 1] = sums
        total_ref[pair] = jnp.dot(kernel, cols[0], preferred_element_type=jnp.float32)


def last_kernel(window, narrow_count, wide_count, me_ref, pairs_ref, *refs):
    square_in, mass_in, sums_in = refs[-6 - wide_count : -3 - wide_count]
    kernel_ref, mass_ref, row_ref = refs[-3 - wide_count : -wide_count]
    shares = refs[-wide_count:]
    for ref in (row_ref, *shares):
        ref[...] = jnp.zeros_like(ref)
    all_rows, chunks = window_parts(window, narrow_count, refs)
    for pair in range(square_in.shape[0]):
        rows, cols = pair_parts(window, all_rows, chunks, pair)
        kernel, sums, mass = scores(rows, cols, square_in[pair])
        kernel_ref[pair] = kernel
        sums = jnp.concatenate([sums_in[pair : pair + 1], sums], axis=1)
        mass = mass_in[pair] + mass
        mass_ref[pair] = mass
        row_ref[pl.ds(pairs_ref[0, pair] & 7, 1)] += jnp.sum(mass.T, axis=0, keepdims=True)
        col = pairs_ref[1, pair]
        shift = (col >> 3) - me_ref[0]
        shift = jnp.where(shift < 0, shift + wide_count, shift)
        for other, ref in enumerate(shares):
            ref[pl.ds(col & 7, 1)] += jnp.where(shift == other, sums, 0.0)


def estimate(pair_count, size):
    return pl.CostEstimate(
        flops=2 * pair_count * BR * size * F,
        transcendentals=pair_count * BR * size,
        bytes_accessed=8 * 1024 * 1024,
    )


def operands(parts):
    return [piece for part in parts for piece in part]


def first_window(rows, cols):
    _, pair_count, _, feat = rows[0][0].shape
    window = WINDOWS[0]
    lanes = pltpu.VMEM((pair_count, BR, LANES), jnp.float32)
    total = pltpu.VMEM((pair_count, BR, feat), jnp.float32)
    args = operands(rows)
    for chunk, _, _ in segments(window):
        args += operands(cols[chunk])
    return pl.pallas_call(
        functools.partial(first_kernel, window, len(cols[0])),
        out_shape=[lanes, lanes, total, pltpu.VMEM((pair_count, window[1]), jnp.float32)],
        in_specs=[vmem()] * len(args),
        out_specs=[vmem()] * 4,
        compiler_params=params(16),
        cost_estimate=pl.CostEstimate(flops=0, transcendentals=0, bytes_accessed=0),
        name="first_window",
    )(*[in_vmem(x) for x in args])


def last_window(me, pairs, rows, cols, square, mass, sums, wide_count):
    pair_count = rows[0][0].shape[1]
    window = WINDOWS[1]
    size = window[1] - window[0]
    by_block = pltpu.VMEM((BLK_DEV, BR), jnp.float32)
    shapes = [
        pltpu.VMEM((pair_count, BR, size), jnp.bfloat16),
        pltpu.VMEM((pair_count, BR, LANES), jnp.float32),
    ] + [by_block] * (1 + wide_count)
    args = operands(rows)
    for chunk, _, _ in segments(window):
        args += operands(cols[chunk])
    args += [square, mass, sums]
    kernel, mass, row_sums, *shares = pl.pallas_call(
        functools.partial(last_kernel, window, len(cols[0]), wide_count),
        out_shape=shapes,
        in_specs=[smem(), smem()] + [vmem()] * len(args),
        out_specs=[vmem()] * len(shapes),
        compiler_params=params(16),
        cost_estimate=estimate(pair_count, size),
        name="last_window",
    )(me, in_hbm(pairs), *[in_vmem(x) for x in args])
    return kernel, mass, row_sums, shares


def keep_kernel(pairs_ref, block_ref, blocks_ref, out_ref, own_ref, sems):
    here = pl.program_id(0)

    def copies():
        for pair in range(own_ref.shape[0]):
            source = blocks_ref.at[pairs_ref[1, pair] & 7]
            yield pltpu.make_async_copy(source, own_ref.at[pair], sems.at[pair])

    @pl.when(here == 0)
    def _():
        for copy in copies():
            copy.start()

    out_ref[...] = block_ref[...]

    @pl.when(here == pl.num_programs(0) - 1)
    def _():
        for copy in copies():
            copy.wait()


def keep(pairs, blocks):
    pair_count = pairs.shape[1]
    block = pl.BlockSpec((1, *blocks.shape[1:]), lambda k: (k, 0, 0))
    return pl.pallas_call(
        keep_kernel,
        out_shape=[
            pltpu.HBM(blocks.shape, blocks.dtype),
            pltpu.VMEM((pair_count, *blocks.shape[1:]), blocks.dtype),
        ],
        grid=(blocks.shape[0],),
        in_specs=[smem(), block, anywhere()],
        out_specs=[block, anywhere()],
        scratch_shapes=[pltpu.SemaphoreType.DMA((pair_count,))],
        compiler_params=params(4),
        name="keep",
    )(in_hbm(pairs), in_hbm(blocks), in_hbm(blocks))


def mean_kernel(window, local_ref, rows_ref, kernel_ref, mass_ref, total_ref, *refs):
    *refs, _, out_ref, part, weight, total, mass, made, sems = refs
    chunks = []
    for chunk, _, _ in segments(window):
        (own,), refs = take_parts(refs, 1, PIECES[chunk])
        chunks.append(own)
    pair_count, _, feat = rows_ref.shape
    local = [local_ref[0, pair] & 7 for pair in range(pair_count)]

    def copy(pair):
        return pltpu.make_async_copy(made.at[pair], out_ref.at[local[pair]], sems.at[pair])

    firsts = []
    for pair in range(pair_count):
        sums = total_ref[pair] + jnp.dot(
            kernel_ref[pair], own_columns(window, chunks, pair), preferred_element_type=jnp.float32
        )
        part[pair] = sums.astype(jnp.bfloat16)
        weight[pair] = jnp.broadcast_to(
            jnp.sum(mass_ref[pair], axis=1, keepdims=True), (BR, LANES)
        )
        same = [local[other] == local[pair] for other in range(pair)]
        firsts.append(jnp.logical_not(functools.reduce(jnp.logical_or, same, jnp.bool_(False))))
    for pair in range(pair_count):

        @pl.when(firsts[pair])
        def _():
            total[...] = rows_ref[pair].astype(jnp.float32) + part[pair].astype(jnp.float32)
            mass[...] = 1.0 + weight[pair]
            for other in range(pair + 1, pair_count):

                @pl.when(local[other] == local[pair])
                def _():
                    total[...] += part[other].astype(jnp.float32)
                    mass[...] += weight[other]

            scale = 1.0 / mass[...]
            for at in range(0, feat, LANES):
                lanes = slice(at, at + LANES)
                made[pair, :, lanes] = (total[:, lanes] * scale).astype(jnp.bfloat16)
            copy(pair).start()

    for pair in range(pair_count):

        @pl.when(firsts[pair])
        def _():
            copy(pair).wait()


def means(pairs, rows, kernel, mass, total, cols, kept):
    pair_count, _, feat = rows.shape
    window = WINDOWS[1]
    own = operands(cols[chunk][0] for chunk, _, _ in segments(window))
    args = [in_vmem(x) for x in (rows, kernel, mass, total, *own)]
    return pl.pallas_call(
        functools.partial(mean_kernel, window),
        out_shape=pltpu.HBM(kept.shape, jnp.bfloat16),
        in_specs=[smem()] + [vmem()] * len(args) + [anywhere()],
        out_specs=anywhere(),
        scratch_shapes=[
            pltpu.VMEM((pair_count, BR, feat), jnp.bfloat16),
            pltpu.VMEM((pair_count, BR, LANES), jnp.float32),
            pltpu.VMEM((BR, feat), jnp.float32),
            pltpu.VMEM((BR, LANES), jnp.float32),
            pltpu.VMEM((pair_count, BR, feat), jnp.bfloat16),
            pltpu.SemaphoreType.DMA((pair_count,)),
        ],
        input_output_aliases={1 + len(args): 0},
        compiler_params=params(16),
        cost_estimate=estimate(pair_count, 128),
        name="means",
    )(in_hbm(pairs), *args, in_hbm(kept))


def weight_kernel(*refs):
    out_ref = refs[-1]
    mass = refs[0][...]
    for ref in refs[1:-1]:
        mass = mass + ref[...]
    weight = 1.0 / (1.0 + mass / BR)
    parts = BR // LANES
    for block in range(BLK_DEV):
        for part in range(parts):
            lanes = slice(part * LANES, (part + 1) * LANES)
            out_ref[block * parts + part : block * parts + part + 1] = weight[block : block + 1, lanes]


def block_weights(sums):
    out = pl.pallas_call(
        weight_kernel,
        out_shape=jax.ShapeDtypeStruct((BLK_DEV * BR // LANES, LANES), jnp.float32),
        in_specs=[vmem()] * len(sums),
        out_specs=vmem(),
        compiler_params=params(4),
        name="weights",
    )(*[in_vmem(x) for x in sums])
    return out.reshape(BLK_DEV * BR)


def hop(parts, step):
    count = lax.axis_size("narrow")
    perm = [(i, i ^ step) for i in range(count)]
    return [[lax.ppermute(piece, "narrow", perm) for piece in part] for part in parts]


def first_hops(part):
    parts = [part]
    step = lax.axis_size("narrow") // 2
    while step > 1:
        parts = parts + hop(parts, step)
        step //= 2
    return parts


def to_wide(pieces):
    count = lax.axis_size("wide")
    return [
        lax.ppermute(piece, "wide", [(i, (i + shift) % count) for i in range(count)])
        for shift, piece in enumerate(pieces, 1)
    ]


def on_device(embeddings, pair_list):
    wide_count = lax.axis_size("wide")
    me = lax.axis_index("wide").astype(jnp.int32).reshape(1)
    pairs = pair_list.T
    pair_count = pairs.shape[1]
    capacity = max(2, 2 * pair_count // wide_count)
    feat = embeddings.shape[1]
    blocks = embeddings.reshape(BLK_DEV, BR, feat)
    lists = to_wide([pairs] * (wide_count - 1))
    fixed = lax.optimization_barrier
    outgoing, row_slices = pack(me, pairs, lists, blocks, capacity)

    def pick(received, chunk):
        return select(me, pairs, own, received, *CHUNKS[chunk], PIECES[chunk])

    rows = jnp.stack([part[0] for part in first_hops([row_slices])])
    rows, received, (kept, own) = fixed((rows, to_wide(outgoing[0]), keep(pairs, blocks)))
    cols_a = first_hops(pick(received, 0))
    rows = [[rows], *hop([[rows]], 1)]
    cols_a, rows, received = fixed((cols_a, rows, to_wide(outgoing[1])))
    cols_b = first_hops(pick(received, 1))
    last_b = hop(cols_b[:1], 1)
    cols_a = cols_a + hop(cols_a, 1)
    carry = first_window(rows, [cols_a])
    cols_b, carry = fixed((cols_b, carry))
    cols_b = cols_b + last_b + hop(cols_b[1:], 1)
    square, mass, total, sums = carry
    kernel, mass, row_sums, shares = last_window(
        me, pairs, rows, [cols_a, cols_b], square, mass, sums, wide_count
    )
    came = to_wide(shares[1:])
    mean = means(pairs, row_slices, kernel, mass, total, [cols_a, cols_b], kept)
    weights = block_weights([row_sums, shares[0], *came])
    return weights, mean.reshape(BLK_DEV * BR, feat)


def solution(mesh):
    in_specs = (P(("groups", "wide"), "narrow"), P(("groups", "wide"), None))
    out_specs = (P(("groups", "wide")), P(("groups", "wide"), "narrow"))
    return jax.shard_map(
        on_device, mesh=mesh, in_specs=in_specs, out_specs=out_specs, check_vma=False
    )
```

```python
import functools

import jax
import jax.numpy as jnp
from jax import lax
from jax.experimental import pallas as pl
from jax.experimental.pallas import tpu as pltpu
from jax.sharding import PartitionSpec as P

F = 1024
BR = 512
BLK_DEV = 8
LANES = 128
CHUNKS = ((0, 256), (256, 160), (416, 96))
STACKED = (True, False, False)
WINDOWS = ((0, 256), (256, 512))


def smem():
    return pl.BlockSpec(memory_space=pltpu.SMEM)


def vmem():
    return pl.BlockSpec(memory_space=pltpu.VMEM)


def anywhere():
    return pl.BlockSpec(memory_space=pl.ANY)


def in_vmem(x):
    return pltpu.with_memory_space_constraint(x, pltpu.VMEM)


def in_hbm(x):
    return pltpu.with_memory_space_constraint(x, pltpu.HBM)


def params(mebibytes):
    return pltpu.CompilerParams(vmem_limit_bytes=mebibytes * 1024 * 1024)


def pack_kernel(wide_count, pair_count, capacity, me_ref, pairs_ref, *refs):
    lists, blocks_ref = refs[: wide_count - 1], refs[wide_count - 1]
    *outs, rows_ref, sems = refs[wide_count:]
    me = me_ref[0]
    copies = []

    def send(source, target):
        copies.append(pltpu.make_async_copy(source, target, sems.at[len(copies)]))
        copies[-1].start()

    for chunk, (start, size) in enumerate(CHUNKS):
        for shift in range(1, wide_count):
            asked = lists[wide_count - shift - 1]
            picks = [jnp.int32(0)] * capacity
            count = jnp.int32(0)
            for pair in range(pair_count):
                col = asked[1, pair]
                mine = (col >> 3) == me
                for slot in range(capacity):
                    picks[slot] = jnp.where(mine & (count == slot), col & 7, picks[slot])
                count = count + mine.astype(jnp.int32)
            out = outs[chunk * (wide_count - 1) + shift - 1]
            for slot in range(capacity):
                send(blocks_ref.at[picks[slot], pl.ds(start, size)], out.at[slot])
    for pair in range(pair_count):
        send(blocks_ref.at[pairs_ref[0, pair] & 7], rows_ref.at[pair])
    for copy in copies:
        copy.wait()


def pack(me, pairs, lists, blocks, capacity):
    wide_count, pair_count = len(lists) + 1, pairs.shape[1]
    feat = blocks.shape[-1]
    shapes = [
        pltpu.VMEM((capacity, size, feat), blocks.dtype)
        for _, size in CHUNKS
        for _ in range(1, wide_count)
    ] + [pltpu.VMEM((pair_count, BR, feat), blocks.dtype)]
    copies = (len(shapes) - 1) * capacity + pair_count
    outs = pl.pallas_call(
        functools.partial(pack_kernel, wide_count, pair_count, capacity),
        out_shape=shapes,
        in_specs=[smem()] * (1 + wide_count) + [anywhere()],
        out_specs=[anywhere()] * len(shapes),
        scratch_shapes=[pltpu.SemaphoreType.DMA((copies,))],
        compiler_params=params(4),
        name="pack",
    )(me, in_hbm(pairs), *lists, in_hbm(blocks))
    each = wide_count - 1
    return [outs[c * each : (c + 1) * each] for c in range(len(CHUNKS))], outs[-1]


def select_kernel(wide_count, start, me_ref, pairs_ref, own_ref, *refs):
    pair_count = own_ref.shape[0]
    *received, out_ref = refs
    owners = [pairs_ref[1, pair] >> 3 for pair in range(pair_count)]
    for pair in range(pair_count):
        shift = me_ref[0] - owners[pair]
        shift = jnp.where(shift < 0, shift + wide_count, shift)
        rank = jnp.int32(0)
        for before in range(pair):
            rank = rank + (owners[before] == owners[pair]).astype(jnp.int32)

        @pl.when(shift == 0)
        def _():
            out_ref[pair] = own_ref[pair, start : start + out_ref.shape[1]]

        for other in range(1, wide_count):

            @pl.when(shift == other)
            def _():
                out_ref[pair] = received[other - 1][rank]


def select(me, pairs, own, received, start, size):
    pair_count, _, feat = own.shape
    return pl.pallas_call(
        functools.partial(select_kernel, len(received) + 1, start),
        out_shape=pltpu.VMEM((pair_count, size, feat), own.dtype),
        in_specs=[smem(), smem()] + [vmem()] * (1 + len(received)),
        out_specs=vmem(),
        compiler_params=params(4),
        name="select",
    )(me, in_hbm(pairs), *[in_vmem(x) for x in (own, *received)])


def tree(parts):
    while len(parts) > 1:
        half = len(parts) // 2
        parts = [parts[i] + parts[i + half] for i in range(half)]
    return parts[0]


def across(left, right):
    return lax.dot_general(
        left, right, (((1,), (1,)), ((), ())), preferred_element_type=jnp.float32
    )


def lane_sum(block):
    square = jnp.square(block.astype(jnp.float32))
    return sum(square[:, at : at + LANES] for at in range(0, square.shape[1], LANES))


def segments(window):
    low, high = window
    held = []
    for chunk, (start, size) in enumerate(CHUNKS):
        first, end = max(low, start), min(high, start + size)
        if first < end:
            held.append((chunk, first - start, end - first))
    return held


def scores(rows, cols, square):
    gram = tree([across(row, col) for row, col in zip(rows, cols)])
    other = jnp.sum(tree([lane_sum(col) for col in cols]).T, axis=0, keepdims=True)
    pieces, mass = [], None
    for at in range(0, gram.shape[1], LANES):
        here = slice(at, at + LANES)
        piece = jnp.exp((square + other[:, here] - 2.0 * gram[:, here]) * (-1.0 / F))
        mass = piece if mass is None else mass + piece
        pieces.append(piece)
    kernel = jnp.concatenate(pieces, axis=1) if len(pieces) > 1 else pieces[0]
    return kernel.astype(jnp.bfloat16), jnp.sum(kernel, axis=0, keepdims=True), mass


def take_parts(refs, narrow_count, stacked):
    if stacked:
        return [ref.at[i] for ref in refs[:2] for i in range(narrow_count // 2)], refs[2:]
    return refs[:narrow_count], refs[narrow_count:]


def window_parts(window, narrow_count, refs):
    rows, refs = take_parts(refs, narrow_count, True)
    chunks = []
    for chunk, _, _ in segments(window):
        cols, refs = take_parts(refs, narrow_count, STACKED[chunk])
        chunks.append(cols)
    return rows, chunks


def own_columns(window, chunks, pair):
    held = segments(window)
    pieces = [ref[pair, at : at + size] for ref, (_, at, size) in zip(chunks, held)]
    return jnp.concatenate(pieces, axis=0) if len(pieces) > 1 else pieces[0]


def pair_parts(window, rows, chunks, pair):
    cols = [own_columns(window, [c[i] for c in chunks], pair) for i in range(len(rows))]
    return [part[pair] for part in rows], cols


def first_kernel(window, narrow_count, *refs):
    square_ref, mass_ref, total_ref, sums_ref = refs[-4:]
    all_rows, chunks = window_parts(window, narrow_count, refs)
    for pair in range(square_ref.shape[0]):
        rows, cols = pair_parts(window, all_rows, chunks, pair)
        square = jnp.sum(tree([lane_sum(row) for row in rows]), axis=1, keepdims=True)
        square = jnp.broadcast_to(square, (BR, LANES))
        kernel, sums, mass = scores(rows, cols, square)
        square_ref[pair] = square
        mass_ref[pair] = mass
        sums_ref[pair : pair + 1] = sums
        total_ref[pair] = jnp.dot(kernel, cols[0], preferred_element_type=jnp.float32)


def last_kernel(window, narrow_count, wide_count, me_ref, pairs_ref, *refs):
    square_in, mass_in, sums_in = refs[-6 - wide_count : -3 - wide_count]
    kernel_ref, mass_ref, row_ref = refs[-3 - wide_count : -wide_count]
    shares = refs[-wide_count:]
    for ref in (row_ref, *shares):
        ref[...] = jnp.zeros_like(ref)
    all_rows, chunks = window_parts(window, narrow_count, refs)
    for pair in range(square_in.shape[0]):
        rows, cols = pair_parts(window, all_rows, chunks, pair)
        kernel, sums, mass = scores(rows, cols, square_in[pair])
        kernel_ref[pair] = kernel
        sums = jnp.concatenate([sums_in[pair : pair + 1], sums], axis=1)
        mass = mass_in[pair] + mass
        mass_ref[pair] = mass
        row_ref[pl.ds(pairs_ref[0, pair] & 7, 1)] += jnp.sum(mass.T, axis=0, keepdims=True)
        col = pairs_ref[1, pair]
        shift = (col >> 3) - me_ref[0]
        shift = jnp.where(shift < 0, shift + wide_count, shift)
        for other, ref in enumerate(shares):
            ref[pl.ds(col & 7, 1)] += jnp.where(shift == other, sums, 0.0)


def estimate(pair_count, size):
    return pl.CostEstimate(
        flops=2 * pair_count * BR * size * F,
        transcendentals=pair_count * BR * size,
        bytes_accessed=8 * 1024 * 1024,
    )


def first_window(rows, cols, narrow_count):
    _, pair_count, _, feat = rows[0].shape
    window = WINDOWS[0]
    lanes = pltpu.VMEM((pair_count, BR, LANES), jnp.float32)
    total = pltpu.VMEM((pair_count, BR, feat), jnp.float32)
    args = list(rows)
    for chunk, _, _ in segments(window):
        args += cols[chunk]
    return pl.pallas_call(
        functools.partial(first_kernel, window, narrow_count),
        out_shape=[lanes, lanes, total, pltpu.VMEM((pair_count, window[1]), jnp.float32)],
        in_specs=[vmem()] * len(args),
        out_specs=[vmem()] * 4,
        compiler_params=params(16),
        cost_estimate=pl.CostEstimate(flops=0, transcendentals=0, bytes_accessed=0),
        name="first_window",
    )(*[in_vmem(x) for x in args])


def last_window(me, pairs, rows, cols, square, mass, sums, narrow_count, wide_count):
    pair_count = rows[0].shape[1]
    window = WINDOWS[1]
    size = window[1] - window[0]
    by_block = pltpu.VMEM((BLK_DEV, BR), jnp.float32)
    shapes = [
        pltpu.VMEM((pair_count, BR, size), jnp.bfloat16),
        pltpu.VMEM((pair_count, BR, LANES), jnp.float32),
    ] + [by_block] * (1 + wide_count)
    args = list(rows)
    for chunk, _, _ in segments(window):
        args += cols[chunk]
    args += [square, mass, sums]
    kernel, mass, row_sums, *shares = pl.pallas_call(
        functools.partial(last_kernel, window, narrow_count, wide_count),
        out_shape=shapes,
        in_specs=[smem(), smem()] + [vmem()] * len(args),
        out_specs=[vmem()] * len(shapes),
        compiler_params=params(16),
        cost_estimate=estimate(pair_count, size),
        name="last_window",
    )(me, in_hbm(pairs), *[in_vmem(x) for x in args])
    return kernel, mass, row_sums, shares


def keep_kernel(pairs_ref, block_ref, blocks_ref, out_ref, own_ref, sems):
    here = pl.program_id(0)

    def copies():
        for pair in range(own_ref.shape[0]):
            source = blocks_ref.at[pairs_ref[1, pair] & 7]
            yield pltpu.make_async_copy(source, own_ref.at[pair], sems.at[pair])

    @pl.when(here == 0)
    def _():
        for copy in copies():
            copy.start()

    out_ref[...] = block_ref[...]

    @pl.when(here == pl.num_programs(0) - 1)
    def _():
        for copy in copies():
            copy.wait()


def keep(pairs, blocks):
    pair_count = pairs.shape[1]
    block = pl.BlockSpec((1, *blocks.shape[1:]), lambda k: (k, 0, 0))
    return pl.pallas_call(
        keep_kernel,
        out_shape=[
            pltpu.HBM(blocks.shape, blocks.dtype),
            pltpu.VMEM((pair_count, *blocks.shape[1:]), blocks.dtype),
        ],
        grid=(blocks.shape[0],),
        in_specs=[smem(), block, anywhere()],
        out_specs=[block, anywhere()],
        scratch_shapes=[pltpu.SemaphoreType.DMA((pair_count,))],
        compiler_params=params(4),
        name="keep",
    )(in_hbm(pairs), in_hbm(blocks), in_hbm(blocks))


def mean_kernel(window, local_ref, rows_ref, kernel_ref, mass_ref, total_ref, *refs):
    *chunks, _, out_ref, part, weight, total, mass, made, sems = refs
    pair_count, _, feat = rows_ref.shape
    local = [local_ref[0, pair] & 7 for pair in range(pair_count)]

    def copy(pair):
        return pltpu.make_async_copy(made.at[pair], out_ref.at[local[pair]], sems.at[pair])

    firsts = []
    for pair in range(pair_count):
        sums = total_ref[pair] + jnp.dot(
            kernel_ref[pair], own_columns(window, chunks, pair), preferred_element_type=jnp.float32
        )
        part[pair] = sums.astype(jnp.bfloat16)
        weight[pair] = jnp.broadcast_to(
            jnp.sum(mass_ref[pair], axis=1, keepdims=True), (BR, LANES)
        )
        same = [local[other] == local[pair] for other in range(pair)]
        firsts.append(jnp.logical_not(functools.reduce(jnp.logical_or, same, jnp.bool_(False))))
    for pair in range(pair_count):

        @pl.when(firsts[pair])
        def _():
            total[...] = rows_ref[pair].astype(jnp.float32) + part[pair].astype(jnp.float32)
            mass[...] = 1.0 + weight[pair]
            for other in range(pair + 1, pair_count):

                @pl.when(local[other] == local[pair])
                def _():
                    total[...] += part[other].astype(jnp.float32)
                    mass[...] += weight[other]

            scale = 1.0 / mass[...]
            for at in range(0, feat, LANES):
                lanes = slice(at, at + LANES)
                made[pair, :, lanes] = (total[:, lanes] * scale).astype(jnp.bfloat16)
            copy(pair).start()

    for pair in range(pair_count):

        @pl.when(firsts[pair])
        def _():
            copy(pair).wait()


def means(pairs, rows, kernel, mass, total, cols, kept):
    pair_count, _, feat = rows.shape
    window = WINDOWS[1]
    own = [cols[chunk][0] for chunk, _, _ in segments(window)]
    args = [in_vmem(x) for x in (rows, kernel, mass, total, *own)]
    return pl.pallas_call(
        functools.partial(mean_kernel, window),
        out_shape=pltpu.HBM(kept.shape, jnp.bfloat16),
        in_specs=[smem()] + [vmem()] * len(args) + [anywhere()],
        out_specs=anywhere(),
        scratch_shapes=[
            pltpu.VMEM((pair_count, BR, feat), jnp.bfloat16),
            pltpu.VMEM((pair_count, BR, LANES), jnp.float32),
            pltpu.VMEM((BR, feat), jnp.float32),
            pltpu.VMEM((BR, LANES), jnp.float32),
            pltpu.VMEM((pair_count, BR, feat), jnp.bfloat16),
            pltpu.SemaphoreType.DMA((pair_count,)),
        ],
        input_output_aliases={1 + len(args): 0},
        compiler_params=params(16),
        cost_estimate=estimate(pair_count, 128),
        name="means",
    )(in_hbm(pairs), *args, in_hbm(kept))


def weight_kernel(*refs):
    out_ref = refs[-1]
    mass = refs[0][...]
    for ref in refs[1:-1]:
        mass = mass + ref[...]
    weight = 1.0 / (1.0 + mass / BR)
    parts = BR // LANES
    for block in range(BLK_DEV):
        for part in range(parts):
            lanes = slice(part * LANES, (part + 1) * LANES)
            out_ref[block * parts + part : block * parts + part + 1] = weight[block : block + 1, lanes]


def block_weights(sums):
    out = pl.pallas_call(
        weight_kernel,
        out_shape=jax.ShapeDtypeStruct((BLK_DEV * BR // LANES, LANES), jnp.float32),
        in_specs=[vmem()] * len(sums),
        out_specs=vmem(),
        compiler_params=params(4),
        name="weights",
    )(*[in_vmem(x) for x in sums])
    return out.reshape(BLK_DEV * BR)


def hop(parts, step):
    count = lax.axis_size("narrow")
    perm = [(i, i ^ step) for i in range(count)]
    return [lax.ppermute(part, "narrow", perm) for part in parts]


def first_hops(parts):
    step = lax.axis_size("narrow") // 2
    while step > 1:
        parts = parts + hop(parts, step)
        step //= 2
    return parts


def to_wide(pieces):
    count = lax.axis_size("wide")
    return [
        lax.ppermute(piece, "wide", [(i, (i + shift) % count) for i in range(count)])
        for shift, piece in enumerate(pieces, 1)
    ]


def on_device(embeddings, pair_list):
    wide_count = lax.axis_size("wide")
    me = lax.axis_index("wide").astype(jnp.int32).reshape(1)
    pairs = pair_list.T
    pair_count = pairs.shape[1]
    capacity = max(2, 2 * pair_count // wide_count)
    feat = embeddings.shape[1]
    blocks = embeddings.reshape(BLK_DEV, BR, feat)
    lists = to_wide([pairs] * (wide_count - 1))
    fixed = lax.optimization_barrier
    outgoing, row_slices = pack(me, pairs, lists, blocks, capacity)

    def pick(received, chunk):
        return select(me, pairs, own, received, *CHUNKS[chunk])

    rows = jnp.stack(first_hops([row_slices]))
    rows, received, (kept, own) = fixed((rows, to_wide(outgoing[0]), keep(pairs, blocks)))
    cols_a = jnp.stack(first_hops([pick(received, 0)]))
    rows = [rows, *hop([rows], 1)]
    cols_a, rows, received = fixed((cols_a, rows, to_wide(outgoing[1])))
    cols_b = first_hops([pick(received, 1)])
    cols_a = [cols_a, *hop([cols_a], 1)]
    cols_a, cols_b, received = fixed((cols_a, cols_b, to_wide(outgoing[2])))
    cols_c = first_hops([pick(received, 2)])
    last_c = hop(cols_c[:1], 1)
    cols_b = cols_b + hop(cols_b, 1)
    narrow_count = len(cols_b)
    carry = first_window(rows, [cols_a], narrow_count)
    cols_b, cols_c, carry = fixed((cols_b, cols_c, carry))
    cols_c = cols_c + last_c + hop(cols_c[1:], 1)
    square, mass, total, sums = carry
    kernel, mass, row_sums, shares = last_window(
        me, pairs, rows, [cols_a, cols_b, cols_c], square, mass, sums, narrow_count, wide_count
    )
    came = to_wide(shares[1:])
    mean = means(pairs, row_slices, kernel, mass, total, [cols_a, cols_b, cols_c], kept)
    weights = block_weights([row_sums, shares[0], *came])
    return weights, mean.reshape(BLK_DEV * BR, feat)


def solution(mesh):
    in_specs = (P(("groups", "wide"), "narrow"), P(("groups", "wide"), None))
    out_specs = (P(("groups", "wide")), P(("groups", "wide"), "narrow"))
    return jax.shard_map(
        on_device, mesh=mesh, in_specs=in_specs, out_specs=out_specs, check_vma=False
    )
```

```python
import functools

import jax
import jax.numpy as jnp
from jax import lax
from jax.experimental import pallas as pl
from jax.experimental.pallas import tpu as pltpu
from jax.sharding import PartitionSpec as P

F = 1024
BR = 512
BLK_DEV = 8
LANES = 128
CHUNKS = ((0, 320), (320, 192))
PIECES = (2, 1)
WINDOWS = ((0, 256), (256, 512))


def smem():
    return pl.BlockSpec(memory_space=pltpu.SMEM)


def vmem():
    return pl.BlockSpec(memory_space=pltpu.VMEM)


def anywhere():
    return pl.BlockSpec(memory_space=pl.ANY)


def in_vmem(x):
    return pltpu.with_memory_space_constraint(x, pltpu.VMEM)


def in_hbm(x):
    return pltpu.with_memory_space_constraint(x, pltpu.HBM)


def params(mebibytes):
    return pltpu.CompilerParams(vmem_limit_bytes=mebibytes * 1024 * 1024)


def pack_kernel(wide_count, pair_count, capacity, me_ref, pairs_ref, *refs):
    lists, blocks_ref = refs[: wide_count - 1], refs[wide_count - 1]
    *outs, rows_ref, sems = refs[wide_count:]
    me = me_ref[0]
    copies = []

    def send(source, target):
        copies.append(pltpu.make_async_copy(source, target, sems.at[len(copies)]))
        copies[-1].start()

    for chunk, (start, size) in enumerate(CHUNKS):
        for shift in range(1, wide_count):
            asked = lists[shift - 1]
            picks = [jnp.int32(0)] * capacity
            count = jnp.int32(0)
            for pair in range(pair_count):
                col = asked[1, pair]
                mine = (col >> 3) == me
                for slot in range(capacity):
                    picks[slot] = jnp.where(mine & (count == slot), col & 7, picks[slot])
                count = count + mine.astype(jnp.int32)
            out = outs[chunk * (wide_count - 1) + shift - 1]
            for slot in range(capacity):
                send(blocks_ref.at[picks[slot], pl.ds(start, size)], out.at[slot])
    for pair in range(pair_count):
        send(blocks_ref.at[pairs_ref[0, pair] & 7], rows_ref.at[pair])
    for copy in copies:
        copy.wait()


def pack(me, pairs, lists, blocks, capacity):
    wide_count, pair_count = len(lists) + 1, pairs.shape[1]
    feat = blocks.shape[-1]
    shapes = [
        pltpu.VMEM((capacity, size, feat), blocks.dtype)
        for _, size in CHUNKS
        for _ in range(1, wide_count)
    ] + [pltpu.VMEM((pair_count, BR, feat), blocks.dtype)]
    copies = (len(shapes) - 1) * capacity + pair_count
    outs = pl.pallas_call(
        functools.partial(pack_kernel, wide_count, pair_count, capacity),
        out_shape=shapes,
        in_specs=[smem()] * (1 + wide_count) + [anywhere()],
        out_specs=[anywhere()] * len(shapes),
        scratch_shapes=[pltpu.SemaphoreType.DMA((copies,))],
        compiler_params=params(4),
        name="pack",
    )(me, in_hbm(pairs), *lists, in_hbm(blocks))
    each = wide_count - 1
    return [outs[c * each : (c + 1) * each] for c in range(len(CHUNKS))], outs[-1]


def select_kernel(wide_count, start, me_ref, pairs_ref, own_ref, *refs):
    pair_count = own_ref.shape[0]
    outs = refs[wide_count - 1 :]
    received = refs[: wide_count - 1]
    each, size, _ = outs[0].shape
    owners = [pairs_ref[1, pair] >> 3 for pair in range(pair_count)]
    for pair in range(pair_count):
        shift = me_ref[0] - owners[pair]
        shift = jnp.where(shift < 0, shift + wide_count, shift)
        rank = jnp.int32(0)
        for before in range(pair):
            rank = rank + (owners[before] == owners[pair]).astype(jnp.int32)

        out = outs[pair // each].at[pair % each]

        @pl.when(shift == 0)
        def _():
            out[...] = own_ref[pair, start : start + size]

        for other in range(1, wide_count):

            @pl.when(shift == other)
            def _():
                out[...] = received[other - 1][rank]


def select(me, pairs, own, received, start, size, pieces):
    pair_count, _, feat = own.shape
    return pl.pallas_call(
        functools.partial(select_kernel, len(received) + 1, start),
        out_shape=[pltpu.VMEM((pair_count // pieces, size, feat), own.dtype)] * pieces,
        in_specs=[smem(), smem()] + [vmem()] * (1 + len(received)),
        out_specs=[vmem()] * pieces,
        compiler_params=params(4),
        name="select",
    )(me, in_hbm(pairs), *[in_vmem(x) for x in (own, *received)])


def tree(parts):
    while len(parts) > 1:
        half = len(parts) // 2
        parts = [parts[i] + parts[i + half] for i in range(half)]
    return parts[0]


def across(left, right):
    return lax.dot_general(
        left, right, (((1,), (1,)), ((), ())), preferred_element_type=jnp.float32
    )


def lane_sum(block):
    square = jnp.square(block.astype(jnp.float32))
    return sum(square[:, at : at + LANES] for at in range(0, square.shape[1], LANES))


def segments(window):
    low, high = window
    held = []
    for chunk, (start, size) in enumerate(CHUNKS):
        first, end = max(low, start), min(high, start + size)
        if first < end:
            held.append((chunk, first - start, end - first))
    return held


def scores(rows, cols, square):
    gram = tree([across(row, col) for row, col in zip(rows, cols)])
    other = jnp.sum(tree([lane_sum(col) for col in cols]).T, axis=0, keepdims=True)
    pieces, mass = [], None
    for at in range(0, gram.shape[1], LANES):
        here = slice(at, at + LANES)
        piece = jnp.exp((square + other[:, here] - 2.0 * gram[:, here]) * (-1.0 / F))
        mass = piece if mass is None else mass + piece
        pieces.append(piece)
    kernel = jnp.concatenate(pieces, axis=1) if len(pieces) > 1 else pieces[0]
    return kernel.astype(jnp.bfloat16), jnp.sum(kernel, axis=0, keepdims=True), mass


def take_parts(refs, narrow_count, pieces):
    parts = [refs[i * pieces : (i + 1) * pieces] for i in range(narrow_count)]
    return parts, refs[narrow_count * pieces :]


def of_pair(part, pair):
    each = part[0].shape[0]
    return part[pair // each].at[pair % each]


def window_parts(window, narrow_count, refs):
    rows, refs = [ref.at[i] for ref in refs[:2] for i in range(narrow_count // 2)], refs[2:]
    chunks = []
    for chunk, _, _ in segments(window):
        cols, refs = take_parts(refs, narrow_count, PIECES[chunk])
        chunks.append(cols)
    return rows, chunks


def own_columns(window, chunks, pair):
    held = segments(window)
    pieces = [of_pair(part, pair)[at : at + size] for part, (_, at, size) in zip(chunks, held)]
    return jnp.concatenate(pieces, axis=0) if len(pieces) > 1 else pieces[0]


def pair_parts(window, rows, chunks, pair):
    cols = [own_columns(window, [c[i] for c in chunks], pair) for i in range(len(rows))]
    return [part[pair] for part in rows], cols


def first_kernel(window, narrow_count, *refs):
    square_ref, mass_ref, total_ref, sums_ref = refs[-4:]
    all_rows, chunks = window_parts(window, narrow_count, refs)
    for pair in range(square_ref.shape[0]):
        rows, cols = pair_parts(window, all_rows, chunks, pair)
        square = jnp.sum(tree([lane_sum(row) for row in rows]), axis=1, keepdims=True)
        square = jnp.broadcast_to(square, (BR, LANES))
        kernel, sums, mass = scores(rows, cols, square)
        square_ref[pair] = square
        mass_ref[pair] = mass
        sums_ref[pair : pair + 1] = sums
        total_ref[pair] = jnp.dot(kernel, cols[0], preferred_element_type=jnp.float32)


def last_kernel(window, narrow_count, wide_count, me_ref, pairs_ref, *refs):
    square_in, mass_in, sums_in = refs[-6 - wide_count : -3 - wide_count]
    kernel_ref, mass_ref, row_ref = refs[-3 - wide_count : -wide_count]
    shares = refs[-wide_count:]
    for ref in (row_ref, *shares):
        ref[...] = jnp.zeros_like(ref)
    all_rows, chunks = window_parts(window, narrow_count, refs)
    for pair in range(square_in.shape[0]):
        rows, cols = pair_parts(window, all_rows, chunks, pair)
        kernel, sums, mass = scores(rows, cols, square_in[pair])
        kernel_ref[pair] = kernel
        sums = jnp.concatenate([sums_in[pair : pair + 1], sums], axis=1)
        mass = mass_in[pair] + mass
        mass_ref[pair] = mass
        row_ref[pl.ds(pairs_ref[0, pair] & 7, 1)] += jnp.sum(mass.T, axis=0, keepdims=True)
        col = pairs_ref[1, pair]
        shift = (col >> 3) - me_ref[0]
        shift = jnp.where(shift < 0, shift + wide_count, shift)
        for other, ref in enumerate(shares):
            ref[pl.ds(col & 7, 1)] += jnp.where(shift == other, sums, 0.0)


def estimate(pair_count, size):
    return pl.CostEstimate(
        flops=2 * pair_count * BR * size * F,
        transcendentals=pair_count * BR * size,
        bytes_accessed=8 * 1024 * 1024,
    )


def operands(parts):
    return [piece for part in parts for piece in part]


def first_window(rows, cols):
    _, pair_count, _, feat = rows[0][0].shape
    window = WINDOWS[0]
    lanes = pltpu.VMEM((pair_count, BR, LANES), jnp.float32)
    total = pltpu.VMEM((pair_count, BR, feat), jnp.float32)
    args = operands(rows)
    for chunk, _, _ in segments(window):
        args += operands(cols[chunk])
    return pl.pallas_call(
        functools.partial(first_kernel, window, len(cols[0])),
        out_shape=[lanes, lanes, total, pltpu.VMEM((pair_count, window[1]), jnp.float32)],
        in_specs=[vmem()] * len(args),
        out_specs=[vmem()] * 4,
        compiler_params=params(16),
        cost_estimate=pl.CostEstimate(flops=0, transcendentals=0, bytes_accessed=0),
        name="first_window",
    )(*[in_vmem(x) for x in args])


def last_window(me, pairs, rows, cols, square, mass, sums, wide_count):
    pair_count = rows[0][0].shape[1]
    window = WINDOWS[1]
    size = window[1] - window[0]
    by_block = pltpu.VMEM((BLK_DEV, BR), jnp.float32)
    shapes = [
        pltpu.VMEM((pair_count, BR, size), jnp.bfloat16),
        pltpu.VMEM((pair_count, BR, LANES), jnp.float32),
    ] + [by_block] * (1 + wide_count)
    args = operands(rows)
    for chunk, _, _ in segments(window):
        args += operands(cols[chunk])
    args += [square, mass, sums]
    kernel, mass, row_sums, *shares = pl.pallas_call(
        functools.partial(last_kernel, window, len(cols[0]), wide_count),
        out_shape=shapes,
        in_specs=[smem(), smem()] + [vmem()] * len(args),
        out_specs=[vmem()] * len(shapes),
        compiler_params=params(16),
        cost_estimate=estimate(pair_count, size),
        name="last_window",
    )(me, in_hbm(pairs), *[in_vmem(x) for x in args])
    return kernel, mass, row_sums, shares


def keep_kernel(pairs_ref, block_ref, blocks_ref, out_ref, own_ref, sems):
    here = pl.program_id(0)

    def copies():
        for pair in range(own_ref.shape[0]):
            source = blocks_ref.at[pairs_ref[1, pair] & 7]
            yield pltpu.make_async_copy(source, own_ref.at[pair], sems.at[pair])

    @pl.when(here == 0)
    def _():
        for copy in copies():
            copy.start()

    out_ref[...] = block_ref[...]

    @pl.when(here == pl.num_programs(0) - 1)
    def _():
        for copy in copies():
            copy.wait()


def keep(pairs, blocks):
    pair_count = pairs.shape[1]
    block = pl.BlockSpec((1, *blocks.shape[1:]), lambda k: (k, 0, 0))
    return pl.pallas_call(
        keep_kernel,
        out_shape=[
            pltpu.HBM(blocks.shape, blocks.dtype),
            pltpu.VMEM((pair_count, *blocks.shape[1:]), blocks.dtype),
        ],
        grid=(blocks.shape[0],),
        in_specs=[smem(), block, anywhere()],
        out_specs=[block, anywhere()],
        scratch_shapes=[pltpu.SemaphoreType.DMA((pair_count,))],
        compiler_params=params(4),
        name="keep",
    )(in_hbm(pairs), in_hbm(blocks), in_hbm(blocks))


def mean_kernel(window, local_ref, rows_ref, kernel_ref, mass_ref, total_ref, *refs):
    *refs, _, out_ref, part, weight, total, mass, made, sems = refs
    chunks = []
    for chunk, _, _ in segments(window):
        (own,), refs = take_parts(refs, 1, PIECES[chunk])
        chunks.append(own)
    pair_count, _, feat = rows_ref.shape
    local = [local_ref[0, pair] & 7 for pair in range(pair_count)]

    def copy(pair):
        return pltpu.make_async_copy(made.at[pair], out_ref.at[local[pair]], sems.at[pair])

    firsts = []
    for pair in range(pair_count):
        sums = total_ref[pair] + jnp.dot(
            kernel_ref[pair], own_columns(window, chunks, pair), preferred_element_type=jnp.float32
        )
        part[pair] = sums.astype(jnp.bfloat16)
        weight[pair] = jnp.broadcast_to(
            jnp.sum(mass_ref[pair], axis=1, keepdims=True), (BR, LANES)
        )
        same = [local[other] == local[pair] for other in range(pair)]
        firsts.append(jnp.logical_not(functools.reduce(jnp.logical_or, same, jnp.bool_(False))))
    for pair in range(pair_count):

        @pl.when(firsts[pair])
        def _():
            total[...] = rows_ref[pair].astype(jnp.float32) + part[pair].astype(jnp.float32)
            mass[...] = 1.0 + weight[pair]
            for other in range(pair + 1, pair_count):

                @pl.when(local[other] == local[pair])
                def _():
                    total[...] += part[other].astype(jnp.float32)
                    mass[...] += weight[other]

            scale = 1.0 / mass[...]
            for at in range(0, feat, LANES):
                lanes = slice(at, at + LANES)
                made[pair, :, lanes] = (total[:, lanes] * scale).astype(jnp.bfloat16)
            copy(pair).start()

    for pair in range(pair_count):

        @pl.when(firsts[pair])
        def _():
            copy(pair).wait()


def means(pairs, rows, kernel, mass, total, cols, kept):
    pair_count, _, feat = rows.shape
    window = WINDOWS[1]
    own = operands(cols[chunk][0] for chunk, _, _ in segments(window))
    args = [in_vmem(x) for x in (rows, kernel, mass, total, *own)]
    return pl.pallas_call(
        functools.partial(mean_kernel, window),
        out_shape=pltpu.HBM(kept.shape, jnp.bfloat16),
        in_specs=[smem()] + [vmem()] * len(args) + [anywhere()],
        out_specs=anywhere(),
        scratch_shapes=[
            pltpu.VMEM((pair_count, BR, feat), jnp.bfloat16),
            pltpu.VMEM((pair_count, BR, LANES), jnp.float32),
            pltpu.VMEM((BR, feat), jnp.float32),
            pltpu.VMEM((BR, LANES), jnp.float32),
            pltpu.VMEM((pair_count, BR, feat), jnp.bfloat16),
            pltpu.SemaphoreType.DMA((pair_count,)),
        ],
        input_output_aliases={1 + len(args): 0},
        compiler_params=params(16),
        cost_estimate=estimate(pair_count, 128),
        name="means",
    )(in_hbm(pairs), *args, in_hbm(kept))


def weight_kernel(*refs):
    out_ref = refs[-1]
    mass = refs[0][...]
    for ref in refs[1:-1]:
        mass = mass + ref[...]
    weight = 1.0 / (1.0 + mass / BR)
    parts = BR // LANES
    for block in range(BLK_DEV):
        for part in range(parts):
            lanes = slice(part * LANES, (part + 1) * LANES)
            out_ref[block * parts + part : block * parts + part + 1] = weight[block : block + 1, lanes]


def block_weights(sums):
    out = pl.pallas_call(
        weight_kernel,
        out_shape=jax.ShapeDtypeStruct((BLK_DEV * BR // LANES, LANES), jnp.float32),
        in_specs=[vmem()] * len(sums),
        out_specs=vmem(),
        compiler_params=params(4),
        name="weights",
    )(*[in_vmem(x) for x in sums])
    return out.reshape(BLK_DEV * BR)


def hop(parts, step):
    count = lax.axis_size("narrow")
    perm = [(i, i ^ step) for i in range(count)]
    return [[lax.ppermute(piece, "narrow", perm) for piece in part] for part in parts]


def first_hops(part):
    parts = [part]
    step = lax.axis_size("narrow") // 2
    while step > 1:
        parts = parts + hop(parts, step)
        step //= 2
    return parts


def to_wide(pieces):
    count = lax.axis_size("wide")
    return [
        lax.ppermute(piece, "wide", [(i, (i + shift) % count) for i in range(count)])
        for shift, piece in enumerate(pieces, 1)
    ]


def on_device(embeddings, pair_list):
    wide_count = lax.axis_size("wide")
    me = lax.axis_index("wide").astype(jnp.int32).reshape(1)
    pairs = pair_list.T
    pair_count = pairs.shape[1]
    capacity = max(2, 2 * pair_count // wide_count)
    feat = embeddings.shape[1]
    blocks = embeddings.reshape(BLK_DEV, BR, feat)
    lists = to_wide([pairs] * (wide_count - 1))[::-1]
    fixed = lax.optimization_barrier
    outgoing, row_slices = pack(me, pairs, lists, blocks, capacity)

    def pick(received, chunk):
        return select(me, pairs, own, received, *CHUNKS[chunk], PIECES[chunk])

    rows = jnp.stack([part[0] for part in first_hops([row_slices])])
    rows, received, (kept, own) = fixed((rows, to_wide(outgoing[0]), keep(pairs, blocks)))
    cols_a = first_hops(pick(received, 0))
    rows = [[rows], *hop([[rows]], 1)]
    cols_a, rows, received = fixed((cols_a, rows, to_wide(outgoing[1])))
    cols_b = first_hops(pick(received, 1))
    last_b = hop(cols_b[:1], 1)
    cols_a = cols_a + hop(cols_a, 1)
    carry = first_window(rows, [cols_a])
    cols_b, carry = fixed((cols_b, carry))
    cols_b = cols_b + last_b + hop(cols_b[1:], 1)
    square, mass, total, sums = carry
    kernel, mass, row_sums, shares = last_window(
        me, pairs, rows, [cols_a, cols_b], square, mass, sums, wide_count
    )
    came = to_wide(shares[1:])
    mean = means(pairs, row_slices, kernel, mass, total, [cols_a, cols_b], kept)
    weights = block_weights([row_sums, shares[0], *came])
    return weights, mean.reshape(BLK_DEV * BR, feat)


def solution(mesh):
    in_specs = (P(("groups", "wide"), "narrow"), P(("groups", "wide"), None))
    out_specs = (P(("groups", "wide")), P(("groups", "wide"), "narrow"))
    return jax.shard_map(
        on_device, mesh=mesh, in_specs=in_specs, out_specs=out_specs, check_vma=False
    )
```

```python
import functools

import jax
import jax.numpy as jnp
from jax import lax
from jax.experimental import pallas as pl
from jax.experimental.pallas import tpu as pltpu
from jax.sharding import PartitionSpec as P

F = 1024
BR = 512
BLK_DEV = 8
LANES = 128
CHUNKS = ((0, 320), (320, 192))
PIECES = (2, 1)
WINDOWS = ((0, 256), (256, 512))


def smem():
    return pl.BlockSpec(memory_space=pltpu.SMEM)


def vmem():
    return pl.BlockSpec(memory_space=pltpu.VMEM)


def anywhere():
    return pl.BlockSpec(memory_space=pl.ANY)


def in_vmem(x):
    return pltpu.with_memory_space_constraint(x, pltpu.VMEM)


def in_hbm(x):
    return pltpu.with_memory_space_constraint(x, pltpu.HBM)


def params(mebibytes):
    return pltpu.CompilerParams(vmem_limit_bytes=mebibytes * 1024 * 1024)


def pack_kernel(wide_count, pair_count, capacity, me_ref, pairs_ref, *refs):
    lists, blocks_ref = refs[: wide_count - 1], refs[wide_count - 1]
    *outs, rows_ref, sems = refs[wide_count:]
    me = me_ref[0]
    copies = []

    def send(source, target):
        copies.append(pltpu.make_async_copy(source, target, sems.at[len(copies)]))
        copies[-1].start()

    for chunk, (start, size) in enumerate(CHUNKS):
        for shift in range(1, wide_count):
            asked = lists[shift - 1]
            picks = [jnp.int32(0)] * capacity
            count = jnp.int32(0)
            for pair in range(pair_count):
                col = asked[1, pair]
                mine = (col >> 3) == me
                for slot in range(capacity):
                    picks[slot] = jnp.where(mine & (count == slot), col & 7, picks[slot])
                count = count + mine.astype(jnp.int32)
            out = outs[chunk * (wide_count - 1) + shift - 1]
            for slot in range(capacity):
                send(blocks_ref.at[picks[slot], pl.ds(start, size)], out.at[slot])
    for pair in range(pair_count):
        send(blocks_ref.at[pairs_ref[0, pair] & 7], rows_ref.at[pair])
    for copy in copies:
        copy.wait()


def pack(me, pairs, lists, blocks, capacity):
    wide_count, pair_count = len(lists) + 1, pairs.shape[1]
    feat = blocks.shape[-1]
    shapes = [
        pltpu.VMEM((capacity, size, feat), blocks.dtype)
        for _, size in CHUNKS
        for _ in range(1, wide_count)
    ] + [pltpu.VMEM((pair_count, BR, feat), blocks.dtype)]
    copies = (len(shapes) - 1) * capacity + pair_count
    outs = pl.pallas_call(
        functools.partial(pack_kernel, wide_count, pair_count, capacity),
        out_shape=shapes,
        in_specs=[smem()] * (1 + wide_count) + [anywhere()],
        out_specs=[anywhere()] * len(shapes),
        scratch_shapes=[pltpu.SemaphoreType.DMA((copies,))],
        compiler_params=params(4),
        name="pack",
    )(me, in_hbm(pairs), *lists, in_hbm(blocks))
    each = wide_count - 1
    return [outs[c * each : (c + 1) * each] for c in range(len(CHUNKS))], outs[-1]


def select_kernel(wide_count, start, me_ref, pairs_ref, own_ref, *refs):
    pair_count = own_ref.shape[0]
    outs = refs[wide_count - 1 :]
    received = refs[: wide_count - 1]
    each, size, _ = outs[0].shape
    owners = [pairs_ref[1, pair] >> 3 for pair in range(pair_count)]
    for pair in range(pair_count):
        shift = me_ref[0] - owners[pair]
        shift = jnp.where(shift < 0, shift + wide_count, shift)
        rank = jnp.int32(0)
        for before in range(pair):
            rank = rank + (owners[before] == owners[pair]).astype(jnp.int32)

        out = outs[pair // each].at[pair % each]

        @pl.when(shift == 0)
        def _():
            out[...] = own_ref[pair, start : start + size]

        for other in range(1, wide_count):

            @pl.when(shift == other)
            def _():
                out[...] = received[other - 1][rank]


def select(me, pairs, own, received, start, size, pieces):
    pair_count, _, feat = own.shape
    return pl.pallas_call(
        functools.partial(select_kernel, len(received) + 1, start),
        out_shape=[pltpu.VMEM((pair_count // pieces, size, feat), own.dtype)] * pieces,
        in_specs=[smem(), smem()] + [vmem()] * (1 + len(received)),
        out_specs=[vmem()] * pieces,
        compiler_params=params(4),
        name="select",
    )(me, in_hbm(pairs), *[in_vmem(x) for x in (own, *received)])


def tree(parts):
    while len(parts) > 1:
        half = len(parts) // 2
        parts = [parts[i] + parts[i + half] for i in range(half)]
    return parts[0]


def across(left, right):
    return lax.dot_general(
        left, right, (((1,), (1,)), ((), ())), preferred_element_type=jnp.float32
    )


def lane_sum(block):
    square = jnp.square(block.astype(jnp.float32))
    return sum(square[:, at : at + LANES] for at in range(0, square.shape[1], LANES))


def segments(window):
    low, high = window
    held = []
    for chunk, (start, size) in enumerate(CHUNKS):
        first, end = max(low, start), min(high, start + size)
        if first < end:
            held.append((chunk, first - start, end - first))
    return held


def scores(rows, cols, square):
    gram = tree([across(row, col) for row, col in zip(rows, cols)])
    other = jnp.sum(tree([lane_sum(col) for col in cols]).T, axis=0, keepdims=True)
    pieces, mass = [], None
    for at in range(0, gram.shape[1], LANES):
        here = slice(at, at + LANES)
        piece = jnp.exp((square + other[:, here] - 2.0 * gram[:, here]) * (-1.0 / F))
        mass = piece if mass is None else mass + piece
        pieces.append(piece)
    kernel = jnp.concatenate(pieces, axis=1) if len(pieces) > 1 else pieces[0]
    return kernel.astype(jnp.bfloat16), jnp.sum(kernel, axis=0, keepdims=True), mass


def take_parts(refs, narrow_count, pieces):
    parts = [refs[i * pieces : (i + 1) * pieces] for i in range(narrow_count)]
    return parts, refs[narrow_count * pieces :]


def of_pair(part, pair):
    each = part[0].shape[0]
    return part[pair // each].at[pair % each]


def window_parts(window, narrow_count, refs):
    rows, refs = refs[0], refs[1:]
    chunks = []
    for chunk, _, _ in segments(window):
        cols, refs = take_parts(refs, narrow_count, PIECES[chunk])
        chunks.append(cols)
    return rows, chunks


def own_columns(window, chunks, pair):
    held = segments(window)
    pieces = [of_pair(part, pair)[at : at + size] for part, (_, at, size) in zip(chunks, held)]
    return jnp.concatenate(pieces, axis=0) if len(pieces) > 1 else pieces[0]


def hop_order(narrow_count):
    order, step = [0], narrow_count // 2
    while step:
        order = order + [other ^ step for other in order]
        step //= 2
    return order


def pair_parts(window, lane, rows, chunks, pair):
    order = hop_order(rows.shape[0])
    cols = [own_columns(window, [c[i] for c in chunks], pair) for i in range(len(order))]
    return [rows[lane ^ other, pair] for other in order], cols


def first_kernel(window, narrow_count, lane_ref, *refs):
    square_ref, mass_ref, total_ref, sums_ref = refs[-4:]
    all_rows, chunks = window_parts(window, narrow_count, refs)
    for pair in range(square_ref.shape[0]):
        rows, cols = pair_parts(window, lane_ref[0], all_rows, chunks, pair)
        square = jnp.sum(tree([lane_sum(row) for row in rows]), axis=1, keepdims=True)
        square = jnp.broadcast_to(square, (BR, LANES))
        kernel, sums, mass = scores(rows, cols, square)
        square_ref[pair] = square
        mass_ref[pair] = mass
        sums_ref[pair : pair + 1] = sums
        total_ref[pair] = jnp.dot(kernel, cols[0], preferred_element_type=jnp.float32)


def last_kernel(window, narrow_count, wide_count, me_ref, lane_ref, pairs_ref, *refs):
    square_in, mass_in, sums_in = refs[-6 - wide_count : -3 - wide_count]
    kernel_ref, mass_ref, row_ref = refs[-3 - wide_count : -wide_count]
    shares = refs[-wide_count:]
    for ref in (row_ref, *shares):
        ref[...] = jnp.zeros_like(ref)
    all_rows, chunks = window_parts(window, narrow_count, refs)
    for pair in range(square_in.shape[0]):
        rows, cols = pair_parts(window, lane_ref[0], all_rows, chunks, pair)
        kernel, sums, mass = scores(rows, cols, square_in[pair])
        kernel_ref[pair] = kernel
        sums = jnp.concatenate([sums_in[pair : pair + 1], sums], axis=1)
        mass = mass_in[pair] + mass
        mass_ref[pair] = mass
        row_ref[pl.ds(pairs_ref[0, pair] & 7, 1)] += jnp.sum(mass.T, axis=0, keepdims=True)
        col = pairs_ref[1, pair]
        shift = (col >> 3) - me_ref[0]
        shift = jnp.where(shift < 0, shift + wide_count, shift)
        for other, ref in enumerate(shares):
            ref[pl.ds(col & 7, 1)] += jnp.where(shift == other, sums, 0.0)


def estimate(pair_count, size):
    return pl.CostEstimate(
        flops=2 * pair_count * BR * size * F,
        transcendentals=pair_count * BR * size,
        bytes_accessed=8 * 1024 * 1024,
    )


def operands(parts):
    return [piece for part in parts for piece in part]


def first_window(lane, rows, cols):
    _, pair_count, _, feat = rows.shape
    window = WINDOWS[0]
    lanes = pltpu.VMEM((pair_count, BR, LANES), jnp.float32)
    total = pltpu.VMEM((pair_count, BR, feat), jnp.float32)
    args = [rows]
    for chunk, _, _ in segments(window):
        args += operands(cols[chunk])
    return pl.pallas_call(
        functools.partial(first_kernel, window, len(cols[0])),
        out_shape=[lanes, lanes, total, pltpu.VMEM((pair_count, window[1]), jnp.float32)],
        in_specs=[smem()] + [vmem()] * len(args),
        out_specs=[vmem()] * 4,
        compiler_params=params(16),
        cost_estimate=pl.CostEstimate(flops=0, transcendentals=0, bytes_accessed=0),
        name="first_window",
    )(lane, *[in_vmem(x) for x in args])


def last_window(me, lane, pairs, rows, cols, square, mass, sums, wide_count):
    pair_count = rows.shape[1]
    window = WINDOWS[1]
    size = window[1] - window[0]
    by_block = pltpu.VMEM((BLK_DEV, BR), jnp.float32)
    shapes = [
        pltpu.VMEM((pair_count, BR, size), jnp.bfloat16),
        pltpu.VMEM((pair_count, BR, LANES), jnp.float32),
    ] + [by_block] * (1 + wide_count)
    args = [rows]
    for chunk, _, _ in segments(window):
        args += operands(cols[chunk])
    args += [square, mass, sums]
    kernel, mass, row_sums, *shares = pl.pallas_call(
        functools.partial(last_kernel, window, len(cols[0]), wide_count),
        out_shape=shapes,
        in_specs=[smem(), smem(), smem()] + [vmem()] * len(args),
        out_specs=[vmem()] * len(shapes),
        compiler_params=params(16),
        cost_estimate=estimate(pair_count, size),
        name="last_window",
    )(me, lane, in_hbm(pairs), *[in_vmem(x) for x in args])
    return kernel, mass, row_sums, shares


def keep_kernel(pairs_ref, block_ref, blocks_ref, out_ref, own_ref, sems):
    here = pl.program_id(0)

    def copies():
        for pair in range(own_ref.shape[0]):
            source = blocks_ref.at[pairs_ref[1, pair] & 7]
            yield pltpu.make_async_copy(source, own_ref.at[pair], sems.at[pair])

    @pl.when(here == 0)
    def _():
        for copy in copies():
            copy.start()

    out_ref[...] = block_ref[...]

    @pl.when(here == pl.num_programs(0) - 1)
    def _():
        for copy in copies():
            copy.wait()


def keep(pairs, blocks):
    pair_count = pairs.shape[1]
    block = pl.BlockSpec((1, *blocks.shape[1:]), lambda k: (k, 0, 0))
    return pl.pallas_call(
        keep_kernel,
        out_shape=[
            pltpu.HBM(blocks.shape, blocks.dtype),
            pltpu.VMEM((pair_count, *blocks.shape[1:]), blocks.dtype),
        ],
        grid=(blocks.shape[0],),
        in_specs=[smem(), block, anywhere()],
        out_specs=[block, anywhere()],
        scratch_shapes=[pltpu.SemaphoreType.DMA((pair_count,))],
        compiler_params=params(4),
        name="keep",
    )(in_hbm(pairs), in_hbm(blocks), in_hbm(blocks))


def mean_kernel(window, local_ref, rows_ref, kernel_ref, mass_ref, total_ref, *refs):
    *refs, _, out_ref, part, weight, total, mass, made, sems = refs
    chunks = []
    for chunk, _, _ in segments(window):
        (own,), refs = take_parts(refs, 1, PIECES[chunk])
        chunks.append(own)
    pair_count, _, feat = rows_ref.shape
    local = [local_ref[0, pair] & 7 for pair in range(pair_count)]

    def copy(pair):
        return pltpu.make_async_copy(made.at[pair], out_ref.at[local[pair]], sems.at[pair])

    firsts = []
    for pair in range(pair_count):
        sums = total_ref[pair] + jnp.dot(
            kernel_ref[pair], own_columns(window, chunks, pair), preferred_element_type=jnp.float32
        )
        part[pair] = sums.astype(jnp.bfloat16)
        weight[pair] = jnp.broadcast_to(
            jnp.sum(mass_ref[pair], axis=1, keepdims=True), (BR, LANES)
        )
        same = [local[other] == local[pair] for other in range(pair)]
        firsts.append(jnp.logical_not(functools.reduce(jnp.logical_or, same, jnp.bool_(False))))
    for pair in range(pair_count):

        @pl.when(firsts[pair])
        def _():
            total[...] = rows_ref[pair].astype(jnp.float32) + part[pair].astype(jnp.float32)
            mass[...] = 1.0 + weight[pair]
            for other in range(pair + 1, pair_count):

                @pl.when(local[other] == local[pair])
                def _():
                    total[...] += part[other].astype(jnp.float32)
                    mass[...] += weight[other]

            scale = 1.0 / mass[...]
            for at in range(0, feat, LANES):
                lanes = slice(at, at + LANES)
                made[pair, :, lanes] = (total[:, lanes] * scale).astype(jnp.bfloat16)
            copy(pair).start()

    for pair in range(pair_count):

        @pl.when(firsts[pair])
        def _():
            copy(pair).wait()


def means(pairs, rows, kernel, mass, total, cols, kept):
    pair_count, _, feat = rows.shape
    window = WINDOWS[1]
    own = operands(cols[chunk][0] for chunk, _, _ in segments(window))
    args = [in_vmem(x) for x in (rows, kernel, mass, total, *own)]
    return pl.pallas_call(
        functools.partial(mean_kernel, window),
        out_shape=pltpu.HBM(kept.shape, jnp.bfloat16),
        in_specs=[smem()] + [vmem()] * len(args) + [anywhere()],
        out_specs=anywhere(),
        scratch_shapes=[
            pltpu.VMEM((pair_count, BR, feat), jnp.bfloat16),
            pltpu.VMEM((pair_count, BR, LANES), jnp.float32),
            pltpu.VMEM((BR, feat), jnp.float32),
            pltpu.VMEM((BR, LANES), jnp.float32),
            pltpu.VMEM((pair_count, BR, feat), jnp.bfloat16),
            pltpu.SemaphoreType.DMA((pair_count,)),
        ],
        input_output_aliases={1 + len(args): 0},
        compiler_params=params(16),
        cost_estimate=estimate(pair_count, 128),
        name="means",
    )(in_hbm(pairs), *args, in_hbm(kept))


def weight_kernel(*refs):
    out_ref = refs[-1]
    mass = refs[0][...]
    for ref in refs[1:-1]:
        mass = mass + ref[...]
    weight = 1.0 / (1.0 + mass / BR)
    parts = BR // LANES
    for block in range(BLK_DEV):
        for part in range(parts):
            lanes = slice(part * LANES, (part + 1) * LANES)
            out_ref[block * parts + part : block * parts + part + 1] = weight[block : block + 1, lanes]


def block_weights(sums):
    out = pl.pallas_call(
        weight_kernel,
        out_shape=jax.ShapeDtypeStruct((BLK_DEV * BR // LANES, LANES), jnp.float32),
        in_specs=[vmem()] * len(sums),
        out_specs=vmem(),
        compiler_params=params(4),
        name="weights",
    )(*[in_vmem(x) for x in sums])
    return out.reshape(BLK_DEV * BR)


def hop(parts, step):
    count = lax.axis_size("narrow")
    perm = [(i, i ^ step) for i in range(count)]
    return [[lax.ppermute(piece, "narrow", perm) for piece in part] for part in parts]


def first_hops(part):
    parts = [part]
    step = lax.axis_size("narrow") // 2
    while step > 1:
        parts = parts + hop(parts, step)
        step //= 2
    return parts


def to_wide(pieces):
    count = lax.axis_size("wide")
    return [
        lax.ppermute(piece, "wide", [(i, (i + shift) % count) for i in range(count)])
        for shift, piece in enumerate(pieces, 1)
    ]


def on_device(embeddings, pair_list):
    wide_count = lax.axis_size("wide")
    me = lax.axis_index("wide").astype(jnp.int32).reshape(1)
    lane = lax.axis_index("narrow").astype(jnp.int32).reshape(1)
    pairs = pair_list.T
    pair_count = pairs.shape[1]
    capacity = max(2, 2 * pair_count // wide_count)
    feat = embeddings.shape[1]
    blocks = embeddings.reshape(BLK_DEV, BR, feat)
    lists = to_wide([pairs] * (wide_count - 1))[::-1]
    fixed = lax.optimization_barrier
    outgoing, row_slices = pack(me, pairs, lists, blocks, capacity)

    def pick(received, chunk):
        return select(me, pairs, own, received, *CHUNKS[chunk], PIECES[chunk])

    rows = lax.all_gather(row_slices, "narrow", axis=0)
    rows, received, (kept, own) = fixed((rows, to_wide(outgoing[0]), keep(pairs, blocks)))
    cols_a = first_hops(pick(received, 0))
    cols_a, received = fixed((cols_a, to_wide(outgoing[1])))
    cols_b = first_hops(pick(received, 1))
    last_b = hop(cols_b[:1], 1)
    cols_a = cols_a + hop(cols_a, 1)
    carry = first_window(lane, rows, [cols_a])
    cols_b, carry = fixed((cols_b, carry))
    cols_b = cols_b + last_b + hop(cols_b[1:], 1)
    square, mass, total, sums = carry
    kernel, mass, row_sums, shares = last_window(
        me, lane, pairs, rows, [cols_a, cols_b], square, mass, sums, wide_count
    )
    came = to_wide(shares[1:])
    mean = means(pairs, row_slices, kernel, mass, total, [cols_a, cols_b], kept)
    weights = block_weights([row_sums, shares[0], *came])
    return weights, mean.reshape(BLK_DEV * BR, feat)


def solution(mesh):
    in_specs = (P(("groups", "wide"), "narrow"), P(("groups", "wide"), None))
    out_specs = (P(("groups", "wide")), P(("groups", "wide"), "narrow"))
    return jax.shard_map(
        on_device, mesh=mesh, in_specs=in_specs, out_specs=out_specs, check_vma=False
    )
```

```python
import functools

import jax
import jax.numpy as jnp
from jax import lax
from jax.experimental import pallas as pl
from jax.experimental.pallas import tpu as pltpu
from jax.sharding import PartitionSpec as P

F = 1024
BR = 512
BLK_DEV = 8
LANES = 128
CHUNKS = ((0, 320), (320, 192))
PIECES = (2, 1)
WINDOWS = ((0, 256), (256, 512))


def smem():
    return pl.BlockSpec(memory_space=pltpu.SMEM)


def vmem():
    return pl.BlockSpec(memory_space=pltpu.VMEM)


def anywhere():
    return pl.BlockSpec(memory_space=pl.ANY)


def in_vmem(x):
    return pltpu.with_memory_space_constraint(x, pltpu.VMEM)


def in_hbm(x):
    return pltpu.with_memory_space_constraint(x, pltpu.HBM)


def params(mebibytes):
    return pltpu.CompilerParams(vmem_limit_bytes=mebibytes * 1024 * 1024)


def pack_kernel(wide_count, narrow_count, capacity, me_ref, lane_ref, pairs_ref, *refs):
    lists, blocks_ref = refs[:narrow_count], refs[narrow_count]
    *outs, rows_ref, sems = refs[narrow_count + 1 :]
    pair_count = pairs_ref.shape[1]
    me = me_ref[0]

    def asked(shift, pair):
        back = wide_count - shift
        other = lane_ref[0] ^ (back % narrow_count)
        cols = [ref[back // narrow_count, 1, pair] for ref in lists]
        return sum(jnp.where(other == place, col, 0) for place, col in enumerate(cols))
    copies = []

    def send(source, target):
        copies.append(pltpu.make_async_copy(source, target, sems.at[len(copies)]))
        copies[-1].start()

    for chunk, (start, size) in enumerate(CHUNKS):
        for shift in range(1, wide_count):
            picks = [jnp.int32(0)] * capacity
            count = jnp.int32(0)
            for pair in range(pair_count):
                col = asked(shift, pair)
                mine = (col >> 3) == me
                for slot in range(capacity):
                    picks[slot] = jnp.where(mine & (count == slot), col & 7, picks[slot])
                count = count + mine.astype(jnp.int32)
            out = outs[chunk * (wide_count - 1) + shift - 1]
            for slot in range(capacity):
                send(blocks_ref.at[picks[slot], pl.ds(start, size)], out.at[slot])
    for pair in range(pair_count):
        send(blocks_ref.at[pairs_ref[0, pair] & 7], rows_ref.at[pair])
    for copy in copies:
        copy.wait()


def pack(me, lane, pairs, lists, blocks, capacity, wide_count):
    pair_count = pairs.shape[1]
    feat = blocks.shape[-1]
    shapes = [
        pltpu.VMEM((capacity, size, feat), blocks.dtype)
        for _, size in CHUNKS
        for _ in range(1, wide_count)
    ] + [pltpu.VMEM((pair_count, BR, feat), blocks.dtype)]
    copies = (len(shapes) - 1) * capacity + pair_count
    outs = pl.pallas_call(
        functools.partial(pack_kernel, wide_count, len(lists), capacity),
        out_shape=shapes,
        in_specs=[smem()] * (3 + len(lists)) + [anywhere()],
        out_specs=[anywhere()] * len(shapes),
        scratch_shapes=[pltpu.SemaphoreType.DMA((copies,))],
        compiler_params=params(4),
        name="pack",
    )(me, lane, in_hbm(pairs), *lists, in_hbm(blocks))
    each = wide_count - 1
    return [outs[c * each : (c + 1) * each] for c in range(len(CHUNKS))], outs[-1]


def select_kernel(wide_count, start, me_ref, pairs_ref, own_ref, *refs):
    pair_count = own_ref.shape[0]
    outs = refs[wide_count - 1 :]
    received = refs[: wide_count - 1]
    each, size, _ = outs[0].shape
    owners = [pairs_ref[1, pair] >> 3 for pair in range(pair_count)]
    for pair in range(pair_count):
        shift = me_ref[0] - owners[pair]
        shift = jnp.where(shift < 0, shift + wide_count, shift)
        rank = jnp.int32(0)
        for before in range(pair):
            rank = rank + (owners[before] == owners[pair]).astype(jnp.int32)

        out = outs[pair // each].at[pair % each]

        @pl.when(shift == 0)
        def _():
            out[...] = own_ref[pair, start : start + size]

        for other in range(1, wide_count):

            @pl.when(shift == other)
            def _():
                out[...] = received[other - 1][rank]


def select(me, pairs, own, received, start, size, pieces):
    pair_count, _, feat = own.shape
    return pl.pallas_call(
        functools.partial(select_kernel, len(received) + 1, start),
        out_shape=[pltpu.VMEM((pair_count // pieces, size, feat), own.dtype)] * pieces,
        in_specs=[smem(), smem()] + [vmem()] * (1 + len(received)),
        out_specs=[vmem()] * pieces,
        compiler_params=params(4),
        name="select",
    )(me, in_hbm(pairs), *[in_vmem(x) for x in (own, *received)])


def tree(parts):
    while len(parts) > 1:
        half = len(parts) // 2
        parts = [parts[i] + parts[i + half] for i in range(half)]
    return parts[0]


def across(left, right):
    return lax.dot_general(
        left, right, (((1,), (1,)), ((), ())), preferred_element_type=jnp.float32
    )


def lane_sum(block):
    square = jnp.square(block.astype(jnp.float32))
    return sum(square[:, at : at + LANES] for at in range(0, square.shape[1], LANES))


def segments(window):
    low, high = window
    held = []
    for chunk, (start, size) in enumerate(CHUNKS):
        first, end = max(low, start), min(high, start + size)
        if first < end:
            held.append((chunk, first - start, end - first))
    return held


def scores(rows, cols, square):
    gram = tree([across(row, col) for row, col in zip(rows, cols)])
    other = jnp.sum(tree([lane_sum(col) for col in cols]).T, axis=0, keepdims=True)
    pieces, mass = [], None
    for at in range(0, gram.shape[1], LANES):
        here = slice(at, at + LANES)
        piece = jnp.exp((square + other[:, here] - 2.0 * gram[:, here]) * (-1.0 / F))
        mass = piece if mass is None else mass + piece
        pieces.append(piece)
    kernel = jnp.concatenate(pieces, axis=1) if len(pieces) > 1 else pieces[0]
    return kernel.astype(jnp.bfloat16), jnp.sum(kernel, axis=0, keepdims=True), mass


def take_parts(refs, narrow_count, pieces):
    parts = [refs[i * pieces : (i + 1) * pieces] for i in range(narrow_count)]
    return parts, refs[narrow_count * pieces :]


def of_pair(part, pair):
    each = part[0].shape[0]
    return part[pair // each].at[pair % each]


def window_parts(window, narrow_count, refs):
    rows, refs = [ref.at[i] for ref in refs[:2] for i in range(narrow_count // 2)], refs[2:]
    chunks = []
    for chunk, _, _ in segments(window):
        cols, refs = take_parts(refs, narrow_count, PIECES[chunk])
        chunks.append(cols)
    return rows, chunks


def own_columns(window, chunks, pair):
    held = segments(window)
    pieces = [of_pair(part, pair)[at : at + size] for part, (_, at, size) in zip(chunks, held)]
    return jnp.concatenate(pieces, axis=0) if len(pieces) > 1 else pieces[0]


def pair_parts(window, rows, chunks, pair):
    cols = [own_columns(window, [c[i] for c in chunks], pair) for i in range(len(rows))]
    return [part[pair] for part in rows], cols


def first_kernel(window, narrow_count, *refs):
    square_ref, mass_ref, total_ref, sums_ref = refs[-4:]
    all_rows, chunks = window_parts(window, narrow_count, refs)
    for pair in range(square_ref.shape[0]):
        rows, cols = pair_parts(window, all_rows, chunks, pair)
        square = jnp.sum(tree([lane_sum(row) for row in rows]), axis=1, keepdims=True)
        square = jnp.broadcast_to(square, (BR, LANES))
        kernel, sums, mass = scores(rows, cols, square)
        square_ref[pair] = square
        mass_ref[pair] = mass
        sums_ref[pair : pair + 1] = sums
        total_ref[pair] = jnp.dot(kernel, cols[0], preferred_element_type=jnp.float32)


def last_kernel(window, narrow_count, wide_count, me_ref, lane_ref, pairs_ref, *refs):
    rounds = wide_count // narrow_count
    square_in, mass_in, sums_in = refs[-6 - rounds : -3 - rounds]
    kernel_ref, mass_ref, row_ref = refs[-3 - rounds : -rounds]
    shares = refs[-rounds:]
    for ref in (row_ref, *shares):
        ref[...] = jnp.zeros_like(ref)
    all_rows, chunks = window_parts(window, narrow_count, refs)
    for pair in range(square_in.shape[0]):
        rows, cols = pair_parts(window, all_rows, chunks, pair)
        kernel, sums, mass = scores(rows, cols, square_in[pair])
        kernel_ref[pair] = kernel
        sums = jnp.concatenate([sums_in[pair : pair + 1], sums], axis=1)
        mass = mass_in[pair] + mass
        mass_ref[pair] = mass
        row_ref[pl.ds(pairs_ref[0, pair] & 7, 1)] += jnp.sum(mass.T, axis=0, keepdims=True)
        col = pairs_ref[1, pair]
        shift = (col >> 3) - me_ref[0]
        shift = jnp.where(shift < 0, shift + wide_count, shift)
        for number, ref in enumerate(shares):
            here = shift == number * narrow_count + lane_ref[0]
            ref[pl.ds(col & 7, 1)] += jnp.where(here, sums, 0.0)


def estimate(pair_count, size):
    return pl.CostEstimate(
        flops=2 * pair_count * BR * size * F,
        transcendentals=pair_count * BR * size,
        bytes_accessed=8 * 1024 * 1024,
    )


def operands(parts):
    return [piece for part in parts for piece in part]


def first_window(rows, cols):
    _, pair_count, _, feat = rows[0][0].shape
    window = WINDOWS[0]
    lanes = pltpu.VMEM((pair_count, BR, LANES), jnp.float32)
    total = pltpu.VMEM((pair_count, BR, feat), jnp.float32)
    args = operands(rows)
    for chunk, _, _ in segments(window):
        args += operands(cols[chunk])
    return pl.pallas_call(
        functools.partial(first_kernel, window, len(cols[0])),
        out_shape=[lanes, lanes, total, pltpu.VMEM((pair_count, window[1]), jnp.float32)],
        in_specs=[vmem()] * len(args),
        out_specs=[vmem()] * 4,
        compiler_params=params(16),
        cost_estimate=pl.CostEstimate(flops=0, transcendentals=0, bytes_accessed=0),
        name="first_window",
    )(*[in_vmem(x) for x in args])


def last_window(me, lane, pairs, rows, cols, square, mass, sums, wide_count):
    pair_count = rows[0][0].shape[1]
    window = WINDOWS[1]
    size = window[1] - window[0]
    by_block = pltpu.VMEM((BLK_DEV, BR), jnp.float32)
    shapes = [
        pltpu.VMEM((pair_count, BR, size), jnp.bfloat16),
        pltpu.VMEM((pair_count, BR, LANES), jnp.float32),
    ] + [by_block] * (1 + wide_count // len(cols[0]))
    args = operands(rows)
    for chunk, _, _ in segments(window):
        args += operands(cols[chunk])
    args += [square, mass, sums]
    kernel, mass, row_sums, *shares = pl.pallas_call(
        functools.partial(last_kernel, window, len(cols[0]), wide_count),
        out_shape=shapes,
        in_specs=[smem(), smem(), smem()] + [vmem()] * len(args),
        out_specs=[vmem()] * len(shapes),
        compiler_params=params(16),
        cost_estimate=estimate(pair_count, size),
        name="last_window",
    )(me, lane, in_hbm(pairs), *[in_vmem(x) for x in args])
    return kernel, mass, row_sums, shares


def keep_kernel(pairs_ref, block_ref, blocks_ref, out_ref, own_ref, sems):
    here = pl.program_id(0)

    def copies():
        for pair in range(own_ref.shape[0]):
            source = blocks_ref.at[pairs_ref[1, pair] & 7]
            yield pltpu.make_async_copy(source, own_ref.at[pair], sems.at[pair])

    @pl.when(here == 0)
    def _():
        for copy in copies():
            copy.start()

    out_ref[...] = block_ref[...]

    @pl.when(here == pl.num_programs(0) - 1)
    def _():
        for copy in copies():
            copy.wait()


def keep(pairs, blocks):
    pair_count = pairs.shape[1]
    block = pl.BlockSpec((1, *blocks.shape[1:]), lambda k: (k, 0, 0))
    return pl.pallas_call(
        keep_kernel,
        out_shape=[
            pltpu.HBM(blocks.shape, blocks.dtype),
            pltpu.VMEM((pair_count, *blocks.shape[1:]), blocks.dtype),
        ],
        grid=(blocks.shape[0],),
        in_specs=[smem(), block, anywhere()],
        out_specs=[block, anywhere()],
        scratch_shapes=[pltpu.SemaphoreType.DMA((pair_count,))],
        compiler_params=params(4),
        name="keep",
    )(in_hbm(pairs), in_hbm(blocks), in_hbm(blocks))


def mean_kernel(window, local_ref, rows_ref, kernel_ref, mass_ref, total_ref, *refs):
    *refs, _, out_ref, part, weight, total, mass, made, sems = refs
    chunks = []
    for chunk, _, _ in segments(window):
        (own,), refs = take_parts(refs, 1, PIECES[chunk])
        chunks.append(own)
    pair_count, _, feat = rows_ref.shape
    local = [local_ref[0, pair] & 7 for pair in range(pair_count)]

    def copy(pair):
        return pltpu.make_async_copy(made.at[pair], out_ref.at[local[pair]], sems.at[pair])

    firsts = []
    for pair in range(pair_count):
        sums = total_ref[pair] + jnp.dot(
            kernel_ref[pair], own_columns(window, chunks, pair), preferred_element_type=jnp.float32
        )
        part[pair] = sums.astype(jnp.bfloat16)
        weight[pair] = jnp.broadcast_to(
            jnp.sum(mass_ref[pair], axis=1, keepdims=True), (BR, LANES)
        )
        same = [local[other] == local[pair] for other in range(pair)]
        firsts.append(jnp.logical_not(functools.reduce(jnp.logical_or, same, jnp.bool_(False))))
    for pair in range(pair_count):

        @pl.when(firsts[pair])
        def _():
            total[...] = rows_ref[pair].astype(jnp.float32) + part[pair].astype(jnp.float32)
            mass[...] = 1.0 + weight[pair]
            for other in range(pair + 1, pair_count):

                @pl.when(local[other] == local[pair])
                def _():
                    total[...] += part[other].astype(jnp.float32)
                    mass[...] += weight[other]

            scale = 1.0 / mass[...]
            for at in range(0, feat, LANES):
                lanes = slice(at, at + LANES)
                made[pair, :, lanes] = (total[:, lanes] * scale).astype(jnp.bfloat16)
            copy(pair).start()

    for pair in range(pair_count):

        @pl.when(firsts[pair])
        def _():
            copy(pair).wait()


def means(pairs, rows, kernel, mass, total, cols, kept):
    pair_count, _, feat = rows.shape
    window = WINDOWS[1]
    own = operands(cols[chunk][0] for chunk, _, _ in segments(window))
    args = [in_vmem(x) for x in (rows, kernel, mass, total, *own)]
    return pl.pallas_call(
        functools.partial(mean_kernel, window),
        out_shape=pltpu.HBM(kept.shape, jnp.bfloat16),
        in_specs=[smem()] + [vmem()] * len(args) + [anywhere()],
        out_specs=anywhere(),
        scratch_shapes=[
            pltpu.VMEM((pair_count, BR, feat), jnp.bfloat16),
            pltpu.VMEM((pair_count, BR, LANES), jnp.float32),
            pltpu.VMEM((BR, feat), jnp.float32),
            pltpu.VMEM((BR, LANES), jnp.float32),
            pltpu.VMEM((pair_count, BR, feat), jnp.bfloat16),
            pltpu.SemaphoreType.DMA((pair_count,)),
        ],
        input_output_aliases={1 + len(args): 0},
        compiler_params=params(16),
        cost_estimate=estimate(pair_count, 128),
        name="means",
    )(in_hbm(pairs), *args, in_hbm(kept))


def weight_kernel(rows_ref, *refs):
    sums, out_ref = refs[:-1], refs[-1]
    mass = rows_ref[...] + jnp.sum(tree([ref[...] for ref in sums]), axis=0)
    weight = 1.0 / (1.0 + mass / BR)
    parts = BR // LANES
    for block in range(BLK_DEV):
        for part in range(parts):
            lanes = slice(part * LANES, (part + 1) * LANES)
            out_ref[block * parts + part : block * parts + part + 1] = weight[block : block + 1, lanes]


def block_weights(row_sums, sums):
    out = pl.pallas_call(
        weight_kernel,
        out_shape=jax.ShapeDtypeStruct((BLK_DEV * BR // LANES, LANES), jnp.float32),
        in_specs=[vmem()] * (1 + len(sums)),
        out_specs=vmem(),
        compiler_params=params(4),
        name="weights",
    )(*[in_vmem(x) for x in (row_sums, *sums)])
    return out.reshape(BLK_DEV * BR)


def hop(parts, step):
    count = lax.axis_size("narrow")
    perm = [(i, i ^ step) for i in range(count)]
    return [[lax.ppermute(piece, "narrow", perm) for piece in part] for part in parts]


def first_hops(part):
    parts = [part]
    step = lax.axis_size("narrow") // 2
    while step > 1:
        parts = parts + hop(parts, step)
        step //= 2
    return parts


def spread(pieces):
    wide_count, narrow_count = lax.axis_size("wide"), lax.axis_size("narrow")
    came = []
    for number, piece in enumerate(pieces):
        perm = []
        for wide in range(wide_count):
            for narrow in range(narrow_count):
                target = (wide + number * narrow_count + narrow) % wide_count
                perm.append((wide * narrow_count + narrow, target * narrow_count + narrow))
        came.append(lax.ppermute(piece, ("wide", "narrow"), perm))
    came = jnp.stack(came)
    return [came] + [
        lax.ppermute(came, "narrow", [(i, i ^ other) for i in range(narrow_count)])
        for other in range(1, narrow_count)
    ]


def to_wide(pieces):
    count = lax.axis_size("wide")
    return [
        lax.ppermute(piece, "wide", [(i, (i + shift) % count) for i in range(count)])
        for shift, piece in enumerate(pieces, 1)
    ]


def on_device(embeddings, pair_list):
    wide_count = lax.axis_size("wide")
    me = lax.axis_index("wide").astype(jnp.int32).reshape(1)
    pairs = pair_list.T
    pair_count = pairs.shape[1]
    capacity = max(2, 2 * pair_count // wide_count)
    feat = embeddings.shape[1]
    blocks = embeddings.reshape(BLK_DEV, BR, feat)
    lane = lax.axis_index("narrow").astype(jnp.int32).reshape(1)
    rounds = wide_count // lax.axis_size("narrow")
    lists = spread([pairs] * rounds)
    fixed = lax.optimization_barrier
    outgoing, row_slices = pack(me, lane, pairs, lists, blocks, capacity, wide_count)

    def pick(received, chunk):
        return select(me, pairs, own, received, *CHUNKS[chunk], PIECES[chunk])

    rows = jnp.stack([part[0] for part in first_hops([row_slices])])
    rows, received, (kept, own) = fixed((rows, to_wide(outgoing[0]), keep(pairs, blocks)))
    cols_a = first_hops(pick(received, 0))
    rows = [[rows], *hop([[rows]], 1)]
    cols_a, rows, received = fixed((cols_a, rows, to_wide(outgoing[1])))
    cols_b = first_hops(pick(received, 1))
    last_b = hop(cols_b[:1], 1)
    cols_a = cols_a + hop(cols_a, 1)
    carry = first_window(rows, [cols_a])
    cols_b, carry = fixed((cols_b, carry))
    cols_b = cols_b + last_b + hop(cols_b[1:], 1)
    square, mass, total, sums = carry
    kernel, mass, row_sums, shares = last_window(
        me, lane, pairs, rows, [cols_a, cols_b], square, mass, sums, wide_count
    )
    col_sums = spread(shares)
    mean = means(pairs, row_slices, kernel, mass, total, [cols_a, cols_b], kept)
    weights = block_weights(row_sums, col_sums)
    return weights, mean.reshape(BLK_DEV * BR, feat)


def solution(mesh):
    in_specs = (P(("groups", "wide"), "narrow"), P(("groups", "wide"), None))
    out_specs = (P(("groups", "wide")), P(("groups", "wide"), "narrow"))
    return jax.shard_map(
        on_device, mesh=mesh, in_specs=in_specs, out_specs=out_specs, check_vma=False
    )
```

```python
import functools

import jax
import jax.numpy as jnp
from jax import lax
from jax.experimental import pallas as pl
from jax.experimental.pallas import tpu as pltpu
from jax.sharding import PartitionSpec as P

F = 1024
BR = 512
BLK_DEV = 8
LANES = 128
CHUNKS = ((0, 320), (320, 192))
WINDOWS = ((0, 256), (256, 512))


def smem():
    return pl.BlockSpec(memory_space=pltpu.SMEM)


def vmem():
    return pl.BlockSpec(memory_space=pltpu.VMEM)


def anywhere():
    return pl.BlockSpec(memory_space=pl.ANY)


def in_vmem(x):
    return pltpu.with_memory_space_constraint(x, pltpu.VMEM)


def in_hbm(x):
    return pltpu.with_memory_space_constraint(x, pltpu.HBM)


def params(mebibytes):
    return pltpu.CompilerParams(vmem_limit_bytes=mebibytes * 1024 * 1024)


def pair_at(lane_ref, pair_count, place):
    half = pair_count // 2
    pair = place + (lane_ref[0] & 1) * half
    return jnp.where(pair >= pair_count, pair - pair_count, pair)


def pack_kernel(wide_count, pair_count, capacity, me_ref, lane_ref, pairs_ref, *refs):
    lists, blocks_ref = refs[: wide_count - 1], refs[wide_count - 1]
    *outs, rows_ref, sems = refs[wide_count:]
    me = me_ref[0]
    copies = []

    def send(source, target):
        copies.append(pltpu.make_async_copy(source, target, sems.at[len(copies)]))
        copies[-1].start()

    for chunk, (start, size) in enumerate(CHUNKS):
        for shift in range(1, wide_count):
            asked = lists[shift - 1]
            picks = [jnp.int32(0)] * capacity
            count = jnp.int32(0)
            for pair in range(pair_count):
                col = asked[1, pair]
                mine = (col >> 3) == me
                for slot in range(capacity):
                    picks[slot] = jnp.where(mine & (count == slot), col & 7, picks[slot])
                count = count + mine.astype(jnp.int32)
            out = outs[chunk * (wide_count - 1) + shift - 1]
            for slot in range(capacity):
                send(blocks_ref.at[picks[slot], pl.ds(start, size)], out.at[slot])
    for place in range(pair_count):
        pair = pair_at(lane_ref, pair_count, place)
        send(blocks_ref.at[pairs_ref[0, pair] & 7], rows_ref.at[place])
    for copy in copies:
        copy.wait()


def pack(me, lane, pairs, lists, blocks, capacity):
    wide_count, pair_count = len(lists) + 1, pairs.shape[1]
    feat = blocks.shape[-1]
    shapes = [
        pltpu.VMEM((capacity, size, feat), blocks.dtype)
        for _, size in CHUNKS
        for _ in range(1, wide_count)
    ] + [pltpu.VMEM((pair_count, BR, feat), blocks.dtype)]
    copies = (len(shapes) - 1) * capacity + pair_count
    outs = pl.pallas_call(
        functools.partial(pack_kernel, wide_count, pair_count, capacity),
        out_shape=shapes,
        in_specs=[smem()] * (2 + wide_count) + [anywhere()],
        out_specs=[anywhere()] * len(shapes),
        scratch_shapes=[pltpu.SemaphoreType.DMA((copies,))],
        compiler_params=params(4),
        name="pack",
    )(me, lane, in_hbm(pairs), *lists, in_hbm(blocks))
    each = wide_count - 1
    return [outs[c * each : (c + 1) * each] for c in range(len(CHUNKS))], outs[-1]


def select_kernel(wide_count, start, me_ref, lane_ref, pairs_ref, own_ref, *refs):
    received, outs = refs[: wide_count - 1], refs[wide_count - 1 :]
    pair_count = own_ref.shape[0]
    each, size, _ = outs[0].shape
    owners = [pairs_ref[1, pair] >> 3 for pair in range(pair_count)]
    for place in range(pair_count):
        pair = pair_at(lane_ref, pair_count, place)
        owner = pairs_ref[1, pair] >> 3
        shift = me_ref[0] - owner
        shift = jnp.where(shift < 0, shift + wide_count, shift)
        rank = jnp.int32(0)
        for before in range(pair_count):
            rank = rank + ((before < pair) & (owners[before] == owner)).astype(jnp.int32)
        out = outs[place // each].at[place % each]

        @pl.when(shift == 0)
        def _():
            out[...] = own_ref[place, start : start + size]

        for other in range(1, wide_count):

            @pl.when(shift == other)
            def _():
                out[...] = received[other - 1][rank]


def select(me, lane, pairs, own, received, start, size):
    pair_count, _, feat = own.shape
    return pl.pallas_call(
        functools.partial(select_kernel, len(received) + 1, start),
        out_shape=[pltpu.VMEM((pair_count // 2, size, feat), own.dtype)] * 2,
        in_specs=[smem(), smem(), smem()] + [vmem()] * (1 + len(received)),
        out_specs=[vmem()] * 2,
        compiler_params=params(4),
        name="select",
    )(me, lane, in_hbm(pairs), *[in_vmem(x) for x in (own, *received)])


def tree(parts):
    while len(parts) > 1:
        half = len(parts) // 2
        parts = [parts[i] + parts[i + half] for i in range(half)]
    return parts[0]


def across(left, right):
    return lax.dot_general(
        left, right, (((1,), (1,)), ((), ())), preferred_element_type=jnp.float32
    )


def lane_sum(block):
    square = jnp.square(block.astype(jnp.float32))
    return sum(square[:, at : at + LANES] for at in range(0, square.shape[1], LANES))


def segments(window):
    low, high = window
    held = []
    for chunk, (start, size) in enumerate(CHUNKS):
        first, end = max(low, start), min(high, start + size)
        if first < end:
            held.append((chunk, first - start, end - first))
    return held


def scores(rows, cols, square):
    gram = tree([across(row, col) for row, col in zip(rows, cols)])
    other = jnp.sum(tree([lane_sum(col) for col in cols]).T, axis=0, keepdims=True)
    pieces, mass = [], None
    for at in range(0, gram.shape[1], LANES):
        here = slice(at, at + LANES)
        piece = jnp.exp((square + other[:, here] - 2.0 * gram[:, here]) * (-1.0 / F))
        mass = piece if mass is None else mass + piece
        pieces.append(piece)
    kernel = jnp.concatenate(pieces, axis=1) if len(pieces) > 1 else pieces[0]
    return kernel.astype(jnp.bfloat16), jnp.sum(kernel, axis=0, keepdims=True), mass


def of_place(part, place):
    each = part[0].shape[0]
    return part[place // each].at[place % each]


def columns(window, refs):
    held = segments(window)
    pieces = [ref[at : at + size] for ref, (_, at, size) in zip(refs, held)]
    return jnp.concatenate(pieces, axis=0) if len(pieces) > 1 else pieces[0]


def window_parts(window, first_count, refs):
    rows, last, refs = refs[:first_count], refs[first_count], refs[first_count + 1 :]
    count = len(segments(window))
    chunks = [refs[i * 2 * first_count :][: 2 * first_count] for i in range(count)]
    half = last.shape[0] // first_count

    def of_pair(pair):
        own = [ref[pair] for ref in rows] + [last[i * half + pair] for i in range(first_count)]
        cols = [
            columns(window, [chunk[i].at[pair] for chunk in chunks]) for i in range(2 * first_count)
        ]
        return own, cols

    return half, of_pair


def first_kernel(window, first_count, *refs):
    square_ref, mass_ref, kernel_ref, sums_ref = refs[-4:]
    half, of_pair = window_parts(window, first_count, refs)
    for pair in range(half):
        rows, cols = of_pair(pair)
        square = jnp.sum(tree([lane_sum(row) for row in rows]), axis=1, keepdims=True)
        square = jnp.broadcast_to(square, (BR, LANES))
        kernel, sums, mass = scores(rows, cols, square)
        square_ref[pair] = square
        mass_ref[pair] = mass
        sums_ref[pair : pair + 1] = sums
        kernel_ref[pair] = kernel


def last_kernel(window, first_count, wide_count, me_ref, lane_ref, pairs_ref, *refs):
    square_in, mass_in, sums_in = refs[-6 - wide_count : -3 - wide_count]
    kernel_ref, line_ref, row_ref = refs[-3 - wide_count : -wide_count]
    shares = refs[-wide_count:]
    for ref in (row_ref, *shares):
        ref[...] = jnp.zeros_like(ref)
    half, of_pair = window_parts(window, first_count, refs)
    for place in range(half):
        rows, cols = of_pair(place)
        kernel, sums, mass = scores(rows, cols, square_in[place])
        kernel_ref[place] = kernel
        sums = jnp.concatenate([sums_in[place : place + 1], sums], axis=1)
        line = jnp.sum((mass_in[place] + mass).T, axis=0, keepdims=True)
        line_ref[place : place + 1] = line
        pair = pair_at(lane_ref, 2 * half, place)
        row_ref[pl.ds(pairs_ref[0, pair] & 7, 1)] += line
        col = pairs_ref[1, pair]
        shift = (col >> 3) - me_ref[0]
        shift = jnp.where(shift < 0, shift + wide_count, shift)
        for other, ref in enumerate(shares):
            ref[pl.ds(col & 7, 1)] += jnp.where(shift == other, sums, 0.0)


def estimate(pair_count, size):
    return pl.CostEstimate(
        flops=2 * pair_count * BR * size * F,
        transcendentals=pair_count * BR * size,
        bytes_accessed=8 * 1024 * 1024,
    )


def nothing():
    return pl.CostEstimate(flops=0, transcendentals=0, bytes_accessed=0)


def window_operands(rows, cols, window):
    first, last = rows
    args = [*first, last]
    for chunk, _, _ in segments(window):
        args += cols[chunk]
    return args


def first_window(rows, cols):
    window = WINDOWS[0]
    first_count = len(rows[0])
    half = rows[0][0].shape[0] // 2
    lanes = pltpu.VMEM((half, BR, LANES), jnp.float32)
    args = window_operands(rows, cols, window)
    return pl.pallas_call(
        functools.partial(first_kernel, window, first_count),
        out_shape=[
            lanes,
            lanes,
            pltpu.VMEM((half, BR, window[1]), jnp.bfloat16),
            pltpu.VMEM((half, window[1]), jnp.float32),
        ],
        in_specs=[vmem()] * len(args),
        out_specs=[vmem()] * 4,
        compiler_params=params(16),
        cost_estimate=nothing(),
        name="first_window",
    )(*[in_vmem(x) for x in args])


def last_window(me, lane, pairs, rows, cols, square, mass, sums, wide_count):
    window = WINDOWS[1]
    first_count = len(rows[0])
    half = rows[0][0].shape[0] // 2
    size = window[1] - window[0]
    by_block = pltpu.VMEM((BLK_DEV, BR), jnp.float32)
    shapes = [
        pltpu.VMEM((half, BR, size), jnp.bfloat16),
        pltpu.VMEM((half, BR), jnp.float32),
    ] + [by_block] * (1 + wide_count)
    args = window_operands(rows, cols, window) + [square, mass, sums]
    kernel, line, row_sums, *shares = pl.pallas_call(
        functools.partial(last_kernel, window, first_count, wide_count),
        out_shape=shapes,
        in_specs=[smem(), smem(), smem()] + [vmem()] * len(args),
        out_specs=[vmem()] * len(shapes),
        compiler_params=params(16),
        cost_estimate=estimate(half, size),
        name="last_window",
    )(me, lane, in_hbm(pairs), *[in_vmem(x) for x in args])
    return kernel, line, row_sums, shares


def keep_kernel(lane_ref, pairs_ref, block_ref, blocks_ref, out_ref, own_ref, sems):
    here = pl.program_id(0)

    def copies():
        for place in range(own_ref.shape[0]):
            pair = pair_at(lane_ref, own_ref.shape[0], place)
            source = blocks_ref.at[pairs_ref[1, pair] & 7]
            yield pltpu.make_async_copy(source, own_ref.at[place], sems.at[place])

    @pl.when(here == 0)
    def _():
        for copy in copies():
            copy.start()

    out_ref[...] = block_ref[...]

    @pl.when(here == pl.num_programs(0) - 1)
    def _():
        for copy in copies():
            copy.wait()


def keep(lane, pairs, blocks):
    pair_count = pairs.shape[1]
    block = pl.BlockSpec((1, *blocks.shape[1:]), lambda k: (k, 0, 0))
    return pl.pallas_call(
        keep_kernel,
        out_shape=[
            pltpu.HBM(blocks.shape, blocks.dtype),
            pltpu.VMEM((pair_count, *blocks.shape[1:]), blocks.dtype),
        ],
        grid=(blocks.shape[0],),
        in_specs=[smem(), smem(), block, anywhere()],
        out_specs=[block, anywhere()],
        scratch_shapes=[pltpu.SemaphoreType.DMA((pair_count,))],
        compiler_params=params(4),
        name="keep",
    )(lane, in_hbm(pairs), in_hbm(blocks), in_hbm(blocks))


def mean_kernel(lane_ref, pairs_ref, rows_ref, *refs):
    kernels = [refs[2 * i : 2 * i + 2] for i in range(len(WINDOWS))]
    lines, refs = refs[2 * len(WINDOWS) :][:2], refs[2 * len(WINDOWS) + 2 :]
    *chunks, _, out_ref, part, weight, total, mass, made, sems = refs
    pair_count, _, feat = rows_ref.shape
    local = [pairs_ref[0, pair_at(lane_ref, pair_count, p)] & 7 for p in range(pair_count)]

    def copy(place):
        return pltpu.make_async_copy(made.at[place], out_ref.at[local[place]], sems.at[place])

    firsts = []
    for place in range(pair_count):
        kernel = jnp.concatenate([of_place(window, place)[...] for window in kernels], axis=1)
        own = [of_place(chunks[2 * i : 2 * i + 2], place)[...] for i in range(len(CHUNKS))]
        sums = jnp.dot(kernel, jnp.concatenate(own, axis=0), preferred_element_type=jnp.float32)
        part[place] = sums.astype(jnp.bfloat16)
        half = pair_count // 2
        line = lines[place // half][place % half : place % half + 1]
        weight[place] = jnp.broadcast_to(line, (LANES, BR)).T
        same = [local[other] == local[place] for other in range(place)]
        firsts.append(jnp.logical_not(functools.reduce(jnp.logical_or, same, jnp.bool_(False))))
    for place in range(pair_count):

        @pl.when(firsts[place])
        def _():
            total[...] = rows_ref[place].astype(jnp.float32) + part[place].astype(jnp.float32)
            mass[...] = 1.0 + weight[place]
            for other in range(place + 1, pair_count):

                @pl.when(local[other] == local[place])
                def _():
                    total[...] += part[other].astype(jnp.float32)
                    mass[...] += weight[other]

            scale = 1.0 / mass[...]
            for at in range(0, feat, LANES):
                lanes = slice(at, at + LANES)
                made[place, :, lanes] = (total[:, lanes] * scale).astype(jnp.bfloat16)
            copy(place).start()

    for place in range(pair_count):

        @pl.when(firsts[place])
        def _():
            copy(place).wait()


def means(lane, pairs, rows, kernels, lines, own, kept):
    pair_count, _, feat = rows.shape
    args = [in_vmem(x) for x in (rows, *kernels, *lines, *own)]
    return pl.pallas_call(
        mean_kernel,
        out_shape=pltpu.HBM(kept.shape, jnp.bfloat16),
        in_specs=[smem(), smem()] + [vmem()] * len(args) + [anywhere()],
        out_specs=anywhere(),
        scratch_shapes=[
            pltpu.VMEM((pair_count, BR, feat), jnp.bfloat16),
            pltpu.VMEM((pair_count, BR, LANES), jnp.float32),
            pltpu.VMEM((BR, feat), jnp.float32),
            pltpu.VMEM((BR, LANES), jnp.float32),
            pltpu.VMEM((pair_count, BR, feat), jnp.bfloat16),
            pltpu.SemaphoreType.DMA((pair_count,)),
        ],
        input_output_aliases={2 + len(args): 0},
        compiler_params=params(16),
        cost_estimate=estimate(pair_count, 128),
        name="means",
    )(lane, in_hbm(pairs), *args, in_hbm(kept))


def mass_kernel(*refs):
    mass = refs[0][...]
    for ref in refs[1:-1]:
        mass = mass + ref[...]
    refs[-1][...] = mass


def masses(sums):
    return pl.pallas_call(
        mass_kernel,
        out_shape=pltpu.VMEM((BLK_DEV, BR), jnp.float32),
        in_specs=[vmem()] * len(sums),
        out_specs=vmem(),
        compiler_params=params(4),
        name="masses",
    )(*[in_vmem(x) for x in sums])


def weight_kernel(*refs):
    out_ref = refs[-1]
    mass = refs[0][...]
    for ref in refs[1:-1]:
        mass = mass + ref[...]
    weight = 1.0 / (1.0 + mass / BR)
    parts = BR // LANES
    for block in range(BLK_DEV):
        for part in range(parts):
            lanes = slice(part * LANES, (part + 1) * LANES)
            out_ref[block * parts + part : block * parts + part + 1] = weight[block : block + 1, lanes]


def block_weights(sums):
    out = pl.pallas_call(
        weight_kernel,
        out_shape=jax.ShapeDtypeStruct((BLK_DEV * BR // LANES, LANES), jnp.float32),
        in_specs=[vmem()] * len(sums),
        out_specs=vmem(),
        compiler_params=params(4),
        name="weights",
    )(*[in_vmem(x) for x in sums])
    return out.reshape(BLK_DEV * BR)


def hop(parts, step):
    count = lax.axis_size("narrow")
    perm = [(i, i ^ step) for i in range(count)]
    return [lax.ppermute(part, "narrow", perm) for part in parts]


def first_hops(part):
    parts = [part]
    step = lax.axis_size("narrow") // 2
    while step > 1:
        parts = parts + hop(parts, step)
        step //= 2
    return parts


def to_wide(pieces):
    count = lax.axis_size("wide")
    return [
        lax.ppermute(piece, "wide", [(i, (i + shift) % count) for i in range(count)])
        for shift, piece in enumerate(pieces, 1)
    ]


def on_device(embeddings, pair_list):
    wide_count = lax.axis_size("wide")
    me = lax.axis_index("wide").astype(jnp.int32).reshape(1)
    lane = lax.axis_index("narrow").astype(jnp.int32).reshape(1)
    pairs = pair_list.T
    pair_count = pairs.shape[1]
    half = pair_count // 2
    capacity = max(2, 2 * pair_count // wide_count)
    feat = embeddings.shape[1]
    blocks = embeddings.reshape(BLK_DEV, BR, feat)
    lists = to_wide([pairs] * (wide_count - 1))[::-1]
    fixed = lax.optimization_barrier
    outgoing, row_slices = pack(me, lane, pairs, lists, blocks, capacity)

    def pick(received, chunk):
        return select(me, lane, pairs, own, received, *CHUNKS[chunk])

    rows = first_hops(row_slices)
    theirs = jnp.concatenate([part[half:] for part in rows], axis=0)
    rows, theirs, received, (kept, own) = fixed(
        (rows, theirs, to_wide(outgoing[0]), keep(lane, pairs, blocks))
    )
    mine_a, theirs_a = pick(received, 0)
    hops_a, hops_theirs_a = first_hops(mine_a), first_hops(theirs_a)
    rows_last = hop([theirs], 1)
    hops_a, hops_theirs_a, rows_last, received = fixed(
        (hops_a, hops_theirs_a, rows_last, to_wide(outgoing[1]))
    )
    rows = (rows, rows_last[0])
    mine_b, theirs_b = pick(received, 1)
    hops_b, hops_theirs_b = first_hops(mine_b), first_hops(theirs_b)
    cols_a = hops_a + hop(hops_theirs_a, 1)
    carry = first_window(rows, [cols_a])
    hops_b, hops_theirs_b, carry = fixed((hops_b, hops_theirs_b, carry))
    square, mass, kernel_a, sums = carry
    last_b, kernel_a = fixed((hop(hops_theirs_b, 1), kernel_a))
    kernels = [kernel_a, *hop([kernel_a], 1)]
    kernel_b, line, row_sums, shares = last_window(
        me, lane, pairs, rows, [cols_a, hops_b + last_b], square, mass, sums, wide_count
    )
    kernels += [kernel_b, *hop([kernel_b], 1)]
    came = to_wide(shares[1:])
    mean = means(
        lane, pairs, row_slices, kernels, [line, *hop([line], 1)], [mine_a, theirs_a, mine_b, theirs_b], kept
    )
    mean, came = fixed((mean, came))
    sums = masses([row_sums, shares[0], *came])
    weights = block_weights([sums, *hop([sums], 1)])
    return weights, mean.reshape(BLK_DEV * BR, feat)


def solution(mesh):
    in_specs = (P(("groups", "wide"), "narrow"), P(("groups", "wide"), None))
    out_specs = (P(("groups", "wide")), P(("groups", "wide"), "narrow"))
    return jax.shard_map(
        on_device, mesh=mesh, in_specs=in_specs, out_specs=out_specs, check_vma=False
    )
```

```python
import functools

import jax
import jax.numpy as jnp
from jax import lax
from jax.experimental import pallas as pl
from jax.experimental.pallas import tpu as pltpu
from jax.sharding import PartitionSpec as P

F = 1024
BR = 512
BLK_DEV = 8
LANES = 128
CHUNKS = ((0, 320), (320, 192))
WINDOWS = ((0, 256), (256, 512))


def smem():
    return pl.BlockSpec(memory_space=pltpu.SMEM)


def vmem():
    return pl.BlockSpec(memory_space=pltpu.VMEM)


def anywhere():
    return pl.BlockSpec(memory_space=pl.ANY)


def in_vmem(x):
    return pltpu.with_memory_space_constraint(x, pltpu.VMEM)


def in_hbm(x):
    return pltpu.with_memory_space_constraint(x, pltpu.HBM)


def params(mebibytes):
    return pltpu.CompilerParams(vmem_limit_bytes=mebibytes * 1024 * 1024)


def others(wide_count):
    return range(wide_count - 1, 0, -1)


def pack_kernel(wide_count, pair_count, capacity, me_ref, pairs_ref, *refs):
    lists, blocks_ref = refs[: wide_count - 1], refs[wide_count - 1]
    *outs, rows_ref, sems = refs[wide_count:]
    me = me_ref[0]
    copies = []

    def send(source, target):
        copies.append(pltpu.make_async_copy(source, target, sems.at[len(copies)]))
        copies[-1].start()

    for chunk, (start, size) in enumerate(CHUNKS):
        for number, other in enumerate(others(wide_count)):
            asked = lists[other - 1]
            picks = [jnp.int32(0)] * capacity
            count = jnp.int32(0)
            for pair in range(pair_count):
                col = asked[1, pair]
                mine = (col >> 3) == me
                for slot in range(capacity):
                    picks[slot] = jnp.where(mine & (count == slot), col & 7, picks[slot])
                count = count + mine.astype(jnp.int32)
            out = outs[chunk * (wide_count - 1) + number]
            for slot in range(capacity):
                send(blocks_ref.at[picks[slot], pl.ds(start, size)], out.at[slot])
    for pair in range(pair_count):
        send(blocks_ref.at[pairs_ref[0, pair] & 7], rows_ref.at[pair])
    for copy in copies:
        copy.wait()


def pack(me, pairs, lists, blocks, capacity):
    wide_count, pair_count = len(lists) + 1, pairs.shape[1]
    feat = blocks.shape[-1]
    shapes = [
        pltpu.VMEM((capacity, size, feat), blocks.dtype)
        for _, size in CHUNKS
        for _ in range(1, wide_count)
    ] + [pltpu.VMEM((pair_count, BR, feat), blocks.dtype)]
    copies = (len(shapes) - 1) * capacity + pair_count
    outs = pl.pallas_call(
        functools.partial(pack_kernel, wide_count, pair_count, capacity),
        out_shape=shapes,
        in_specs=[smem()] * (1 + wide_count) + [anywhere()],
        out_specs=[anywhere()] * len(shapes),
        scratch_shapes=[pltpu.SemaphoreType.DMA((copies,))],
        compiler_params=params(4),
        name="pack",
    )(me, in_hbm(pairs), *lists, in_hbm(blocks))
    each = wide_count - 1
    return [outs[c * each : (c + 1) * each] for c in range(len(CHUNKS))], outs[-1]


def select_kernel(wide_count, groups, start, me_ref, pairs_ref, own_ref, *refs):
    pair_count = own_ref.shape[0]
    outs = refs[wide_count - 1 :]
    received = refs[: wide_count - 1]
    size = outs[0].shape[1]
    owners = [pairs_ref[1, pair] >> 3 for pair in range(pair_count)]
    for pair in range(pair_count):
        apart = me_ref[0] ^ owners[pair]
        rank = jnp.int32(0)
        for before in range(pair):
            rank = rank + (owners[before] == owners[pair]).astype(jnp.int32)

        places, rest = [], outs
        for pieces in groups:
            places.append(of_pair(rest[:pieces], pair))
            rest = rest[pieces:]

        @pl.when(apart == 0)
        def _():
            for out in places:
                out[...] = own_ref[pair, start : start + size]

        for number, other in enumerate(others(wide_count)):

            @pl.when(apart == other)
            def _():
                for out in places:
                    out[...] = received[number][rank]


def select(me, pairs, own, received, start, size, groups):
    pair_count, _, feat = own.shape
    shapes = [
        pltpu.VMEM((pair_count // pieces, size, feat), own.dtype)
        for pieces in groups
        for _ in range(pieces)
    ]
    outs = pl.pallas_call(
        functools.partial(select_kernel, len(received) + 1, groups, start),
        out_shape=shapes,
        in_specs=[smem(), smem()] + [vmem()] * (1 + len(received)),
        out_specs=[vmem()] * len(shapes),
        compiler_params=params(4),
        name="select",
    )(me, in_hbm(pairs), *[in_vmem(x) for x in (own, *received)])
    return take_parts(outs, groups)[0]


def tree(parts):
    while len(parts) > 1:
        half = len(parts) // 2
        parts = [parts[i] + parts[i + half] for i in range(half)]
    return parts[0]


def across(left, right):
    return lax.dot_general(
        left, right, (((1,), (1,)), ((), ())), preferred_element_type=jnp.float32
    )


def lane_sum(block):
    square = jnp.square(block.astype(jnp.float32))
    return sum(square[:, at : at + LANES] for at in range(0, square.shape[1], LANES))


def segments(window):
    low, high = window
    held = []
    for chunk, (start, size) in enumerate(CHUNKS):
        first, end = max(low, start), min(high, start + size)
        if first < end:
            held.append((chunk, first - start, end - first))
    return held


def scores(rows, cols, square):
    gram = tree([across(row, col) for row, col in zip(rows, cols)])
    other = jnp.sum(tree([lane_sum(col) for col in cols]).T, axis=0, keepdims=True)
    pieces, mass = [], None
    for at in range(0, gram.shape[1], LANES):
        here = slice(at, at + LANES)
        piece = jnp.exp((square + other[:, here] - 2.0 * gram[:, here]) * (-1.0 / F))
        mass = piece if mass is None else mass + piece
        pieces.append(piece)
    kernel = jnp.concatenate(pieces, axis=1) if len(pieces) > 1 else pieces[0]
    return kernel.astype(jnp.bfloat16), jnp.sum(kernel, axis=0, keepdims=True), mass


def take_parts(refs, counts):
    parts = []
    for count in counts:
        parts.append(refs[:count])
        refs = refs[count:]
    return parts, refs


def of_pair(part, pair):
    each = part[0].shape[0]
    return part[pair // each].at[pair % each]


def window_parts(counts, refs):
    half = len(counts[0]) // 2
    rows, refs = [ref.at[i] for ref in refs[:2] for i in range(half)], refs[2:]
    chunks = []
    for chunk_counts in counts:
        cols, refs = take_parts(refs, chunk_counts)
        chunks.append(cols)
    return rows, chunks


def own_columns(window, chunks, pair):
    held = segments(window)
    pieces = [of_pair(part, pair)[at : at + size] for part, (_, at, size) in zip(chunks, held)]
    return jnp.concatenate(pieces, axis=0) if len(pieces) > 1 else pieces[0]


def pair_parts(window, rows, chunks, pair):
    cols = [own_columns(window, [c[i] for c in chunks], pair) for i in range(len(rows))]
    return [part[pair] for part in rows], cols


def first_kernel(window, counts, *refs):
    square_ref, mass_ref, total_ref, sums_ref = refs[-4:]
    all_rows, chunks = window_parts(counts, refs)
    for pair in range(square_ref.shape[0]):
        rows, cols = pair_parts(window, all_rows, chunks, pair)
        square = jnp.sum(tree([lane_sum(row) for row in rows]), axis=1, keepdims=True)
        square = jnp.broadcast_to(square, (BR, LANES))
        kernel, sums, mass = scores(rows, cols, square)
        square_ref[pair] = square
        mass_ref[pair] = mass
        sums_ref[pair : pair + 1] = sums
        total_ref[pair] = jnp.dot(kernel, cols[0], preferred_element_type=jnp.float32)


def last_kernel(window, counts, wide_count, me_ref, pairs_ref, *refs):
    square_in, mass_in, sums_in = refs[-6 - wide_count : -3 - wide_count]
    kernel_ref, mass_ref, row_ref = refs[-3 - wide_count : -wide_count]
    shares = refs[-wide_count:]
    for ref in (row_ref, *shares):
        ref[...] = jnp.zeros_like(ref)
    all_rows, chunks = window_parts(counts, refs)
    for pair in range(square_in.shape[0]):
        rows, cols = pair_parts(window, all_rows, chunks, pair)
        kernel, sums, mass = scores(rows, cols, square_in[pair])
        kernel_ref[pair] = kernel
        sums = jnp.concatenate([sums_in[pair : pair + 1], sums], axis=1)
        mass = mass_in[pair] + mass
        mass_ref[pair] = mass
        row_ref[pl.ds(pairs_ref[0, pair] & 7, 1)] += jnp.sum(mass.T, axis=0, keepdims=True)
        col = pairs_ref[1, pair]
        apart = (col >> 3) ^ me_ref[0]
        for other, ref in zip([*others(wide_count), 0], shares):
            ref[pl.ds(col & 7, 1)] += jnp.where(apart == other, sums, 0.0)


def estimate(pair_count, size):
    return pl.CostEstimate(
        flops=2 * pair_count * BR * size * F,
        transcendentals=pair_count * BR * size,
        bytes_accessed=8 * 1024 * 1024,
    )


def piece_counts(window, cols):
    return tuple(tuple(len(part) for part in cols[chunk]) for chunk, _, _ in segments(window))


def operands(parts):
    return [piece for part in parts for piece in part]


def first_window(rows, cols):
    _, pair_count, _, feat = rows[0][0].shape
    window = WINDOWS[0]
    lanes = pltpu.VMEM((pair_count, BR, LANES), jnp.float32)
    total = pltpu.VMEM((pair_count, BR, feat), jnp.float32)
    args = operands(rows)
    for chunk, _, _ in segments(window):
        args += operands(cols[chunk])
    return pl.pallas_call(
        functools.partial(first_kernel, window, piece_counts(window, cols)),
        out_shape=[lanes, lanes, total, pltpu.VMEM((pair_count, window[1]), jnp.float32)],
        in_specs=[vmem()] * len(args),
        out_specs=[vmem()] * 4,
        compiler_params=params(16),
        cost_estimate=pl.CostEstimate(flops=0, transcendentals=0, bytes_accessed=0),
        name="first_window",
    )(*[in_vmem(x) for x in args])


def last_window(me, pairs, rows, cols, square, mass, sums, wide_count):
    pair_count = rows[0][0].shape[1]
    window = WINDOWS[1]
    size = window[1] - window[0]
    by_block = pltpu.VMEM((BLK_DEV, BR), jnp.float32)
    shapes = [
        pltpu.VMEM((pair_count, BR, size), jnp.bfloat16),
        pltpu.VMEM((pair_count, BR, LANES), jnp.float32),
    ] + [by_block] * (1 + wide_count)
    args = operands(rows)
    for chunk, _, _ in segments(window):
        args += operands(cols[chunk])
    args += [square, mass, sums]
    kernel, mass, row_sums, *shares = pl.pallas_call(
        functools.partial(last_kernel, window, piece_counts(window, cols), wide_count),
        out_shape=shapes,
        in_specs=[smem(), smem()] + [vmem()] * len(args),
        out_specs=[vmem()] * len(shapes),
        compiler_params=params(16),
        cost_estimate=estimate(pair_count, size),
        name="last_window",
    )(me, in_hbm(pairs), *[in_vmem(x) for x in args])
    return kernel, mass, row_sums, shares


def keep_kernel(pairs_ref, block_ref, blocks_ref, out_ref, own_ref, sems):
    here = pl.program_id(0)

    def copies():
        for pair in range(own_ref.shape[0]):
            source = blocks_ref.at[pairs_ref[1, pair] & 7]
            yield pltpu.make_async_copy(source, own_ref.at[pair], sems.at[pair])

    @pl.when(here == 0)
    def _():
        for copy in copies():
            copy.start()

    out_ref[...] = block_ref[...]

    @pl.when(here == pl.num_programs(0) - 1)
    def _():
        for copy in copies():
            copy.wait()


def keep(pairs, blocks):
    pair_count = pairs.shape[1]
    block = pl.BlockSpec((1, *blocks.shape[1:]), lambda k: (k, 0, 0))
    return pl.pallas_call(
        keep_kernel,
        out_shape=[
            pltpu.HBM(blocks.shape, blocks.dtype),
            pltpu.VMEM((pair_count, *blocks.shape[1:]), blocks.dtype),
        ],
        grid=(blocks.shape[0],),
        in_specs=[smem(), block, anywhere()],
        out_specs=[block, anywhere()],
        scratch_shapes=[pltpu.SemaphoreType.DMA((pair_count,))],
        compiler_params=params(4),
        name="keep",
    )(in_hbm(pairs), in_hbm(blocks), in_hbm(blocks))


def mean_kernel(window, counts, local_ref, rows_ref, kernel_ref, mass_ref, total_ref, *refs):
    *refs, _, out_ref, part, weight, total, mass, made, sems = refs
    chunks = []
    for chunk, _, _ in segments(window):
        (own,), refs = take_parts(refs, counts[len(chunks)][:1])
        chunks.append(own)
    pair_count, _, feat = rows_ref.shape
    local = [local_ref[0, pair] & 7 for pair in range(pair_count)]

    def copy(pair):
        return pltpu.make_async_copy(made.at[pair], out_ref.at[local[pair]], sems.at[pair])

    firsts = []
    for pair in range(pair_count):
        sums = total_ref[pair] + jnp.dot(
            kernel_ref[pair], own_columns(window, chunks, pair), preferred_element_type=jnp.float32
        )
        part[pair] = sums.astype(jnp.bfloat16)
        weight[pair] = jnp.broadcast_to(
            jnp.sum(mass_ref[pair], axis=1, keepdims=True), (BR, LANES)
        )
        same = [local[other] == local[pair] for other in range(pair)]
        firsts.append(jnp.logical_not(functools.reduce(jnp.logical_or, same, jnp.bool_(False))))
    for pair in range(pair_count):

        @pl.when(firsts[pair])
        def _():
            total[...] = rows_ref[pair].astype(jnp.float32) + part[pair].astype(jnp.float32)
            mass[...] = 1.0 + weight[pair]
            for other in range(pair + 1, pair_count):

                @pl.when(local[other] == local[pair])
                def _():
                    total[...] += part[other].astype(jnp.float32)
                    mass[...] += weight[other]

            scale = 1.0 / mass[...]
            for at in range(0, feat, LANES):
                lanes = slice(at, at + LANES)
                made[pair, :, lanes] = (total[:, lanes] * scale).astype(jnp.bfloat16)
            copy(pair).start()

    for pair in range(pair_count):

        @pl.when(firsts[pair])
        def _():
            copy(pair).wait()


def means(pairs, rows, kernel, mass, total, cols, kept):
    pair_count, _, feat = rows.shape
    window = WINDOWS[1]
    own = operands(cols[chunk][0] for chunk, _, _ in segments(window))
    args = [in_vmem(x) for x in (rows, kernel, mass, total, *own)]
    return pl.pallas_call(
        functools.partial(mean_kernel, window, piece_counts(window, cols)),
        out_shape=pltpu.HBM(kept.shape, jnp.bfloat16),
        in_specs=[smem()] + [vmem()] * len(args) + [anywhere()],
        out_specs=anywhere(),
        scratch_shapes=[
            pltpu.VMEM((pair_count, BR, feat), jnp.bfloat16),
            pltpu.VMEM((pair_count, BR, LANES), jnp.float32),
            pltpu.VMEM((BR, feat), jnp.float32),
            pltpu.VMEM((BR, LANES), jnp.float32),
            pltpu.VMEM((pair_count, BR, feat), jnp.bfloat16),
            pltpu.SemaphoreType.DMA((pair_count,)),
        ],
        input_output_aliases={1 + len(args): 0},
        compiler_params=params(16),
        cost_estimate=estimate(pair_count, 128),
        name="means",
    )(in_hbm(pairs), *args, in_hbm(kept))


def weight_kernel(*refs):
    out_ref = refs[-1]
    mass = refs[0][...]
    for ref in refs[1:-1]:
        mass = mass + ref[...]
    weight = 1.0 / (1.0 + mass / BR)
    parts = BR // LANES
    for block in range(BLK_DEV):
        for part in range(parts):
            lanes = slice(part * LANES, (part + 1) * LANES)
            out_ref[block * parts + part : block * parts + part + 1] = weight[block : block + 1, lanes]


def block_weights(sums):
    out = pl.pallas_call(
        weight_kernel,
        out_shape=jax.ShapeDtypeStruct((BLK_DEV * BR // LANES, LANES), jnp.float32),
        in_specs=[vmem()] * len(sums),
        out_specs=vmem(),
        compiler_params=params(4),
        name="weights",
    )(*[in_vmem(x) for x in sums])
    return out.reshape(BLK_DEV * BR)


def hop(parts, step):
    count = lax.axis_size("narrow")
    perm = [(i, i ^ step) for i in range(count)]
    return [[lax.ppermute(piece, "narrow", perm) for piece in part] for part in parts]


def first_hops(part):
    parts = [part]
    step = lax.axis_size("narrow") // 2
    while step > 1:
        parts = parts + hop(parts, step)
        step //= 2
    return parts


def to_wide(pieces, apart):
    count = lax.axis_size("wide")
    return [
        lax.ppermute(piece, "wide", [(i, i ^ other) for i in range(count)])
        for piece, other in zip(pieces, apart)
    ]


def on_device(embeddings, pair_list):
    wide_count = lax.axis_size("wide")
    me = lax.axis_index("wide").astype(jnp.int32).reshape(1)
    pairs = pair_list.T
    pair_count = pairs.shape[1]
    capacity = max(2, 2 * pair_count // wide_count)
    feat = embeddings.shape[1]
    blocks = embeddings.reshape(BLK_DEV, BR, feat)
    apart = others(wide_count)
    lists = to_wide([pairs] * (wide_count - 1), apart[::-1])
    fixed = lax.optimization_barrier
    outgoing, row_slices = pack(me, pairs, lists, blocks, capacity)

    def pick(received, chunk, *groups):
        return select(me, pairs, own, received, *CHUNKS[chunk], groups)

    def halves(part):
        middle = pair_count // 2
        return [part[0][:middle], part[0][middle:]]

    rows = jnp.stack([part[0] for part in first_hops([row_slices])])
    received = to_wide(outgoing[0], apart)
    near = to_wide(outgoing[1][-1:], apart[-1:])
    rows, received, near, (kept, own) = fixed((rows, received, near, keep(pairs, blocks)))
    own_a, whole_a = pick(received, 0, 2, 1)
    cols_a = [own_a] + first_hops(whole_a)[1:]
    rows = [[rows], *hop([[rows]], 1)]
    cols_a, rows, received = fixed((cols_a, rows, to_wide(outgoing[1][:-1], apart[:-1])))
    cols_b = first_hops(*pick([*received, *near], 1, 1))
    last_b = hop(cols_b[:1], 1)
    cols_a = cols_a + hop([own_a] + [halves(part) for part in cols_a[1:]], 1)
    carry = first_window(rows, [cols_a])
    cols_b, carry = fixed((cols_b, carry))
    cols_b = cols_b + last_b + hop(cols_b[1:], 1)
    square, mass, total, sums = carry
    kernel, mass, row_sums, shares = last_window(
        me, pairs, rows, [cols_a, cols_b], square, mass, sums, wide_count
    )
    came = to_wide(shares[:-1], apart)
    mean = means(pairs, row_slices, kernel, mass, total, [cols_a, cols_b], kept)
    weights = block_weights([row_sums, shares[-1], *came])
    return weights, mean.reshape(BLK_DEV * BR, feat)


def solution(mesh):
    in_specs = (P(("groups", "wide"), "narrow"), P(("groups", "wide"), None))
    out_specs = (P(("groups", "wide")), P(("groups", "wide"), "narrow"))
    return jax.shard_map(
        on_device, mesh=mesh, in_specs=in_specs, out_specs=out_specs, check_vma=False
    )
```

```python
import functools

import jax
import jax.numpy as jnp
from jax import lax
from jax.experimental import pallas as pl
from jax.experimental.pallas import tpu as pltpu
from jax.sharding import PartitionSpec as P

F = 1024
BR = 512
BLK_DEV = 8
LANES = 128
CHUNKS = ((0, 336), (336, 176))
WINDOWS = ((0, 256), (256, 512))


def smem():
    return pl.BlockSpec(memory_space=pltpu.SMEM)


def vmem():
    return pl.BlockSpec(memory_space=pltpu.VMEM)


def anywhere():
    return pl.BlockSpec(memory_space=pl.ANY)


def in_vmem(x):
    return pltpu.with_memory_space_constraint(x, pltpu.VMEM)


def in_hbm(x):
    return pltpu.with_memory_space_constraint(x, pltpu.HBM)


def params(mebibytes):
    return pltpu.CompilerParams(vmem_limit_bytes=mebibytes * 1024 * 1024)


def others(wide_count):
    return range(wide_count - 1, 0, -1)


def pack_kernel(wide_count, pair_count, capacity, me_ref, pairs_ref, *refs):
    lists, blocks_ref = refs[: wide_count - 1], refs[wide_count - 1]
    *outs, rows_ref, sems = refs[wide_count:]
    me = me_ref[0]
    copies = []

    def send(source, target):
        copies.append(pltpu.make_async_copy(source, target, sems.at[len(copies)]))
        copies[-1].start()

    for chunk, (start, size) in enumerate(CHUNKS):
        for number, other in enumerate(others(wide_count)):
            asked = lists[list_order(wide_count).index(other)]
            picks = [jnp.int32(0)] * capacity
            count = jnp.int32(0)
            for pair in range(pair_count):
                col = asked[1, pair]
                mine = (col >> 3) == me
                for slot in range(capacity):
                    picks[slot] = jnp.where(mine & (count == slot), col & 7, picks[slot])
                count = count + mine.astype(jnp.int32)
            out = outs[chunk * (wide_count - 1) + number]
            for slot in range(capacity):
                send(blocks_ref.at[picks[slot], pl.ds(start, size)], out.at[slot])
    for pair in range(pair_count):
        send(blocks_ref.at[pairs_ref[0, pair] & 7], rows_ref.at[pair])
    for copy in copies:
        copy.wait()


def list_order(wide_count):
    middle = wide_count // 2
    return [other for other in range(1, wide_count) if other != middle] + [middle]


def pack(me, pairs, lists, blocks, capacity):
    wide_count, pair_count = len(lists) + 1, pairs.shape[1]
    feat = blocks.shape[-1]
    shapes = [
        pltpu.VMEM((capacity, size, feat), blocks.dtype)
        for _, size in CHUNKS
        for _ in range(1, wide_count)
    ] + [pltpu.VMEM((pair_count, BR, feat), blocks.dtype)]
    copies = (len(shapes) - 1) * capacity + pair_count
    outs = pl.pallas_call(
        functools.partial(pack_kernel, wide_count, pair_count, capacity),
        out_shape=shapes,
        in_specs=[smem()] * (1 + wide_count) + [anywhere()],
        out_specs=[anywhere()] * len(shapes),
        scratch_shapes=[pltpu.SemaphoreType.DMA((copies,))],
        compiler_params=params(4),
        name="pack",
    )(me, in_hbm(pairs), *[lists[other - 1] for other in list_order(wide_count)], in_hbm(blocks))
    each = wide_count - 1
    return [outs[c * each : (c + 1) * each] for c in range(len(CHUNKS))], outs[-1]


def select_kernel(wide_count, groups, start, me_ref, pairs_ref, own_ref, *refs):
    pair_count = own_ref.shape[0]
    outs = refs[wide_count - 1 :]
    received = refs[: wide_count - 1]
    size = outs[0].shape[1]
    owners = [pairs_ref[1, pair] >> 3 for pair in range(pair_count)]
    for pair in range(pair_count):
        apart = me_ref[0] ^ owners[pair]
        rank = jnp.int32(0)
        for before in range(pair):
            rank = rank + (owners[before] == owners[pair]).astype(jnp.int32)

        places, rest = [], outs
        for pieces in groups:
            places.append(of_pair(rest[:pieces], pair))
            rest = rest[pieces:]

        @pl.when(apart == 0)
        def _():
            for out in places:
                out[...] = own_ref[pair, start : start + size]

        for number, other in enumerate(others(wide_count)):

            @pl.when(apart == other)
            def _():
                for out in places:
                    out[...] = received[number][rank]


def select(me, pairs, own, received, start, size, groups):
    pair_count, _, feat = own.shape
    shapes = [
        pltpu.VMEM((pair_count // pieces, size, feat), own.dtype)
        for pieces in groups
        for _ in range(pieces)
    ]
    outs = pl.pallas_call(
        functools.partial(select_kernel, len(received) + 1, groups, start),
        out_shape=shapes,
        in_specs=[smem(), smem()] + [vmem()] * (1 + len(received)),
        out_specs=[vmem()] * len(shapes),
        compiler_params=params(4),
        name="select",
    )(me, in_hbm(pairs), *[in_vmem(x) for x in (own, *received)])
    return take_parts(outs, groups)[0]


def tree(parts):
    while len(parts) > 1:
        half = len(parts) // 2
        parts = [parts[i] + parts[i + half] for i in range(half)]
    return parts[0]


def across(left, right):
    return lax.dot_general(
        left, right, (((1,), (1,)), ((), ())), preferred_element_type=jnp.float32
    )


def lane_sum(block):
    square = jnp.square(block.astype(jnp.float32))
    return sum(square[:, at : at + LANES] for at in range(0, square.shape[1], LANES))


def segments(window):
    low, high = window
    held = []
    for chunk, (start, size) in enumerate(CHUNKS):
        first, end = max(low, start), min(high, start + size)
        if first < end:
            held.append((chunk, first - start, end - first))
    return held


def scores(rows, cols, square):
    gram = tree([across(row, col) for row, col in zip(rows, cols)])
    other = jnp.sum(tree([lane_sum(col) for col in cols]).T, axis=0, keepdims=True)
    pieces, mass = [], None
    for at in range(0, gram.shape[1], LANES):
        here = slice(at, at + LANES)
        piece = jnp.exp((square + other[:, here] - 2.0 * gram[:, here]) * (-1.0 / F))
        mass = piece if mass is None else mass + piece
        pieces.append(piece)
    kernel = jnp.concatenate(pieces, axis=1) if len(pieces) > 1 else pieces[0]
    return kernel.astype(jnp.bfloat16), jnp.sum(kernel, axis=0, keepdims=True), mass


def take_parts(refs, counts):
    parts = []
    for count in counts:
        parts.append(refs[:count])
        refs = refs[count:]
    return parts, refs


def of_pair(part, pair):
    each = part[0].shape[0]
    return part[pair // each].at[pair % each]


def window_parts(counts, refs):
    half = len(counts[0]) // 2
    rows, refs = [ref.at[i] for ref in refs[:2] for i in range(half)], refs[2:]
    chunks = []
    for chunk_counts in counts:
        cols, refs = take_parts(refs, chunk_counts)
        chunks.append(cols)
    return rows, chunks


def own_columns(window, chunks, pair):
    held = segments(window)
    pieces = [of_pair(part, pair)[at : at + size] for part, (_, at, size) in zip(chunks, held)]
    return jnp.concatenate(pieces, axis=0) if len(pieces) > 1 else pieces[0]


def pair_parts(window, rows, chunks, pair):
    cols = [own_columns(window, [c[i] for c in chunks], pair) for i in range(len(rows))]
    return [part[pair] for part in rows], cols


def first_kernel(window, counts, *refs):
    square_ref, mass_ref, total_ref, sums_ref = refs[-4:]
    all_rows, chunks = window_parts(counts, refs)
    for pair in range(square_ref.shape[0]):
        rows, cols = pair_parts(window, all_rows, chunks, pair)
        square = jnp.sum(tree([lane_sum(row) for row in rows]), axis=1, keepdims=True)
        square = jnp.broadcast_to(square, (BR, LANES))
        kernel, sums, mass = scores(rows, cols, square)
        square_ref[pair] = square
        mass_ref[pair] = mass
        sums_ref[pair : pair + 1] = sums
        total_ref[pair] = jnp.dot(kernel, cols[0], preferred_element_type=jnp.float32)


def last_kernel(window, counts, wide_count, me_ref, pairs_ref, *refs):
    square_in, mass_in, sums_in = refs[-6 - wide_count : -3 - wide_count]
    kernel_ref, mass_ref, row_ref = refs[-3 - wide_count : -wide_count]
    shares = refs[-wide_count:]
    for ref in (row_ref, *shares):
        ref[...] = jnp.zeros_like(ref)
    all_rows, chunks = window_parts(counts, refs)
    for pair in range(square_in.shape[0]):
        rows, cols = pair_parts(window, all_rows, chunks, pair)
        kernel, sums, mass = scores(rows, cols, square_in[pair])
        kernel_ref[pair] = kernel
        sums = jnp.concatenate([sums_in[pair : pair + 1], sums], axis=1)
        mass = mass_in[pair] + mass
        mass_ref[pair] = mass
        row_ref[pl.ds(pairs_ref[0, pair] & 7, 1)] += jnp.sum(mass.T, axis=0, keepdims=True)
        col = pairs_ref[1, pair]
        apart = (col >> 3) ^ me_ref[0]
        for other, ref in zip([*others(wide_count), 0], shares):
            ref[pl.ds(col & 7, 1)] += jnp.where(apart == other, sums, 0.0)


def estimate(pair_count, size):
    return pl.CostEstimate(
        flops=2 * pair_count * BR * size * F,
        transcendentals=pair_count * BR * size,
        bytes_accessed=8 * 1024 * 1024,
    )


def piece_counts(window, cols):
    return tuple(tuple(len(part) for part in cols[chunk]) for chunk, _, _ in segments(window))


def operands(parts):
    return [piece for part in parts for piece in part]


def first_window(rows, cols):
    _, pair_count, _, feat = rows[0][0].shape
    window = WINDOWS[0]
    lanes = pltpu.VMEM((pair_count, BR, LANES), jnp.float32)
    total = pltpu.VMEM((pair_count, BR, feat), jnp.float32)
    args = operands(rows)
    for chunk, _, _ in segments(window):
        args += operands(cols[chunk])
    return pl.pallas_call(
        functools.partial(first_kernel, window, piece_counts(window, cols)),
        out_shape=[lanes, lanes, total, pltpu.VMEM((pair_count, window[1]), jnp.float32)],
        in_specs=[vmem()] * len(args),
        out_specs=[vmem()] * 4,
        compiler_params=params(16),
        cost_estimate=pl.CostEstimate(flops=0, transcendentals=0, bytes_accessed=0),
        name="first_window",
    )(*[in_vmem(x) for x in args])


def last_window(me, pairs, rows, cols, square, mass, sums, wide_count):
    pair_count = rows[0][0].shape[1]
    window = WINDOWS[1]
    size = window[1] - window[0]
    by_block = pltpu.VMEM((BLK_DEV, BR), jnp.float32)
    shapes = [
        pltpu.VMEM((pair_count, BR, size), jnp.bfloat16),
        pltpu.VMEM((pair_count, BR, LANES), jnp.float32),
    ] + [by_block] * (1 + wide_count)
    args = operands(rows)
    for chunk, _, _ in segments(window):
        args += operands(cols[chunk])
    args += [square, mass, sums]
    kernel, mass, row_sums, *shares = pl.pallas_call(
        functools.partial(last_kernel, window, piece_counts(window, cols), wide_count),
        out_shape=shapes,
        in_specs=[smem(), smem()] + [vmem()] * len(args),
        out_specs=[vmem()] * len(shapes),
        compiler_params=params(16),
        cost_estimate=estimate(pair_count, size),
        name="last_window",
    )(me, in_hbm(pairs), *[in_vmem(x) for x in args])
    return kernel, mass, row_sums, shares


def keep_kernel(pairs_ref, block_ref, blocks_ref, out_ref, own_ref, sems):
    here = pl.program_id(0)

    def copies():
        for pair in range(own_ref.shape[0]):
            source = blocks_ref.at[pairs_ref[1, pair] & 7]
            yield pltpu.make_async_copy(source, own_ref.at[pair], sems.at[pair])

    @pl.when(here == 0)
    def _():
        for copy in copies():
            copy.start()

    out_ref[...] = block_ref[...]

    @pl.when(here == pl.num_programs(0) - 1)
    def _():
        for copy in copies():
            copy.wait()


def keep(pairs, blocks):
    pair_count = pairs.shape[1]
    block = pl.BlockSpec((1, *blocks.shape[1:]), lambda k: (k, 0, 0))
    return pl.pallas_call(
        keep_kernel,
        out_shape=[
            pltpu.HBM(blocks.shape, blocks.dtype),
            pltpu.VMEM((pair_count, *blocks.shape[1:]), blocks.dtype),
        ],
        grid=(blocks.shape[0],),
        in_specs=[smem(), block, anywhere()],
        out_specs=[block, anywhere()],
        scratch_shapes=[pltpu.SemaphoreType.DMA((pair_count,))],
        compiler_params=params(4),
        name="keep",
    )(in_hbm(pairs), in_hbm(blocks), in_hbm(blocks))


def mean_kernel(window, counts, local_ref, rows_ref, kernel_ref, mass_ref, total_ref, *refs):
    *refs, _, out_ref, part, weight, total, mass, made, sems = refs
    chunks = []
    for chunk, _, _ in segments(window):
        (own,), refs = take_parts(refs, counts[len(chunks)][:1])
        chunks.append(own)
    pair_count, _, feat = rows_ref.shape
    local = [local_ref[0, pair] & 7 for pair in range(pair_count)]

    def copy(pair):
        return pltpu.make_async_copy(made.at[pair], out_ref.at[local[pair]], sems.at[pair])

    firsts = []
    for pair in range(pair_count):
        sums = total_ref[pair] + jnp.dot(
            kernel_ref[pair], own_columns(window, chunks, pair), preferred_element_type=jnp.float32
        )
        part[pair] = sums.astype(jnp.bfloat16)
        weight[pair] = jnp.broadcast_to(
            jnp.sum(mass_ref[pair], axis=1, keepdims=True), (BR, LANES)
        )
        same = [local[other] == local[pair] for other in range(pair)]
        firsts.append(jnp.logical_not(functools.reduce(jnp.logical_or, same, jnp.bool_(False))))
    for pair in range(pair_count):

        @pl.when(firsts[pair])
        def _():
            total[...] = rows_ref[pair].astype(jnp.float32) + part[pair].astype(jnp.float32)
            mass[...] = 1.0 + weight[pair]
            for other in range(pair + 1, pair_count):

                @pl.when(local[other] == local[pair])
                def _():
                    total[...] += part[other].astype(jnp.float32)
                    mass[...] += weight[other]

            scale = 1.0 / mass[...]
            for at in range(0, feat, LANES):
                lanes = slice(at, at + LANES)
                made[pair, :, lanes] = (total[:, lanes] * scale).astype(jnp.bfloat16)
            copy(pair).start()

    for pair in range(pair_count):

        @pl.when(firsts[pair])
        def _():
            copy(pair).wait()


def means(pairs, rows, kernel, mass, total, cols, kept):
    pair_count, _, feat = rows.shape
    window = WINDOWS[1]
    own = operands(cols[chunk][0] for chunk, _, _ in segments(window))
    args = [in_vmem(x) for x in (rows, kernel, mass, total, *own)]
    return pl.pallas_call(
        functools.partial(mean_kernel, window, piece_counts(window, cols)),
        out_shape=pltpu.HBM(kept.shape, jnp.bfloat16),
        in_specs=[smem()] + [vmem()] * len(args) + [anywhere()],
        out_specs=anywhere(),
        scratch_shapes=[
            pltpu.VMEM((pair_count, BR, feat), jnp.bfloat16),
            pltpu.VMEM((pair_count, BR, LANES), jnp.float32),
            pltpu.VMEM((BR, feat), jnp.float32),
            pltpu.VMEM((BR, LANES), jnp.float32),
            pltpu.VMEM((pair_count, BR, feat), jnp.bfloat16),
            pltpu.SemaphoreType.DMA((pair_count,)),
        ],
        input_output_aliases={1 + len(args): 0},
        compiler_params=params(16),
        cost_estimate=estimate(pair_count, 128),
        name="means",
    )(in_hbm(pairs), *args, in_hbm(kept))


def weight_kernel(*refs):
    out_ref = refs[-1]
    mass = refs[0][...]
    for ref in refs[1:-1]:
        mass = mass + ref[...]
    weight = 1.0 / (1.0 + mass / BR)
    parts = BR // LANES
    for block in range(BLK_DEV):
        for part in range(parts):
            lanes = slice(part * LANES, (part + 1) * LANES)
            out_ref[block * parts + part : block * parts + part + 1] = weight[block : block + 1, lanes]


def block_weights(sums):
    out = pl.pallas_call(
        weight_kernel,
        out_shape=jax.ShapeDtypeStruct((BLK_DEV * BR // LANES, LANES), jnp.float32),
        in_specs=[vmem()] * len(sums),
        out_specs=vmem(),
        compiler_params=params(4),
        name="weights",
    )(*[in_vmem(x) for x in sums])
    return out.reshape(BLK_DEV * BR)


def hop(parts, step):
    count = lax.axis_size("narrow")
    perm = [(i, i ^ step) for i in range(count)]
    return [[lax.ppermute(piece, "narrow", perm) for piece in part] for part in parts]


def first_hops(part):
    parts = [part]
    step = lax.axis_size("narrow") // 2
    while step > 1:
        parts = parts + hop(parts, step)
        step //= 2
    return parts


def to_wide(pieces, apart):
    count = lax.axis_size("wide")
    return [
        lax.ppermute(piece, "wide", [(i, i ^ other) for i in range(count)])
        for piece, other in zip(pieces, apart)
    ]


def on_device(embeddings, pair_list):
    wide_count = lax.axis_size("wide")
    me = lax.axis_index("wide").astype(jnp.int32).reshape(1)
    pairs = pair_list.T
    pair_count = pairs.shape[1]
    capacity = max(2, 2 * pair_count // wide_count)
    feat = embeddings.shape[1]
    blocks = embeddings.reshape(BLK_DEV, BR, feat)
    apart = others(wide_count)
    lists = to_wide([pairs] * (wide_count - 1), apart[::-1])
    fixed = lax.optimization_barrier
    outgoing, row_slices = pack(me, pairs, lists, blocks, capacity)

    def pick(received, chunk, *groups):
        return select(me, pairs, own, received, *CHUNKS[chunk], groups)

    def halves(part):
        middle = pair_count // 2
        return [part[0][:middle], part[0][middle:]]

    rows = jnp.stack([part[0] for part in first_hops([row_slices])])
    received = to_wide(outgoing[0], apart)
    near = to_wide(outgoing[1][-1:], apart[-1:])
    rows, received, near, (kept, own) = fixed((rows, received, near, keep(pairs, blocks)))
    own_a, whole_a = pick(received, 0, 2, 1)
    cols_a = [own_a] + first_hops(whole_a)[1:]
    rows = [[rows], *hop([[rows]], 1)]
    cols_a, rows, received = fixed((cols_a, rows, to_wide(outgoing[1][:-1], apart[:-1])))
    cols_b = first_hops(*pick([*received, *near], 1, 1))
    last_b = hop(cols_b[:1], 1)
    cols_a = cols_a + hop([own_a] + [halves(part) for part in cols_a[1:]], 1)
    carry = first_window(rows, [cols_a])
    cols_b, carry = fixed((cols_b, carry))
    cols_b = cols_b + last_b + hop(cols_b[1:], 1)
    square, mass, total, sums = carry
    kernel, mass, row_sums, shares = last_window(
        me, pairs, rows, [cols_a, cols_b], square, mass, sums, wide_count
    )
    came = to_wide(shares[:-1], apart)
    mean = means(pairs, row_slices, kernel, mass, total, [cols_a, cols_b], kept)
    weights = block_weights([row_sums, shares[-1], *came])
    return weights, mean.reshape(BLK_DEV * BR, feat)


def solution(mesh):
    in_specs = (P(("groups", "wide"), "narrow"), P(("groups", "wide"), None))
    out_specs = (P(("groups", "wide")), P(("groups", "wide"), "narrow"))
    return jax.shard_map(
        on_device, mesh=mesh, in_specs=in_specs, out_specs=out_specs, check_vma=False
    )
```

```python
import functools

import jax
import jax.numpy as jnp
from jax import lax
from jax.experimental import pallas as pl
from jax.experimental.pallas import tpu as pltpu
from jax.sharding import PartitionSpec as P

F = 1024
BR = 512
BLK_DEV = 8
LANES = 128
CHUNKS = ((0, 336), (336, 176))
WINDOWS = ((0, 256), (256, 512))


def smem():
    return pl.BlockSpec(memory_space=pltpu.SMEM)


def vmem():
    return pl.BlockSpec(memory_space=pltpu.VMEM)


def anywhere():
    return pl.BlockSpec(memory_space=pl.ANY)


def in_vmem(x):
    return pltpu.with_memory_space_constraint(x, pltpu.VMEM)


def in_hbm(x):
    return pltpu.with_memory_space_constraint(x, pltpu.HBM)


def params(mebibytes):
    return pltpu.CompilerParams(vmem_limit_bytes=mebibytes * 1024 * 1024)


def others(wide_count):
    return range(wide_count - 1, 0, -1)


def pack_kernel(wide_count, pair_count, capacity, me_ref, pairs_ref, *refs):
    lists, blocks_ref = refs[: wide_count - 1], refs[wide_count - 1]
    *outs, rows_ref, sems = refs[wide_count:]
    me = me_ref[0]
    copies = []

    def send(source, target):
        copies.append(pltpu.make_async_copy(source, target, sems.at[len(copies)]))
        copies[-1].start()

    for chunk, (start, size) in enumerate(CHUNKS):
        for number, other in enumerate(others(wide_count)):
            asked = lists[list_order(wide_count).index(other)]
            picks = [jnp.int32(0)] * capacity
            count = jnp.int32(0)
            for pair in range(pair_count):
                col = asked[1, pair]
                mine = (col >> 3) == me
                for slot in range(capacity):
                    picks[slot] = jnp.where(mine & (count == slot), col & 7, picks[slot])
                count = count + mine.astype(jnp.int32)
            out = outs[chunk * (wide_count - 1) + number]
            for slot in range(capacity):
                send(blocks_ref.at[picks[slot], pl.ds(start, size)], out.at[slot])
    for pair in range(pair_count):
        send(blocks_ref.at[pairs_ref[0, pair] & 7], rows_ref.at[pair])
    for copy in copies:
        copy.wait()


def list_order(wide_count):
    middle = wide_count // 2
    return [other for other in range(1, wide_count) if other != middle] + [middle]


def sum_order(wide_count):
    return list_order(wide_count)[::-1]


def pack(me, pairs, lists, blocks, capacity):
    wide_count, pair_count = len(lists) + 1, pairs.shape[1]
    feat = blocks.shape[-1]
    shapes = [
        pltpu.VMEM((capacity, size, feat), blocks.dtype)
        for _, size in CHUNKS
        for _ in range(1, wide_count)
    ] + [pltpu.VMEM((pair_count, BR, feat), blocks.dtype)]
    copies = (len(shapes) - 1) * capacity + pair_count
    outs = pl.pallas_call(
        functools.partial(pack_kernel, wide_count, pair_count, capacity),
        out_shape=shapes,
        in_specs=[smem()] * (1 + wide_count) + [anywhere()],
        out_specs=[anywhere()] * len(shapes),
        scratch_shapes=[pltpu.SemaphoreType.DMA((copies,))],
        compiler_params=params(4),
        name="pack",
    )(me, in_hbm(pairs), *[lists[other - 1] for other in list_order(wide_count)], in_hbm(blocks))
    each = wide_count - 1
    return [outs[c * each : (c + 1) * each] for c in range(len(CHUNKS))], outs[-1]


def select_kernel(wide_count, groups, start, me_ref, pairs_ref, own_ref, *refs):
    pair_count = own_ref.shape[0]
    outs = refs[wide_count - 1 :]
    received = refs[: wide_count - 1]
    size = outs[0].shape[1]
    owners = [pairs_ref[1, pair] >> 3 for pair in range(pair_count)]
    for pair in range(pair_count):
        apart = me_ref[0] ^ owners[pair]
        rank = jnp.int32(0)
        for before in range(pair):
            rank = rank + (owners[before] == owners[pair]).astype(jnp.int32)

        places, rest = [], outs
        for pieces in groups:
            places.append(of_pair(rest[:pieces], pair))
            rest = rest[pieces:]

        @pl.when(apart == 0)
        def _():
            for out in places:
                out[...] = own_ref[pair, start : start + size]

        for number, other in enumerate(others(wide_count)):

            @pl.when(apart == other)
            def _():
                for out in places:
                    out[...] = received[number][rank]


def select(me, pairs, own, received, start, size, groups):
    pair_count, _, feat = own.shape
    shapes = [
        pltpu.VMEM((pair_count // pieces, size, feat), own.dtype)
        for pieces in groups
        for _ in range(pieces)
    ]
    outs = pl.pallas_call(
        functools.partial(select_kernel, len(received) + 1, groups, start),
        out_shape=shapes,
        in_specs=[smem(), smem()] + [vmem()] * (1 + len(received)),
        out_specs=[vmem()] * len(shapes),
        compiler_params=params(4),
        name="select",
    )(me, in_hbm(pairs), *[in_vmem(x) for x in (own, *received)])
    return take_parts(outs, groups)[0]


def tree(parts):
    while len(parts) > 1:
        half = len(parts) // 2
        parts = [parts[i] + parts[i + half] for i in range(half)]
    return parts[0]


def across(left, right):
    return lax.dot_general(
        left, right, (((1,), (1,)), ((), ())), preferred_element_type=jnp.float32
    )


def lane_sum(block):
    square = jnp.square(block.astype(jnp.float32))
    return sum(square[:, at : at + LANES] for at in range(0, square.shape[1], LANES))


def segments(window):
    low, high = window
    held = []
    for chunk, (start, size) in enumerate(CHUNKS):
        first, end = max(low, start), min(high, start + size)
        if first < end:
            held.append((chunk, first - start, end - first))
    return held


def scores(rows, cols, square):
    gram = tree([across(row, col) for row, col in zip(rows, cols)])
    other = jnp.sum(tree([lane_sum(col) for col in cols]).T, axis=0, keepdims=True)
    pieces, mass = [], None
    for at in range(0, gram.shape[1], LANES):
        here = slice(at, at + LANES)
        piece = jnp.exp((square + other[:, here] - 2.0 * gram[:, here]) * (-1.0 / F))
        mass = piece if mass is None else mass + piece
        pieces.append(piece)
    kernel = jnp.concatenate(pieces, axis=1) if len(pieces) > 1 else pieces[0]
    return kernel.astype(jnp.bfloat16), jnp.sum(kernel, axis=0, keepdims=True), mass


def take_parts(refs, counts):
    parts = []
    for count in counts:
        parts.append(refs[:count])
        refs = refs[count:]
    return parts, refs


def of_pair(part, pair):
    each = part[0].shape[0]
    return part[pair // each].at[pair % each]


def window_parts(counts, refs):
    half = len(counts[0]) // 2
    rows, refs = [ref.at[i] for ref in refs[:2] for i in range(half)], refs[2:]
    chunks = []
    for chunk_counts in counts:
        cols, refs = take_parts(refs, chunk_counts)
        chunks.append(cols)
    return rows, chunks


def own_columns(window, chunks, pair):
    held = segments(window)
    pieces = [of_pair(part, pair)[at : at + size] for part, (_, at, size) in zip(chunks, held)]
    return jnp.concatenate(pieces, axis=0) if len(pieces) > 1 else pieces[0]


def pair_parts(window, rows, chunks, pair):
    cols = [own_columns(window, [c[i] for c in chunks], pair) for i in range(len(rows))]
    return [part[pair] for part in rows], cols


def first_kernel(window, counts, *refs):
    square_ref, mass_ref, total_ref, sums_ref = refs[-4:]
    all_rows, chunks = window_parts(counts, refs)
    for pair in range(square_ref.shape[0]):
        rows, cols = pair_parts(window, all_rows, chunks, pair)
        square = jnp.sum(tree([lane_sum(row) for row in rows]), axis=1, keepdims=True)
        square = jnp.broadcast_to(square, (BR, LANES))
        kernel, sums, mass = scores(rows, cols, square)
        square_ref[pair] = square
        mass_ref[pair] = mass
        sums_ref[pair : pair + 1] = sums
        total_ref[pair] = jnp.dot(kernel, cols[0], preferred_element_type=jnp.float32)


def last_kernel(window, counts, wide_count, me_ref, pairs_ref, *refs):
    square_in, mass_in, sums_in = refs[-6 - wide_count : -3 - wide_count]
    kernel_ref, mass_ref, row_ref = refs[-3 - wide_count : -wide_count]
    shares = refs[-wide_count:]
    for ref in (row_ref, *shares):
        ref[...] = jnp.zeros_like(ref)
    all_rows, chunks = window_parts(counts, refs)
    for pair in range(square_in.shape[0]):
        rows, cols = pair_parts(window, all_rows, chunks, pair)
        kernel, sums, mass = scores(rows, cols, square_in[pair])
        kernel_ref[pair] = kernel
        sums = jnp.concatenate([sums_in[pair : pair + 1], sums], axis=1)
        mass = mass_in[pair] + mass
        mass_ref[pair] = mass
        row_ref[pl.ds(pairs_ref[0, pair] & 7, 1)] += jnp.sum(mass.T, axis=0, keepdims=True)
        col = pairs_ref[1, pair]
        apart = (col >> 3) ^ me_ref[0]
        for other, ref in zip([*sum_order(wide_count), 0], shares):
            ref[pl.ds(col & 7, 1)] += jnp.where(apart == other, sums, 0.0)


def estimate(pair_count, size):
    return pl.CostEstimate(
        flops=2 * pair_count * BR * size * F,
        transcendentals=pair_count * BR * size,
        bytes_accessed=8 * 1024 * 1024,
    )


def piece_counts(window, cols):
    return tuple(tuple(len(part) for part in cols[chunk]) for chunk, _, _ in segments(window))


def operands(parts):
    return [piece for part in parts for piece in part]


def first_window(rows, cols):
    _, pair_count, _, feat = rows[0][0].shape
    window = WINDOWS[0]
    lanes = pltpu.VMEM((pair_count, BR, LANES), jnp.float32)
    total = pltpu.VMEM((pair_count, BR, feat), jnp.float32)
    args = operands(rows)
    for chunk, _, _ in segments(window):
        args += operands(cols[chunk])
    return pl.pallas_call(
        functools.partial(first_kernel, window, piece_counts(window, cols)),
        out_shape=[lanes, lanes, total, pltpu.VMEM((pair_count, window[1]), jnp.float32)],
        in_specs=[vmem()] * len(args),
        out_specs=[vmem()] * 4,
        compiler_params=params(16),
        cost_estimate=pl.CostEstimate(flops=0, transcendentals=0, bytes_accessed=0),
        name="first_window",
    )(*[in_vmem(x) for x in args])


def last_window(me, pairs, rows, cols, square, mass, sums, wide_count):
    pair_count = rows[0][0].shape[1]
    window = WINDOWS[1]
    size = window[1] - window[0]
    by_block = pltpu.VMEM((BLK_DEV, BR), jnp.float32)
    shapes = [
        pltpu.VMEM((pair_count, BR, size), jnp.bfloat16),
        pltpu.VMEM((pair_count, BR, LANES), jnp.float32),
    ] + [by_block] * (1 + wide_count)
    args = operands(rows)
    for chunk, _, _ in segments(window):
        args += operands(cols[chunk])
    args += [square, mass, sums]
    kernel, mass, row_sums, *shares = pl.pallas_call(
        functools.partial(last_kernel, window, piece_counts(window, cols), wide_count),
        out_shape=shapes,
        in_specs=[smem(), smem()] + [vmem()] * len(args),
        out_specs=[vmem()] * len(shapes),
        compiler_params=params(16),
        cost_estimate=estimate(pair_count, size),
        name="last_window",
    )(me, in_hbm(pairs), *[in_vmem(x) for x in args])
    return kernel, mass, row_sums, shares


def keep_kernel(pairs_ref, block_ref, blocks_ref, out_ref, own_ref, sems):
    here = pl.program_id(0)

    def copies():
        for pair in range(own_ref.shape[0]):
            source = blocks_ref.at[pairs_ref[1, pair] & 7]
            yield pltpu.make_async_copy(source, own_ref.at[pair], sems.at[pair])

    @pl.when(here == 0)
    def _():
        for copy in copies():
            copy.start()

    out_ref[...] = block_ref[...]

    @pl.when(here == pl.num_programs(0) - 1)
    def _():
        for copy in copies():
            copy.wait()


def keep(pairs, blocks):
    pair_count = pairs.shape[1]
    block = pl.BlockSpec((1, *blocks.shape[1:]), lambda k: (k, 0, 0))
    return pl.pallas_call(
        keep_kernel,
        out_shape=[
            pltpu.HBM(blocks.shape, blocks.dtype),
            pltpu.VMEM((pair_count, *blocks.shape[1:]), blocks.dtype),
        ],
        grid=(blocks.shape[0],),
        in_specs=[smem(), block, anywhere()],
        out_specs=[block, anywhere()],
        scratch_shapes=[pltpu.SemaphoreType.DMA((pair_count,))],
        compiler_params=params(4),
        name="keep",
    )(in_hbm(pairs), in_hbm(blocks), in_hbm(blocks))


def mean_kernel(window, counts, local_ref, rows_ref, kernel_ref, mass_ref, total_ref, *refs):
    *refs, _, out_ref, part, weight, total, mass, made, sems = refs
    chunks = []
    for chunk, _, _ in segments(window):
        (own,), refs = take_parts(refs, counts[len(chunks)][:1])
        chunks.append(own)
    pair_count, _, feat = rows_ref.shape
    local = [local_ref[0, pair] & 7 for pair in range(pair_count)]

    def copy(pair):
        return pltpu.make_async_copy(made.at[pair], out_ref.at[local[pair]], sems.at[pair])

    firsts = []
    for pair in range(pair_count):
        sums = total_ref[pair] + jnp.dot(
            kernel_ref[pair], own_columns(window, chunks, pair), preferred_element_type=jnp.float32
        )
        part[pair] = sums.astype(jnp.bfloat16)
        weight[pair] = jnp.broadcast_to(
            jnp.sum(mass_ref[pair], axis=1, keepdims=True), (BR, LANES)
        )
        same = [local[other] == local[pair] for other in range(pair)]
        firsts.append(jnp.logical_not(functools.reduce(jnp.logical_or, same, jnp.bool_(False))))
    for pair in range(pair_count):

        @pl.when(firsts[pair])
        def _():
            total[...] = rows_ref[pair].astype(jnp.float32) + part[pair].astype(jnp.float32)
            mass[...] = 1.0 + weight[pair]
            for other in range(pair + 1, pair_count):

                @pl.when(local[other] == local[pair])
                def _():
                    total[...] += part[other].astype(jnp.float32)
                    mass[...] += weight[other]

            scale = 1.0 / mass[...]
            for at in range(0, feat, LANES):
                lanes = slice(at, at + LANES)
                made[pair, :, lanes] = (total[:, lanes] * scale).astype(jnp.bfloat16)
            copy(pair).start()

    for pair in range(pair_count):

        @pl.when(firsts[pair])
        def _():
            copy(pair).wait()


def means(pairs, rows, kernel, mass, total, cols, kept):
    pair_count, _, feat = rows.shape
    window = WINDOWS[1]
    own = operands(cols[chunk][0] for chunk, _, _ in segments(window))
    args = [in_vmem(x) for x in (rows, kernel, mass, total, *own)]
    return pl.pallas_call(
        functools.partial(mean_kernel, window, piece_counts(window, cols)),
        out_shape=pltpu.HBM(kept.shape, jnp.bfloat16),
        in_specs=[smem()] + [vmem()] * len(args) + [anywhere()],
        out_specs=anywhere(),
        scratch_shapes=[
            pltpu.VMEM((pair_count, BR, feat), jnp.bfloat16),
            pltpu.VMEM((pair_count, BR, LANES), jnp.float32),
            pltpu.VMEM((BR, feat), jnp.float32),
            pltpu.VMEM((BR, LANES), jnp.float32),
            pltpu.VMEM((pair_count, BR, feat), jnp.bfloat16),
            pltpu.SemaphoreType.DMA((pair_count,)),
        ],
        input_output_aliases={1 + len(args): 0},
        compiler_params=params(16),
        cost_estimate=estimate(pair_count, 128),
        name="means",
    )(in_hbm(pairs), *args, in_hbm(kept))


def weight_kernel(*refs):
    out_ref = refs[-1]
    mass = refs[0][...]
    for ref in refs[1:-1]:
        mass = mass + ref[...]
    weight = 1.0 / (1.0 + mass / BR)
    parts = BR // LANES
    for block in range(BLK_DEV):
        for part in range(parts):
            lanes = slice(part * LANES, (part + 1) * LANES)
            out_ref[block * parts + part : block * parts + part + 1] = weight[block : block + 1, lanes]


def block_weights(sums):
    out = pl.pallas_call(
        weight_kernel,
        out_shape=jax.ShapeDtypeStruct((BLK_DEV * BR // LANES, LANES), jnp.float32),
        in_specs=[vmem()] * len(sums),
        out_specs=vmem(),
        compiler_params=params(4),
        name="weights",
    )(*[in_vmem(x) for x in sums])
    return out.reshape(BLK_DEV * BR)


def hop(parts, step):
    count = lax.axis_size("narrow")
    perm = [(i, i ^ step) for i in range(count)]
    return [[lax.ppermute(piece, "narrow", perm) for piece in part] for part in parts]


def first_hops(part):
    parts = [part]
    step = lax.axis_size("narrow") // 2
    while step > 1:
        parts = parts + hop(parts, step)
        step //= 2
    return parts


def to_wide(pieces, apart):
    count = lax.axis_size("wide")
    return [
        lax.ppermute(piece, "wide", [(i, i ^ other) for i in range(count)])
        for piece, other in zip(pieces, apart)
    ]


def on_device(embeddings, pair_list):
    wide_count = lax.axis_size("wide")
    me = lax.axis_index("wide").astype(jnp.int32).reshape(1)
    pairs = pair_list.T
    pair_count = pairs.shape[1]
    capacity = max(2, 2 * pair_count // wide_count)
    feat = embeddings.shape[1]
    blocks = embeddings.reshape(BLK_DEV, BR, feat)
    apart = others(wide_count)
    lists = to_wide([pairs] * (wide_count - 1), apart[::-1])
    fixed = lax.optimization_barrier
    outgoing, row_slices = pack(me, pairs, lists, blocks, capacity)

    def pick(received, chunk, *groups):
        return select(me, pairs, own, received, *CHUNKS[chunk], groups)

    def halves(part):
        middle = pair_count // 2
        return [part[0][:middle], part[0][middle:]]

    rows = jnp.stack([part[0] for part in first_hops([row_slices])])
    received = to_wide(outgoing[0], apart)
    near = to_wide(outgoing[1][-1:], apart[-1:])
    rows, received, near, (kept, own) = fixed((rows, received, near, keep(pairs, blocks)))
    own_a, whole_a = pick(received, 0, 2, 1)
    cols_a = [own_a] + first_hops(whole_a)[1:]
    rows = [[rows], *hop([[rows]], 1)]
    cols_a, rows, received = fixed((cols_a, rows, to_wide(outgoing[1][:-1], apart[:-1])))
    cols_b = first_hops(*pick([*received, *near], 1, 1))
    last_b = hop(cols_b[:1], 1)
    cols_a = cols_a + hop([own_a] + [halves(part) for part in cols_a[1:]], 1)
    carry = first_window(rows, [cols_a])
    cols_b, carry = fixed((cols_b, carry))
    cols_b = cols_b + last_b + hop(cols_b[1:], 1)
    square, mass, total, sums = carry
    kernel, mass, row_sums, shares = last_window(
        me, pairs, rows, [cols_a, cols_b], square, mass, sums, wide_count
    )
    came = to_wide(shares[:-1], sum_order(wide_count))
    mean = means(pairs, row_slices, kernel, mass, total, [cols_a, cols_b], kept)
    weights = block_weights([row_sums, shares[-1], *came])
    return weights, mean.reshape(BLK_DEV * BR, feat)


def solution(mesh):
    in_specs = (P(("groups", "wide"), "narrow"), P(("groups", "wide"), None))
    out_specs = (P(("groups", "wide")), P(("groups", "wide"), "narrow"))
    return jax.shard_map(
        on_device, mesh=mesh, in_specs=in_specs, out_specs=out_specs, check_vma=False
    )
```

```python
import functools

import jax
import jax.numpy as jnp
from jax import lax
from jax.experimental import pallas as pl
from jax.experimental.pallas import tpu as pltpu
from jax.sharding import PartitionSpec as P

F = 1024
BR = 512
BLK_DEV = 8
LANES = 128
CHUNKS = ((0, 336), (336, 176))
WINDOWS = ((0, 256), (256, 512))


def smem():
    return pl.BlockSpec(memory_space=pltpu.SMEM)


def vmem():
    return pl.BlockSpec(memory_space=pltpu.VMEM)


def anywhere():
    return pl.BlockSpec(memory_space=pl.ANY)


def in_vmem(x):
    return pltpu.with_memory_space_constraint(x, pltpu.VMEM)


def in_hbm(x):
    return pltpu.with_memory_space_constraint(x, pltpu.HBM)


def params(mebibytes):
    return pltpu.CompilerParams(vmem_limit_bytes=mebibytes * 1024 * 1024)


def others(wide_count):
    return range(wide_count - 1, 0, -1)


def pack_kernel(wide_count, pair_count, capacity, me_ref, pairs_ref, *refs):
    lists, blocks_ref = refs[: wide_count - 1], refs[wide_count - 1]
    *outs, rows_ref, sems = refs[wide_count:]
    me = me_ref[0]
    copies = []

    def send(source, target):
        copies.append(pltpu.make_async_copy(source, target, sems.at[len(copies)]))
        copies[-1].start()

    for chunk, (start, size) in enumerate(CHUNKS):
        for number, other in enumerate(others(wide_count)):
            asked = lists[list_order(wide_count).index(other)]
            picks = [jnp.int32(0)] * capacity
            count = jnp.int32(0)
            for pair in range(pair_count):
                col = asked[1, pair]
                mine = (col >> 3) == me
                for slot in range(capacity):
                    picks[slot] = jnp.where(mine & (count == slot), col & 7, picks[slot])
                count = count + mine.astype(jnp.int32)
            out = outs[chunk * (wide_count - 1) + number]
            for slot in range(capacity):
                send(blocks_ref.at[picks[slot], pl.ds(start, size)], out.at[slot])
    for place, pair in enumerate(in_order(wide_count, me_ref, pairs_ref)):
        send(blocks_ref.at[pairs_ref[0, pair] & 7], rows_ref.at[place])
    for copy in copies:
        copy.wait()


def in_order(wide_count, me_ref, pairs_ref):
    pair_count = pairs_ref.shape[1]
    far = [
        ((pairs_ref[1, pair] >> 3) ^ me_ref[0] == wide_count // 2).astype(jnp.int32)
        for pair in range(pair_count)
    ]
    place_near, place_far = jnp.int32(0), pair_count - sum(far)
    places = []
    for is_far in far:
        places.append(jnp.where(is_far == 1, place_far, place_near))
        place_near, place_far = place_near + 1 - is_far, place_far + is_far
    return [
        sum(jnp.where(at == place, pair, 0) for pair, at in enumerate(places))
        for place in range(pair_count)
    ]


def list_order(wide_count):
    middle = wide_count // 2
    return [other for other in range(1, wide_count) if other != middle] + [middle]


def sum_order(wide_count):
    return list_order(wide_count)[::-1]


def pack(me, pairs, lists, blocks, capacity):
    wide_count, pair_count = len(lists) + 1, pairs.shape[1]
    feat = blocks.shape[-1]
    shapes = [
        pltpu.VMEM((capacity, size, feat), blocks.dtype)
        for _, size in CHUNKS
        for _ in range(1, wide_count)
    ] + [pltpu.VMEM((pair_count, BR, feat), blocks.dtype)]
    copies = (len(shapes) - 1) * capacity + pair_count
    outs = pl.pallas_call(
        functools.partial(pack_kernel, wide_count, pair_count, capacity),
        out_shape=shapes,
        in_specs=[smem()] * (1 + wide_count) + [anywhere()],
        out_specs=[anywhere()] * len(shapes),
        scratch_shapes=[pltpu.SemaphoreType.DMA((copies,))],
        compiler_params=params(4),
        name="pack",
    )(me, in_hbm(pairs), *[lists[other - 1] for other in list_order(wide_count)], in_hbm(blocks))
    each = wide_count - 1
    return [outs[c * each : (c + 1) * each] for c in range(len(CHUNKS))], outs[-1]


def select_kernel(wide_count, apart, groups, first, start, me_ref, pairs_ref, own_ref, *refs):
    received, outs = refs[: len(apart)], refs[len(apart) :]
    pair_count = own_ref.shape[0]
    size = outs[0].shape[1]
    count = sum(ref.shape[0] for ref in outs[: groups[0]])
    owners = [pairs_ref[1, pair] >> 3 for pair in range(pair_count)]
    order = in_order(wide_count, me_ref, pairs_ref)
    for place in range(first, first + count):
        pair = order[place]
        owner = pairs_ref[1, pair] >> 3
        away = me_ref[0] ^ owner
        rank = jnp.int32(0)
        for before in range(pair_count):
            rank = rank + ((before < pair) & (owners[before] == owner)).astype(jnp.int32)
        targets, rest = [], outs
        for pieces in groups:
            targets.append(of_pair(rest[:pieces], place - first))
            rest = rest[pieces:]

        @pl.when(away == 0)
        def _():
            for out in targets:
                out[...] = own_ref[place, start : start + size]

        for number, other in enumerate(apart):

            @pl.when(away == other)
            def _():
                for out in targets:
                    out[...] = received[number][rank]


def select(me, pairs, own, received, apart, wide_count, places, start, size, groups):
    _, _, feat = own.shape
    first, count = places
    shapes = [
        pltpu.VMEM((count // pieces, size, feat), own.dtype)
        for pieces in groups
        for _ in range(pieces)
    ]
    outs = pl.pallas_call(
        functools.partial(select_kernel, wide_count, apart, groups, first, start),
        out_shape=shapes,
        in_specs=[smem(), smem()] + [vmem()] * (1 + len(received)),
        out_specs=[vmem()] * len(shapes),
        compiler_params=params(4),
        cost_estimate=nothing(),
        name="select",
    )(me, in_hbm(pairs), *[in_vmem(x) for x in (own, *received)])
    return take_parts(outs, groups)[0]


def nothing():
    return pl.CostEstimate(flops=0, transcendentals=0, bytes_accessed=0)


def tree(parts):
    while len(parts) > 1:
        half = len(parts) // 2
        parts = [parts[i] + parts[i + half] for i in range(half)]
    return parts[0]


def across(left, right):
    return lax.dot_general(
        left, right, (((1,), (1,)), ((), ())), preferred_element_type=jnp.float32
    )


def lane_sum(block):
    square = jnp.square(block.astype(jnp.float32))
    return sum(square[:, at : at + LANES] for at in range(0, square.shape[1], LANES))


def segments(window):
    low, high = window
    held = []
    for chunk, (start, size) in enumerate(CHUNKS):
        first, end = max(low, start), min(high, start + size)
        if first < end:
            held.append((chunk, first - start, end - first))
    return held


def scores(rows, cols, square):
    gram = tree([across(row, col) for row, col in zip(rows, cols)])
    other = jnp.sum(tree([lane_sum(col) for col in cols]).T, axis=0, keepdims=True)
    pieces, mass = [], None
    for at in range(0, gram.shape[1], LANES):
        here = slice(at, at + LANES)
        piece = jnp.exp((square + other[:, here] - 2.0 * gram[:, here]) * (-1.0 / F))
        mass = piece if mass is None else mass + piece
        pieces.append(piece)
    kernel = jnp.concatenate(pieces, axis=1) if len(pieces) > 1 else pieces[0]
    return kernel.astype(jnp.bfloat16), jnp.sum(kernel, axis=0, keepdims=True), mass


def take_parts(refs, counts):
    parts = []
    for count in counts:
        parts.append(refs[:count])
        refs = refs[count:]
    return parts, refs


def of_pair(part, pair):
    each = part[0].shape[0]
    return part[pair // each].at[pair % each]


def window_parts(counts, refs):
    half = len(counts[0]) // 2
    rows, refs = [ref.at[i] for ref in refs[:2] for i in range(half)], refs[2:]
    chunks = []
    for chunk_counts in counts:
        cols, refs = take_parts(refs, chunk_counts)
        chunks.append(cols)
    return rows, chunks


def own_columns(window, chunks, pair):
    held = segments(window)
    pieces = [of_pair(part, pair)[at : at + size] for part, (_, at, size) in zip(chunks, held)]
    return jnp.concatenate(pieces, axis=0) if len(pieces) > 1 else pieces[0]


def pair_parts(window, rows, chunks, pair):
    cols = [own_columns(window, [c[i] for c in chunks], pair) for i in range(len(rows))]
    return [part[pair] for part in rows], cols


def first_kernel(window, counts, *refs):
    square_ref, mass_ref, total_ref, sums_ref = refs[-4:]
    all_rows, chunks = window_parts(counts, refs)
    for pair in range(square_ref.shape[0]):
        rows, cols = pair_parts(window, all_rows, chunks, pair)
        square = jnp.sum(tree([lane_sum(row) for row in rows]), axis=1, keepdims=True)
        square = jnp.broadcast_to(square, (BR, LANES))
        kernel, sums, mass = scores(rows, cols, square)
        square_ref[pair] = square
        mass_ref[pair] = mass
        sums_ref[pair : pair + 1] = sums
        total_ref[pair] = jnp.dot(kernel, cols[0], preferred_element_type=jnp.float32)


def last_kernel(window, counts, wide_count, me_ref, pairs_ref, *refs):
    square_in, mass_in, sums_in = refs[-6 - wide_count : -3 - wide_count]
    kernel_ref, mass_ref, row_ref = refs[-3 - wide_count : -wide_count]
    shares = refs[-wide_count:]
    for ref in (row_ref, *shares):
        ref[...] = jnp.zeros_like(ref)
    all_rows, chunks = window_parts(counts, refs)
    order = in_order(wide_count, me_ref, pairs_ref)
    for place, pair in enumerate(order):
        rows, cols = pair_parts(window, all_rows, chunks, place)
        kernel, sums, mass = scores(rows, cols, square_in[place])
        kernel_ref[place] = kernel
        sums = jnp.concatenate([sums_in[place : place + 1], sums], axis=1)
        mass = mass_in[place] + mass
        mass_ref[place] = mass
        row_ref[pl.ds(pairs_ref[0, pair] & 7, 1)] += jnp.sum(mass.T, axis=0, keepdims=True)
        col = pairs_ref[1, pair]
        apart = (col >> 3) ^ me_ref[0]
        for other, ref in zip([*sum_order(wide_count), 0], shares):
            ref[pl.ds(col & 7, 1)] += jnp.where(apart == other, sums, 0.0)


def estimate(pair_count, size):
    return pl.CostEstimate(
        flops=2 * pair_count * BR * size * F,
        transcendentals=pair_count * BR * size,
        bytes_accessed=8 * 1024 * 1024,
    )


def piece_counts(window, cols):
    return tuple(tuple(len(part) for part in cols[chunk]) for chunk, _, _ in segments(window))


def operands(parts):
    return [piece for part in parts for piece in part]


def first_window(rows, cols):
    _, pair_count, _, feat = rows[0][0].shape
    window = WINDOWS[0]
    lanes = pltpu.VMEM((pair_count, BR, LANES), jnp.float32)
    total = pltpu.VMEM((pair_count, BR, feat), jnp.float32)
    args = operands(rows)
    for chunk, _, _ in segments(window):
        args += operands(cols[chunk])
    return pl.pallas_call(
        functools.partial(first_kernel, window, piece_counts(window, cols)),
        out_shape=[lanes, lanes, total, pltpu.VMEM((pair_count, window[1]), jnp.float32)],
        in_specs=[vmem()] * len(args),
        out_specs=[vmem()] * 4,
        compiler_params=params(16),
        cost_estimate=pl.CostEstimate(flops=0, transcendentals=0, bytes_accessed=0),
        name="first_window",
    )(*[in_vmem(x) for x in args])


def last_window(me, pairs, rows, cols, square, mass, sums, wide_count):
    pair_count = rows[0][0].shape[1]
    window = WINDOWS[1]
    size = window[1] - window[0]
    by_block = pltpu.VMEM((BLK_DEV, BR), jnp.float32)
    shapes = [
        pltpu.VMEM((pair_count, BR, size), jnp.bfloat16),
        pltpu.VMEM((pair_count, BR, LANES), jnp.float32),
    ] + [by_block] * (1 + wide_count)
    args = operands(rows)
    for chunk, _, _ in segments(window):
        args += operands(cols[chunk])
    args += [square, mass, sums]
    kernel, mass, row_sums, *shares = pl.pallas_call(
        functools.partial(last_kernel, window, piece_counts(window, cols), wide_count),
        out_shape=shapes,
        in_specs=[smem(), smem()] + [vmem()] * len(args),
        out_specs=[vmem()] * len(shapes),
        compiler_params=params(16),
        cost_estimate=estimate(pair_count, size),
        name="last_window",
    )(me, in_hbm(pairs), *[in_vmem(x) for x in args])
    return kernel, mass, row_sums, shares


def keep_kernel(wide_count, me_ref, pairs_ref, block_ref, blocks_ref, out_ref, own_ref, sems):
    here = pl.program_id(0)

    def copies():
        for place, pair in enumerate(in_order(wide_count, me_ref, pairs_ref)):
            source = blocks_ref.at[pairs_ref[1, pair] & 7]
            yield pltpu.make_async_copy(source, own_ref.at[place], sems.at[place])

    @pl.when(here == 0)
    def _():
        for copy in copies():
            copy.start()

    out_ref[...] = block_ref[...]

    @pl.when(here == pl.num_programs(0) - 1)
    def _():
        for copy in copies():
            copy.wait()


def keep(me, pairs, blocks, wide_count):
    pair_count = pairs.shape[1]
    block = pl.BlockSpec((1, *blocks.shape[1:]), lambda k: (k, 0, 0))
    return pl.pallas_call(
        functools.partial(keep_kernel, wide_count),
        out_shape=[
            pltpu.HBM(blocks.shape, blocks.dtype),
            pltpu.VMEM((pair_count, *blocks.shape[1:]), blocks.dtype),
        ],
        grid=(blocks.shape[0],),
        in_specs=[smem(), smem(), block, anywhere()],
        out_specs=[block, anywhere()],
        scratch_shapes=[pltpu.SemaphoreType.DMA((pair_count,))],
        compiler_params=params(4),
        name="keep",
    )(me, in_hbm(pairs), in_hbm(blocks), in_hbm(blocks))


def mean_kernel(window, counts, wide_count, me_ref, local_ref, rows_ref, kernel_ref, mass_ref, total_ref, *refs):
    *refs, _, out_ref, part, weight, total, mass, made, sems = refs
    chunks = []
    for chunk, _, _ in segments(window):
        (own,), refs = take_parts(refs, counts[len(chunks)][:1])
        chunks.append(own)
    pair_count, _, feat = rows_ref.shape
    local = [local_ref[0, pair] & 7 for pair in in_order(wide_count, me_ref, local_ref)]

    def copy(pair):
        return pltpu.make_async_copy(made.at[pair], out_ref.at[local[pair]], sems.at[pair])

    firsts = []
    for pair in range(pair_count):
        sums = total_ref[pair] + jnp.dot(
            kernel_ref[pair], own_columns(window, chunks, pair), preferred_element_type=jnp.float32
        )
        part[pair] = sums.astype(jnp.bfloat16)
        weight[pair] = jnp.broadcast_to(
            jnp.sum(mass_ref[pair], axis=1, keepdims=True), (BR, LANES)
        )
        same = [local[other] == local[pair] for other in range(pair)]
        firsts.append(jnp.logical_not(functools.reduce(jnp.logical_or, same, jnp.bool_(False))))
    for pair in range(pair_count):

        @pl.when(firsts[pair])
        def _():
            total[...] = rows_ref[pair].astype(jnp.float32) + part[pair].astype(jnp.float32)
            mass[...] = 1.0 + weight[pair]
            for other in range(pair + 1, pair_count):

                @pl.when(local[other] == local[pair])
                def _():
                    total[...] += part[other].astype(jnp.float32)
                    mass[...] += weight[other]

            scale = 1.0 / mass[...]
            for at in range(0, feat, LANES):
                lanes = slice(at, at + LANES)
                made[pair, :, lanes] = (total[:, lanes] * scale).astype(jnp.bfloat16)
            copy(pair).start()

    for pair in range(pair_count):

        @pl.when(firsts[pair])
        def _():
            copy(pair).wait()


def means(me, wide_count, pairs, rows, kernel, mass, total, cols, kept):
    pair_count, _, feat = rows.shape
    window = WINDOWS[1]
    own = operands(cols[chunk][0] for chunk, _, _ in segments(window))
    args = [in_vmem(x) for x in (rows, kernel, mass, total, *own)]
    return pl.pallas_call(
        functools.partial(mean_kernel, window, piece_counts(window, cols), wide_count),
        out_shape=pltpu.HBM(kept.shape, jnp.bfloat16),
        in_specs=[smem(), smem()] + [vmem()] * len(args) + [anywhere()],
        out_specs=anywhere(),
        scratch_shapes=[
            pltpu.VMEM((pair_count, BR, feat), jnp.bfloat16),
            pltpu.VMEM((pair_count, BR, LANES), jnp.float32),
            pltpu.VMEM((BR, feat), jnp.float32),
            pltpu.VMEM((BR, LANES), jnp.float32),
            pltpu.VMEM((pair_count, BR, feat), jnp.bfloat16),
            pltpu.SemaphoreType.DMA((pair_count,)),
        ],
        input_output_aliases={2 + len(args): 0},
        compiler_params=params(16),
        cost_estimate=estimate(pair_count, 128),
        name="means",
    )(me, in_hbm(pairs), *args, in_hbm(kept))


def weight_kernel(*refs):
    out_ref = refs[-1]
    mass = refs[0][...]
    for ref in refs[1:-1]:
        mass = mass + ref[...]
    weight = 1.0 / (1.0 + mass / BR)
    parts = BR // LANES
    for block in range(BLK_DEV):
        for part in range(parts):
            lanes = slice(part * LANES, (part + 1) * LANES)
            out_ref[block * parts + part : block * parts + part + 1] = weight[block : block + 1, lanes]


def block_weights(sums):
    out = pl.pallas_call(
        weight_kernel,
        out_shape=jax.ShapeDtypeStruct((BLK_DEV * BR // LANES, LANES), jnp.float32),
        in_specs=[vmem()] * len(sums),
        out_specs=vmem(),
        compiler_params=params(4),
        name="weights",
    )(*[in_vmem(x) for x in sums])
    return out.reshape(BLK_DEV * BR)


def hop(parts, step):
    count = lax.axis_size("narrow")
    perm = [(i, i ^ step) for i in range(count)]
    return [[lax.ppermute(piece, "narrow", perm) for piece in part] for part in parts]


def first_hops(part):
    parts = [part]
    step = lax.axis_size("narrow") // 2
    while step > 1:
        parts = parts + hop(parts, step)
        step //= 2
    return parts


def to_wide(pieces, apart):
    count = lax.axis_size("wide")
    return [
        lax.ppermute(piece, "wide", [(i, i ^ other) for i in range(count)])
        for piece, other in zip(pieces, apart)
    ]


def on_device(embeddings, pair_list):
    wide_count = lax.axis_size("wide")
    me = lax.axis_index("wide").astype(jnp.int32).reshape(1)
    pairs = pair_list.T
    pair_count = pairs.shape[1]
    capacity = max(2, 2 * pair_count // wide_count)
    feat = embeddings.shape[1]
    blocks = embeddings.reshape(BLK_DEV, BR, feat)
    apart = others(wide_count)
    lists = to_wide([pairs] * (wide_count - 1), apart[::-1])
    fixed = lax.optimization_barrier
    outgoing, row_slices = pack(me, pairs, lists, blocks, capacity)

    def pick(received, apart, chunk, places, *groups):
        start, size = CHUNKS[chunk]
        return select(me, pairs, own, received, tuple(apart), wide_count, places, start, size, groups)

    def halves(part):
        middle = pair_count // 2
        return [part[0][:middle], part[0][middle:]]

    half, middle = pair_count // 2, wide_count // 2
    rows = jnp.stack([part[0] for part in first_hops([row_slices])])
    received = to_wide(outgoing[0], apart)
    near = to_wide(outgoing[1][-1:], apart[-1:])
    rows, received, near, (kept, own) = fixed((rows, received, near, keep(me, pairs, blocks, wide_count)))
    own_a, whole_a = pick(received, apart, 0, (0, pair_count), 2, 1)
    cols_a = [own_a] + first_hops(whole_a)[1:]
    rows = [[rows], *hop([[rows]], 1)]
    came = dict(zip(apart, to_wide(outgoing[1][:-1], apart[:-1]) + near))
    early = {other: piece for other, piece in came.items() if other != middle}
    cols_b = first_hops(*pick(list(early.values()), early, 1, (0, half), 1))
    cols_a, rows, cols_b, came = fixed((cols_a, rows, cols_b, came))
    late_b, cols_a = fixed((pick(list(came.values()), came, 1, (half, half), 1), cols_a))
    late_b = first_hops(*late_b)
    cols_a = cols_a + hop([own_a] + [halves(part) for part in cols_a[1:]], 1)
    carry = first_window(rows, [cols_a])
    late_b, carry = fixed((late_b, carry))
    cols_b = [early + late for early, late in zip(cols_b, late_b)]
    cols_b = cols_b + hop(cols_b, 1)
    square, mass, total, sums = carry
    kernel, mass, row_sums, shares = last_window(
        me, pairs, rows, [cols_a, cols_b], square, mass, sums, wide_count
    )
    came = to_wide(shares[:-1], sum_order(wide_count))
    mean = means(me, wide_count, pairs, row_slices, kernel, mass, total, [cols_a, cols_b], kept)
    weights = block_weights([row_sums, shares[-1], *came])
    return weights, mean.reshape(BLK_DEV * BR, feat)


def solution(mesh):
    in_specs = (P(("groups", "wide"), "narrow"), P(("groups", "wide"), None))
    out_specs = (P(("groups", "wide")), P(("groups", "wide"), "narrow"))
    return jax.shard_map(
        on_device, mesh=mesh, in_specs=in_specs, out_specs=out_specs, check_vma=False
    )
```

```python
import functools

import jax
import jax.numpy as jnp
from jax import lax
from jax.experimental import pallas as pl
from jax.experimental.pallas import tpu as pltpu
from jax.sharding import PartitionSpec as P

F = 1024
BR = 512
BLK_DEV = 8
LANES = 128
CHUNKS = ((0, 304), (304, 208))
WINDOWS = ((0, 256), (256, 512))


def smem():
    return pl.BlockSpec(memory_space=pltpu.SMEM)


def vmem():
    return pl.BlockSpec(memory_space=pltpu.VMEM)


def anywhere():
    return pl.BlockSpec(memory_space=pl.ANY)


def in_vmem(x):
    return pltpu.with_memory_space_constraint(x, pltpu.VMEM)


def in_hbm(x):
    return pltpu.with_memory_space_constraint(x, pltpu.HBM)


def params(mebibytes):
    return pltpu.CompilerParams(vmem_limit_bytes=mebibytes * 1024 * 1024)


def others(wide_count):
    return range(wide_count - 1, 0, -1)


def pack_kernel(wide_count, pair_count, capacity, me_ref, pairs_ref, *refs):
    lists, blocks_ref = refs[: wide_count - 1], refs[wide_count - 1]
    *outs, rows_ref, sems = refs[wide_count:]
    me = me_ref[0]
    copies = []

    def send(source, target):
        copies.append(pltpu.make_async_copy(source, target, sems.at[len(copies)]))
        copies[-1].start()

    for chunk, (start, size) in enumerate(CHUNKS):
        for number, other in enumerate(others(wide_count)):
            asked = lists[list_order(wide_count).index(other)]
            picks = [jnp.int32(0)] * capacity
            count = jnp.int32(0)
            for pair in range(pair_count):
                col = asked[1, pair]
                mine = (col >> 3) == me
                for slot in range(capacity):
                    picks[slot] = jnp.where(mine & (count == slot), col & 7, picks[slot])
                count = count + mine.astype(jnp.int32)
            out = outs[chunk * (wide_count - 1) + number]
            for slot in range(capacity):
                send(blocks_ref.at[picks[slot], pl.ds(start, size)], out.at[slot])
    for place, pair in enumerate(in_order(wide_count, me_ref, pairs_ref)):
        send(blocks_ref.at[pairs_ref[0, pair] & 7], rows_ref.at[place])
    for copy in copies:
        copy.wait()


def in_order(wide_count, me_ref, pairs_ref):
    pair_count = pairs_ref.shape[1]
    far = [
        ((pairs_ref[1, pair] >> 3) ^ me_ref[0] == wide_count // 2).astype(jnp.int32)
        for pair in range(pair_count)
    ]
    place_near, place_far = jnp.int32(0), pair_count - sum(far)
    places = []
    for is_far in far:
        places.append(jnp.where(is_far == 1, place_far, place_near))
        place_near, place_far = place_near + 1 - is_far, place_far + is_far
    return [
        sum(jnp.where(at == place, pair, 0) for pair, at in enumerate(places))
        for place in range(pair_count)
    ]


def list_order(wide_count):
    middle = wide_count // 2
    return [other for other in range(1, wide_count) if other != middle] + [middle]


def sum_order(wide_count):
    return list_order(wide_count)[::-1]


def pack(me, pairs, lists, blocks, capacity):
    wide_count, pair_count = len(lists) + 1, pairs.shape[1]
    feat = blocks.shape[-1]
    shapes = [
        pltpu.VMEM((capacity, size, feat), blocks.dtype)
        for _, size in CHUNKS
        for _ in range(1, wide_count)
    ] + [pltpu.VMEM((pair_count, BR, feat), blocks.dtype)]
    copies = (len(shapes) - 1) * capacity + pair_count
    outs = pl.pallas_call(
        functools.partial(pack_kernel, wide_count, pair_count, capacity),
        out_shape=shapes,
        in_specs=[smem()] * (1 + wide_count) + [anywhere()],
        out_specs=[anywhere()] * len(shapes),
        scratch_shapes=[pltpu.SemaphoreType.DMA((copies,))],
        compiler_params=params(4),
        name="pack",
    )(me, in_hbm(pairs), *[lists[other - 1] for other in list_order(wide_count)], in_hbm(blocks))
    each = wide_count - 1
    return [outs[c * each : (c + 1) * each] for c in range(len(CHUNKS))], outs[-1]


def select_kernel(wide_count, apart, groups, first, start, me_ref, pairs_ref, own_ref, *refs):
    received, outs = refs[: len(apart)], refs[len(apart) :]
    pair_count = own_ref.shape[0]
    size = outs[0].shape[1]
    count = sum(ref.shape[0] for ref in outs[: groups[0]])
    owners = [pairs_ref[1, pair] >> 3 for pair in range(pair_count)]
    order = in_order(wide_count, me_ref, pairs_ref)
    for place in range(first, first + count):
        pair = order[place]
        owner = pairs_ref[1, pair] >> 3
        away = me_ref[0] ^ owner
        rank = jnp.int32(0)
        for before in range(pair_count):
            rank = rank + ((before < pair) & (owners[before] == owner)).astype(jnp.int32)
        targets, rest = [], outs
        for pieces in groups:
            targets.append(of_pair(rest[:pieces], place - first))
            rest = rest[pieces:]

        @pl.when(away == 0)
        def _():
            for out in targets:
                out[...] = own_ref[place, start : start + size]

        for number, other in enumerate(apart):

            @pl.when(away == other)
            def _():
                for out in targets:
                    out[...] = received[number][rank]


def select(me, pairs, own, received, apart, wide_count, places, start, size, groups):
    _, _, feat = own.shape
    first, count = places
    shapes = [
        pltpu.VMEM((count // pieces, size, feat), own.dtype)
        for pieces in groups
        for _ in range(pieces)
    ]
    outs = pl.pallas_call(
        functools.partial(select_kernel, wide_count, apart, groups, first, start),
        out_shape=shapes,
        in_specs=[smem(), smem()] + [vmem()] * (1 + len(received)),
        out_specs=[vmem()] * len(shapes),
        compiler_params=params(4),
        cost_estimate=nothing(),
        name="select",
    )(me, in_hbm(pairs), *[in_vmem(x) for x in (own, *received)])
    return take_parts(outs, groups)[0]


def nothing():
    return pl.CostEstimate(flops=0, transcendentals=0, bytes_accessed=0)


def tree(parts):
    while len(parts) > 1:
        half = len(parts) // 2
        parts = [parts[i] + parts[i + half] for i in range(half)]
    return parts[0]


def across(left, right):
    return lax.dot_general(
        left, right, (((1,), (1,)), ((), ())), preferred_element_type=jnp.float32
    )


def lane_sum(block):
    square = jnp.square(block.astype(jnp.float32))
    return sum(square[:, at : at + LANES] for at in range(0, square.shape[1], LANES))


def segments(window):
    low, high = window
    held = []
    for chunk, (start, size) in enumerate(CHUNKS):
        first, end = max(low, start), min(high, start + size)
        if first < end:
            held.append((chunk, first - start, end - first))
    return held


def scores(rows, cols, square):
    gram = tree([across(row, col) for row, col in zip(rows, cols)])
    other = jnp.sum(tree([lane_sum(col) for col in cols]).T, axis=0, keepdims=True)
    pieces, mass = [], None
    for at in range(0, gram.shape[1], LANES):
        here = slice(at, at + LANES)
        piece = jnp.exp((square + other[:, here] - 2.0 * gram[:, here]) * (-1.0 / F))
        mass = piece if mass is None else mass + piece
        pieces.append(piece)
    kernel = jnp.concatenate(pieces, axis=1) if len(pieces) > 1 else pieces[0]
    return kernel.astype(jnp.bfloat16), jnp.sum(kernel, axis=0, keepdims=True), mass


def take_parts(refs, counts):
    parts = []
    for count in counts:
        parts.append(refs[:count])
        refs = refs[count:]
    return parts, refs


def of_pair(part, pair):
    each = part[0].shape[0]
    return part[pair // each].at[pair % each]


def window_parts(counts, refs):
    half = len(counts[0]) // 2
    rows, refs = [ref.at[i] for ref in refs[:2] for i in range(half)], refs[2:]
    chunks = []
    for chunk_counts in counts:
        cols, refs = take_parts(refs, chunk_counts)
        chunks.append(cols)
    return rows, chunks


def own_columns(window, chunks, pair):
    held = segments(window)
    pieces = [of_pair(part, pair)[at : at + size] for part, (_, at, size) in zip(chunks, held)]
    return jnp.concatenate(pieces, axis=0) if len(pieces) > 1 else pieces[0]


def pair_parts(window, rows, chunks, pair):
    cols = [own_columns(window, [c[i] for c in chunks], pair) for i in range(len(rows))]
    return [part[pair] for part in rows], cols


def first_kernel(window, counts, *refs):
    square_ref, mass_ref, total_ref, sums_ref = refs[-4:]
    all_rows, chunks = window_parts(counts, refs)
    for pair in range(square_ref.shape[0]):
        rows, cols = pair_parts(window, all_rows, chunks, pair)
        square = jnp.sum(tree([lane_sum(row) for row in rows]), axis=1, keepdims=True)
        square = jnp.broadcast_to(square, (BR, LANES))
        kernel, sums, mass = scores(rows, cols, square)
        square_ref[pair] = square
        mass_ref[pair] = mass
        sums_ref[pair : pair + 1] = sums
        total_ref[pair] = jnp.dot(kernel, cols[0], preferred_element_type=jnp.float32)


def last_kernel(window, counts, wide_count, me_ref, pairs_ref, *refs):
    square_in, mass_in, sums_in = refs[-6 - wide_count : -3 - wide_count]
    kernel_ref, mass_ref, row_ref = refs[-3 - wide_count : -wide_count]
    shares = refs[-wide_count:]
    for ref in (row_ref, *shares):
        ref[...] = jnp.zeros_like(ref)
    all_rows, chunks = window_parts(counts, refs)
    order = in_order(wide_count, me_ref, pairs_ref)
    for place, pair in enumerate(order):
        rows, cols = pair_parts(window, all_rows, chunks, place)
        kernel, sums, mass = scores(rows, cols, square_in[place])
        kernel_ref[place] = kernel
        sums = jnp.concatenate([sums_in[place : place + 1], sums], axis=1)
        mass = mass_in[place] + mass
        mass_ref[place] = mass
        row_ref[pl.ds(pairs_ref[0, pair] & 7, 1)] += jnp.sum(mass.T, axis=0, keepdims=True)
        col = pairs_ref[1, pair]
        apart = (col >> 3) ^ me_ref[0]
        for other, ref in zip([*sum_order(wide_count), 0], shares):
            ref[pl.ds(col & 7, 1)] += jnp.where(apart == other, sums, 0.0)


def estimate(pair_count, size):
    return pl.CostEstimate(
        flops=2 * pair_count * BR * size * F,
        transcendentals=pair_count * BR * size,
        bytes_accessed=8 * 1024 * 1024,
    )


def piece_counts(window, cols):
    return tuple(tuple(len(part) for part in cols[chunk]) for chunk, _, _ in segments(window))


def operands(parts):
    return [piece for part in parts for piece in part]


def first_window(rows, cols):
    _, pair_count, _, feat = rows[0][0].shape
    window = WINDOWS[0]
    lanes = pltpu.VMEM((pair_count, BR, LANES), jnp.float32)
    total = pltpu.VMEM((pair_count, BR, feat), jnp.float32)
    args = operands(rows)
    for chunk, _, _ in segments(window):
        args += operands(cols[chunk])
    return pl.pallas_call(
        functools.partial(first_kernel, window, piece_counts(window, cols)),
        out_shape=[lanes, lanes, total, pltpu.VMEM((pair_count, window[1]), jnp.float32)],
        in_specs=[vmem()] * len(args),
        out_specs=[vmem()] * 4,
        compiler_params=params(16),
        cost_estimate=pl.CostEstimate(flops=0, transcendentals=0, bytes_accessed=0),
        name="first_window",
    )(*[in_vmem(x) for x in args])


def last_window(me, pairs, rows, cols, square, mass, sums, wide_count):
    pair_count = rows[0][0].shape[1]
    window = WINDOWS[1]
    size = window[1] - window[0]
    by_block = pltpu.VMEM((BLK_DEV, BR), jnp.float32)
    shapes = [
        pltpu.VMEM((pair_count, BR, size), jnp.bfloat16),
        pltpu.VMEM((pair_count, BR, LANES), jnp.float32),
    ] + [by_block] * (1 + wide_count)
    args = operands(rows)
    for chunk, _, _ in segments(window):
        args += operands(cols[chunk])
    args += [square, mass, sums]
    kernel, mass, row_sums, *shares = pl.pallas_call(
        functools.partial(last_kernel, window, piece_counts(window, cols), wide_count),
        out_shape=shapes,
        in_specs=[smem(), smem()] + [vmem()] * len(args),
        out_specs=[vmem()] * len(shapes),
        compiler_params=params(16),
        cost_estimate=estimate(pair_count, size),
        name="last_window",
    )(me, in_hbm(pairs), *[in_vmem(x) for x in args])
    return kernel, mass, row_sums, shares


def keep_kernel(wide_count, me_ref, pairs_ref, block_ref, blocks_ref, out_ref, own_ref, sems):
    here = pl.program_id(0)

    def copies():
        for place, pair in enumerate(in_order(wide_count, me_ref, pairs_ref)):
            source = blocks_ref.at[pairs_ref[1, pair] & 7]
            yield pltpu.make_async_copy(source, own_ref.at[place], sems.at[place])

    @pl.when(here == 0)
    def _():
        for copy in copies():
            copy.start()

    out_ref[...] = block_ref[...]

    @pl.when(here == pl.num_programs(0) - 1)
    def _():
        for copy in copies():
            copy.wait()


def keep(me, pairs, blocks, wide_count):
    pair_count = pairs.shape[1]
    block = pl.BlockSpec((1, *blocks.shape[1:]), lambda k: (k, 0, 0))
    return pl.pallas_call(
        functools.partial(keep_kernel, wide_count),
        out_shape=[
            pltpu.HBM(blocks.shape, blocks.dtype),
            pltpu.VMEM((pair_count, *blocks.shape[1:]), blocks.dtype),
        ],
        grid=(blocks.shape[0],),
        in_specs=[smem(), smem(), block, anywhere()],
        out_specs=[block, anywhere()],
        scratch_shapes=[pltpu.SemaphoreType.DMA((pair_count,))],
        compiler_params=params(4),
        name="keep",
    )(me, in_hbm(pairs), in_hbm(blocks), in_hbm(blocks))


def mean_kernel(window, counts, wide_count, me_ref, local_ref, rows_ref, kernel_ref, mass_ref, total_ref, *refs):
    *refs, _, out_ref, part, weight, total, mass, made, sems = refs
    chunks = []
    for chunk, _, _ in segments(window):
        (own,), refs = take_parts(refs, counts[len(chunks)][:1])
        chunks.append(own)
    pair_count, _, feat = rows_ref.shape
    local = [local_ref[0, pair] & 7 for pair in in_order(wide_count, me_ref, local_ref)]

    def copy(pair):
        return pltpu.make_async_copy(made.at[pair], out_ref.at[local[pair]], sems.at[pair])

    firsts = []
    for pair in range(pair_count):
        sums = total_ref[pair] + jnp.dot(
            kernel_ref[pair], own_columns(window, chunks, pair), preferred_element_type=jnp.float32
        )
        part[pair] = sums.astype(jnp.bfloat16)
        weight[pair] = jnp.broadcast_to(
            jnp.sum(mass_ref[pair], axis=1, keepdims=True), (BR, LANES)
        )
        same = [local[other] == local[pair] for other in range(pair)]
        firsts.append(jnp.logical_not(functools.reduce(jnp.logical_or, same, jnp.bool_(False))))
    for pair in range(pair_count):

        @pl.when(firsts[pair])
        def _():
            total[...] = rows_ref[pair].astype(jnp.float32) + part[pair].astype(jnp.float32)
            mass[...] = 1.0 + weight[pair]
            for other in range(pair + 1, pair_count):

                @pl.when(local[other] == local[pair])
                def _():
                    total[...] += part[other].astype(jnp.float32)
                    mass[...] += weight[other]

            scale = 1.0 / mass[...]
            for at in range(0, feat, LANES):
                lanes = slice(at, at + LANES)
                made[pair, :, lanes] = (total[:, lanes] * scale).astype(jnp.bfloat16)
            copy(pair).start()

    for pair in range(pair_count):

        @pl.when(firsts[pair])
        def _():
            copy(pair).wait()


def means(me, wide_count, pairs, rows, kernel, mass, total, cols, kept):
    pair_count, _, feat = rows.shape
    window = WINDOWS[1]
    own = operands(cols[chunk][0] for chunk, _, _ in segments(window))
    args = [in_vmem(x) for x in (rows, kernel, mass, total, *own)]
    return pl.pallas_call(
        functools.partial(mean_kernel, window, piece_counts(window, cols), wide_count),
        out_shape=pltpu.HBM(kept.shape, jnp.bfloat16),
        in_specs=[smem(), smem()] + [vmem()] * len(args) + [anywhere()],
        out_specs=anywhere(),
        scratch_shapes=[
            pltpu.VMEM((pair_count, BR, feat), jnp.bfloat16),
            pltpu.VMEM((pair_count, BR, LANES), jnp.float32),
            pltpu.VMEM((BR, feat), jnp.float32),
            pltpu.VMEM((BR, LANES), jnp.float32),
            pltpu.VMEM((pair_count, BR, feat), jnp.bfloat16),
            pltpu.SemaphoreType.DMA((pair_count,)),
        ],
        input_output_aliases={2 + len(args): 0},
        compiler_params=params(16),
        cost_estimate=estimate(pair_count, 128),
        name="means",
    )(me, in_hbm(pairs), *args, in_hbm(kept))


def weight_kernel(*refs):
    out_ref = refs[-1]
    mass = refs[0][...]
    for ref in refs[1:-1]:
        mass = mass + ref[...]
    weight = 1.0 / (1.0 + mass / BR)
    parts = BR // LANES
    for block in range(BLK_DEV):
        for part in range(parts):
            lanes = slice(part * LANES, (part + 1) * LANES)
            out_ref[block * parts + part : block * parts + part + 1] = weight[block : block + 1, lanes]


def block_weights(sums):
    out = pl.pallas_call(
        weight_kernel,
        out_shape=jax.ShapeDtypeStruct((BLK_DEV * BR // LANES, LANES), jnp.float32),
        in_specs=[vmem()] * len(sums),
        out_specs=vmem(),
        compiler_params=params(4),
        name="weights",
    )(*[in_vmem(x) for x in sums])
    return out.reshape(BLK_DEV * BR)


def hop(parts, step):
    count = lax.axis_size("narrow")
    perm = [(i, i ^ step) for i in range(count)]
    return [[lax.ppermute(piece, "narrow", perm) for piece in part] for part in parts]


def first_hops(part):
    parts = [part]
    step = lax.axis_size("narrow") // 2
    while step > 1:
        parts = parts + hop(parts, step)
        step //= 2
    return parts


def to_wide(pieces, apart):
    count = lax.axis_size("wide")
    return [
        lax.ppermute(piece, "wide", [(i, i ^ other) for i in range(count)])
        for piece, other in zip(pieces, apart)
    ]


def on_device(embeddings, pair_list):
    wide_count = lax.axis_size("wide")
    me = lax.axis_index("wide").astype(jnp.int32).reshape(1)
    pairs = pair_list.T
    pair_count = pairs.shape[1]
    capacity = max(2, 2 * pair_count // wide_count)
    feat = embeddings.shape[1]
    blocks = embeddings.reshape(BLK_DEV, BR, feat)
    apart = others(wide_count)
    lists = to_wide([pairs] * (wide_count - 1), apart[::-1])
    fixed = lax.optimization_barrier
    outgoing, row_slices = pack(me, pairs, lists, blocks, capacity)

    def pick(received, apart, chunk, places, *groups):
        start, size = CHUNKS[chunk]
        return select(me, pairs, own, received, tuple(apart), wide_count, places, start, size, groups)

    def halves(part):
        middle = pair_count // 2
        return [part[0][:middle], part[0][middle:]]

    half, middle = pair_count // 2, wide_count // 2
    rows = jnp.stack([part[0] for part in first_hops([row_slices])])
    received = to_wide(outgoing[0], apart)
    near = to_wide(outgoing[1][-1:], apart[-1:])
    rows, received, near, (kept, own) = fixed((rows, received, near, keep(me, pairs, blocks, wide_count)))
    own_a, whole_a = pick(received, apart, 0, (0, pair_count), 2, 1)
    cols_a = [own_a] + first_hops(whole_a)[1:]
    rows = [[rows], *hop([[rows]], 1)]
    came = dict(zip(apart, to_wide(outgoing[1][:-1], apart[:-1]) + near))
    early = {other: piece for other, piece in came.items() if other != middle}
    cols_b = first_hops(*pick(list(early.values()), early, 1, (0, half), 1))
    cols_a, rows, cols_b, came = fixed((cols_a, rows, cols_b, came))
    late_b, cols_a = fixed((pick(list(came.values()), came, 1, (half, half), 1), cols_a))
    late_b = first_hops(*late_b)
    cols_a = cols_a + hop([own_a] + [halves(part) for part in cols_a[1:]], 1)
    carry = first_window(rows, [cols_a])
    late_b, carry = fixed((late_b, carry))
    cols_b = [early + late for early, late in zip(cols_b, late_b)]
    cols_b = cols_b + hop(cols_b, 1)
    square, mass, total, sums = carry
    kernel, mass, row_sums, shares = last_window(
        me, pairs, rows, [cols_a, cols_b], square, mass, sums, wide_count
    )
    came = to_wide(shares[:-1], sum_order(wide_count))
    mean = means(me, wide_count, pairs, row_slices, kernel, mass, total, [cols_a, cols_b], kept)
    weights = block_weights([row_sums, shares[-1], *came])
    return weights, mean.reshape(BLK_DEV * BR, feat)


def solution(mesh):
    in_specs = (P(("groups", "wide"), "narrow"), P(("groups", "wide"), None))
    out_specs = (P(("groups", "wide")), P(("groups", "wide"), "narrow"))
    return jax.shard_map(
        on_device, mesh=mesh, in_specs=in_specs, out_specs=out_specs, check_vma=False
    )
```

```python
import functools

import jax
import jax.numpy as jnp
from jax import lax
from jax.experimental import pallas as pl
from jax.experimental.pallas import tpu as pltpu
from jax.sharding import PartitionSpec as P

F = 1024
BR = 512
BLK_DEV = 8
LANES = 128
CHUNKS = ((0, 320), (320, 192))
WINDOWS = ((0, 256), (256, 512))


def smem():
    return pl.BlockSpec(memory_space=pltpu.SMEM)


def vmem():
    return pl.BlockSpec(memory_space=pltpu.VMEM)


def anywhere():
    return pl.BlockSpec(memory_space=pl.ANY)


def in_vmem(x):
    return pltpu.with_memory_space_constraint(x, pltpu.VMEM)


def in_hbm(x):
    return pltpu.with_memory_space_constraint(x, pltpu.HBM)


def params(mebibytes):
    return pltpu.CompilerParams(vmem_limit_bytes=mebibytes * 1024 * 1024)


def others(wide_count):
    return range(wide_count - 1, 0, -1)


def pack_kernel(wide_count, pair_count, capacity, me_ref, pairs_ref, *refs):
    lists, blocks_ref = refs[: wide_count - 1], refs[wide_count - 1]
    *outs, rows_ref, sems = refs[wide_count:]
    me = me_ref[0]
    copies = []

    def send(source, target):
        copies.append(pltpu.make_async_copy(source, target, sems.at[len(copies)]))
        copies[-1].start()

    for chunk, (start, size) in enumerate(CHUNKS):
        for number, other in enumerate(others(wide_count)):
            asked = lists[list_order(wide_count).index(other)]
            picks = [jnp.int32(0)] * capacity
            count = jnp.int32(0)
            for pair in range(pair_count):
                col = asked[1, pair]
                mine = (col >> 3) == me
                for slot in range(capacity):
                    picks[slot] = jnp.where(mine & (count == slot), col & 7, picks[slot])
                count = count + mine.astype(jnp.int32)
            out = outs[chunk * (wide_count - 1) + number]
            for slot in range(capacity):
                send(blocks_ref.at[picks[slot], pl.ds(start, size)], out.at[slot])
    for place, pair in enumerate(in_order(wide_count, me_ref, pairs_ref)):
        send(blocks_ref.at[pairs_ref[0, pair] & 7], rows_ref.at[place])
    for copy in copies:
        copy.wait()


def in_order(wide_count, me_ref, pairs_ref):
    pair_count = pairs_ref.shape[1]
    far = [
        ((pairs_ref[1, pair] >> 3) ^ me_ref[0] == wide_count - 1).astype(jnp.int32)
        for pair in range(pair_count)
    ]
    place_near, place_far = jnp.int32(0), pair_count - sum(far)
    places = []
    for is_far in far:
        places.append(jnp.where(is_far == 1, place_far, place_near))
        place_near, place_far = place_near + 1 - is_far, place_far + is_far
    return [
        sum(jnp.where(at == place, pair, 0) for pair, at in enumerate(places))
        for place in range(pair_count)
    ]


def list_order(wide_count):
    middle = wide_count // 2
    return [other for other in range(1, wide_count) if other != middle] + [middle]


def sum_order(wide_count):
    return list_order(wide_count)[::-1]


def pack(me, pairs, lists, blocks, capacity):
    wide_count, pair_count = len(lists) + 1, pairs.shape[1]
    feat = blocks.shape[-1]
    shapes = [
        pltpu.VMEM((capacity, size, feat), blocks.dtype)
        for _, size in CHUNKS
        for _ in range(1, wide_count)
    ] + [pltpu.VMEM((pair_count, BR, feat), blocks.dtype)]
    copies = (len(shapes) - 1) * capacity + pair_count
    outs = pl.pallas_call(
        functools.partial(pack_kernel, wide_count, pair_count, capacity),
        out_shape=shapes,
        in_specs=[smem()] * (1 + wide_count) + [anywhere()],
        out_specs=[anywhere()] * len(shapes),
        scratch_shapes=[pltpu.SemaphoreType.DMA((copies,))],
        compiler_params=params(4),
        name="pack",
    )(me, in_hbm(pairs), *[lists[other - 1] for other in list_order(wide_count)], in_hbm(blocks))
    each = wide_count - 1
    return [outs[c * each : (c + 1) * each] for c in range(len(CHUNKS))], outs[-1]


def select_kernel(wide_count, apart, groups, first, start, me_ref, pairs_ref, own_ref, *refs):
    received, outs = refs[: len(apart)], refs[len(apart) :]
    pair_count = own_ref.shape[0]
    size = outs[0].shape[1]
    count = sum(ref.shape[0] for ref in outs[: groups[0]])
    owners = [pairs_ref[1, pair] >> 3 for pair in range(pair_count)]
    order = in_order(wide_count, me_ref, pairs_ref)
    for place in range(first, first + count):
        pair = order[place]
        owner = pairs_ref[1, pair] >> 3
        away = me_ref[0] ^ owner
        rank = jnp.int32(0)
        for before in range(pair_count):
            rank = rank + ((before < pair) & (owners[before] == owner)).astype(jnp.int32)
        targets, rest = [], outs
        for pieces in groups:
            targets.append(of_pair(rest[:pieces], place - first))
            rest = rest[pieces:]

        @pl.when(away == 0)
        def _():
            for out in targets:
                out[...] = own_ref[place, start : start + size]

        for number, other in enumerate(apart):

            @pl.when(away == other)
            def _():
                for out in targets:
                    out[...] = received[number][rank]


def select(me, pairs, own, received, apart, wide_count, places, start, size, groups):
    _, _, feat = own.shape
    first, count = places
    shapes = [
        pltpu.VMEM((count // pieces, size, feat), own.dtype)
        for pieces in groups
        for _ in range(pieces)
    ]
    outs = pl.pallas_call(
        functools.partial(select_kernel, wide_count, apart, groups, first, start),
        out_shape=shapes,
        in_specs=[smem(), smem()] + [vmem()] * (1 + len(received)),
        out_specs=[vmem()] * len(shapes),
        compiler_params=params(4),
        cost_estimate=nothing(),
        name="select",
    )(me, in_hbm(pairs), *[in_vmem(x) for x in (own, *received)])
    return take_parts(outs, groups)[0]


def nothing():
    return pl.CostEstimate(flops=0, transcendentals=0, bytes_accessed=0)


def tree(parts):
    while len(parts) > 1:
        half = len(parts) // 2
        parts = [parts[i] + parts[i + half] for i in range(half)]
    return parts[0]


def across(left, right):
    return lax.dot_general(
        left, right, (((1,), (1,)), ((), ())), preferred_element_type=jnp.float32
    )


def lane_sum(block):
    square = jnp.square(block.astype(jnp.float32))
    return sum(square[:, at : at + LANES] for at in range(0, square.shape[1], LANES))


def segments(window):
    low, high = window
    held = []
    for chunk, (start, size) in enumerate(CHUNKS):
        first, end = max(low, start), min(high, start + size)
        if first < end:
            held.append((chunk, first - start, end - first))
    return held


def scores(rows, cols, square):
    gram = tree([across(row, col) for row, col in zip(rows, cols)])
    other = jnp.sum(tree([lane_sum(col) for col in cols]).T, axis=0, keepdims=True)
    pieces, mass = [], None
    for at in range(0, gram.shape[1], LANES):
        here = slice(at, at + LANES)
        piece = jnp.exp((square + other[:, here] - 2.0 * gram[:, here]) * (-1.0 / F))
        mass = piece if mass is None else mass + piece
        pieces.append(piece)
    kernel = jnp.concatenate(pieces, axis=1) if len(pieces) > 1 else pieces[0]
    return kernel.astype(jnp.bfloat16), jnp.sum(kernel, axis=0, keepdims=True), mass


def take_parts(refs, counts):
    parts = []
    for count in counts:
        parts.append(refs[:count])
        refs = refs[count:]
    return parts, refs


def of_pair(part, pair):
    each = part[0].shape[0]
    return part[pair // each].at[pair % each]


def window_parts(counts, refs):
    half = len(counts[0]) // 2
    rows, refs = [ref.at[i] for ref in refs[:2] for i in range(half)], refs[2:]
    chunks = []
    for chunk_counts in counts:
        cols, refs = take_parts(refs, chunk_counts)
        chunks.append(cols)
    return rows, chunks


def own_columns(window, chunks, pair):
    held = segments(window)
    pieces = [of_pair(part, pair)[at : at + size] for part, (_, at, size) in zip(chunks, held)]
    return jnp.concatenate(pieces, axis=0) if len(pieces) > 1 else pieces[0]


def pair_parts(window, rows, chunks, pair):
    cols = [own_columns(window, [c[i] for c in chunks], pair) for i in range(len(rows))]
    return [part[pair] for part in rows], cols


def first_kernel(window, counts, *refs):
    square_ref, mass_ref, total_ref, sums_ref = refs[-4:]
    all_rows, chunks = window_parts(counts, refs)
    for pair in range(square_ref.shape[0]):
        rows, cols = pair_parts(window, all_rows, chunks, pair)
        square = jnp.sum(tree([lane_sum(row) for row in rows]), axis=1, keepdims=True)
        square = jnp.broadcast_to(square, (BR, LANES))
        kernel, sums, mass = scores(rows, cols, square)
        square_ref[pair] = square
        mass_ref[pair] = mass
        sums_ref[pair : pair + 1] = sums
        total_ref[pair] = jnp.dot(kernel, cols[0], preferred_element_type=jnp.float32)


def last_kernel(window, counts, wide_count, me_ref, pairs_ref, *refs):
    square_in, mass_in, sums_in = refs[-6 - wide_count : -3 - wide_count]
    kernel_ref, mass_ref, row_ref = refs[-3 - wide_count : -wide_count]
    shares = refs[-wide_count:]
    for ref in (row_ref, *shares):
        ref[...] = jnp.zeros_like(ref)
    all_rows, chunks = window_parts(counts, refs)
    order = in_order(wide_count, me_ref, pairs_ref)
    for place, pair in enumerate(order):
        rows, cols = pair_parts(window, all_rows, chunks, place)
        kernel, sums, mass = scores(rows, cols, square_in[place])
        kernel_ref[place] = kernel
        sums = jnp.concatenate([sums_in[place : place + 1], sums], axis=1)
        mass = mass_in[place] + mass
        mass_ref[place] = mass
        row_ref[pl.ds(pairs_ref[0, pair] & 7, 1)] += jnp.sum(mass.T, axis=0, keepdims=True)
        col = pairs_ref[1, pair]
        apart = (col >> 3) ^ me_ref[0]
        for other, ref in zip([*sum_order(wide_count), 0], shares):
            ref[pl.ds(col & 7, 1)] += jnp.where(apart == other, sums, 0.0)


def estimate(pair_count, size):
    return pl.CostEstimate(
        flops=2 * pair_count * BR * size * F,
        transcendentals=pair_count * BR * size,
        bytes_accessed=8 * 1024 * 1024,
    )


def piece_counts(window, cols):
    return tuple(tuple(len(part) for part in cols[chunk]) for chunk, _, _ in segments(window))


def operands(parts):
    return [piece for part in parts for piece in part]


def first_window(rows, cols):
    _, pair_count, _, feat = rows[0][0].shape
    window = WINDOWS[0]
    lanes = pltpu.VMEM((pair_count, BR, LANES), jnp.float32)
    total = pltpu.VMEM((pair_count, BR, feat), jnp.float32)
    args = operands(rows)
    for chunk, _, _ in segments(window):
        args += operands(cols[chunk])
    return pl.pallas_call(
        functools.partial(first_kernel, window, piece_counts(window, cols)),
        out_shape=[lanes, lanes, total, pltpu.VMEM((pair_count, window[1]), jnp.float32)],
        in_specs=[vmem()] * len(args),
        out_specs=[vmem()] * 4,
        compiler_params=params(16),
        cost_estimate=pl.CostEstimate(flops=0, transcendentals=0, bytes_accessed=0),
        name="first_window",
    )(*[in_vmem(x) for x in args])


def last_window(me, pairs, rows, cols, square, mass, sums, wide_count):
    pair_count = rows[0][0].shape[1]
    window = WINDOWS[1]
    size = window[1] - window[0]
    by_block = pltpu.VMEM((BLK_DEV, BR), jnp.float32)
    shapes = [
        pltpu.VMEM((pair_count, BR, size), jnp.bfloat16),
        pltpu.VMEM((pair_count, BR, LANES), jnp.float32),
    ] + [by_block] * (1 + wide_count)
    args = operands(rows)
    for chunk, _, _ in segments(window):
        args += operands(cols[chunk])
    args += [square, mass, sums]
    kernel, mass, row_sums, *shares = pl.pallas_call(
        functools.partial(last_kernel, window, piece_counts(window, cols), wide_count),
        out_shape=shapes,
        in_specs=[smem(), smem()] + [vmem()] * len(args),
        out_specs=[vmem()] * len(shapes),
        compiler_params=params(16),
        cost_estimate=estimate(pair_count, size),
        name="last_window",
    )(me, in_hbm(pairs), *[in_vmem(x) for x in args])
    return kernel, mass, row_sums, shares


def keep_kernel(wide_count, me_ref, pairs_ref, block_ref, blocks_ref, out_ref, own_ref, sems):
    here = pl.program_id(0)

    def copies():
        for place, pair in enumerate(in_order(wide_count, me_ref, pairs_ref)):
            source = blocks_ref.at[pairs_ref[1, pair] & 7]
            yield pltpu.make_async_copy(source, own_ref.at[place], sems.at[place])

    @pl.when(here == 0)
    def _():
        for copy in copies():
            copy.start()

    out_ref[...] = block_ref[...]

    @pl.when(here == pl.num_programs(0) - 1)
    def _():
        for copy in copies():
            copy.wait()


def keep(me, pairs, blocks, wide_count):
    pair_count = pairs.shape[1]
    block = pl.BlockSpec((1, *blocks.shape[1:]), lambda k: (k, 0, 0))
    return pl.pallas_call(
        functools.partial(keep_kernel, wide_count),
        out_shape=[
            pltpu.HBM(blocks.shape, blocks.dtype),
            pltpu.VMEM((pair_count, *blocks.shape[1:]), blocks.dtype),
        ],
        grid=(blocks.shape[0],),
        in_specs=[smem(), smem(), block, anywhere()],
        out_specs=[block, anywhere()],
        scratch_shapes=[pltpu.SemaphoreType.DMA((pair_count,))],
        compiler_params=params(4),
        name="keep",
    )(me, in_hbm(pairs), in_hbm(blocks), in_hbm(blocks))


def mean_kernel(window, counts, wide_count, me_ref, local_ref, rows_ref, kernel_ref, mass_ref, total_ref, *refs):
    *refs, _, out_ref, part, weight, total, mass, made, sems = refs
    chunks = []
    for chunk, _, _ in segments(window):
        (own,), refs = take_parts(refs, counts[len(chunks)][:1])
        chunks.append(own)
    pair_count, _, feat = rows_ref.shape
    local = [local_ref[0, pair] & 7 for pair in in_order(wide_count, me_ref, local_ref)]

    def copy(pair):
        return pltpu.make_async_copy(made.at[pair], out_ref.at[local[pair]], sems.at[pair])

    firsts = []
    for pair in range(pair_count):
        sums = total_ref[pair] + jnp.dot(
            kernel_ref[pair], own_columns(window, chunks, pair), preferred_element_type=jnp.float32
        )
        part[pair] = sums.astype(jnp.bfloat16)
        weight[pair] = jnp.broadcast_to(
            jnp.sum(mass_ref[pair], axis=1, keepdims=True), (BR, LANES)
        )
        same = [local[other] == local[pair] for other in range(pair)]
        firsts.append(jnp.logical_not(functools.reduce(jnp.logical_or, same, jnp.bool_(False))))
    for pair in range(pair_count):

        @pl.when(firsts[pair])
        def _():
            total[...] = rows_ref[pair].astype(jnp.float32) + part[pair].astype(jnp.float32)
            mass[...] = 1.0 + weight[pair]
            for other in range(pair + 1, pair_count):

                @pl.when(local[other] == local[pair])
                def _():
                    total[...] += part[other].astype(jnp.float32)
                    mass[...] += weight[other]

            scale = 1.0 / mass[...]
            for at in range(0, feat, LANES):
                lanes = slice(at, at + LANES)
                made[pair, :, lanes] = (total[:, lanes] * scale).astype(jnp.bfloat16)
            copy(pair).start()

    for pair in range(pair_count):

        @pl.when(firsts[pair])
        def _():
            copy(pair).wait()


def means(me, wide_count, pairs, rows, kernel, mass, total, cols, kept):
    pair_count, _, feat = rows.shape
    window = WINDOWS[1]
    own = operands(cols[chunk][0] for chunk, _, _ in segments(window))
    args = [in_vmem(x) for x in (rows, kernel, mass, total, *own)]
    return pl.pallas_call(
        functools.partial(mean_kernel, window, piece_counts(window, cols), wide_count),
        out_shape=pltpu.HBM(kept.shape, jnp.bfloat16),
        in_specs=[smem(), smem()] + [vmem()] * len(args) + [anywhere()],
        out_specs=anywhere(),
        scratch_shapes=[
            pltpu.VMEM((pair_count, BR, feat), jnp.bfloat16),
            pltpu.VMEM((pair_count, BR, LANES), jnp.float32),
            pltpu.VMEM((BR, feat), jnp.float32),
            pltpu.VMEM((BR, LANES), jnp.float32),
            pltpu.VMEM((pair_count, BR, feat), jnp.bfloat16),
            pltpu.SemaphoreType.DMA((pair_count,)),
        ],
        input_output_aliases={2 + len(args): 0},
        compiler_params=params(16),
        cost_estimate=estimate(pair_count, 128),
        name="means",
    )(me, in_hbm(pairs), *args, in_hbm(kept))


def weight_kernel(*refs):
    out_ref = refs[-1]
    mass = refs[0][...]
    for ref in refs[1:-1]:
        mass = mass + ref[...]
    weight = 1.0 / (1.0 + mass / BR)
    parts = BR // LANES
    for block in range(BLK_DEV):
        for part in range(parts):
            lanes = slice(part * LANES, (part + 1) * LANES)
            out_ref[block * parts + part : block * parts + part + 1] = weight[block : block + 1, lanes]


def block_weights(sums):
    out = pl.pallas_call(
        weight_kernel,
        out_shape=jax.ShapeDtypeStruct((BLK_DEV * BR // LANES, LANES), jnp.float32),
        in_specs=[vmem()] * len(sums),
        out_specs=vmem(),
        compiler_params=params(4),
        name="weights",
    )(*[in_vmem(x) for x in sums])
    return out.reshape(BLK_DEV * BR)


def hop(parts, step):
    count = lax.axis_size("narrow")
    perm = [(i, i ^ step) for i in range(count)]
    return [[lax.ppermute(piece, "narrow", perm) for piece in part] for part in parts]


def first_hops(part):
    parts = [part]
    step = lax.axis_size("narrow") // 2
    while step > 1:
        parts = parts + hop(parts, step)
        step //= 2
    return parts


def to_wide(pieces, apart):
    count = lax.axis_size("wide")
    return [
        lax.ppermute(piece, "wide", [(i, i ^ other) for i in range(count)])
        for piece, other in zip(pieces, apart)
    ]


def on_device(embeddings, pair_list):
    wide_count = lax.axis_size("wide")
    me = lax.axis_index("wide").astype(jnp.int32).reshape(1)
    pairs = pair_list.T
    pair_count = pairs.shape[1]
    capacity = max(2, 2 * pair_count // wide_count)
    feat = embeddings.shape[1]
    blocks = embeddings.reshape(BLK_DEV, BR, feat)
    apart = others(wide_count)
    lists = to_wide([pairs] * (wide_count - 1), apart[::-1])
    fixed = lax.optimization_barrier
    outgoing, row_slices = pack(me, pairs, lists, blocks, capacity)

    def pick(received, apart, chunk, places, *groups):
        start, size = CHUNKS[chunk]
        return select(me, pairs, own, received, tuple(apart), wide_count, places, start, size, groups)

    def halves(part):
        middle = pair_count // 2
        return [part[0][:middle], part[0][middle:]]

    half, far = pair_count // 2, apart[0]
    rows = jnp.stack([part[0] for part in first_hops([row_slices])])
    received = to_wide(outgoing[0], apart)
    near = to_wide(outgoing[1][-1:], apart[-1:])
    rows, received, near, (kept, own) = fixed((rows, received, near, keep(me, pairs, blocks, wide_count)))
    own_a, whole_a = pick(received, apart, 0, (0, pair_count), 2, 1)
    cols_a = [own_a] + first_hops(whole_a)[1:]
    rows = [[rows], *hop([[rows]], 1)]
    later = [*apart[1:-1], far]
    pieces = [*outgoing[1][1:-1], outgoing[1][0]]
    came = dict(zip([*later, apart[-1]], to_wide(pieces, later) + near))
    early = {other: piece for other, piece in came.items() if other != far}
    cols_b = first_hops(*pick(list(early.values()), early, 1, (0, half), 1))
    cols_a, rows, cols_b, came = fixed((cols_a, rows, cols_b, came))
    late_b, cols_a = fixed((pick(list(came.values()), came, 1, (half, half), 1), cols_a))
    late_b = first_hops(*late_b)
    cols_a = cols_a + hop([own_a] + [halves(part) for part in cols_a[1:]], 1)
    carry = first_window(rows, [cols_a])
    late_b, carry = fixed((late_b, carry))
    cols_b = [early + late for early, late in zip(cols_b, late_b)]
    cols_b = cols_b + hop(cols_b, 1)
    square, mass, total, sums = carry
    kernel, mass, row_sums, shares = last_window(
        me, pairs, rows, [cols_a, cols_b], square, mass, sums, wide_count
    )
    came = to_wide(shares[:-1], sum_order(wide_count))
    mean = means(me, wide_count, pairs, row_slices, kernel, mass, total, [cols_a, cols_b], kept)
    weights = block_weights([row_sums, shares[-1], *came])
    return weights, mean.reshape(BLK_DEV * BR, feat)


def solution(mesh):
    in_specs = (P(("groups", "wide"), "narrow"), P(("groups", "wide"), None))
    out_specs = (P(("groups", "wide")), P(("groups", "wide"), "narrow"))
    return jax.shard_map(
        on_device, mesh=mesh, in_specs=in_specs, out_specs=out_specs, check_vma=False
    )
```

```python
import functools

import jax
import jax.numpy as jnp
from jax import lax
from jax.experimental import pallas as pl
from jax.experimental.pallas import tpu as pltpu
from jax.sharding import PartitionSpec as P

F = 1024
BR = 512
BLK_DEV = 8
LANES = 128
CHUNKS = ((0, 336), (336, 176))
WINDOWS = ((0, 256), (256, 512))


def smem():
    return pl.BlockSpec(memory_space=pltpu.SMEM)


def vmem():
    return pl.BlockSpec(memory_space=pltpu.VMEM)


def anywhere():
    return pl.BlockSpec(memory_space=pl.ANY)


def in_vmem(x):
    return pltpu.with_memory_space_constraint(x, pltpu.VMEM)


def in_hbm(x):
    return pltpu.with_memory_space_constraint(x, pltpu.HBM)


def params(mebibytes):
    return pltpu.CompilerParams(vmem_limit_bytes=mebibytes * 1024 * 1024)


def others(wide_count):
    return range(wide_count - 1, 0, -1)


def pack_kernel(wide_count, pair_count, capacity, me_ref, pairs_ref, *refs):
    lists, blocks_ref = refs[: wide_count - 1], refs[wide_count - 1]
    *outs, rows_ref, sems = refs[wide_count:]
    me = me_ref[0]
    copies = []

    def send(source, target):
        copies.append(pltpu.make_async_copy(source, target, sems.at[len(copies)]))
        copies[-1].start()

    for chunk, (start, size) in enumerate(CHUNKS):
        for number, other in enumerate(others(wide_count)):
            asked = lists[list_order(wide_count).index(other)]
            picks = [jnp.int32(0)] * capacity
            count = jnp.int32(0)
            for pair in range(pair_count):
                col = asked[1, pair]
                mine = (col >> 3) == me
                for slot in range(capacity):
                    picks[slot] = jnp.where(mine & (count == slot), col & 7, picks[slot])
                count = count + mine.astype(jnp.int32)
            out = outs[chunk * (wide_count - 1) + number]
            for slot in range(capacity):
                send(blocks_ref.at[picks[slot], pl.ds(start, size)], out.at[slot])
    for pair in range(pair_count):
        send(blocks_ref.at[pairs_ref[0, pair] & 7], rows_ref.at[pair])
    for copy in copies:
        copy.wait()


def list_order(wide_count):
    middle = wide_count // 2
    return [other for other in range(1, wide_count) if other != middle] + [middle]


def pack(me, pairs, lists, blocks, capacity):
    wide_count, pair_count = len(lists) + 1, pairs.shape[1]
    feat = blocks.shape[-1]
    shapes = [
        pltpu.VMEM((capacity, size, feat), blocks.dtype)
        for _, size in CHUNKS
        for _ in range(1, wide_count)
    ] + [pltpu.VMEM((pair_count, BR, feat), blocks.dtype)]
    copies = (len(shapes) - 1) * capacity + pair_count
    outs = pl.pallas_call(
        functools.partial(pack_kernel, wide_count, pair_count, capacity),
        out_shape=shapes,
        in_specs=[smem()] * (1 + wide_count) + [anywhere()],
        out_specs=[anywhere()] * len(shapes),
        scratch_shapes=[pltpu.SemaphoreType.DMA((copies,))],
        compiler_params=params(4),
        name="pack",
    )(me, in_hbm(pairs), *[lists[other - 1] for other in list_order(wide_count)], in_hbm(blocks))
    each = wide_count - 1
    return [outs[c * each : (c + 1) * each] for c in range(len(CHUNKS))], outs[-1]


def select_kernel(wide_count, groups, start, me_ref, pairs_ref, own_ref, *refs):
    pair_count = own_ref.shape[0]
    outs = refs[wide_count - 1 :]
    received = refs[: wide_count - 1]
    size = outs[0].shape[1]
    owners = [pairs_ref[1, pair] >> 3 for pair in range(pair_count)]
    for pair in range(pair_count):
        apart = me_ref[0] ^ owners[pair]
        rank = jnp.int32(0)
        for before in range(pair):
            rank = rank + (owners[before] == owners[pair]).astype(jnp.int32)

        places, rest = [], outs
        for pieces in groups:
            places.append(of_pair(rest[:pieces], pair))
            rest = rest[pieces:]

        @pl.when(apart == 0)
        def _():
            for out in places:
                out[...] = own_ref[pair, start : start + size]

        for number, other in enumerate(others(wide_count)):

            @pl.when(apart == other)
            def _():
                for out in places:
                    out[...] = received[number][rank]


def select(me, pairs, own, received, start, size, groups):
    pair_count, _, feat = own.shape
    shapes = [
        pltpu.VMEM((pair_count // pieces, size, feat), own.dtype)
        for pieces in groups
        for _ in range(pieces)
    ]
    outs = pl.pallas_call(
        functools.partial(select_kernel, len(received) + 1, groups, start),
        out_shape=shapes,
        in_specs=[smem(), smem()] + [vmem()] * (1 + len(received)),
        out_specs=[vmem()] * len(shapes),
        compiler_params=params(4),
        name="select",
    )(me, in_hbm(pairs), *[in_vmem(x) for x in (own, *received)])
    return take_parts(outs, groups)[0]


def tree(parts):
    while len(parts) > 1:
        half = len(parts) // 2
        parts = [parts[i] + parts[i + half] for i in range(half)]
    return parts[0]


def across(left, right):
    return lax.dot_general(
        left, right, (((1,), (1,)), ((), ())), preferred_element_type=jnp.float32
    )


def lane_sum(block):
    square = jnp.square(block.astype(jnp.float32))
    return sum(square[:, at : at + LANES] for at in range(0, square.shape[1], LANES))


def segments(window):
    low, high = window
    held = []
    for chunk, (start, size) in enumerate(CHUNKS):
        first, end = max(low, start), min(high, start + size)
        if first < end:
            held.append((chunk, first - start, end - first))
    return held


def scores(rows, cols, square):
    gram = tree([across(row, col) for row, col in zip(rows, cols)])
    other = jnp.sum(tree([lane_sum(col) for col in cols]).T, axis=0, keepdims=True)
    pieces, mass = [], None
    for at in range(0, gram.shape[1], LANES):
        here = slice(at, at + LANES)
        piece = jnp.exp((square + other[:, here] - 2.0 * gram[:, here]) * (-1.0 / F))
        mass = piece if mass is None else mass + piece
        pieces.append(piece)
    kernel = jnp.concatenate(pieces, axis=1) if len(pieces) > 1 else pieces[0]
    return kernel.astype(jnp.bfloat16), jnp.sum(kernel, axis=0, keepdims=True), mass


def take_parts(refs, counts):
    parts = []
    for count in counts:
        parts.append(refs[:count])
        refs = refs[count:]
    return parts, refs


def of_pair(part, pair):
    each = part[0].shape[0]
    return part[pair // each].at[pair % each]


def window_parts(counts, refs):
    half = len(counts[0]) // 2
    rows, refs = [ref.at[i] for ref in refs[:2] for i in range(half)], refs[2:]
    chunks = []
    for chunk_counts in counts:
        cols, refs = take_parts(refs, chunk_counts)
        chunks.append(cols)
    return rows, chunks


def own_columns(window, chunks, pair):
    held = segments(window)
    pieces = [of_pair(part, pair)[at : at + size] for part, (_, at, size) in zip(chunks, held)]
    return jnp.concatenate(pieces, axis=0) if len(pieces) > 1 else pieces[0]


def pair_parts(window, rows, chunks, pair):
    cols = [own_columns(window, [c[i] for c in chunks], pair) for i in range(len(rows))]
    return [part[pair] for part in rows], cols


def first_kernel(window, counts, *refs):
    square_ref, mass_ref, total_ref, sums_ref = refs[-4:]
    all_rows, chunks = window_parts(counts, refs)
    for pair in range(square_ref.shape[0]):
        rows, cols = pair_parts(window, all_rows, chunks, pair)
        square = jnp.sum(tree([lane_sum(row) for row in rows]), axis=1, keepdims=True)
        square = jnp.broadcast_to(square, (BR, LANES))
        kernel, sums, mass = scores(rows, cols, square)
        square_ref[pair] = square
        mass_ref[pair] = mass
        sums_ref[pair : pair + 1] = sums
        total_ref[pair] = jnp.dot(kernel, cols[0], preferred_element_type=jnp.float32)


def last_kernel(window, counts, wide_count, me_ref, pairs_ref, *refs):
    square_in, mass_in, sums_in, kernel_ref, mass_ref, row_ref, near_ref, far_ref = refs[-8:]
    half = wide_count // 2
    for ref in (row_ref, near_ref, far_ref):
        ref[...] = jnp.zeros_like(ref)
    all_rows, chunks = window_parts(counts, refs)
    for pair in range(square_in.shape[0]):
        rows, cols = pair_parts(window, all_rows, chunks, pair)
        kernel, sums, mass = scores(rows, cols, square_in[pair])
        kernel_ref[pair] = kernel
        sums = jnp.concatenate([sums_in[pair : pair + 1], sums], axis=1)
        mass = mass_in[pair] + mass
        mass_ref[pair] = mass
        row_ref[pl.ds(pairs_ref[0, pair] & 7, 1)] += jnp.sum(mass.T, axis=0, keepdims=True)
        col = pairs_ref[1, pair]
        apart = (col >> 3) ^ me_ref[0]
        for share, ref in enumerate((near_ref, far_ref)):
            here = jnp.where((apart >= half) == (share == 1), sums, 0.0)
            ref[apart & (half - 1), pl.ds(col & 7, 1)] += here


def estimate(pair_count, size):
    return pl.CostEstimate(
        flops=2 * pair_count * BR * size * F,
        transcendentals=pair_count * BR * size,
        bytes_accessed=8 * 1024 * 1024,
    )


def piece_counts(window, cols):
    return tuple(tuple(len(part) for part in cols[chunk]) for chunk, _, _ in segments(window))


def operands(parts):
    return [piece for part in parts for piece in part]


def first_window(rows, cols):
    _, pair_count, _, feat = rows[0][0].shape
    window = WINDOWS[0]
    lanes = pltpu.VMEM((pair_count, BR, LANES), jnp.float32)
    total = pltpu.VMEM((pair_count, BR, feat), jnp.float32)
    args = operands(rows)
    for chunk, _, _ in segments(window):
        args += operands(cols[chunk])
    return pl.pallas_call(
        functools.partial(first_kernel, window, piece_counts(window, cols)),
        out_shape=[lanes, lanes, total, pltpu.VMEM((pair_count, window[1]), jnp.float32)],
        in_specs=[vmem()] * len(args),
        out_specs=[vmem()] * 4,
        compiler_params=params(16),
        cost_estimate=pl.CostEstimate(flops=0, transcendentals=0, bytes_accessed=0),
        name="first_window",
    )(*[in_vmem(x) for x in args])


def last_window(me, pairs, rows, cols, square, mass, sums, wide_count):
    pair_count = rows[0][0].shape[1]
    window = WINDOWS[1]
    size = window[1] - window[0]
    by_block = pltpu.VMEM((BLK_DEV, BR), jnp.float32)
    shapes = [
        pltpu.VMEM((pair_count, BR, size), jnp.bfloat16),
        pltpu.VMEM((pair_count, BR, LANES), jnp.float32),
    ] + [by_block] + [pltpu.VMEM((wide_count // 2, BLK_DEV, BR), jnp.float32)] * 2
    args = operands(rows)
    for chunk, _, _ in segments(window):
        args += operands(cols[chunk])
    args += [square, mass, sums]
    kernel, mass, row_sums, near, far = pl.pallas_call(
        functools.partial(last_kernel, window, piece_counts(window, cols), wide_count),
        out_shape=shapes,
        in_specs=[smem(), smem()] + [vmem()] * len(args),
        out_specs=[vmem()] * len(shapes),
        compiler_params=params(16),
        cost_estimate=estimate(pair_count, size),
        name="last_window",
    )(me, in_hbm(pairs), *[in_vmem(x) for x in args])
    return kernel, mass, row_sums, near, far


def keep_kernel(pairs_ref, block_ref, blocks_ref, out_ref, own_ref, sems):
    here = pl.program_id(0)

    def copies():
        for pair in range(own_ref.shape[0]):
            source = blocks_ref.at[pairs_ref[1, pair] & 7]
            yield pltpu.make_async_copy(source, own_ref.at[pair], sems.at[pair])

    @pl.when(here == 0)
    def _():
        for copy in copies():
            copy.start()

    out_ref[...] = block_ref[...]

    @pl.when(here == pl.num_programs(0) - 1)
    def _():
        for copy in copies():
            copy.wait()


def keep(pairs, blocks):
    pair_count = pairs.shape[1]
    block = pl.BlockSpec((1, *blocks.shape[1:]), lambda k: (k, 0, 0))
    return pl.pallas_call(
        keep_kernel,
        out_shape=[
            pltpu.HBM(blocks.shape, blocks.dtype),
            pltpu.VMEM((pair_count, *blocks.shape[1:]), blocks.dtype),
        ],
        grid=(blocks.shape[0],),
        in_specs=[smem(), block, anywhere()],
        out_specs=[block, anywhere()],
        scratch_shapes=[pltpu.SemaphoreType.DMA((pair_count,))],
        compiler_params=params(4),
        name="keep",
    )(in_hbm(pairs), in_hbm(blocks), in_hbm(blocks))


def mean_kernel(window, counts, local_ref, rows_ref, kernel_ref, mass_ref, total_ref, *refs):
    *refs, _, out_ref, part, weight, total, mass, made, sems = refs
    chunks = []
    for chunk, _, _ in segments(window):
        (own,), refs = take_parts(refs, counts[len(chunks)][:1])
        chunks.append(own)
    pair_count, _, feat = rows_ref.shape
    local = [local_ref[0, pair] & 7 for pair in range(pair_count)]

    def copy(pair):
        return pltpu.make_async_copy(made.at[pair], out_ref.at[local[pair]], sems.at[pair])

    firsts = []
    for pair in range(pair_count):
        sums = total_ref[pair] + jnp.dot(
            kernel_ref[pair], own_columns(window, chunks, pair), preferred_element_type=jnp.float32
        )
        part[pair] = sums.astype(jnp.bfloat16)
        weight[pair] = jnp.broadcast_to(
            jnp.sum(mass_ref[pair], axis=1, keepdims=True), (BR, LANES)
        )
        same = [local[other] == local[pair] for other in range(pair)]
        firsts.append(jnp.logical_not(functools.reduce(jnp.logical_or, same, jnp.bool_(False))))
    for pair in range(pair_count):

        @pl.when(firsts[pair])
        def _():
            total[...] = rows_ref[pair].astype(jnp.float32) + part[pair].astype(jnp.float32)
            mass[...] = 1.0 + weight[pair]
            for other in range(pair + 1, pair_count):

                @pl.when(local[other] == local[pair])
                def _():
                    total[...] += part[other].astype(jnp.float32)
                    mass[...] += weight[other]

            scale = 1.0 / mass[...]
            for at in range(0, feat, LANES):
                lanes = slice(at, at + LANES)
                made[pair, :, lanes] = (total[:, lanes] * scale).astype(jnp.bfloat16)
            copy(pair).start()

    for pair in range(pair_count):

        @pl.when(firsts[pair])
        def _():
            copy(pair).wait()


def means(pairs, rows, kernel, mass, total, cols, kept):
    pair_count, _, feat = rows.shape
    window = WINDOWS[1]
    own = operands(cols[chunk][0] for chunk, _, _ in segments(window))
    args = [in_vmem(x) for x in (rows, kernel, mass, total, *own)]
    return pl.pallas_call(
        functools.partial(mean_kernel, window, piece_counts(window, cols)),
        out_shape=pltpu.HBM(kept.shape, jnp.bfloat16),
        in_specs=[smem()] + [vmem()] * len(args) + [anywhere()],
        out_specs=anywhere(),
        scratch_shapes=[
            pltpu.VMEM((pair_count, BR, feat), jnp.bfloat16),
            pltpu.VMEM((pair_count, BR, LANES), jnp.float32),
            pltpu.VMEM((BR, feat), jnp.float32),
            pltpu.VMEM((BR, LANES), jnp.float32),
            pltpu.VMEM((pair_count, BR, feat), jnp.bfloat16),
            pltpu.SemaphoreType.DMA((pair_count,)),
        ],
        input_output_aliases={1 + len(args): 0},
        compiler_params=params(16),
        cost_estimate=estimate(pair_count, 128),
        name="means",
    )(in_hbm(pairs), *args, in_hbm(kept))


def fold_kernel(near_ref, came_ref, low_ref, high_ref):
    half = low_ref.shape[0]
    low_ref[...] = near_ref[:half] + came_ref[:half]
    high_ref[...] = near_ref[half:] + came_ref[half:]


def fold(near, came):
    half = pltpu.VMEM((near.shape[0] // 2, *near.shape[1:]), jnp.float32)
    return pl.pallas_call(
        fold_kernel,
        out_shape=[half, half],
        in_specs=[vmem(), vmem()],
        out_specs=[vmem(), vmem()],
        compiler_params=params(4),
        name="fold",
    )(in_vmem(near), in_vmem(came))


def weight_kernel(rows_ref, near_ref, came_ref, out_ref):
    weight = 1.0 / (1.0 + (rows_ref[...] + near_ref[0] + came_ref[0]) / BR)
    parts = BR // LANES
    for block in range(BLK_DEV):
        for part in range(parts):
            lanes = slice(part * LANES, (part + 1) * LANES)
            out_ref[block * parts + part : block * parts + part + 1] = weight[block : block + 1, lanes]


def block_weights(row_sums, near, far, beside):
    step = lax.axis_size("wide") // 2
    while step > 1:
        (came,) = to_wide([far], [step])
        came, beside = lax.optimization_barrier((came, beside))
        near, far = fold(near, came)
        step //= 2
    (came,) = to_wide([far], [1])
    out = pl.pallas_call(
        weight_kernel,
        out_shape=jax.ShapeDtypeStruct((BLK_DEV * BR // LANES, LANES), jnp.float32),
        in_specs=[vmem()] * 3,
        out_specs=vmem(),
        compiler_params=params(4),
        name="weights",
    )(*[in_vmem(x) for x in (row_sums, near, came)])
    return out.reshape(BLK_DEV * BR), beside


def hop(parts, step):
    count = lax.axis_size("narrow")
    perm = [(i, i ^ step) for i in range(count)]
    return [[lax.ppermute(piece, "narrow", perm) for piece in part] for part in parts]


def first_hops(part):
    parts = [part]
    step = lax.axis_size("narrow") // 2
    while step > 1:
        parts = parts + hop(parts, step)
        step //= 2
    return parts


def to_wide(pieces, apart):
    count = lax.axis_size("wide")
    return [
        lax.ppermute(piece, "wide", [(i, i ^ other) for i in range(count)])
        for piece, other in zip(pieces, apart)
    ]


def on_device(embeddings, pair_list):
    wide_count = lax.axis_size("wide")
    me = lax.axis_index("wide").astype(jnp.int32).reshape(1)
    pairs = pair_list.T
    pair_count = pairs.shape[1]
    capacity = max(2, 2 * pair_count // wide_count)
    feat = embeddings.shape[1]
    blocks = embeddings.reshape(BLK_DEV, BR, feat)
    apart = others(wide_count)
    lists = to_wide([pairs] * (wide_count - 1), apart[::-1])
    fixed = lax.optimization_barrier
    outgoing, row_slices = pack(me, pairs, lists, blocks, capacity)

    def pick(received, chunk, *groups):
        return select(me, pairs, own, received, *CHUNKS[chunk], groups)

    def halves(part):
        middle = pair_count // 2
        return [part[0][:middle], part[0][middle:]]

    rows = jnp.stack([part[0] for part in first_hops([row_slices])])
    received = to_wide(outgoing[0], apart)
    near = to_wide(outgoing[1][-1:], apart[-1:])
    rows, received, near, (kept, own) = fixed((rows, received, near, keep(pairs, blocks)))
    own_a, whole_a = pick(received, 0, 2, 1)
    cols_a = [own_a] + first_hops(whole_a)[1:]
    rows = [[rows], *hop([[rows]], 1)]
    cols_a, rows, received = fixed((cols_a, rows, to_wide(outgoing[1][:-1], apart[:-1])))
    cols_b = first_hops(*pick([*received, *near], 1, 1))
    last_b = hop(cols_b[:1], 1)
    cols_a = cols_a + hop([own_a] + [halves(part) for part in cols_a[1:]], 1)
    carry = first_window(rows, [cols_a])
    cols_b, carry = fixed((cols_b, carry))
    cols_b = cols_b + last_b + hop(cols_b[1:], 1)
    square, mass, total, sums = carry
    kernel, mass, row_sums, near_sums, far_sums = last_window(
        me, pairs, rows, [cols_a, cols_b], square, mass, sums, wide_count
    )
    mean = means(pairs, row_slices, kernel, mass, total, [cols_a, cols_b], kept)
    weights, mean = block_weights(row_sums, near_sums, far_sums, mean)
    return weights, mean.reshape(BLK_DEV * BR, feat)


def solution(mesh):
    in_specs = (P(("groups", "wide"), "narrow"), P(("groups", "wide"), None))
    out_specs = (P(("groups", "wide")), P(("groups", "wide"), "narrow"))
    return jax.shard_map(
        on_device, mesh=mesh, in_specs=in_specs, out_specs=out_specs, check_vma=False
    )
```

```python
import functools

import jax
import jax.numpy as jnp
from jax import lax
from jax.experimental import pallas as pl
from jax.experimental.pallas import tpu as pltpu
from jax.sharding import PartitionSpec as P

F = 1024
BR = 512
BLK_DEV = 8
LANES = 128
CHUNKS = ((0, 336), (336, 176))
WINDOWS = ((0, 256), (256, 512))


def smem():
    return pl.BlockSpec(memory_space=pltpu.SMEM)


def vmem():
    return pl.BlockSpec(memory_space=pltpu.VMEM)


def anywhere():
    return pl.BlockSpec(memory_space=pl.ANY)


def in_vmem(x):
    return pltpu.with_memory_space_constraint(x, pltpu.VMEM)


def in_hbm(x):
    return pltpu.with_memory_space_constraint(x, pltpu.HBM)


def params(mebibytes):
    return pltpu.CompilerParams(vmem_limit_bytes=mebibytes * 1024 * 1024)


def others(wide_count):
    return range(wide_count - 1, 0, -1)


def pack_kernel(chunk, with_rows, wide_count, pair_count, capacity, me_ref, pairs_ref, *refs):
    lists, blocks_ref = refs[: wide_count - 1], refs[wide_count - 1]
    *outs, sems = refs[wide_count:]
    me = me_ref[0]
    start, size = CHUNKS[chunk]
    copies = []

    def send(source, target):
        copies.append(pltpu.make_async_copy(source, target, sems.at[len(copies)]))
        copies[-1].start()

    for number, other in enumerate(others(wide_count)):
        asked = lists[list_order(wide_count).index(other)]
        picks = [jnp.int32(0)] * capacity
        count = jnp.int32(0)
        for pair in range(pair_count):
            col = asked[1, pair]
            mine = (col >> 3) == me
            for slot in range(capacity):
                picks[slot] = jnp.where(mine & (count == slot), col & 7, picks[slot])
            count = count + mine.astype(jnp.int32)
        for slot in range(capacity):
            send(blocks_ref.at[picks[slot], pl.ds(start, size)], outs[number].at[slot])
    if with_rows:
        for pair in range(pair_count):
            send(blocks_ref.at[pairs_ref[0, pair] & 7], outs[-1].at[pair])
    for copy in copies:
        copy.wait()


def list_order(wide_count):
    middle = wide_count // 2
    return [other for other in range(1, wide_count) if other != middle] + [middle]


def sum_order(wide_count):
    return list_order(wide_count)[::-1]


def pack(me, pairs, lists, blocks, capacity, chunk, with_rows):
    wide_count, pair_count = len(lists) + 1, pairs.shape[1]
    feat = blocks.shape[-1]
    shapes = [pltpu.VMEM((capacity, CHUNKS[chunk][1], feat), blocks.dtype)] * (wide_count - 1)
    copies = len(shapes) * capacity
    if with_rows:
        shapes.append(pltpu.VMEM((pair_count, BR, feat), blocks.dtype))
        copies += pair_count
    return pl.pallas_call(
        functools.partial(pack_kernel, chunk, with_rows, wide_count, pair_count, capacity),
        out_shape=shapes,
        in_specs=[smem()] * (1 + wide_count) + [anywhere()],
        out_specs=[anywhere()] * len(shapes),
        scratch_shapes=[pltpu.SemaphoreType.DMA((copies,))],
        compiler_params=params(4),
        name="pack",
    )(me, in_hbm(pairs), *[lists[other - 1] for other in list_order(wide_count)], in_hbm(blocks))


def select_kernel(wide_count, groups, start, me_ref, pairs_ref, own_ref, *refs):
    pair_count = own_ref.shape[0]
    outs = refs[wide_count - 1 :]
    received = refs[: wide_count - 1]
    size = outs[0].shape[1]
    owners = [pairs_ref[1, pair] >> 3 for pair in range(pair_count)]
    for pair in range(pair_count):
        apart = me_ref[0] ^ owners[pair]
        rank = jnp.int32(0)
        for before in range(pair):
            rank = rank + (owners[before] == owners[pair]).astype(jnp.int32)

        places, rest = [], outs
        for pieces in groups:
            places.append(of_pair(rest[:pieces], pair))
            rest = rest[pieces:]

        @pl.when(apart == 0)
        def _():
            for out in places:
                out[...] = own_ref[pair, start : start + size]

        for number, other in enumerate(others(wide_count)):

            @pl.when(apart == other)
            def _():
                for out in places:
                    out[...] = received[number][rank]


def select(me, pairs, own, received, start, size, groups):
    pair_count, _, feat = own.shape
    shapes = [
        pltpu.VMEM((pair_count // pieces, size, feat), own.dtype)
        for pieces in groups
        for _ in range(pieces)
    ]
    outs = pl.pallas_call(
        functools.partial(select_kernel, len(received) + 1, groups, start),
        out_shape=shapes,
        in_specs=[smem(), smem()] + [vmem()] * (1 + len(received)),
        out_specs=[vmem()] * len(shapes),
        compiler_params=params(4),
        name="select",
    )(me, in_hbm(pairs), *[in_vmem(x) for x in (own, *received)])
    return take_parts(outs, groups)[0]


def tree(parts):
    while len(parts) > 1:
        half = len(parts) // 2
        parts = [parts[i] + parts[i + half] for i in range(half)]
    return parts[0]


def across(left, right):
    return lax.dot_general(
        left, right, (((1,), (1,)), ((), ())), preferred_element_type=jnp.float32
    )


def lane_sum(block):
    square = jnp.square(block.astype(jnp.float32))
    return sum(square[:, at : at + LANES] for at in range(0, square.shape[1], LANES))


def segments(window):
    low, high = window
    held = []
    for chunk, (start, size) in enumerate(CHUNKS):
        first, end = max(low, start), min(high, start + size)
        if first < end:
            held.append((chunk, first - start, end - first))
    return held


def scores(rows, cols, square):
    gram = tree([across(row, col) for row, col in zip(rows, cols)])
    other = jnp.sum(tree([lane_sum(col) for col in cols]).T, axis=0, keepdims=True)
    pieces, mass = [], None
    for at in range(0, gram.shape[1], LANES):
        here = slice(at, at + LANES)
        piece = jnp.exp((square + other[:, here] - 2.0 * gram[:, here]) * (-1.0 / F))
        mass = piece if mass is None else mass + piece
        pieces.append(piece)
    kernel = jnp.concatenate(pieces, axis=1) if len(pieces) > 1 else pieces[0]
    return kernel.astype(jnp.bfloat16), jnp.sum(kernel, axis=0, keepdims=True), mass


def take_parts(refs, counts):
    parts = []
    for count in counts:
        parts.append(refs[:count])
        refs = refs[count:]
    return parts, refs


def of_pair(part, pair):
    each = part[0].shape[0]
    return part[pair // each].at[pair % each]


def window_parts(counts, refs):
    half = len(counts[0]) // 2
    rows, refs = [ref.at[i] for ref in refs[:2] for i in range(half)], refs[2:]
    chunks = []
    for chunk_counts in counts:
        cols, refs = take_parts(refs, chunk_counts)
        chunks.append(cols)
    return rows, chunks


def own_columns(window, chunks, pair):
    held = segments(window)
    pieces = [of_pair(part, pair)[at : at + size] for part, (_, at, size) in zip(chunks, held)]
    return jnp.concatenate(pieces, axis=0) if len(pieces) > 1 else pieces[0]


def pair_parts(window, rows, chunks, pair):
    cols = [own_columns(window, [c[i] for c in chunks], pair) for i in range(len(rows))]
    return [part[pair] for part in rows], cols


def first_kernel(window, counts, *refs):
    square_ref, mass_ref, total_ref, sums_ref = refs[-4:]
    all_rows, chunks = window_parts(counts, refs)
    for pair in range(square_ref.shape[0]):
        rows, cols = pair_parts(window, all_rows, chunks, pair)
        square = jnp.sum(tree([lane_sum(row) for row in rows]), axis=1, keepdims=True)
        square = jnp.broadcast_to(square, (BR, LANES))
        kernel, sums, mass = scores(rows, cols, square)
        square_ref[pair] = square
        mass_ref[pair] = mass
        sums_ref[pair : pair + 1] = sums
        total_ref[pair] = jnp.dot(kernel, cols[0], preferred_element_type=jnp.float32)


def last_kernel(window, counts, wide_count, me_ref, pairs_ref, *refs):
    square_in, mass_in, sums_in = refs[-6 - wide_count : -3 - wide_count]
    kernel_ref, mass_ref, row_ref = refs[-3 - wide_count : -wide_count]
    shares = refs[-wide_count:]
    for ref in (row_ref, *shares):
        ref[...] = jnp.zeros_like(ref)
    all_rows, chunks = window_parts(counts, refs)
    for pair in range(square_in.shape[0]):
        rows, cols = pair_parts(window, all_rows, chunks, pair)
        kernel, sums, mass = scores(rows, cols, square_in[pair])
        kernel_ref[pair] = kernel
        sums = jnp.concatenate([sums_in[pair : pair + 1], sums], axis=1)
        mass = mass_in[pair] + mass
        mass_ref[pair] = mass
        row_ref[pl.ds(pairs_ref[0, pair] & 7, 1)] += jnp.sum(mass.T, axis=0, keepdims=True)
        col = pairs_ref[1, pair]
        apart = (col >> 3) ^ me_ref[0]
        for other, ref in zip([*sum_order(wide_count), 0], shares):
            ref[pl.ds(col & 7, 1)] += jnp.where(apart == other, sums, 0.0)


def estimate(pair_count, size):
    return pl.CostEstimate(
        flops=2 * pair_count * BR * size * F,
        transcendentals=pair_count * BR * size,
        bytes_accessed=8 * 1024 * 1024,
    )


def piece_counts(window, cols):
    return tuple(tuple(len(part) for part in cols[chunk]) for chunk, _, _ in segments(window))


def operands(parts):
    return [piece for part in parts for piece in part]


def first_window(rows, cols):
    _, pair_count, _, feat = rows[0][0].shape
    window = WINDOWS[0]
    lanes = pltpu.VMEM((pair_count, BR, LANES), jnp.float32)
    total = pltpu.VMEM((pair_count, BR, feat), jnp.float32)
    args = operands(rows)
    for chunk, _, _ in segments(window):
        args += operands(cols[chunk])
    return pl.pallas_call(
        functools.partial(first_kernel, window, piece_counts(window, cols)),
        out_shape=[lanes, lanes, total, pltpu.VMEM((pair_count, window[1]), jnp.float32)],
        in_specs=[vmem()] * len(args),
        out_specs=[vmem()] * 4,
        compiler_params=params(16),
        cost_estimate=pl.CostEstimate(flops=0, transcendentals=0, bytes_accessed=0),
        name="first_window",
    )(*[in_vmem(x) for x in args])


def last_window(me, pairs, rows, cols, square, mass, sums, wide_count):
    pair_count = rows[0][0].shape[1]
    window = WINDOWS[1]
    size = window[1] - window[0]
    by_block = pltpu.VMEM((BLK_DEV, BR), jnp.float32)
    shapes = [
        pltpu.VMEM((pair_count, BR, size), jnp.bfloat16),
        pltpu.VMEM((pair_count, BR, LANES), jnp.float32),
    ] + [by_block] * (1 + wide_count)
    args = operands(rows)
    for chunk, _, _ in segments(window):
        args += operands(cols[chunk])
    args += [square, mass, sums]
    kernel, mass, row_sums, *shares = pl.pallas_call(
        functools.partial(last_kernel, window, piece_counts(window, cols), wide_count),
        out_shape=shapes,
        in_specs=[smem(), smem()] + [vmem()] * len(args),
        out_specs=[vmem()] * len(shapes),
        compiler_params=params(16),
        cost_estimate=estimate(pair_count, size),
        name="last_window",
    )(me, in_hbm(pairs), *[in_vmem(x) for x in args])
    return kernel, mass, row_sums, shares


def keep_kernel(pairs_ref, block_ref, blocks_ref, out_ref, own_ref, sems):
    here = pl.program_id(0)

    def copies():
        for pair in range(own_ref.shape[0]):
            source = blocks_ref.at[pairs_ref[1, pair] & 7]
            yield pltpu.make_async_copy(source, own_ref.at[pair], sems.at[pair])

    @pl.when(here == 0)
    def _():
        for copy in copies():
            copy.start()

    out_ref[...] = block_ref[...]

    @pl.when(here == pl.num_programs(0) - 1)
    def _():
        for copy in copies():
            copy.wait()


def keep(pairs, blocks):
    pair_count = pairs.shape[1]
    block = pl.BlockSpec((1, *blocks.shape[1:]), lambda k: (k, 0, 0))
    return pl.pallas_call(
        keep_kernel,
        out_shape=[
            pltpu.HBM(blocks.shape, blocks.dtype),
            pltpu.VMEM((pair_count, *blocks.shape[1:]), blocks.dtype),
        ],
        grid=(blocks.shape[0],),
        in_specs=[smem(), block, anywhere()],
        out_specs=[block, anywhere()],
        scratch_shapes=[pltpu.SemaphoreType.DMA((pair_count,))],
        compiler_params=params(4),
        name="keep",
    )(in_hbm(pairs), in_hbm(blocks), in_hbm(blocks))


def mean_kernel(window, counts, local_ref, rows_ref, kernel_ref, mass_ref, total_ref, *refs):
    *refs, _, out_ref, part, weight, total, mass, made, sems = refs
    chunks = []
    for chunk, _, _ in segments(window):
        (own,), refs = take_parts(refs, counts[len(chunks)][:1])
        chunks.append(own)
    pair_count, _, feat = rows_ref.shape
    local = [local_ref[0, pair] & 7 for pair in range(pair_count)]

    def copy(pair):
        return pltpu.make_async_copy(made.at[pair], out_ref.at[local[pair]], sems.at[pair])

    def either(found):
        return functools.reduce(jnp.logical_or, found, jnp.bool_(False))

    def finish(pair, total, scale):
        for at in range(0, feat, LANES):
            lanes = slice(at, at + LANES)
            made[pair, :, lanes] = (total[:, lanes] * scale).astype(jnp.bfloat16)
        copy(pair).start()

    firsts, alone = [], []
    for pair in range(pair_count):
        before = either([local[other] == local[pair] for other in range(pair)])
        after = either([local[other] == local[pair] for other in range(pair + 1, pair_count)])
        firsts.append(jnp.logical_not(before))
        alone.append(jnp.logical_not(before | after))
        sums = total_ref[pair] + jnp.dot(
            kernel_ref[pair], own_columns(window, chunks, pair), preferred_element_type=jnp.float32
        )
        sums = sums.astype(jnp.bfloat16)
        lines = jnp.broadcast_to(jnp.sum(mass_ref[pair], axis=1, keepdims=True), (BR, LANES))
        part[pair] = sums
        weight[pair] = lines

        @pl.when(alone[pair])
        def _():
            mean = rows_ref[pair].astype(jnp.float32) + sums.astype(jnp.float32)
            finish(pair, mean, 1.0 / (1.0 + lines))

    for pair in range(pair_count):

        @pl.when(firsts[pair] & jnp.logical_not(alone[pair]))
        def _():
            total[...] = rows_ref[pair].astype(jnp.float32) + part[pair].astype(jnp.float32)
            mass[...] = 1.0 + weight[pair]
            for other in range(pair + 1, pair_count):

                @pl.when(local[other] == local[pair])
                def _():
                    total[...] += part[other].astype(jnp.float32)
                    mass[...] += weight[other]

            finish(pair, total, 1.0 / mass[...])

    for pair in range(pair_count):

        @pl.when(firsts[pair])
        def _():
            copy(pair).wait()


def means(pairs, rows, kernel, mass, total, cols, kept):
    pair_count, _, feat = rows.shape
    window = WINDOWS[1]
    own = operands(cols[chunk][0] for chunk, _, _ in segments(window))
    args = [in_vmem(x) for x in (rows, kernel, mass, total, *own)]
    return pl.pallas_call(
        functools.partial(mean_kernel, window, piece_counts(window, cols)),
        out_shape=pltpu.HBM(kept.shape, jnp.bfloat16),
        in_specs=[smem()] + [vmem()] * len(args) + [anywhere()],
        out_specs=anywhere(),
        scratch_shapes=[
            pltpu.VMEM((pair_count, BR, feat), jnp.bfloat16),
            pltpu.VMEM((pair_count, BR, LANES), jnp.float32),
            pltpu.VMEM((BR, feat), jnp.float32),
            pltpu.VMEM((BR, LANES), jnp.float32),
            pltpu.VMEM((pair_count, BR, feat), jnp.bfloat16),
            pltpu.SemaphoreType.DMA((pair_count,)),
        ],
        input_output_aliases={1 + len(args): 0},
        compiler_params=params(16),
        cost_estimate=estimate(pair_count, 128),
        name="means",
    )(in_hbm(pairs), *args, in_hbm(kept))


def weight_kernel(*refs):
    out_ref = refs[-1]
    mass = refs[0][...]
    for ref in refs[1:-1]:
        mass = mass + ref[...]
    weight = 1.0 / (1.0 + mass / BR)
    parts = BR // LANES
    for block in range(BLK_DEV):
        for part in range(parts):
            lanes = slice(part * LANES, (part + 1) * LANES)
            out_ref[block * parts + part : block * parts + part + 1] = weight[block : block + 1, lanes]


def block_weights(sums):
    out = pl.pallas_call(
        weight_kernel,
        out_shape=jax.ShapeDtypeStruct((BLK_DEV * BR // LANES, LANES), jnp.float32),
        in_specs=[vmem()] * len(sums),
        out_specs=vmem(),
        compiler_params=params(4),
        name="weights",
    )(*[in_vmem(x) for x in sums])
    return out.reshape(BLK_DEV * BR)


def hop(parts, step):
    count = lax.axis_size("narrow")
    perm = [(i, i ^ step) for i in range(count)]
    return [[lax.ppermute(piece, "narrow", perm) for piece in part] for part in parts]


def first_hops(part):
    parts = [part]
    step = lax.axis_size("narrow") // 2
    while step > 1:
        parts = parts + hop(parts, step)
        step //= 2
    return parts


def to_wide(pieces, apart):
    count = lax.axis_size("wide")
    return [
        lax.ppermute(piece, "wide", [(i, i ^ other) for i in range(count)])
        for piece, other in zip(pieces, apart)
    ]


def on_device(embeddings, pair_list):
    wide_count = lax.axis_size("wide")
    me = lax.axis_index("wide").astype(jnp.int32).reshape(1)
    pairs = pair_list.T
    pair_count = pairs.shape[1]
    capacity = max(2, 2 * pair_count // wide_count)
    feat = embeddings.shape[1]
    blocks = embeddings.reshape(BLK_DEV, BR, feat)
    apart = others(wide_count)
    lists = to_wide([pairs] * (wide_count - 1), apart[::-1])
    fixed = lax.optimization_barrier
    *outgoing, row_slices = pack(me, pairs, lists, blocks, capacity, 0, True)
    later = pack(me, pairs, lists, blocks, capacity, 1, False)

    def pick(received, chunk, *groups):
        return select(me, pairs, own, received, *CHUNKS[chunk], groups)

    def halves(part):
        middle = pair_count // 2
        return [part[0][:middle], part[0][middle:]]

    rows = jnp.stack([part[0] for part in first_hops([row_slices])])
    received = to_wide(outgoing, apart)
    near = to_wide(later[-1:], apart[-1:])
    rows, received, near, (kept, own) = fixed((rows, received, near, keep(pairs, blocks)))
    own_a, whole_a = pick(received, 0, 2, 1)
    cols_a = [own_a] + first_hops(whole_a)[1:]
    rows = [[rows], *hop([[rows]], 1)]
    cols_a, rows, received = fixed((cols_a, rows, to_wide(later[:-1], apart[:-1])))
    cols_b = first_hops(*pick([*received, *near], 1, 1))
    last_b = hop(cols_b[:1], 1)
    cols_a = cols_a + hop([own_a] + [halves(part) for part in cols_a[1:]], 1)
    carry = first_window(rows, [cols_a])
    cols_b, carry = fixed((cols_b, carry))
    cols_b = cols_b + last_b + hop(cols_b[1:], 1)
    square, mass, total, sums = carry
    kernel, mass, row_sums, shares = last_window(
        me, pairs, rows, [cols_a, cols_b], square, mass, sums, wide_count
    )
    came = to_wide(shares[:-1], sum_order(wide_count))
    mean = means(pairs, row_slices, kernel, mass, total, [cols_a, cols_b], kept)
    weights = block_weights([row_sums, shares[-1], *came])
    return weights, mean.reshape(BLK_DEV * BR, feat)


def solution(mesh):
    in_specs = (P(("groups", "wide"), "narrow"), P(("groups", "wide"), None))
    out_specs = (P(("groups", "wide")), P(("groups", "wide"), "narrow"))
    return jax.shard_map(
        on_device, mesh=mesh, in_specs=in_specs, out_specs=out_specs, check_vma=False
    )
```

```python
import functools

import jax
import jax.numpy as jnp
from jax import lax
from jax.experimental import pallas as pl
from jax.experimental.pallas import tpu as pltpu
from jax.sharding import PartitionSpec as P

F = 1024
BR = 512
BLK_DEV = 8
LANES = 128
CHUNKS = ((0, 352), (352, 160))
WINDOWS = ((0, 256), (256, 512))


def smem():
    return pl.BlockSpec(memory_space=pltpu.SMEM)


def vmem():
    return pl.BlockSpec(memory_space=pltpu.VMEM)


def anywhere():
    return pl.BlockSpec(memory_space=pl.ANY)


def in_vmem(x):
    return pltpu.with_memory_space_constraint(x, pltpu.VMEM)


def in_hbm(x):
    return pltpu.with_memory_space_constraint(x, pltpu.HBM)


def params(mebibytes):
    return pltpu.CompilerParams(vmem_limit_bytes=mebibytes * 1024 * 1024)


def others(wide_count):
    return range(wide_count - 1, 0, -1)


def pack_kernel(chunk, with_rows, wide_count, pair_count, capacity, me_ref, pairs_ref, *refs):
    lists, blocks_ref = refs[: wide_count - 1], refs[wide_count - 1]
    *outs, sems = refs[wide_count:]
    me = me_ref[0]
    start, size = CHUNKS[chunk]
    copies = []

    def send(source, target):
        copies.append(pltpu.make_async_copy(source, target, sems.at[len(copies)]))
        copies[-1].start()

    for number, other in enumerate(others(wide_count)):
        asked = lists[list_order(wide_count).index(other)]
        picks = [jnp.int32(0)] * capacity
        count = jnp.int32(0)
        for pair in range(pair_count):
            col = asked[1, pair]
            mine = (col >> 3) == me
            for slot in range(capacity):
                picks[slot] = jnp.where(mine & (count == slot), col & 7, picks[slot])
            count = count + mine.astype(jnp.int32)
        for slot in range(capacity):
            send(blocks_ref.at[picks[slot], pl.ds(start, size)], outs[number].at[slot])
    if with_rows:
        for pair in range(pair_count):
            send(blocks_ref.at[pairs_ref[0, pair] & 7], outs[-1].at[pair])
    for copy in copies:
        copy.wait()


def list_order(wide_count):
    middle = wide_count // 2
    return [other for other in range(1, wide_count) if other != middle] + [middle]


def sum_order(wide_count):
    return list_order(wide_count)[::-1]


def pack(me, pairs, lists, blocks, capacity, chunk, with_rows):
    wide_count, pair_count = len(lists) + 1, pairs.shape[1]
    feat = blocks.shape[-1]
    shapes = [pltpu.VMEM((capacity, CHUNKS[chunk][1], feat), blocks.dtype)] * (wide_count - 1)
    copies = len(shapes) * capacity
    if with_rows:
        shapes.append(pltpu.VMEM((pair_count, BR, feat), blocks.dtype))
        copies += pair_count
    return pl.pallas_call(
        functools.partial(pack_kernel, chunk, with_rows, wide_count, pair_count, capacity),
        out_shape=shapes,
        in_specs=[smem()] * (1 + wide_count) + [anywhere()],
        out_specs=[anywhere()] * len(shapes),
        scratch_shapes=[pltpu.SemaphoreType.DMA((copies,))],
        compiler_params=params(4),
        name="pack",
    )(me, in_hbm(pairs), *[lists[other - 1] for other in list_order(wide_count)], in_hbm(blocks))


def select_kernel(wide_count, groups, start, me_ref, pairs_ref, own_ref, *refs):
    pair_count = own_ref.shape[0]
    outs = refs[wide_count - 1 :]
    received = refs[: wide_count - 1]
    size = outs[0].shape[1]
    owners = [pairs_ref[1, pair] >> 3 for pair in range(pair_count)]
    for pair in range(pair_count):
        apart = me_ref[0] ^ owners[pair]
        rank = jnp.int32(0)
        for before in range(pair):
            rank = rank + (owners[before] == owners[pair]).astype(jnp.int32)

        places, rest = [], outs
        for pieces in groups:
            places.append(of_pair(rest[:pieces], pair))
            rest = rest[pieces:]

        @pl.when(apart == 0)
        def _():
            for out in places:
                out[...] = own_ref[pair, start : start + size]

        for number, other in enumerate(others(wide_count)):

            @pl.when(apart == other)
            def _():
                for out in places:
                    out[...] = received[number][rank]


def select(me, pairs, own, received, start, size, groups):
    pair_count, _, feat = own.shape
    shapes = [
        pltpu.VMEM((pair_count // pieces, size, feat), own.dtype)
        for pieces in groups
        for _ in range(pieces)
    ]
    outs = pl.pallas_call(
        functools.partial(select_kernel, len(received) + 1, groups, start),
        out_shape=shapes,
        in_specs=[smem(), smem()] + [vmem()] * (1 + len(received)),
        out_specs=[vmem()] * len(shapes),
        compiler_params=params(4),
        name="select",
    )(me, in_hbm(pairs), *[in_vmem(x) for x in (own, *received)])
    return take_parts(outs, groups)[0]


def tree(parts):
    while len(parts) > 1:
        half = len(parts) // 2
        parts = [parts[i] + parts[i + half] for i in range(half)]
    return parts[0]


def across(left, right):
    return lax.dot_general(
        left, right, (((1,), (1,)), ((), ())), preferred_element_type=jnp.float32
    )


def lane_sum(block):
    square = jnp.square(block.astype(jnp.float32))
    return sum(square[:, at : at + LANES] for at in range(0, square.shape[1], LANES))


def segments(window):
    low, high = window
    held = []
    for chunk, (start, size) in enumerate(CHUNKS):
        first, end = max(low, start), min(high, start + size)
        if first < end:
            held.append((chunk, first - start, end - first))
    return held


def scores(rows, cols, square):
    gram = tree([across(row, col) for row, col in zip(rows, cols)])
    other = jnp.sum(tree([lane_sum(col) for col in cols]).T, axis=0, keepdims=True)
    pieces, mass = [], None
    for at in range(0, gram.shape[1], LANES):
        here = slice(at, at + LANES)
        piece = jnp.exp((square + other[:, here] - 2.0 * gram[:, here]) * (-1.0 / F))
        mass = piece if mass is None else mass + piece
        pieces.append(piece)
    kernel = jnp.concatenate(pieces, axis=1) if len(pieces) > 1 else pieces[0]
    return kernel.astype(jnp.bfloat16), jnp.sum(kernel, axis=0, keepdims=True), mass


def take_parts(refs, counts):
    parts = []
    for count in counts:
        parts.append(refs[:count])
        refs = refs[count:]
    return parts, refs


def of_pair(part, pair):
    each = part[0].shape[0]
    return part[pair // each].at[pair % each]


def window_parts(counts, refs):
    half = len(counts[0]) // 2
    rows, refs = [ref.at[i] for ref in refs[:2] for i in range(half)], refs[2:]
    chunks = []
    for chunk_counts in counts:
        cols, refs = take_parts(refs, chunk_counts)
        chunks.append(cols)
    return rows, chunks


def own_columns(window, chunks, pair):
    held = segments(window)
    pieces = [of_pair(part, pair)[at : at + size] for part, (_, at, size) in zip(chunks, held)]
    return jnp.concatenate(pieces, axis=0) if len(pieces) > 1 else pieces[0]


def pair_parts(window, rows, chunks, pair):
    cols = [own_columns(window, [c[i] for c in chunks], pair) for i in range(len(rows))]
    return [part[pair] for part in rows], cols


def first_kernel(window, counts, *refs):
    square_ref, mass_ref, total_ref, sums_ref = refs[-4:]
    all_rows, chunks = window_parts(counts, refs)
    for pair in range(square_ref.shape[0]):
        rows, cols = pair_parts(window, all_rows, chunks, pair)
        square = jnp.sum(tree([lane_sum(row) for row in rows]), axis=1, keepdims=True)
        square = jnp.broadcast_to(square, (BR, LANES))
        kernel, sums, mass = scores(rows, cols, square)
        square_ref[pair] = square
        mass_ref[pair] = mass
        sums_ref[pair : pair + 1] = sums
        total_ref[pair] = jnp.dot(kernel, cols[0], preferred_element_type=jnp.float32)


def last_kernel(window, counts, wide_count, me_ref, pairs_ref, *refs):
    square_in, mass_in, sums_in = refs[-6 - wide_count : -3 - wide_count]
    kernel_ref, mass_ref, row_ref = refs[-3 - wide_count : -wide_count]
    shares = refs[-wide_count:]
    for ref in (row_ref, *shares):
        ref[...] = jnp.zeros_like(ref)
    all_rows, chunks = window_parts(counts, refs)
    for pair in range(square_in.shape[0]):
        rows, cols = pair_parts(window, all_rows, chunks, pair)
        kernel, sums, mass = scores(rows, cols, square_in[pair])
        kernel_ref[pair] = kernel
        sums = jnp.concatenate([sums_in[pair : pair + 1], sums], axis=1)
        mass = mass_in[pair] + mass
        mass_ref[pair] = mass
        row_ref[pl.ds(pairs_ref[0, pair] & 7, 1)] += jnp.sum(mass.T, axis=0, keepdims=True)
        col = pairs_ref[1, pair]
        apart = (col >> 3) ^ me_ref[0]
        for other, ref in zip([*sum_order(wide_count), 0], shares):
            ref[pl.ds(col & 7, 1)] += jnp.where(apart == other, sums, 0.0)


def estimate(pair_count, size):
    return pl.CostEstimate(
        flops=2 * pair_count * BR * size * F,
        transcendentals=pair_count * BR * size,
        bytes_accessed=8 * 1024 * 1024,
    )


def piece_counts(window, cols):
    return tuple(tuple(len(part) for part in cols[chunk]) for chunk, _, _ in segments(window))


def operands(parts):
    return [piece for part in parts for piece in part]


def first_window(rows, cols):
    _, pair_count, _, feat = rows[0][0].shape
    window = WINDOWS[0]
    lanes = pltpu.VMEM((pair_count, BR, LANES), jnp.float32)
    total = pltpu.VMEM((pair_count, BR, feat), jnp.float32)
    args = operands(rows)
    for chunk, _, _ in segments(window):
        args += operands(cols[chunk])
    return pl.pallas_call(
        functools.partial(first_kernel, window, piece_counts(window, cols)),
        out_shape=[lanes, lanes, total, pltpu.VMEM((pair_count, window[1]), jnp.float32)],
        in_specs=[vmem()] * len(args),
        out_specs=[vmem()] * 4,
        compiler_params=params(16),
        cost_estimate=pl.CostEstimate(flops=0, transcendentals=0, bytes_accessed=0),
        name="first_window",
    )(*[in_vmem(x) for x in args])


def last_window(me, pairs, rows, cols, square, mass, sums, wide_count):
    pair_count = rows[0][0].shape[1]
    window = WINDOWS[1]
    size = window[1] - window[0]
    by_block = pltpu.VMEM((BLK_DEV, BR), jnp.float32)
    shapes = [
        pltpu.VMEM((pair_count, BR, size), jnp.bfloat16),
        pltpu.VMEM((pair_count, BR, LANES), jnp.float32),
    ] + [by_block] * (1 + wide_count)
    args = operands(rows)
    for chunk, _, _ in segments(window):
        args += operands(cols[chunk])
    args += [square, mass, sums]
    kernel, mass, row_sums, *shares = pl.pallas_call(
        functools.partial(last_kernel, window, piece_counts(window, cols), wide_count),
        out_shape=shapes,
        in_specs=[smem(), smem()] + [vmem()] * len(args),
        out_specs=[vmem()] * len(shapes),
        compiler_params=params(16),
        cost_estimate=estimate(pair_count, size),
        name="last_window",
    )(me, in_hbm(pairs), *[in_vmem(x) for x in args])
    return kernel, mass, row_sums, shares


def keep_kernel(pairs_ref, block_ref, blocks_ref, out_ref, own_ref, sems):
    here = pl.program_id(0)

    def copies():
        for pair in range(own_ref.shape[0]):
            source = blocks_ref.at[pairs_ref[1, pair] & 7]
            yield pltpu.make_async_copy(source, own_ref.at[pair], sems.at[pair])

    @pl.when(here == 0)
    def _():
        for copy in copies():
            copy.start()

    out_ref[...] = block_ref[...]

    @pl.when(here == pl.num_programs(0) - 1)
    def _():
        for copy in copies():
            copy.wait()


def keep(pairs, blocks):
    pair_count = pairs.shape[1]
    block = pl.BlockSpec((1, *blocks.shape[1:]), lambda k: (k, 0, 0))
    return pl.pallas_call(
        keep_kernel,
        out_shape=[
            pltpu.HBM(blocks.shape, blocks.dtype),
            pltpu.VMEM((pair_count, *blocks.shape[1:]), blocks.dtype),
        ],
        grid=(blocks.shape[0],),
        in_specs=[smem(), block, anywhere()],
        out_specs=[block, anywhere()],
        scratch_shapes=[pltpu.SemaphoreType.DMA((pair_count,))],
        compiler_params=params(4),
        name="keep",
    )(in_hbm(pairs), in_hbm(blocks), in_hbm(blocks))


def mean_kernel(window, counts, local_ref, rows_ref, kernel_ref, mass_ref, total_ref, *refs):
    *refs, _, out_ref, part, weight, total, mass, made, sems = refs
    chunks = []
    for chunk, _, _ in segments(window):
        (own,), refs = take_parts(refs, counts[len(chunks)][:1])
        chunks.append(own)
    pair_count, _, feat = rows_ref.shape
    local = [local_ref[0, pair] & 7 for pair in range(pair_count)]

    def copy(pair):
        return pltpu.make_async_copy(made.at[pair], out_ref.at[local[pair]], sems.at[pair])

    firsts = []
    for pair in range(pair_count):
        sums = total_ref[pair] + jnp.dot(
            kernel_ref[pair], own_columns(window, chunks, pair), preferred_element_type=jnp.float32
        )
        part[pair] = sums.astype(jnp.bfloat16)
        weight[pair] = jnp.broadcast_to(
            jnp.sum(mass_ref[pair], axis=1, keepdims=True), (BR, LANES)
        )
        same = [local[other] == local[pair] for other in range(pair)]
        firsts.append(jnp.logical_not(functools.reduce(jnp.logical_or, same, jnp.bool_(False))))
    for pair in range(pair_count):

        @pl.when(firsts[pair])
        def _():
            total[...] = rows_ref[pair].astype(jnp.float32) + part[pair].astype(jnp.float32)
            mass[...] = 1.0 + weight[pair]
            for other in range(pair + 1, pair_count):

                @pl.when(local[other] == local[pair])
                def _():
                    total[...] += part[other].astype(jnp.float32)
                    mass[...] += weight[other]

            scale = 1.0 / mass[...]
            for at in range(0, feat, LANES):
                lanes = slice(at, at + LANES)
                made[pair, :, lanes] = (total[:, lanes] * scale).astype(jnp.bfloat16)
            copy(pair).start()

    for pair in range(pair_count):

        @pl.when(firsts[pair])
        def _():
            copy(pair).wait()


def means(pairs, rows, kernel, mass, total, cols, kept):
    pair_count, _, feat = rows.shape
    window = WINDOWS[1]
    own = operands(cols[chunk][0] for chunk, _, _ in segments(window))
    args = [in_vmem(x) for x in (rows, kernel, mass, total, *own)]
    return pl.pallas_call(
        functools.partial(mean_kernel, window, piece_counts(window, cols)),
        out_shape=pltpu.HBM(kept.shape, jnp.bfloat16),
        in_specs=[smem()] + [vmem()] * len(args) + [anywhere()],
        out_specs=anywhere(),
        scratch_shapes=[
            pltpu.VMEM((pair_count, BR, feat), jnp.bfloat16),
            pltpu.VMEM((pair_count, BR, LANES), jnp.float32),
            pltpu.VMEM((BR, feat), jnp.float32),
            pltpu.VMEM((BR, LANES), jnp.float32),
            pltpu.VMEM((pair_count, BR, feat), jnp.bfloat16),
            pltpu.SemaphoreType.DMA((pair_count,)),
        ],
        input_output_aliases={1 + len(args): 0},
        compiler_params=params(16),
        cost_estimate=estimate(pair_count, 128),
        name="means",
    )(in_hbm(pairs), *args, in_hbm(kept))


def weight_kernel(*refs):
    out_ref = refs[-1]
    mass = refs[0][...]
    for ref in refs[1:-1]:
        mass = mass + ref[...]
    weight = 1.0 / (1.0 + mass / BR)
    parts = BR // LANES
    for block in range(BLK_DEV):
        for part in range(parts):
            lanes = slice(part * LANES, (part + 1) * LANES)
            out_ref[block * parts + part : block * parts + part + 1] = weight[block : block + 1, lanes]


def block_weights(sums):
    out = pl.pallas_call(
        weight_kernel,
        out_shape=jax.ShapeDtypeStruct((BLK_DEV * BR // LANES, LANES), jnp.float32),
        in_specs=[vmem()] * len(sums),
        out_specs=vmem(),
        compiler_params=params(4),
        name="weights",
    )(*[in_vmem(x) for x in sums])
    return out.reshape(BLK_DEV * BR)


def hop(parts, step):
    count = lax.axis_size("narrow")
    perm = [(i, i ^ step) for i in range(count)]
    return [[lax.ppermute(piece, "narrow", perm) for piece in part] for part in parts]


def first_hops(part):
    parts = [part]
    step = lax.axis_size("narrow") // 2
    while step > 1:
        parts = parts + hop(parts, step)
        step //= 2
    return parts


def to_wide(pieces, apart):
    count = lax.axis_size("wide")
    return [
        lax.ppermute(piece, "wide", [(i, i ^ other) for i in range(count)])
        for piece, other in zip(pieces, apart)
    ]


def on_device(embeddings, pair_list):
    wide_count = lax.axis_size("wide")
    me = lax.axis_index("wide").astype(jnp.int32).reshape(1)
    pairs = pair_list.T
    pair_count = pairs.shape[1]
    capacity = max(2, 2 * pair_count // wide_count)
    feat = embeddings.shape[1]
    blocks = embeddings.reshape(BLK_DEV, BR, feat)
    apart = others(wide_count)
    lists = to_wide([pairs] * (wide_count - 1), apart[::-1])
    fixed = lax.optimization_barrier
    *outgoing, row_slices = pack(me, pairs, lists, blocks, capacity, 0, True)
    later = pack(me, pairs, lists, blocks, capacity, 1, False)

    def pick(received, chunk, *groups):
        return select(me, pairs, own, received, *CHUNKS[chunk], groups)

    def halves(part):
        middle = pair_count // 2
        return [part[0][:middle], part[0][middle:]]

    rows = jnp.stack([part[0] for part in first_hops([row_slices])])
    received = to_wide(outgoing, apart)
    near = to_wide(later[-1:], apart[-1:])
    rows, received, near, (kept, own) = fixed((rows, received, near, keep(pairs, blocks)))
    own_a, whole_a = pick(received, 0, 2, 1)
    cols_a = [own_a] + first_hops(whole_a)[1:]
    rows = [[rows], *hop([[rows]], 1)]
    cols_a, rows, received = fixed((cols_a, rows, to_wide(later[:-1], apart[:-1])))
    cols_b = first_hops(*pick([*received, *near], 1, 1))
    last_b = hop(cols_b[:1], 1)
    cols_a = cols_a + hop([own_a] + [halves(part) for part in cols_a[1:]], 1)
    carry = first_window(rows, [cols_a])
    cols_b, carry = fixed((cols_b, carry))
    cols_b = cols_b + last_b + hop(cols_b[1:], 1)
    square, mass, total, sums = carry
    kernel, mass, row_sums, shares = last_window(
        me, pairs, rows, [cols_a, cols_b], square, mass, sums, wide_count
    )
    came = to_wide(shares[:-1], sum_order(wide_count))
    mean = means(pairs, row_slices, kernel, mass, total, [cols_a, cols_b], kept)
    weights = block_weights([row_sums, shares[-1], *came])
    return weights, mean.reshape(BLK_DEV * BR, feat)


def solution(mesh):
    in_specs = (P(("groups", "wide"), "narrow"), P(("groups", "wide"), None))
    out_specs = (P(("groups", "wide")), P(("groups", "wide"), "narrow"))
    return jax.shard_map(
        on_device, mesh=mesh, in_specs=in_specs, out_specs=out_specs, check_vma=False
    )
```

```python
import functools

import jax
import jax.numpy as jnp
from jax import lax
from jax.experimental import pallas as pl
from jax.experimental.pallas import tpu as pltpu
from jax.sharding import PartitionSpec as P

F = 1024
BR = 512
BLK_DEV = 8
LANES = 128
CHUNKS = ((0, 336), (336, 176))
WINDOWS = ((0, 256), (256, 512))


def smem():
    return pl.BlockSpec(memory_space=pltpu.SMEM)


def vmem():
    return pl.BlockSpec(memory_space=pltpu.VMEM)


def anywhere():
    return pl.BlockSpec(memory_space=pl.ANY)


def in_vmem(x):
    return pltpu.with_memory_space_constraint(x, pltpu.VMEM)


def in_hbm(x):
    return pltpu.with_memory_space_constraint(x, pltpu.HBM)


def params(mebibytes):
    return pltpu.CompilerParams(vmem_limit_bytes=mebibytes * 1024 * 1024)


def others(wide_count):
    return range(wide_count - 1, 0, -1)


def pack_kernel(chunk, with_rows, wide_count, pair_count, capacity, me_ref, pairs_ref, *refs):
    lists, blocks_ref = refs[: wide_count - 1], refs[wide_count - 1]
    *outs, sems = refs[wide_count:]
    me = me_ref[0]
    start, size = CHUNKS[chunk]
    copies = []

    def send(source, target):
        copies.append(pltpu.make_async_copy(source, target, sems.at[len(copies)]))
        copies[-1].start()

    for number, other in enumerate(others(wide_count)):
        asked = lists[list_order(wide_count).index(other)]
        picks = [jnp.int32(0)] * capacity
        count = jnp.int32(0)
        for pair in range(pair_count):
            col = asked[1, pair]
            mine = (col >> 3) == me
            for slot in range(capacity):
                picks[slot] = jnp.where(mine & (count == slot), col & 7, picks[slot])
            count = count + mine.astype(jnp.int32)
        for slot in range(capacity):
            send(blocks_ref.at[picks[slot], pl.ds(start, size)], outs[number].at[slot])
    if with_rows:
        for pair in range(pair_count):
            send(blocks_ref.at[pairs_ref[0, pair] & 7], outs[-1].at[pair])
    for copy in copies:
        copy.wait()


def list_order(wide_count):
    middle = wide_count // 2
    return [other for other in range(1, wide_count) if other != middle] + [middle]


def sum_order(wide_count):
    return list_order(wide_count)[::-1]


def pack(me, pairs, lists, blocks, capacity, chunk, with_rows):
    wide_count, pair_count = len(lists) + 1, pairs.shape[1]
    feat = blocks.shape[-1]
    shapes = [pltpu.VMEM((capacity, CHUNKS[chunk][1], feat), blocks.dtype)] * (wide_count - 1)
    copies = len(shapes) * capacity
    if with_rows:
        shapes.append(pltpu.VMEM((pair_count, BR, feat), blocks.dtype))
        copies += pair_count
    return pl.pallas_call(
        functools.partial(pack_kernel, chunk, with_rows, wide_count, pair_count, capacity),
        out_shape=shapes,
        in_specs=[smem()] * (1 + wide_count) + [anywhere()],
        out_specs=[anywhere()] * len(shapes),
        scratch_shapes=[pltpu.SemaphoreType.DMA((copies,))],
        compiler_params=params(4),
        name="pack",
    )(me, in_hbm(pairs), *[lists[other - 1] for other in list_order(wide_count)], in_hbm(blocks))


def select_kernel(wide_count, groups, start, me_ref, pairs_ref, own_ref, *refs):
    pair_count = own_ref.shape[0]
    outs = refs[wide_count - 1 :]
    received = refs[: wide_count - 1]
    size = outs[0].shape[1]
    owners = [pairs_ref[1, pair] >> 3 for pair in range(pair_count)]
    for pair in range(pair_count):
        apart = me_ref[0] ^ owners[pair]
        rank = jnp.int32(0)
        for before in range(pair):
            rank = rank + (owners[before] == owners[pair]).astype(jnp.int32)

        places, rest = [], outs
        for pieces in groups:
            places.append(of_pair(rest[:pieces], pair))
            rest = rest[pieces:]

        @pl.when(apart == 0)
        def _():
            for out in places:
                out[...] = own_ref[pair, start : start + size]

        for number, other in enumerate(others(wide_count)):

            @pl.when(apart == other)
            def _():
                for out in places:
                    out[...] = received[number][rank]


def select(me, pairs, own, received, start, size, groups):
    pair_count, _, feat = own.shape
    shapes = [
        pltpu.VMEM((pair_count // pieces, size, feat), own.dtype)
        for pieces in groups
        for _ in range(pieces)
    ]
    outs = pl.pallas_call(
        functools.partial(select_kernel, len(received) + 1, groups, start),
        out_shape=shapes,
        in_specs=[smem(), smem()] + [vmem()] * (1 + len(received)),
        out_specs=[vmem()] * len(shapes),
        compiler_params=params(4),
        name="select",
    )(me, in_hbm(pairs), *[in_vmem(x) for x in (own, *received)])
    return take_parts(outs, groups)[0]


def tree(parts):
    while len(parts) > 1:
        half = len(parts) // 2
        parts = [parts[i] + parts[i + half] for i in range(half)]
    return parts[0]


def across(left, right):
    return lax.dot_general(
        left, right, (((1,), (1,)), ((), ())), preferred_element_type=jnp.float32
    )


def lane_sum(block):
    square = jnp.square(block.astype(jnp.float32))
    return sum(square[:, at : at + LANES] for at in range(0, square.shape[1], LANES))


def segments(window):
    low, high = window
    held = []
    for chunk, (start, size) in enumerate(CHUNKS):
        first, end = max(low, start), min(high, start + size)
        if first < end:
            held.append((chunk, first - start, end - first))
    return held


def scores(rows, cols, square):
    gram = tree([across(row, col) for row, col in zip(rows, cols)])
    other = jnp.sum(tree([lane_sum(col) for col in cols]).T, axis=0, keepdims=True)
    pieces, mass = [], None
    for at in range(0, gram.shape[1], LANES):
        here = slice(at, at + LANES)
        piece = jnp.exp((square + other[:, here] - 2.0 * gram[:, here]) * (-1.0 / F))
        mass = piece if mass is None else mass + piece
        pieces.append(piece)
    kernel = jnp.concatenate(pieces, axis=1) if len(pieces) > 1 else pieces[0]
    return kernel.astype(jnp.bfloat16), jnp.sum(kernel, axis=0, keepdims=True), mass


def take_parts(refs, counts):
    parts = []
    for count in counts:
        parts.append(refs[:count])
        refs = refs[count:]
    return parts, refs


def of_pair(part, pair):
    each = part[0].shape[0]
    return part[pair // each].at[pair % each]


def window_parts(counts, refs):
    half = len(counts[0]) // 2
    rows, refs = [ref.at[i] for ref in refs[:2] for i in range(half)], refs[2:]
    chunks = []
    for chunk_counts in counts:
        cols, refs = take_parts(refs, chunk_counts)
        chunks.append(cols)
    return rows, chunks


def own_columns(window, chunks, pair):
    held = segments(window)
    pieces = [of_pair(part, pair)[at : at + size] for part, (_, at, size) in zip(chunks, held)]
    return jnp.concatenate(pieces, axis=0) if len(pieces) > 1 else pieces[0]


def pair_parts(window, rows, chunks, pair):
    cols = [own_columns(window, [c[i] for c in chunks], pair) for i in range(len(rows))]
    return [part[pair] for part in rows], cols


def first_kernel(window, counts, *refs):
    square_ref, mass_ref, total_ref, sums_ref = refs[-4:]
    all_rows, chunks = window_parts(counts, refs)
    for pair in range(square_ref.shape[0]):
        rows, cols = pair_parts(window, all_rows, chunks, pair)
        square = jnp.sum(tree([lane_sum(row) for row in rows]), axis=1, keepdims=True)
        square = jnp.broadcast_to(square, (BR, LANES))
        kernel, sums, mass = scores(rows, cols, square)
        square_ref[pair] = square
        mass_ref[pair] = mass
        sums_ref[pair : pair + 1] = sums
        total_ref[pair] = jnp.dot(kernel, cols[0], preferred_element_type=jnp.float32)


def last_kernel(window, counts, wide_count, me_ref, pairs_ref, *refs):
    square_in, mass_in, sums_in = refs[-6 - wide_count : -3 - wide_count]
    kernel_ref, mass_ref, row_ref = refs[-3 - wide_count : -wide_count]
    shares = refs[-wide_count:]
    for ref in (row_ref, *shares):
        ref[...] = jnp.zeros_like(ref)
    all_rows, chunks = window_parts(counts, refs)
    for pair in range(square_in.shape[0]):
        rows, cols = pair_parts(window, all_rows, chunks, pair)
        kernel, sums, mass = scores(rows, cols, square_in[pair])
        kernel_ref[pair] = kernel
        sums = jnp.concatenate([sums_in[pair : pair + 1], sums], axis=1)
        mass = mass_in[pair] + mass
        mass_ref[pair] = mass
        row_ref[pl.ds(pairs_ref[0, pair] & 7, 1)] += jnp.sum(mass.T, axis=0, keepdims=True)
        col = pairs_ref[1, pair]
        apart = (col >> 3) ^ me_ref[0]
        for other, ref in zip([*sum_order(wide_count), 0], shares):
            ref[pl.ds(col & 7, 1)] += jnp.where(apart == other, sums, 0.0)


def estimate(pair_count, size):
    return pl.CostEstimate(
        flops=2 * pair_count * BR * size * F,
        transcendentals=pair_count * BR * size,
        bytes_accessed=8 * 1024 * 1024,
    )


def piece_counts(window, cols):
    return tuple(tuple(len(part) for part in cols[chunk]) for chunk, _, _ in segments(window))


def operands(parts):
    return [piece for part in parts for piece in part]


def first_window(rows, cols):
    _, pair_count, _, feat = rows[0][0].shape
    window = WINDOWS[0]
    lanes = pltpu.VMEM((pair_count, BR, LANES), jnp.float32)
    total = pltpu.VMEM((pair_count, BR, feat), jnp.float32)
    args = operands(rows)
    for chunk, _, _ in segments(window):
        args += operands(cols[chunk])
    return pl.pallas_call(
        functools.partial(first_kernel, window, piece_counts(window, cols)),
        out_shape=[lanes, lanes, total, pltpu.VMEM((pair_count, window[1]), jnp.float32)],
        in_specs=[vmem()] * len(args),
        out_specs=[vmem()] * 4,
        compiler_params=params(16),
        cost_estimate=pl.CostEstimate(flops=0, transcendentals=0, bytes_accessed=0),
        name="first_window",
    )(*[in_vmem(x) for x in args])


def last_window(me, pairs, rows, cols, square, mass, sums, wide_count):
    pair_count = rows[0][0].shape[1]
    window = WINDOWS[1]
    size = window[1] - window[0]
    by_block = pltpu.VMEM((BLK_DEV, BR), jnp.float32)
    shapes = [
        pltpu.VMEM((pair_count, BR, size), jnp.bfloat16),
        pltpu.VMEM((pair_count, BR, LANES), jnp.float32),
    ] + [by_block] * (1 + wide_count)
    args = operands(rows)
    for chunk, _, _ in segments(window):
        args += operands(cols[chunk])
    args += [square, mass, sums]
    kernel, mass, row_sums, *shares = pl.pallas_call(
        functools.partial(last_kernel, window, piece_counts(window, cols), wide_count),
        out_shape=shapes,
        in_specs=[smem(), smem()] + [vmem()] * len(args),
        out_specs=[vmem()] * len(shapes),
        compiler_params=params(16),
        cost_estimate=estimate(pair_count, size),
        name="last_window",
    )(me, in_hbm(pairs), *[in_vmem(x) for x in args])
    return kernel, mass, row_sums, shares


def keep_kernel(pairs_ref, block_ref, blocks_ref, out_ref, own_ref, sems):
    here = pl.program_id(0)

    def copies():
        for pair in range(own_ref.shape[0]):
            source = blocks_ref.at[pairs_ref[1, pair] & 7]
            yield pltpu.make_async_copy(source, own_ref.at[pair], sems.at[pair])

    @pl.when(here == 0)
    def _():
        for copy in copies():
            copy.start()

    out_ref[...] = block_ref[...]

    @pl.when(here == pl.num_programs(0) - 1)
    def _():
        for copy in copies():
            copy.wait()


def keep(pairs, blocks):
    pair_count = pairs.shape[1]
    block = pl.BlockSpec((1, *blocks.shape[1:]), lambda k: (k, 0, 0))
    return pl.pallas_call(
        keep_kernel,
        out_shape=[
            pltpu.HBM(blocks.shape, blocks.dtype),
            pltpu.VMEM((pair_count, *blocks.shape[1:]), blocks.dtype),
        ],
        grid=(blocks.shape[0],),
        in_specs=[smem(), block, anywhere()],
        out_specs=[block, anywhere()],
        scratch_shapes=[pltpu.SemaphoreType.DMA((pair_count,))],
        compiler_params=params(4),
        name="keep",
    )(in_hbm(pairs), in_hbm(blocks), in_hbm(blocks))


def mean_kernel(window, counts, local_ref, rows_ref, kernel_ref, mass_ref, total_ref, *refs):
    *refs, _, out_ref, part, weight, total, mass, made, sems = refs
    chunks = []
    for chunk, _, _ in segments(window):
        (own,), refs = take_parts(refs, counts[len(chunks)][:1])
        chunks.append(own)
    pair_count, _, feat = rows_ref.shape
    local = [local_ref[0, pair] & 7 for pair in range(pair_count)]

    def copy(pair):
        return pltpu.make_async_copy(made.at[pair], out_ref.at[local[pair]], sems.at[pair])

    firsts = []
    for pair in range(pair_count):
        sums = total_ref[pair] + jnp.dot(
            kernel_ref[pair], own_columns(window, chunks, pair), preferred_element_type=jnp.float32
        )
        part[pair] = sums.astype(jnp.bfloat16)
        weight[pair] = jnp.broadcast_to(
            jnp.sum(mass_ref[pair], axis=1, keepdims=True), (BR, LANES)
        )
        same = [local[other] == local[pair] for other in range(pair)]
        firsts.append(jnp.logical_not(functools.reduce(jnp.logical_or, same, jnp.bool_(False))))
    for pair in range(pair_count):

        @pl.when(firsts[pair])
        def _():
            total[...] = rows_ref[pair].astype(jnp.float32) + part[pair].astype(jnp.float32)
            mass[...] = 1.0 + weight[pair]
            for other in range(pair + 1, pair_count):

                @pl.when(local[other] == local[pair])
                def _():
                    total[...] += part[other].astype(jnp.float32)
                    mass[...] += weight[other]

            scale = 1.0 / mass[...]
            for at in range(0, feat, LANES):
                lanes = slice(at, at + LANES)
                made[pair, :, lanes] = (total[:, lanes] * scale).astype(jnp.bfloat16)
            copy(pair).start()

    for pair in range(pair_count):

        @pl.when(firsts[pair])
        def _():
            copy(pair).wait()


def means(pairs, rows, kernel, mass, total, cols, kept):
    pair_count, _, feat = rows.shape
    window = WINDOWS[1]
    own = operands(cols[chunk][0] for chunk, _, _ in segments(window))
    args = [in_vmem(x) for x in (rows, kernel, mass, total, *own)]
    return pl.pallas_call(
        functools.partial(mean_kernel, window, piece_counts(window, cols)),
        out_shape=pltpu.HBM(kept.shape, jnp.bfloat16),
        in_specs=[smem()] + [vmem()] * len(args) + [anywhere()],
        out_specs=anywhere(),
        scratch_shapes=[
            pltpu.VMEM((pair_count, BR, feat), jnp.bfloat16),
            pltpu.VMEM((pair_count, BR, LANES), jnp.float32),
            pltpu.VMEM((BR, feat), jnp.float32),
            pltpu.VMEM((BR, LANES), jnp.float32),
            pltpu.VMEM((pair_count, BR, feat), jnp.bfloat16),
            pltpu.SemaphoreType.DMA((pair_count,)),
        ],
        input_output_aliases={1 + len(args): 0},
        compiler_params=params(16),
        cost_estimate=estimate(pair_count, 128),
        name="means",
    )(in_hbm(pairs), *args, in_hbm(kept))


def weight_kernel(*refs):
    out_ref = refs[-1]
    mass = refs[0][...]
    for ref in refs[1:-1]:
        mass = mass + ref[...]
    weight = 1.0 / (1.0 + mass / BR)
    parts = BR // LANES
    for block in range(BLK_DEV):
        for part in range(parts):
            lanes = slice(part * LANES, (part + 1) * LANES)
            out_ref[block * parts + part : block * parts + part + 1] = weight[block : block + 1, lanes]


def block_weights(sums):
    out = pl.pallas_call(
        weight_kernel,
        out_shape=jax.ShapeDtypeStruct((BLK_DEV * BR // LANES, LANES), jnp.float32),
        in_specs=[vmem()] * len(sums),
        out_specs=vmem(),
        compiler_params=params(4),
        name="weights",
    )(*[in_vmem(x) for x in sums])
    return out.reshape(BLK_DEV * BR)


def hop(parts, step):
    count = lax.axis_size("narrow")
    perm = [(i, i ^ step) for i in range(count)]
    return [[lax.ppermute(piece, "narrow", perm) for piece in part] for part in parts]


def first_hops(part):
    parts = [part]
    step = lax.axis_size("narrow") // 2
    while step > 1:
        parts = parts + hop(parts, step)
        step //= 2
    return parts


def to_wide(pieces, apart):
    count = lax.axis_size("wide")
    return [
        lax.ppermute(piece, "wide", [(i, i ^ other) for i in range(count)])
        for piece, other in zip(pieces, apart)
    ]


def on_device(embeddings, pair_list):
    wide_count = lax.axis_size("wide")
    me = lax.axis_index("wide").astype(jnp.int32).reshape(1)
    pairs = pair_list.T
    pair_count = pairs.shape[1]
    capacity = max(2, 2 * pair_count // wide_count)
    feat = embeddings.shape[1]
    blocks = embeddings.reshape(BLK_DEV, BR, feat)
    apart = others(wide_count)
    lists = to_wide([pairs] * (wide_count - 1), apart[::-1])
    fixed = lax.optimization_barrier
    *outgoing, row_slices = pack(me, pairs, lists, blocks, capacity, 0, True)
    later = pack(me, pairs, lists, blocks, capacity, 1, False)

    def pick(received, chunk, *groups):
        return select(me, pairs, own, received, *CHUNKS[chunk], groups)

    def halves(part):
        middle = pair_count // 2
        return [part[0][:middle], part[0][middle:]]

    rows = jnp.stack([part[0] for part in first_hops([row_slices])])
    received = to_wide(outgoing, apart)
    near = to_wide(later[-1:], apart[-1:])
    rows, received, near, (kept, own) = fixed((rows, received, near, keep(pairs, blocks)))
    own_a, whole_a = pick(received, 0, 2, 1)
    cols_a = [own_a] + first_hops(whole_a)[1:]
    rows = [[rows], *hop([[rows]], 1)]
    cols_a, rows, received = fixed((cols_a, rows, to_wide(later[:-1], apart[:-1])))
    cols_b = first_hops(*pick([*received, *near], 1, 1))
    last_b = hop(cols_b[:1], 1)
    cols_a = cols_a + hop([own_a] + [halves(part) for part in cols_a[1:]], 1)
    carry = first_window(rows, [cols_a])
    cols_b, carry = fixed((cols_b, carry))
    cols_b = cols_b + last_b + hop(cols_b[1:], 1)
    square, mass, total, sums = carry
    kernel, mass, row_sums, shares = last_window(
        me, pairs, rows, [cols_a, cols_b], square, mass, sums, wide_count
    )
    came = to_wide(shares[:-1], sum_order(wide_count))
    mean = means(pairs, row_slices, kernel, mass, total, [cols_a, cols_b], kept)
    weights = block_weights([row_sums, shares[-1], *came])
    return weights, mean.reshape(BLK_DEV * BR, feat)


def solution(mesh):
    in_specs = (P(("groups", "wide"), "narrow"), P(("groups", "wide"), None))
    out_specs = (P(("groups", "wide")), P(("groups", "wide"), "narrow"))
    return jax.shard_map(
        on_device, mesh=mesh, in_specs=in_specs, out_specs=out_specs, check_vma=False
    )
```

```python
import functools

import jax
import jax.numpy as jnp
from jax import lax
from jax.experimental import pallas as pl
from jax.experimental.pallas import tpu as pltpu
from jax.sharding import PartitionSpec as P

F = 1024
BR = 512
BLK_DEV = 8
LANES = 128
CHUNKS = ((0, 336), (336, 176))
WINDOWS = ((0, 256), (256, 512))


def smem():
    return pl.BlockSpec(memory_space=pltpu.SMEM)


def vmem():
    return pl.BlockSpec(memory_space=pltpu.VMEM)


def anywhere():
    return pl.BlockSpec(memory_space=pl.ANY)


def in_vmem(x):
    return pltpu.with_memory_space_constraint(x, pltpu.VMEM)


def in_hbm(x):
    return pltpu.with_memory_space_constraint(x, pltpu.HBM)


def params(mebibytes):
    return pltpu.CompilerParams(vmem_limit_bytes=mebibytes * 1024 * 1024)


def others(wide_count):
    middle = wide_count // 2
    return [middle] + [other for other in range(wide_count - 1, 0, -1) if other != middle]


def pack_kernel(chunk, with_rows, wide_count, pair_count, capacity, me_ref, pairs_ref, *refs):
    lists, blocks_ref = refs[: wide_count - 1], refs[wide_count - 1]
    *outs, sems = refs[wide_count:]
    me = me_ref[0]
    start, size = CHUNKS[chunk]
    copies = []

    def send(source, target):
        copies.append(pltpu.make_async_copy(source, target, sems.at[len(copies)]))
        copies[-1].start()

    for number, other in enumerate(others(wide_count)):
        asked = lists[list_order(wide_count).index(other)]
        picks = [jnp.int32(0)] * capacity
        count = jnp.int32(0)
        for pair in range(pair_count):
            col = asked[1, pair]
            mine = (col >> 3) == me
            for slot in range(capacity):
                picks[slot] = jnp.where(mine & (count == slot), col & 7, picks[slot])
            count = count + mine.astype(jnp.int32)
        for slot in range(capacity):
            send(blocks_ref.at[picks[slot], pl.ds(start, size)], outs[number].at[slot])
    if with_rows:
        for pair in range(pair_count):
            send(blocks_ref.at[pairs_ref[0, pair] & 7], outs[-1].at[pair])
    for copy in copies:
        copy.wait()


def list_order(wide_count):
    middle = wide_count // 2
    return [other for other in range(1, wide_count) if other != middle] + [middle]


def sum_order(wide_count):
    return list_order(wide_count)[::-1]


def pack(me, pairs, lists, blocks, capacity, chunk, with_rows):
    wide_count, pair_count = len(lists) + 1, pairs.shape[1]
    feat = blocks.shape[-1]
    shapes = [pltpu.VMEM((capacity, CHUNKS[chunk][1], feat), blocks.dtype)] * (wide_count - 1)
    copies = len(shapes) * capacity
    if with_rows:
        shapes.append(pltpu.VMEM((pair_count, BR, feat), blocks.dtype))
        copies += pair_count
    return pl.pallas_call(
        functools.partial(pack_kernel, chunk, with_rows, wide_count, pair_count, capacity),
        out_shape=shapes,
        in_specs=[smem()] * (1 + wide_count) + [anywhere()],
        out_specs=[anywhere()] * len(shapes),
        scratch_shapes=[pltpu.SemaphoreType.DMA((copies,))],
        compiler_params=params(4),
        name="pack",
    )(me, in_hbm(pairs), *[lists[other - 1] for other in list_order(wide_count)], in_hbm(blocks))


def select_kernel(wide_count, groups, start, me_ref, pairs_ref, own_ref, *refs):
    pair_count = own_ref.shape[0]
    outs = refs[wide_count - 1 :]
    received = refs[: wide_count - 1]
    size = outs[0].shape[1]
    owners = [pairs_ref[1, pair] >> 3 for pair in range(pair_count)]
    for pair in range(pair_count):
        apart = me_ref[0] ^ owners[pair]
        rank = jnp.int32(0)
        for before in range(pair):
            rank = rank + (owners[before] == owners[pair]).astype(jnp.int32)

        places, rest = [], outs
        for pieces in groups:
            places.append(of_pair(rest[:pieces], pair))
            rest = rest[pieces:]

        @pl.when(apart == 0)
        def _():
            for out in places:
                out[...] = own_ref[pair, start : start + size]

        for number, other in enumerate(others(wide_count)):

            @pl.when(apart == other)
            def _():
                for out in places:
                    out[...] = received[number][rank]


def select(me, pairs, own, received, start, size, groups):
    pair_count, _, feat = own.shape
    shapes = [
        pltpu.VMEM((pair_count // pieces, size, feat), own.dtype)
        for pieces in groups
        for _ in range(pieces)
    ]
    outs = pl.pallas_call(
        functools.partial(select_kernel, len(received) + 1, groups, start),
        out_shape=shapes,
        in_specs=[smem(), smem()] + [vmem()] * (1 + len(received)),
        out_specs=[vmem()] * len(shapes),
        compiler_params=params(4),
        name="select",
    )(me, in_hbm(pairs), *[in_vmem(x) for x in (own, *received)])
    return take_parts(outs, groups)[0]


def tree(parts):
    while len(parts) > 1:
        half = len(parts) // 2
        parts = [parts[i] + parts[i + half] for i in range(half)]
    return parts[0]


def across(left, right):
    return lax.dot_general(
        left, right, (((1,), (1,)), ((), ())), preferred_element_type=jnp.float32
    )


def lane_sum(block):
    square = jnp.square(block.astype(jnp.float32))
    return sum(square[:, at : at + LANES] for at in range(0, square.shape[1], LANES))


def segments(window):
    low, high = window
    held = []
    for chunk, (start, size) in enumerate(CHUNKS):
        first, end = max(low, start), min(high, start + size)
        if first < end:
            held.append((chunk, first - start, end - first))
    return held


def scores(rows, cols, square):
    gram = tree([across(row, col) for row, col in zip(rows, cols)])
    other = jnp.sum(tree([lane_sum(col) for col in cols]).T, axis=0, keepdims=True)
    pieces, mass = [], None
    for at in range(0, gram.shape[1], LANES):
        here = slice(at, at + LANES)
        piece = jnp.exp((square + other[:, here] - 2.0 * gram[:, here]) * (-1.0 / F))
        mass = piece if mass is None else mass + piece
        pieces.append(piece)
    kernel = jnp.concatenate(pieces, axis=1) if len(pieces) > 1 else pieces[0]
    return kernel.astype(jnp.bfloat16), jnp.sum(kernel, axis=0, keepdims=True), mass


def take_parts(refs, counts):
    parts = []
    for count in counts:
        parts.append(refs[:count])
        refs = refs[count:]
    return parts, refs


def of_pair(part, pair):
    each = part[0].shape[0]
    return part[pair // each].at[pair % each]


def window_parts(counts, refs):
    half = len(counts[0]) // 2
    rows, refs = [ref.at[i] for ref in refs[:2] for i in range(half)], refs[2:]
    chunks = []
    for chunk_counts in counts:
        cols, refs = take_parts(refs, chunk_counts)
        chunks.append(cols)
    return rows, chunks


def own_columns(window, chunks, pair):
    held = segments(window)
    pieces = [of_pair(part, pair)[at : at + size] for part, (_, at, size) in zip(chunks, held)]
    return jnp.concatenate(pieces, axis=0) if len(pieces) > 1 else pieces[0]


def pair_parts(window, rows, chunks, pair):
    cols = [own_columns(window, [c[i] for c in chunks], pair) for i in range(len(rows))]
    return [part[pair] for part in rows], cols


def first_kernel(window, counts, *refs):
    square_ref, mass_ref, total_ref, sums_ref = refs[-4:]
    all_rows, chunks = window_parts(counts, refs)
    for pair in range(square_ref.shape[0]):
        rows, cols = pair_parts(window, all_rows, chunks, pair)
        square = jnp.sum(tree([lane_sum(row) for row in rows]), axis=1, keepdims=True)
        square = jnp.broadcast_to(square, (BR, LANES))
        kernel, sums, mass = scores(rows, cols, square)
        square_ref[pair] = square
        mass_ref[pair] = mass
        sums_ref[pair : pair + 1] = sums
        total_ref[pair] = jnp.dot(kernel, cols[0], preferred_element_type=jnp.float32)


def last_kernel(window, counts, wide_count, me_ref, pairs_ref, *refs):
    square_in, mass_in, sums_in = refs[-6 - wide_count : -3 - wide_count]
    kernel_ref, mass_ref, row_ref = refs[-3 - wide_count : -wide_count]
    shares = refs[-wide_count:]
    for ref in (row_ref, *shares):
        ref[...] = jnp.zeros_like(ref)
    all_rows, chunks = window_parts(counts, refs)
    for pair in range(square_in.shape[0]):
        rows, cols = pair_parts(window, all_rows, chunks, pair)
        kernel, sums, mass = scores(rows, cols, square_in[pair])
        kernel_ref[pair] = kernel
        sums = jnp.concatenate([sums_in[pair : pair + 1], sums], axis=1)
        mass = mass_in[pair] + mass
        mass_ref[pair] = mass
        row_ref[pl.ds(pairs_ref[0, pair] & 7, 1)] += jnp.sum(mass.T, axis=0, keepdims=True)
        col = pairs_ref[1, pair]
        apart = (col >> 3) ^ me_ref[0]
        for other, ref in zip([*sum_order(wide_count), 0], shares):
            ref[pl.ds(col & 7, 1)] += jnp.where(apart == other, sums, 0.0)


def estimate(pair_count, size):
    return pl.CostEstimate(
        flops=2 * pair_count * BR * size * F,
        transcendentals=pair_count * BR * size,
        bytes_accessed=8 * 1024 * 1024,
    )


def piece_counts(window, cols):
    return tuple(tuple(len(part) for part in cols[chunk]) for chunk, _, _ in segments(window))


def operands(parts):
    return [piece for part in parts for piece in part]


def first_window(rows, cols):
    _, pair_count, _, feat = rows[0][0].shape
    window = WINDOWS[0]
    lanes = pltpu.VMEM((pair_count, BR, LANES), jnp.float32)
    total = pltpu.VMEM((pair_count, BR, feat), jnp.float32)
    args = operands(rows)
    for chunk, _, _ in segments(window):
        args += operands(cols[chunk])
    return pl.pallas_call(
        functools.partial(first_kernel, window, piece_counts(window, cols)),
        out_shape=[lanes, lanes, total, pltpu.VMEM((pair_count, window[1]), jnp.float32)],
        in_specs=[vmem()] * len(args),
        out_specs=[vmem()] * 4,
        compiler_params=params(16),
        cost_estimate=pl.CostEstimate(flops=0, transcendentals=0, bytes_accessed=0),
        name="first_window",
    )(*[in_vmem(x) for x in args])


def last_window(me, pairs, rows, cols, square, mass, sums, wide_count):
    pair_count = rows[0][0].shape[1]
    window = WINDOWS[1]
    size = window[1] - window[0]
    by_block = pltpu.VMEM((BLK_DEV, BR), jnp.float32)
    shapes = [
        pltpu.VMEM((pair_count, BR, size), jnp.bfloat16),
        pltpu.VMEM((pair_count, BR, LANES), jnp.float32),
    ] + [by_block] * (1 + wide_count)
    args = operands(rows)
    for chunk, _, _ in segments(window):
        args += operands(cols[chunk])
    args += [square, mass, sums]
    kernel, mass, row_sums, *shares = pl.pallas_call(
        functools.partial(last_kernel, window, piece_counts(window, cols), wide_count),
        out_shape=shapes,
        in_specs=[smem(), smem()] + [vmem()] * len(args),
        out_specs=[vmem()] * len(shapes),
        compiler_params=params(16),
        cost_estimate=estimate(pair_count, size),
        name="last_window",
    )(me, in_hbm(pairs), *[in_vmem(x) for x in args])
    return kernel, mass, row_sums, shares


def keep_kernel(pairs_ref, block_ref, blocks_ref, out_ref, own_ref, sems):
    here = pl.program_id(0)

    def copies():
        for pair in range(own_ref.shape[0]):
            source = blocks_ref.at[pairs_ref[1, pair] & 7]
            yield pltpu.make_async_copy(source, own_ref.at[pair], sems.at[pair])

    @pl.when(here == 0)
    def _():
        for copy in copies():
            copy.start()

    out_ref[...] = block_ref[...]

    @pl.when(here == pl.num_programs(0) - 1)
    def _():
        for copy in copies():
            copy.wait()


def keep(pairs, blocks):
    pair_count = pairs.shape[1]
    block = pl.BlockSpec((1, *blocks.shape[1:]), lambda k: (k, 0, 0))
    return pl.pallas_call(
        keep_kernel,
        out_shape=[
            pltpu.HBM(blocks.shape, blocks.dtype),
            pltpu.VMEM((pair_count, *blocks.shape[1:]), blocks.dtype),
        ],
        grid=(blocks.shape[0],),
        in_specs=[smem(), block, anywhere()],
        out_specs=[block, anywhere()],
        scratch_shapes=[pltpu.SemaphoreType.DMA((pair_count,))],
        compiler_params=params(4),
        name="keep",
    )(in_hbm(pairs), in_hbm(blocks), in_hbm(blocks))


def mean_kernel(window, counts, local_ref, rows_ref, kernel_ref, mass_ref, total_ref, *refs):
    *refs, _, out_ref, part, weight, total, mass, made, sems = refs
    chunks = []
    for chunk, _, _ in segments(window):
        (own,), refs = take_parts(refs, counts[len(chunks)][:1])
        chunks.append(own)
    pair_count, _, feat = rows_ref.shape
    local = [local_ref[0, pair] & 7 for pair in range(pair_count)]

    def copy(pair):
        return pltpu.make_async_copy(made.at[pair], out_ref.at[local[pair]], sems.at[pair])

    firsts = []
    for pair in range(pair_count):
        sums = total_ref[pair] + jnp.dot(
            kernel_ref[pair], own_columns(window, chunks, pair), preferred_element_type=jnp.float32
        )
        part[pair] = sums.astype(jnp.bfloat16)
        weight[pair] = jnp.broadcast_to(
            jnp.sum(mass_ref[pair], axis=1, keepdims=True), (BR, LANES)
        )
        same = [local[other] == local[pair] for other in range(pair)]
        firsts.append(jnp.logical_not(functools.reduce(jnp.logical_or, same, jnp.bool_(False))))
    for pair in range(pair_count):

        @pl.when(firsts[pair])
        def _():
            total[...] = rows_ref[pair].astype(jnp.float32) + part[pair].astype(jnp.float32)
            mass[...] = 1.0 + weight[pair]
            for other in range(pair + 1, pair_count):

                @pl.when(local[other] == local[pair])
                def _():
                    total[...] += part[other].astype(jnp.float32)
                    mass[...] += weight[other]

            scale = 1.0 / mass[...]
            for at in range(0, feat, LANES):
                lanes = slice(at, at + LANES)
                made[pair, :, lanes] = (total[:, lanes] * scale).astype(jnp.bfloat16)
            copy(pair).start()

    for pair in range(pair_count):

        @pl.when(firsts[pair])
        def _():
            copy(pair).wait()


def means(pairs, rows, kernel, mass, total, cols, kept):
    pair_count, _, feat = rows.shape
    window = WINDOWS[1]
    own = operands(cols[chunk][0] for chunk, _, _ in segments(window))
    args = [in_vmem(x) for x in (rows, kernel, mass, total, *own)]
    return pl.pallas_call(
        functools.partial(mean_kernel, window, piece_counts(window, cols)),
        out_shape=pltpu.HBM(kept.shape, jnp.bfloat16),
        in_specs=[smem()] + [vmem()] * len(args) + [anywhere()],
        out_specs=anywhere(),
        scratch_shapes=[
            pltpu.VMEM((pair_count, BR, feat), jnp.bfloat16),
            pltpu.VMEM((pair_count, BR, LANES), jnp.float32),
            pltpu.VMEM((BR, feat), jnp.float32),
            pltpu.VMEM((BR, LANES), jnp.float32),
            pltpu.VMEM((pair_count, BR, feat), jnp.bfloat16),
            pltpu.SemaphoreType.DMA((pair_count,)),
        ],
        input_output_aliases={1 + len(args): 0},
        compiler_params=params(16),
        cost_estimate=estimate(pair_count, 128),
        name="means",
    )(in_hbm(pairs), *args, in_hbm(kept))


def weight_kernel(*refs):
    out_ref = refs[-1]
    mass = refs[0][...]
    for ref in refs[1:-1]:
        mass = mass + ref[...]
    weight = 1.0 / (1.0 + mass / BR)
    parts = BR // LANES
    for block in range(BLK_DEV):
        for part in range(parts):
            lanes = slice(part * LANES, (part + 1) * LANES)
            out_ref[block * parts + part : block * parts + part + 1] = weight[block : block + 1, lanes]


def block_weights(sums):
    out = pl.pallas_call(
        weight_kernel,
        out_shape=jax.ShapeDtypeStruct((BLK_DEV * BR // LANES, LANES), jnp.float32),
        in_specs=[vmem()] * len(sums),
        out_specs=vmem(),
        compiler_params=params(4),
        name="weights",
    )(*[in_vmem(x) for x in sums])
    return out.reshape(BLK_DEV * BR)


def hop(parts, step):
    count = lax.axis_size("narrow")
    perm = [(i, i ^ step) for i in range(count)]
    return [[lax.ppermute(piece, "narrow", perm) for piece in part] for part in parts]


def first_hops(part):
    parts = [part]
    step = lax.axis_size("narrow") // 2
    while step > 1:
        parts = parts + hop(parts, step)
        step //= 2
    return parts


def to_wide(pieces, apart):
    count = lax.axis_size("wide")
    return [
        lax.ppermute(piece, "wide", [(i, i ^ other) for i in range(count)])
        for piece, other in zip(pieces, apart)
    ]


def on_device(embeddings, pair_list):
    wide_count = lax.axis_size("wide")
    me = lax.axis_index("wide").astype(jnp.int32).reshape(1)
    pairs = pair_list.T
    pair_count = pairs.shape[1]
    capacity = max(2, 2 * pair_count // wide_count)
    feat = embeddings.shape[1]
    blocks = embeddings.reshape(BLK_DEV, BR, feat)
    apart = others(wide_count)
    lists = to_wide([pairs] * (wide_count - 1), range(1, wide_count))
    fixed = lax.optimization_barrier
    *outgoing, row_slices = pack(me, pairs, lists, blocks, capacity, 0, True)
    later = pack(me, pairs, lists, blocks, capacity, 1, False)

    def pick(received, chunk, *groups):
        return select(me, pairs, own, received, *CHUNKS[chunk], groups)

    def halves(part):
        middle = pair_count // 2
        return [part[0][:middle], part[0][middle:]]

    rows = jnp.stack([part[0] for part in first_hops([row_slices])])
    received = to_wide(outgoing, apart)
    near = to_wide(later[-1:], apart[-1:])
    rows, received, near, (kept, own) = fixed((rows, received, near, keep(pairs, blocks)))
    own_a, whole_a = pick(received, 0, 2, 1)
    cols_a = [own_a] + first_hops(whole_a)[1:]
    rows = [[rows], *hop([[rows]], 1)]
    cols_a, rows, received = fixed((cols_a, rows, to_wide(later[:-1], apart[:-1])))
    cols_b = first_hops(*pick([*received, *near], 1, 1))
    last_b = hop(cols_b[:1], 1)
    cols_a = cols_a + hop([own_a] + [halves(part) for part in cols_a[1:]], 1)
    carry = first_window(rows, [cols_a])
    cols_b, carry = fixed((cols_b, carry))
    cols_b = cols_b + last_b + hop(cols_b[1:], 1)
    square, mass, total, sums = carry
    kernel, mass, row_sums, shares = last_window(
        me, pairs, rows, [cols_a, cols_b], square, mass, sums, wide_count
    )
    came = to_wide(shares[:-1], sum_order(wide_count))
    mean = means(pairs, row_slices, kernel, mass, total, [cols_a, cols_b], kept)
    weights = block_weights([row_sums, shares[-1], *came])
    return weights, mean.reshape(BLK_DEV * BR, feat)


def solution(mesh):
    in_specs = (P(("groups", "wide"), "narrow"), P(("groups", "wide"), None))
    out_specs = (P(("groups", "wide")), P(("groups", "wide"), "narrow"))
    return jax.shard_map(
        on_device, mesh=mesh, in_specs=in_specs, out_specs=out_specs, check_vma=False
    )
```

```python
import functools

import jax
import jax.numpy as jnp
from jax import lax
from jax.experimental import pallas as pl
from jax.experimental.pallas import tpu as pltpu
from jax.sharding import PartitionSpec as P

F = 1024
BR = 512
BLK_DEV = 8
LANES = 128
CHUNKS = ((0, 336), (336, 176))
WINDOWS = ((0, 256), (256, 512))


def smem():
    return pl.BlockSpec(memory_space=pltpu.SMEM)


def vmem():
    return pl.BlockSpec(memory_space=pltpu.VMEM)


def anywhere():
    return pl.BlockSpec(memory_space=pl.ANY)


def in_vmem(x):
    return pltpu.with_memory_space_constraint(x, pltpu.VMEM)


def in_hbm(x):
    return pltpu.with_memory_space_constraint(x, pltpu.HBM)


def params(mebibytes):
    return pltpu.CompilerParams(vmem_limit_bytes=mebibytes * 1024 * 1024)


def others(wide_count):
    return range(wide_count - 1, 0, -1)


def pack_kernel(chunk, with_rows, wide_count, pair_count, capacity, me_ref, pairs_ref, *refs):
    lists, blocks_ref = refs[: wide_count - 1], refs[wide_count - 1]
    *outs, sems = refs[wide_count:]
    me = me_ref[0]
    start, size = CHUNKS[chunk]
    copies = []

    def send(source, target):
        copies.append(pltpu.make_async_copy(source, target, sems.at[len(copies)]))
        copies[-1].start()

    for number, other in enumerate(others(wide_count)):
        asked = lists[list_order(wide_count).index(other)]
        picks = [jnp.int32(0)] * capacity
        count = jnp.int32(0)
        for pair in range(pair_count):
            col = asked[1, pair]
            mine = (col >> 3) == me
            for slot in range(capacity):
                picks[slot] = jnp.where(mine & (count == slot), col & 7, picks[slot])
            count = count + mine.astype(jnp.int32)
        for slot in range(capacity):
            send(blocks_ref.at[picks[slot], pl.ds(start, size)], outs[number].at[slot])
    if with_rows:
        for pair in range(pair_count):
            send(blocks_ref.at[pairs_ref[0, pair] & 7], outs[-1].at[pair])
    for copy in copies:
        copy.wait()


def list_order(wide_count):
    middle = wide_count // 2
    return [other for other in range(1, wide_count) if other != middle] + [middle]


def sum_order(wide_count):
    return list_order(wide_count)[::-1]


def pack(me, pairs, lists, blocks, capacity, chunk, with_rows):
    wide_count, pair_count = len(lists) + 1, pairs.shape[1]
    feat = blocks.shape[-1]
    shapes = [pltpu.VMEM((capacity, CHUNKS[chunk][1], feat), blocks.dtype)] * (wide_count - 1)
    copies = len(shapes) * capacity
    if with_rows:
        shapes.append(pltpu.VMEM((pair_count, BR, feat), blocks.dtype))
        copies += pair_count
    return pl.pallas_call(
        functools.partial(pack_kernel, chunk, with_rows, wide_count, pair_count, capacity),
        out_shape=shapes,
        in_specs=[smem()] * (1 + wide_count) + [anywhere()],
        out_specs=[anywhere()] * len(shapes),
        scratch_shapes=[pltpu.SemaphoreType.DMA((copies,))],
        compiler_params=params(4),
        name="pack",
    )(me, in_hbm(pairs), *[lists[other - 1] for other in list_order(wide_count)], in_hbm(blocks))


def select_kernel(apart_of, groups, start, me_ref, pairs_ref, own_ref, *refs):
    pair_count = own_ref.shape[0]
    outs = refs[len(apart_of) :]
    received = refs[: len(apart_of)]
    size = outs[0].shape[1]
    owners = [pairs_ref[1, pair] >> 3 for pair in range(pair_count)]
    for pair in range(pair_count):
        apart = me_ref[0] ^ owners[pair]
        rank = jnp.int32(0)
        for before in range(pair):
            rank = rank + (owners[before] == owners[pair]).astype(jnp.int32)

        places, rest = [], outs
        for pieces in groups:
            places.append(of_pair(rest[:pieces], pair))
            rest = rest[pieces:]

        @pl.when(apart == 0)
        def _():
            for out in places:
                out[...] = own_ref[pair, start : start + size]

        for number, other in enumerate(apart_of):

            @pl.when(apart == other)
            def _():
                for out in places:
                    out[...] = received[number][rank]


def select(me, pairs, own, received, apart, start, size, groups):
    pair_count, _, feat = own.shape
    shapes = [
        pltpu.VMEM((pair_count // pieces, size, feat), own.dtype)
        for pieces in groups
        for _ in range(pieces)
    ]
    outs = pl.pallas_call(
        functools.partial(select_kernel, tuple(apart), groups, start),
        out_shape=shapes,
        in_specs=[smem(), smem()] + [vmem()] * (1 + len(received)),
        out_specs=[vmem()] * len(shapes),
        compiler_params=params(4),
        name="select",
    )(me, in_hbm(pairs), *[in_vmem(x) for x in (own, *received)])
    return take_parts(outs, groups)[0]


def tree(parts):
    while len(parts) > 1:
        half = len(parts) // 2
        parts = [parts[i] + parts[i + half] for i in range(half)]
    return parts[0]


def across(left, right):
    return lax.dot_general(
        left, right, (((1,), (1,)), ((), ())), preferred_element_type=jnp.float32
    )


def lane_sum(block):
    square = jnp.square(block.astype(jnp.float32))
    return sum(square[:, at : at + LANES] for at in range(0, square.shape[1], LANES))


def segments(window):
    low, high = window
    held = []
    for chunk, (start, size) in enumerate(CHUNKS):
        first, end = max(low, start), min(high, start + size)
        if first < end:
            held.append((chunk, first - start, end - first))
    return held


def scores(rows, cols, square):
    gram = tree([across(row, col) for row, col in zip(rows, cols)])
    other = jnp.sum(tree([lane_sum(col) for col in cols]).T, axis=0, keepdims=True)
    pieces, mass = [], None
    for at in range(0, gram.shape[1], LANES):
        here = slice(at, at + LANES)
        piece = jnp.exp((square + other[:, here] - 2.0 * gram[:, here]) * (-1.0 / F))
        mass = piece if mass is None else mass + piece
        pieces.append(piece)
    kernel = jnp.concatenate(pieces, axis=1) if len(pieces) > 1 else pieces[0]
    return kernel.astype(jnp.bfloat16), jnp.sum(kernel, axis=0, keepdims=True), mass


def take_parts(refs, counts):
    parts = []
    for count in counts:
        parts.append(refs[:count])
        refs = refs[count:]
    return parts, refs


def of_pair(part, pair):
    each = part[0].shape[0]
    return part[pair // each].at[pair % each]


def window_parts(counts, refs):
    half = len(counts[0]) // 2
    rows, refs = [ref.at[i] for ref in refs[:2] for i in range(half)], refs[2:]
    chunks = []
    for chunk_counts in counts:
        cols, refs = take_parts(refs, chunk_counts)
        chunks.append(cols)
    return rows, chunks


def own_columns(window, chunks, pair):
    held = segments(window)
    pieces = [of_pair(part, pair)[at : at + size] for part, (_, at, size) in zip(chunks, held)]
    return jnp.concatenate(pieces, axis=0) if len(pieces) > 1 else pieces[0]


def pair_parts(window, rows, chunks, pair):
    cols = [own_columns(window, [c[i] for c in chunks], pair) for i in range(len(rows))]
    return [part[pair] for part in rows], cols


def first_kernel(window, counts, *refs):
    square_ref, mass_ref, total_ref, sums_ref = refs[-4:]
    all_rows, chunks = window_parts(counts, refs)
    for pair in range(square_ref.shape[0]):
        rows, cols = pair_parts(window, all_rows, chunks, pair)
        square = jnp.sum(tree([lane_sum(row) for row in rows]), axis=1, keepdims=True)
        square = jnp.broadcast_to(square, (BR, LANES))
        kernel, sums, mass = scores(rows, cols, square)
        square_ref[pair] = square
        mass_ref[pair] = mass
        sums_ref[pair : pair + 1] = sums
        total_ref[pair] = jnp.dot(kernel, cols[0], preferred_element_type=jnp.float32)


def last_kernel(window, counts, wide_count, me_ref, pairs_ref, *refs):
    square_in, mass_in, sums_in = refs[-6 - wide_count : -3 - wide_count]
    kernel_ref, mass_ref, row_ref = refs[-3 - wide_count : -wide_count]
    shares = refs[-wide_count:]
    for ref in (row_ref, *shares):
        ref[...] = jnp.zeros_like(ref)
    all_rows, chunks = window_parts(counts, refs)
    for pair in range(square_in.shape[0]):
        rows, cols = pair_parts(window, all_rows, chunks, pair)
        kernel, sums, mass = scores(rows, cols, square_in[pair])
        kernel_ref[pair] = kernel
        sums = jnp.concatenate([sums_in[pair : pair + 1], sums], axis=1)
        mass = mass_in[pair] + mass
        mass_ref[pair] = mass
        row_ref[pl.ds(pairs_ref[0, pair] & 7, 1)] += jnp.sum(mass.T, axis=0, keepdims=True)
        col = pairs_ref[1, pair]
        apart = (col >> 3) ^ me_ref[0]
        for other, ref in zip([*sum_order(wide_count), 0], shares):
            ref[pl.ds(col & 7, 1)] += jnp.where(apart == other, sums, 0.0)


def estimate(pair_count, size):
    return pl.CostEstimate(
        flops=2 * pair_count * BR * size * F,
        transcendentals=pair_count * BR * size,
        bytes_accessed=8 * 1024 * 1024,
    )


def piece_counts(window, cols):
    return tuple(tuple(len(part) for part in cols[chunk]) for chunk, _, _ in segments(window))


def operands(parts):
    return [piece for part in parts for piece in part]


def first_window(rows, cols):
    _, pair_count, _, feat = rows[0][0].shape
    window = WINDOWS[0]
    lanes = pltpu.VMEM((pair_count, BR, LANES), jnp.float32)
    total = pltpu.VMEM((pair_count, BR, feat), jnp.float32)
    args = operands(rows)
    for chunk, _, _ in segments(window):
        args += operands(cols[chunk])
    return pl.pallas_call(
        functools.partial(first_kernel, window, piece_counts(window, cols)),
        out_shape=[lanes, lanes, total, pltpu.VMEM((pair_count, window[1]), jnp.float32)],
        in_specs=[vmem()] * len(args),
        out_specs=[vmem()] * 4,
        compiler_params=params(16),
        cost_estimate=pl.CostEstimate(flops=0, transcendentals=0, bytes_accessed=0),
        name="first_window",
    )(*[in_vmem(x) for x in args])


def last_window(me, pairs, rows, cols, square, mass, sums, wide_count):
    pair_count = rows[0][0].shape[1]
    window = WINDOWS[1]
    size = window[1] - window[0]
    by_block = pltpu.VMEM((BLK_DEV, BR), jnp.float32)
    shapes = [
        pltpu.VMEM((pair_count, BR, size), jnp.bfloat16),
        pltpu.VMEM((pair_count, BR, LANES), jnp.float32),
    ] + [by_block] * (1 + wide_count)
    args = operands(rows)
    for chunk, _, _ in segments(window):
        args += operands(cols[chunk])
    args += [square, mass, sums]
    kernel, mass, row_sums, *shares = pl.pallas_call(
        functools.partial(last_kernel, window, piece_counts(window, cols), wide_count),
        out_shape=shapes,
        in_specs=[smem(), smem()] + [vmem()] * len(args),
        out_specs=[vmem()] * len(shapes),
        compiler_params=params(16),
        cost_estimate=estimate(pair_count, size),
        name="last_window",
    )(me, in_hbm(pairs), *[in_vmem(x) for x in args])
    return kernel, mass, row_sums, shares


def keep_kernel(pairs_ref, block_ref, blocks_ref, out_ref, own_ref, sems):
    here = pl.program_id(0)

    def copies():
        for pair in range(own_ref.shape[0]):
            source = blocks_ref.at[pairs_ref[1, pair] & 7]
            yield pltpu.make_async_copy(source, own_ref.at[pair], sems.at[pair])

    @pl.when(here == 0)
    def _():
        for copy in copies():
            copy.start()

    out_ref[...] = block_ref[...]

    @pl.when(here == pl.num_programs(0) - 1)
    def _():
        for copy in copies():
            copy.wait()


def keep(pairs, blocks):
    pair_count = pairs.shape[1]
    block = pl.BlockSpec((1, *blocks.shape[1:]), lambda k: (k, 0, 0))
    return pl.pallas_call(
        keep_kernel,
        out_shape=[
            pltpu.HBM(blocks.shape, blocks.dtype),
            pltpu.VMEM((pair_count, *blocks.shape[1:]), blocks.dtype),
        ],
        grid=(blocks.shape[0],),
        in_specs=[smem(), block, anywhere()],
        out_specs=[block, anywhere()],
        scratch_shapes=[pltpu.SemaphoreType.DMA((pair_count,))],
        compiler_params=params(4),
        name="keep",
    )(in_hbm(pairs), in_hbm(blocks), in_hbm(blocks))


def mean_kernel(window, counts, local_ref, rows_ref, kernel_ref, mass_ref, total_ref, *refs):
    *refs, _, out_ref, part, weight, total, mass, made, sems = refs
    chunks = []
    for chunk, _, _ in segments(window):
        (own,), refs = take_parts(refs, counts[len(chunks)][:1])
        chunks.append(own)
    pair_count, _, feat = rows_ref.shape
    local = [local_ref[0, pair] & 7 for pair in range(pair_count)]

    def copy(pair):
        return pltpu.make_async_copy(made.at[pair], out_ref.at[local[pair]], sems.at[pair])

    firsts = []
    for pair in range(pair_count):
        sums = total_ref[pair] + jnp.dot(
            kernel_ref[pair], own_columns(window, chunks, pair), preferred_element_type=jnp.float32
        )
        part[pair] = sums.astype(jnp.bfloat16)
        weight[pair] = jnp.broadcast_to(
            jnp.sum(mass_ref[pair], axis=1, keepdims=True), (BR, LANES)
        )
        same = [local[other] == local[pair] for other in range(pair)]
        firsts.append(jnp.logical_not(functools.reduce(jnp.logical_or, same, jnp.bool_(False))))
    for pair in range(pair_count):

        @pl.when(firsts[pair])
        def _():
            total[...] = rows_ref[pair].astype(jnp.float32) + part[pair].astype(jnp.float32)
            mass[...] = 1.0 + weight[pair]
            for other in range(pair + 1, pair_count):

                @pl.when(local[other] == local[pair])
                def _():
                    total[...] += part[other].astype(jnp.float32)
                    mass[...] += weight[other]

            scale = 1.0 / mass[...]
            for at in range(0, feat, LANES):
                lanes = slice(at, at + LANES)
                made[pair, :, lanes] = (total[:, lanes] * scale).astype(jnp.bfloat16)
            copy(pair).start()

    for pair in range(pair_count):

        @pl.when(firsts[pair])
        def _():
            copy(pair).wait()


def means(pairs, rows, kernel, mass, total, cols, kept):
    pair_count, _, feat = rows.shape
    window = WINDOWS[1]
    own = operands(cols[chunk][0] for chunk, _, _ in segments(window))
    args = [in_vmem(x) for x in (rows, kernel, mass, total, *own)]
    return pl.pallas_call(
        functools.partial(mean_kernel, window, piece_counts(window, cols)),
        out_shape=pltpu.HBM(kept.shape, jnp.bfloat16),
        in_specs=[smem()] + [vmem()] * len(args) + [anywhere()],
        out_specs=anywhere(),
        scratch_shapes=[
            pltpu.VMEM((pair_count, BR, feat), jnp.bfloat16),
            pltpu.VMEM((pair_count, BR, LANES), jnp.float32),
            pltpu.VMEM((BR, feat), jnp.float32),
            pltpu.VMEM((BR, LANES), jnp.float32),
            pltpu.VMEM((pair_count, BR, feat), jnp.bfloat16),
            pltpu.SemaphoreType.DMA((pair_count,)),
        ],
        input_output_aliases={1 + len(args): 0},
        compiler_params=params(16),
        cost_estimate=estimate(pair_count, 128),
        name="means",
    )(in_hbm(pairs), *args, in_hbm(kept))


def weight_kernel(*refs):
    out_ref = refs[-1]
    mass = refs[0][...]
    for ref in refs[1:-1]:
        mass = mass + ref[...]
    weight = 1.0 / (1.0 + mass / BR)
    parts = BR // LANES
    for block in range(BLK_DEV):
        for part in range(parts):
            lanes = slice(part * LANES, (part + 1) * LANES)
            out_ref[block * parts + part : block * parts + part + 1] = weight[block : block + 1, lanes]


def block_weights(sums):
    out = pl.pallas_call(
        weight_kernel,
        out_shape=jax.ShapeDtypeStruct((BLK_DEV * BR // LANES, LANES), jnp.float32),
        in_specs=[vmem()] * len(sums),
        out_specs=vmem(),
        compiler_params=params(4),
        name="weights",
    )(*[in_vmem(x) for x in sums])
    return out.reshape(BLK_DEV * BR)


def hop(parts, step):
    count = lax.axis_size("narrow")
    perm = [(i, i ^ step) for i in range(count)]
    return [[lax.ppermute(piece, "narrow", perm) for piece in part] for part in parts]


def first_hops(part):
    parts = [part]
    step = lax.axis_size("narrow") // 2
    while step > 1:
        parts = parts + hop(parts, step)
        step //= 2
    return parts


def to_wide(pieces, apart):
    count = lax.axis_size("wide")
    return [
        lax.ppermute(piece, "wide", [(i, i ^ other) for i in range(count)])
        for piece, other in zip(pieces, apart)
    ]


def on_device(embeddings, pair_list):
    wide_count = lax.axis_size("wide")
    me = lax.axis_index("wide").astype(jnp.int32).reshape(1)
    pairs = pair_list.T
    pair_count = pairs.shape[1]
    capacity = max(2, 2 * pair_count // wide_count)
    feat = embeddings.shape[1]
    blocks = embeddings.reshape(BLK_DEV, BR, feat)
    apart = others(wide_count)
    lists = to_wide([pairs] * (wide_count - 1), apart[::-1])
    fixed = lax.optimization_barrier
    *outgoing, row_slices = pack(me, pairs, lists, blocks, capacity, 0, True)
    later = pack(me, pairs, lists, blocks, capacity, 1, False)

    def pick(received, apart, chunk, *groups):
        return select(me, pairs, own, received, apart, *CHUNKS[chunk], groups)

    def halves(part):
        middle = pair_count // 2
        return [part[0][:middle], part[0][middle:]]

    rows = jnp.stack([part[0] for part in first_hops([row_slices])])
    received = to_wide(outgoing, apart)
    near = to_wide(later[-1:], apart[-1:])
    rows, received, near, (kept, own) = fixed((rows, received, near, keep(pairs, blocks)))
    own_a, whole_a = pick(received, apart, 0, 2, 1)
    cols_a = [own_a] + first_hops(whole_a)[1:]
    rows = [[rows], *hop([[rows]], 1)]
    back = apart[:-1][::-1]
    cols_a, rows, received = fixed((cols_a, rows, to_wide(later[:-1][::-1], back)))
    cols_b = first_hops(*pick([*received, *near], [*back, apart[-1]], 1, 1))
    last_b = hop(cols_b[:1], 1)
    cols_a = cols_a + hop([own_a] + [halves(part) for part in cols_a[1:]], 1)
    carry = first_window(rows, [cols_a])
    cols_b, carry = fixed((cols_b, carry))
    cols_b = cols_b + last_b + hop(cols_b[1:], 1)
    square, mass, total, sums = carry
    kernel, mass, row_sums, shares = last_window(
        me, pairs, rows, [cols_a, cols_b], square, mass, sums, wide_count
    )
    came = to_wide(shares[:-1], sum_order(wide_count))
    mean = means(pairs, row_slices, kernel, mass, total, [cols_a, cols_b], kept)
    weights = block_weights([row_sums, shares[-1], *came])
    return weights, mean.reshape(BLK_DEV * BR, feat)


def solution(mesh):
    in_specs = (P(("groups", "wide"), "narrow"), P(("groups", "wide"), None))
    out_specs = (P(("groups", "wide")), P(("groups", "wide"), "narrow"))
    return jax.shard_map(
        on_device, mesh=mesh, in_specs=in_specs, out_specs=out_specs, check_vma=False
    )
```

```python
import functools

import jax
import jax.numpy as jnp
from jax import lax
from jax.experimental import pallas as pl
from jax.experimental.pallas import tpu as pltpu
from jax.sharding import PartitionSpec as P

F = 1024
BR = 512
BLK_DEV = 8
LANES = 128
CHUNKS = ((0, 336), (336, 176))
WINDOWS = ((0, 256), (256, 512))


def smem():
    return pl.BlockSpec(memory_space=pltpu.SMEM)


def vmem():
    return pl.BlockSpec(memory_space=pltpu.VMEM)


def anywhere():
    return pl.BlockSpec(memory_space=pl.ANY)


def in_vmem(x):
    return pltpu.with_memory_space_constraint(x, pltpu.VMEM)


def in_hbm(x):
    return pltpu.with_memory_space_constraint(x, pltpu.HBM)


def params(mebibytes):
    return pltpu.CompilerParams(vmem_limit_bytes=mebibytes * 1024 * 1024)


def others(wide_count):
    return range(wide_count - 1, 0, -1)


def pack_kernel(chunk, with_rows, wide_count, pair_count, capacity, me_ref, pairs_ref, *refs):
    lists, blocks_ref = refs[: wide_count - 1], refs[wide_count - 1]
    *outs, sems = refs[wide_count:]
    me = me_ref[0]
    start, size = CHUNKS[chunk]
    copies = []

    def send(source, target):
        copies.append(pltpu.make_async_copy(source, target, sems.at[len(copies)]))
        copies[-1].start()

    for number, other in enumerate(others(wide_count)):
        asked = lists[list_order(wide_count).index(other)]
        picks = [jnp.int32(0)] * capacity
        count = jnp.int32(0)
        for pair in range(pair_count):
            col = asked[1, pair]
            mine = (col >> 3) == me
            for slot in range(capacity):
                picks[slot] = jnp.where(mine & (count == slot), col & 7, picks[slot])
            count = count + mine.astype(jnp.int32)
        for slot in range(capacity):
            send(blocks_ref.at[picks[slot], pl.ds(start, size)], outs[number].at[slot])
    if with_rows:
        for pair in range(pair_count):
            send(blocks_ref.at[pairs_ref[0, pair] & 7], outs[-1].at[pair])
    for copy in copies:
        copy.wait()


def list_order(wide_count):
    middle = wide_count // 2
    return [other for other in range(1, wide_count) if other != middle] + [middle]


def sum_order(wide_count):
    return list_order(wide_count)[::-1]


def pack(me, pairs, lists, blocks, capacity, chunk, with_rows):
    wide_count, pair_count = len(lists) + 1, pairs.shape[1]
    feat = blocks.shape[-1]
    shapes = [pltpu.VMEM((capacity, CHUNKS[chunk][1], feat), blocks.dtype)] * (wide_count - 1)
    copies = len(shapes) * capacity
    if with_rows:
        shapes.append(pltpu.VMEM((pair_count, BR, feat), blocks.dtype))
        copies += pair_count
    return pl.pallas_call(
        functools.partial(pack_kernel, chunk, with_rows, wide_count, pair_count, capacity),
        out_shape=shapes,
        in_specs=[smem()] * (1 + wide_count) + [anywhere()],
        out_specs=[anywhere()] * len(shapes),
        scratch_shapes=[pltpu.SemaphoreType.DMA((copies,))],
        compiler_params=params(4),
        name="pack",
    )(me, in_hbm(pairs), *[lists[other - 1] for other in list_order(wide_count)], in_hbm(blocks))


def select_kernel(wide_count, groups, start, me_ref, pairs_ref, own_ref, *refs):
    pair_count = own_ref.shape[0]
    outs = refs[wide_count - 1 :]
    received = refs[: wide_count - 1]
    size = outs[0].shape[1]
    owners = [pairs_ref[1, pair] >> 3 for pair in range(pair_count)]
    for pair in range(pair_count):
        apart = me_ref[0] ^ owners[pair]
        rank = jnp.int32(0)
        for before in range(pair):
            rank = rank + (owners[before] == owners[pair]).astype(jnp.int32)

        places, rest = [], outs
        for pieces in groups:
            places.append(of_pair(rest[:pieces], pair))
            rest = rest[pieces:]

        @pl.when(apart == 0)
        def _():
            for out in places:
                out[...] = own_ref[pair, start : start + size]

        for number, other in enumerate(others(wide_count)):

            @pl.when(apart == other)
            def _():
                for out in places:
                    out[...] = received[number][rank]


def select(me, pairs, own, received, start, size, groups):
    pair_count, _, feat = own.shape
    shapes = [
        pltpu.VMEM((pair_count // pieces, size, feat), own.dtype)
        for pieces in groups
        for _ in range(pieces)
    ]
    outs = pl.pallas_call(
        functools.partial(select_kernel, len(received) + 1, groups, start),
        out_shape=shapes,
        in_specs=[smem(), smem()] + [vmem()] * (1 + len(received)),
        out_specs=[vmem()] * len(shapes),
        compiler_params=params(4),
        name="select",
    )(me, in_hbm(pairs), *[in_vmem(x) for x in (own, *received)])
    return take_parts(outs, groups)[0]


def tree(parts):
    while len(parts) > 1:
        half = len(parts) // 2
        parts = [parts[i] + parts[i + half] for i in range(half)]
    return parts[0]


def across(left, right):
    return lax.dot_general(
        left, right, (((1,), (1,)), ((), ())), preferred_element_type=jnp.float32
    )


def lane_sum(block):
    square = jnp.square(block.astype(jnp.float32))
    return sum(square[:, at : at + LANES] for at in range(0, square.shape[1], LANES))


def segments(window):
    low, high = window
    held = []
    for chunk, (start, size) in enumerate(CHUNKS):
        first, end = max(low, start), min(high, start + size)
        if first < end:
            held.append((chunk, first - start, end - first))
    return held


def scores(rows, cols, square):
    gram = tree([across(row, col) for row, col in zip(rows, cols)])
    other = jnp.sum(tree([lane_sum(col) for col in cols]).T, axis=0, keepdims=True)
    pieces, mass = [], None
    for at in range(0, gram.shape[1], LANES):
        here = slice(at, at + LANES)
        piece = jnp.exp((square + other[:, here] - 2.0 * gram[:, here]) * (-1.0 / F))
        mass = piece if mass is None else mass + piece
        pieces.append(piece)
    kernel = jnp.concatenate(pieces, axis=1) if len(pieces) > 1 else pieces[0]
    return kernel.astype(jnp.bfloat16), jnp.sum(kernel, axis=0, keepdims=True), mass


def take_parts(refs, counts):
    parts = []
    for count in counts:
        parts.append(refs[:count])
        refs = refs[count:]
    return parts, refs


def of_pair(part, pair):
    each = part[0].shape[0]
    return part[pair // each].at[pair % each]


def window_parts(counts, refs):
    half = len(counts[0]) // 2
    rows, refs = [ref.at[i] for ref in refs[:2] for i in range(half)], refs[2:]
    chunks = []
    for chunk_counts in counts:
        cols, refs = take_parts(refs, chunk_counts)
        chunks.append(cols)
    return rows, chunks


def own_columns(window, chunks, pair):
    held = segments(window)
    pieces = [of_pair(part, pair)[at : at + size] for part, (_, at, size) in zip(chunks, held)]
    return jnp.concatenate(pieces, axis=0) if len(pieces) > 1 else pieces[0]


def pair_parts(window, rows, chunks, pair):
    cols = [own_columns(window, [c[i] for c in chunks], pair) for i in range(len(rows))]
    return [part[pair] for part in rows], cols


def first_kernel(window, counts, *refs):
    square_ref, mass_ref, total_ref, sums_ref = refs[-4:]
    all_rows, chunks = window_parts(counts, refs)
    for pair in range(square_ref.shape[0]):
        rows, cols = pair_parts(window, all_rows, chunks, pair)
        square = jnp.sum(tree([lane_sum(row) for row in rows]), axis=1, keepdims=True)
        square = jnp.broadcast_to(square, (BR, LANES))
        kernel, sums, mass = scores(rows, cols, square)
        square_ref[pair] = square
        mass_ref[pair] = mass
        sums_ref[pair : pair + 1] = sums
        total_ref[pair] = jnp.dot(kernel, cols[0], preferred_element_type=jnp.float32)


def last_kernel(window, counts, wide_count, me_ref, pairs_ref, *refs):
    square_in, mass_in, sums_in = refs[-6 - wide_count : -3 - wide_count]
    kernel_ref, mass_ref, row_ref = refs[-3 - wide_count : -wide_count]
    shares = refs[-wide_count:]
    for ref in (row_ref, *shares):
        ref[...] = jnp.zeros_like(ref)
    all_rows, chunks = window_parts(counts, refs)
    each = LANES // square_in.shape[0]
    lane = lax.broadcasted_iota(jnp.int32, (BR, LANES), 1)
    for pair in range(square_in.shape[0]):
        rows, cols = pair_parts(window, all_rows, chunks, pair)
        kernel, sums, mass = scores(rows, cols, square_in[pair])
        kernel_ref[pair] = kernel
        sums = jnp.concatenate([sums_in[pair : pair + 1], sums], axis=1)
        mass = mass_in[pair] + mass
        mass = jnp.broadcast_to(jnp.sum(mass, axis=1, keepdims=True), (BR, LANES))
        mass_ref[pair] = mass
        packed = mass if pair == 0 else jnp.where(lane >= pair * each, mass, packed)
        col = pairs_ref[1, pair]
        apart = (col >> 3) ^ me_ref[0]
        for other, ref in zip([*sum_order(wide_count), 0], shares):
            ref[pl.ds(col & 7, 1)] += jnp.where(apart == other, sums, 0.0)
    lines = packed.T
    for pair in range(square_in.shape[0]):
        row_ref[pl.ds(pairs_ref[0, pair] & 7, 1)] += lines[pair * each : pair * each + 1]


def estimate(pair_count, size):
    return pl.CostEstimate(
        flops=2 * pair_count * BR * size * F,
        transcendentals=pair_count * BR * size,
        bytes_accessed=8 * 1024 * 1024,
    )


def piece_counts(window, cols):
    return tuple(tuple(len(part) for part in cols[chunk]) for chunk, _, _ in segments(window))


def operands(parts):
    return [piece for part in parts for piece in part]


def first_window(rows, cols):
    _, pair_count, _, feat = rows[0][0].shape
    window = WINDOWS[0]
    lanes = pltpu.VMEM((pair_count, BR, LANES), jnp.float32)
    total = pltpu.VMEM((pair_count, BR, feat), jnp.float32)
    args = operands(rows)
    for chunk, _, _ in segments(window):
        args += operands(cols[chunk])
    return pl.pallas_call(
        functools.partial(first_kernel, window, piece_counts(window, cols)),
        out_shape=[lanes, lanes, total, pltpu.VMEM((pair_count, window[1]), jnp.float32)],
        in_specs=[vmem()] * len(args),
        out_specs=[vmem()] * 4,
        compiler_params=params(16),
        cost_estimate=pl.CostEstimate(flops=0, transcendentals=0, bytes_accessed=0),
        name="first_window",
    )(*[in_vmem(x) for x in args])


def last_window(me, pairs, rows, cols, square, mass, sums, wide_count):
    pair_count = rows[0][0].shape[1]
    window = WINDOWS[1]
    size = window[1] - window[0]
    by_block = pltpu.VMEM((BLK_DEV, BR), jnp.float32)
    shapes = [
        pltpu.VMEM((pair_count, BR, size), jnp.bfloat16),
        pltpu.VMEM((pair_count, BR, LANES), jnp.float32),
    ] + [by_block] * (1 + wide_count)
    args = operands(rows)
    for chunk, _, _ in segments(window):
        args += operands(cols[chunk])
    args += [square, mass, sums]
    kernel, mass, row_sums, *shares = pl.pallas_call(
        functools.partial(last_kernel, window, piece_counts(window, cols), wide_count),
        out_shape=shapes,
        in_specs=[smem(), smem()] + [vmem()] * len(args),
        out_specs=[vmem()] * len(shapes),
        compiler_params=params(16),
        cost_estimate=estimate(pair_count, size),
        name="last_window",
    )(me, in_hbm(pairs), *[in_vmem(x) for x in args])
    return kernel, mass, row_sums, shares


def keep_kernel(pairs_ref, block_ref, blocks_ref, out_ref, own_ref, sems):
    here = pl.program_id(0)

    def copies():
        for pair in range(own_ref.shape[0]):
            source = blocks_ref.at[pairs_ref[1, pair] & 7]
            yield pltpu.make_async_copy(source, own_ref.at[pair], sems.at[pair])

    @pl.when(here == 0)
    def _():
        for copy in copies():
            copy.start()

    out_ref[...] = block_ref[...]

    @pl.when(here == pl.num_programs(0) - 1)
    def _():
        for copy in copies():
            copy.wait()


def keep(pairs, blocks):
    pair_count = pairs.shape[1]
    block = pl.BlockSpec((1, *blocks.shape[1:]), lambda k: (k, 0, 0))
    return pl.pallas_call(
        keep_kernel,
        out_shape=[
            pltpu.HBM(blocks.shape, blocks.dtype),
            pltpu.VMEM((pair_count, *blocks.shape[1:]), blocks.dtype),
        ],
        grid=(blocks.shape[0],),
        in_specs=[smem(), block, anywhere()],
        out_specs=[block, anywhere()],
        scratch_shapes=[pltpu.SemaphoreType.DMA((pair_count,))],
        compiler_params=params(4),
        name="keep",
    )(in_hbm(pairs), in_hbm(blocks), in_hbm(blocks))


def mean_kernel(window, counts, local_ref, rows_ref, kernel_ref, mass_ref, total_ref, *refs):
    *refs, _, out_ref, part, weight, total, mass, made, sems = refs
    chunks = []
    for chunk, _, _ in segments(window):
        (own,), refs = take_parts(refs, counts[len(chunks)][:1])
        chunks.append(own)
    pair_count, _, feat = rows_ref.shape
    local = [local_ref[0, pair] & 7 for pair in range(pair_count)]

    def copy(pair):
        return pltpu.make_async_copy(made.at[pair], out_ref.at[local[pair]], sems.at[pair])

    firsts = []
    for pair in range(pair_count):
        sums = total_ref[pair] + jnp.dot(
            kernel_ref[pair], own_columns(window, chunks, pair), preferred_element_type=jnp.float32
        )
        part[pair] = sums.astype(jnp.bfloat16)
        weight[pair] = mass_ref[pair]
        same = [local[other] == local[pair] for other in range(pair)]
        firsts.append(jnp.logical_not(functools.reduce(jnp.logical_or, same, jnp.bool_(False))))
    for pair in range(pair_count):

        @pl.when(firsts[pair])
        def _():
            total[...] = rows_ref[pair].astype(jnp.float32) + part[pair].astype(jnp.float32)
            mass[...] = 1.0 + weight[pair]
            for other in range(pair + 1, pair_count):

                @pl.when(local[other] == local[pair])
                def _():
                    total[...] += part[other].astype(jnp.float32)
                    mass[...] += weight[other]

            scale = 1.0 / mass[...]
            for at in range(0, feat, LANES):
                lanes = slice(at, at + LANES)
                made[pair, :, lanes] = (total[:, lanes] * scale).astype(jnp.bfloat16)
            copy(pair).start()

    for pair in range(pair_count):

        @pl.when(firsts[pair])
        def _():
            copy(pair).wait()


def means(pairs, rows, kernel, mass, total, cols, kept):
    pair_count, _, feat = rows.shape
    window = WINDOWS[1]
    own = operands(cols[chunk][0] for chunk, _, _ in segments(window))
    args = [in_vmem(x) for x in (rows, kernel, mass, total, *own)]
    return pl.pallas_call(
        functools.partial(mean_kernel, window, piece_counts(window, cols)),
        out_shape=pltpu.HBM(kept.shape, jnp.bfloat16),
        in_specs=[smem()] + [vmem()] * len(args) + [anywhere()],
        out_specs=anywhere(),
        scratch_shapes=[
            pltpu.VMEM((pair_count, BR, feat), jnp.bfloat16),
            pltpu.VMEM((pair_count, BR, LANES), jnp.float32),
            pltpu.VMEM((BR, feat), jnp.float32),
            pltpu.VMEM((BR, LANES), jnp.float32),
            pltpu.VMEM((pair_count, BR, feat), jnp.bfloat16),
            pltpu.SemaphoreType.DMA((pair_count,)),
        ],
        input_output_aliases={1 + len(args): 0},
        compiler_params=params(16),
        cost_estimate=estimate(pair_count, 128),
        name="means",
    )(in_hbm(pairs), *args, in_hbm(kept))


def weight_kernel(*refs):
    out_ref = refs[-1]
    mass = refs[0][...]
    for ref in refs[1:-1]:
        mass = mass + ref[...]
    weight = 1.0 / (1.0 + mass / BR)
    parts = BR // LANES
    for block in range(BLK_DEV):
        for part in range(parts):
            lanes = slice(part * LANES, (part + 1) * LANES)
            out_ref[block * parts + part : block * parts + part + 1] = weight[block : block + 1, lanes]


def block_weights(sums):
    out = pl.pallas_call(
        weight_kernel,
        out_shape=jax.ShapeDtypeStruct((BLK_DEV * BR // LANES, LANES), jnp.float32),
        in_specs=[vmem()] * len(sums),
        out_specs=vmem(),
        compiler_params=params(4),
        name="weights",
    )(*[in_vmem(x) for x in sums])
    return out.reshape(BLK_DEV * BR)


def hop(parts, step):
    count = lax.axis_size("narrow")
    perm = [(i, i ^ step) for i in range(count)]
    return [[lax.ppermute(piece, "narrow", perm) for piece in part] for part in parts]


def first_hops(part):
    parts = [part]
    step = lax.axis_size("narrow") // 2
    while step > 1:
        parts = parts + hop(parts, step)
        step //= 2
    return parts


def to_wide(pieces, apart):
    count = lax.axis_size("wide")
    return [
        lax.ppermute(piece, "wide", [(i, i ^ other) for i in range(count)])
        for piece, other in zip(pieces, apart)
    ]


def on_device(embeddings, pair_list):
    wide_count = lax.axis_size("wide")
    me = lax.axis_index("wide").astype(jnp.int32).reshape(1)
    pairs = pair_list.T
    pair_count = pairs.shape[1]
    capacity = max(2, 2 * pair_count // wide_count)
    feat = embeddings.shape[1]
    blocks = embeddings.reshape(BLK_DEV, BR, feat)
    apart = others(wide_count)
    lists = to_wide([pairs] * (wide_count - 1), apart[::-1])
    fixed = lax.optimization_barrier
    *outgoing, row_slices = pack(me, pairs, lists, blocks, capacity, 0, True)
    later = pack(me, pairs, lists, blocks, capacity, 1, False)

    def pick(received, chunk, *groups):
        return select(me, pairs, own, received, *CHUNKS[chunk], groups)

    def halves(part):
        middle = pair_count // 2
        return [part[0][:middle], part[0][middle:]]

    rows = jnp.stack([part[0] for part in first_hops([row_slices])])
    received = to_wide(outgoing, apart)
    near = to_wide(later[-1:], apart[-1:])
    rows, received, near, (kept, own) = fixed((rows, received, near, keep(pairs, blocks)))
    own_a, whole_a = pick(received, 0, 2, 1)
    cols_a = [own_a] + first_hops(whole_a)[1:]
    rows = [[rows], *hop([[rows]], 1)]
    cols_a, rows, received = fixed((cols_a, rows, to_wide(later[:-1], apart[:-1])))
    cols_b = first_hops(*pick([*received, *near], 1, 1))
    last_b = hop(cols_b[:1], 1)
    cols_a = cols_a + hop([own_a] + [halves(part) for part in cols_a[1:]], 1)
    carry = first_window(rows, [cols_a])
    cols_b, carry = fixed((cols_b, carry))
    cols_b = cols_b + last_b + hop(cols_b[1:], 1)
    square, mass, total, sums = carry
    kernel, mass, row_sums, shares = last_window(
        me, pairs, rows, [cols_a, cols_b], square, mass, sums, wide_count
    )
    came = to_wide(shares[:-1], sum_order(wide_count))
    mean = means(pairs, row_slices, kernel, mass, total, [cols_a, cols_b], kept)
    weights = block_weights([row_sums, shares[-1], *came])
    return weights, mean.reshape(BLK_DEV * BR, feat)


def solution(mesh):
    in_specs = (P(("groups", "wide"), "narrow"), P(("groups", "wide"), None))
    out_specs = (P(("groups", "wide")), P(("groups", "wide"), "narrow"))
    return jax.shard_map(
        on_device, mesh=mesh, in_specs=in_specs, out_specs=out_specs, check_vma=False
    )
```
